32 devices in a mesh: groups: 2 (over x), grid: 16 (over z, y, core).
Axes of the slice: x: 2, y: 2, z: 4, core: 2. Of those that a mesh axis runs over, the one named last changes fastest.
Arguments:
- hist: float32 [768, 256, 256], P('groups', 'grid'), parts along dimension 0, may hold values from 0.2 to 2
- drift: float32 [2, 256, 256], P(None, 'grid'), may hold values from -0.5 to 0.5
- shocks: int32 [768, 2], P('groups'), parts along dimension 0, may hold values from 0 to 7
- shock_table: float32 [16, 2], P('groups'), parts along dimension 0, may hold values from -0.3 to 0.3
- first_weight: bfloat16 [131072, 2048], P(('groups', 'grid')), parts along dimension 0, may hold values from -0.03125 to 0.03125
- mid_weight: bfloat16 [4096, 2048], P('groups', 'grid'), parts along dimension 0, may hold values from -0.1875 to 0.1875
- head_weight: float32 [4096], P(('groups', 'grid')), parts along dimension 0, may hold values from -0.125 to 0.125
- cotangent: float32 [768], P('groups'), parts along dimension 0, may hold values from -6 to 6
Outputs:
- hist_next: float32 [768, 256, 256], P('groups', 'grid'), parts along dimension 0
- value: float32 [768], P('groups'), parts along dimension 0
- grad_first: bfloat16 [131072, 2048], P(('groups', 'grid')), parts along dimension 0
- grad_mid: bfloat16 [4096, 2048], P('groups', 'grid'), parts along dimension 0
- grad_head: float32 [4096], P(('groups', 'grid')), parts along dimension 0
The draws below stay inside these ranges and needn't reach their ends.
There are 2 independent parts, one for each index of `groups`. The reference program is written for one: setup_inputs(seed, part) draws one part's arguments, and reference() takes and returns one part's arrays. A program takes and returns all parts, laid end to end along the dimension named above; an argument that names none is the same for every part. Nothing has to cross between parts.
All inputs are finite; a program needn't handle non-finite values.
Results may differ from the reference program's by a relative error of at most 0.0173.
Values may be sent and summed in bfloat16 or wider, within the bound.
No kernel may reach another device: no remote copies, remote signals or barrier semaphores. Data moves between devices by JAX's collectives and lax.ppermute only.
A program may use at most 128 MiB of HBM per device.

```python
import math
import jax
import jax.numpy as jnp
from jax import lax

G = 256
HID = 2048
S = 384
STEPS = 2
NSHOCK = 8
CELLS = 65536


def set_ends(result, key, low, high):
    longest = result.shape.index(max(result.shape))
    spots = []
    for shift in (0, 1):
        where = [jax.random.randint(jax.random.fold_in(key, axis), (), 0, length) for axis, length in enumerate(result.shape)]
        where[longest] = (where[longest] + shift) % result.shape[longest]
        spots.append(tuple(where))
    return result.at[spots[0]].set(low).at[spots[1]].set(high)


def raised(values, stream_key, source, target, parts, factor):
    owner, partner = [(jnp.arange(values.shape[dim]) // (values.shape[dim] // parts)).reshape([-1 if axis == dim else 1 for axis in range(values.ndim)]) for dim in (source, target)]
    chosen = jax.random.permutation(stream_key, parts)[partner]
    strong = (owner == chosen) | (owner == (partner + parts // 2) % parts)
    return jnp.where(strong, factor * values, values)


def levels(stream_key, extent, shards, smallest, top_value):
    factor_of = 1.0
    for axis_at, blocks in shards:
        heights = jax.random.uniform(jax.random.fold_in(jax.random.fold_in(stream_key, 6), axis_at), (blocks,), jnp.float32, smallest / len(shards), top_value / len(shards))
        factor_of = factor_of * jnp.repeat(jnp.exp(heights), extent[axis_at] // blocks).reshape((-1,) + (1,) * (len(extent) - 1 - axis_at))
    return factor_of


def bell_draw(key, extent, width, reach, shards=(), kind=jnp.bfloat16):
    drawn = width * jax.random.normal(key, extent, jnp.float32)
    if shards:
        drawn = drawn * levels(key, extent, shards, -0.22, 0.18)
    return jnp.clip(drawn, -reach, reach).astype(kind)


def bell_draw_with(own_key, shape, deviation, bound, shards, heavy, kind=jnp.bfloat16):
    drawn = deviation * jax.random.normal(own_key, shape, jnp.float32)
    if shards:
        drawn = drawn * levels(own_key, shape, shards, -0.22, 0.18)
    return jnp.clip(raised(drawn, jax.random.fold_in(own_key, 3), *heavy), -bound, bound).astype(kind)


def setup_inputs(seed: int = 0, part: int = 0) -> dict:
    key_of = jax.random.split(jax.random.key(seed), 9)
    own_keys = jax.random.split(jax.random.fold_in(key_of[8], part), 9)
    hist = jnp.clip(jnp.exp(math.log(2.0) - 2.3025851 * jax.random.uniform(own_keys[0], (S, G, G), jnp.float32) ** levels(own_keys[0], (S, G, G), ((1, 16),), -0.2, 0.2)), 0.2, 2.0)
    drift = jnp.clip(jax.random.uniform(key_of[1], (2, G, G), jnp.float32, -0.5, 0.5) * levels(key_of[1], (2, G, G), ((1, 16),), -0.4, 0.0), -0.5, 0.5)
    shocks = set_ends(jax.random.randint(own_keys[2], (S, STEPS), 0, NSHOCK), jax.random.fold_in(own_keys[2], 1), 0, NSHOCK - 1).astype(jnp.int32)
    shock_table = jnp.clip(jax.random.uniform(own_keys[3], (NSHOCK, 2), jnp.float32, -0.3, 0.3), -0.3, 0.3)
    first_weight = bell_draw_with(own_keys[4], (CELLS, HID), CELLS ** -0.5, 0.03125, ((0, 16),), (0, 1, 16, 2.0))
    mid_weight = bell_draw_with(own_keys[5], (HID, HID), HID ** -0.5, 0.1875, ((1, 16),), (1, 0, 16, 2.0))
    head_weight = bell_draw(own_keys[6], (HID,), HID ** -0.5, 0.125, ((0, 16),), jnp.float32)
    cotangent = bell_draw(own_keys[7], (S,), 1.0, 6.0, (), jnp.float32)
    return dict(hist=hist, drift=drift, shocks=shocks, shock_table=shock_table, first_weight=first_weight, mid_weight=mid_weight, head_weight=head_weight, cotangent=cotangent)


diffusion_rate = 0.24


def column_shift(values, offset):
    zero_col = jnp.zeros_like(values[..., :1])
    if offset > 0:
        return jnp.concatenate([values[..., 1:], zero_col], axis=-1)
    return jnp.concatenate([zero_col, values[..., :-1]], axis=-1)


def shock_shift(levels_now, table):
    level_ids = jnp.arange(table.shape[0], dtype=jnp.int32)
    onehot = (levels_now[:, None] == level_ids[None, :]).astype(jnp.float32)
    return jnp.sum(onehot[:, :, None] * table[None, :, :], axis=1)


def kfe_step(padded, drift_rows, shift_x, shift_y):
    velocity_x = drift_rows[0][None] + shift_x[:, None, None]
    velocity_y = drift_rows[1][1:-1][None] + shift_y[:, None, None]
    flux_x = velocity_x * padded
    centre = padded[:, 1:-1]
    flux_y = velocity_y * centre
    spread = padded[:, 2:] + padded[:, :-2] + column_shift(centre, 1) + column_shift(centre, -1) - 4.0 * centre
    carried = 0.5 * (flux_x[:, 2:] - flux_x[:, :-2]) + 0.5 * (column_shift(flux_y, 1) - column_shift(flux_y, -1))
    return centre + diffusion_rate * spread - carried


def reference(hist, drift, shocks, shock_table, first_weight, mid_weight, head_weight, cotangent):
    density = hist
    drift_pad = jnp.pad(drift, ((0, 0), (1, 1), (0, 0)))
    for section_no in range(STEPS):
        shifts = shock_shift(shocks[:, section_no], shock_table)
        padded = jnp.pad(density, ((0, 0), (1, 1), (0, 0)))
        density = kfe_step(padded, drift_pad, shifts[:, 0], shifts[:, 1])
    inputs = density.astype(jnp.bfloat16).reshape(S, G * G)
    first = jnp.tanh(jnp.dot(inputs, first_weight, preferred_element_type=jnp.float32)).astype(jnp.bfloat16)
    second = jnp.tanh(jnp.dot(first, mid_weight, preferred_element_type=jnp.float32)).astype(jnp.bfloat16)
    second_f = second.astype(jnp.float32)
    value = jnp.dot(second_f, head_weight, precision=lax.Precision.HIGHEST)
    grad_head = jnp.dot(cotangent, second_f, precision=lax.Precision.HIGHEST)
    back_second = (cotangent[:, None] * head_weight[None, :] * (1.0 - second_f * second_f)).astype(jnp.bfloat16)
    grad_mid = jnp.dot(first.T, back_second, preferred_element_type=jnp.float32).astype(jnp.bfloat16)
    back_raw = jnp.dot(back_second, mid_weight.T, preferred_element_type=jnp.float32)
    first_f = first.astype(jnp.float32)
    back_first = (back_raw * (1.0 - first_f * first_f)).astype(jnp.bfloat16)
    grad_first = jnp.dot(inputs.T, back_first, preferred_element_type=jnp.float32).astype(jnp.bfloat16)
    return density, value, grad_first, grad_mid, grad_head
```

```python
import functools
import jax
import jax.numpy as jnp
from jax import lax
from jax.experimental import pallas as pl
from jax.experimental.pallas import tpu as pltpu
from jax.sharding import PartitionSpec as P

diffusion_rate = 0.24
VMEM_BYTES = 48 * 1024 * 1024
EXTRA = 16
bf16 = jnp.bfloat16
f32 = jnp.float32


def params():
    return pltpu.CompilerParams(vmem_limit_bytes=VMEM_BYTES)


def scenario_block(scenarios):
    for size in (64, 32, 16):
        if scenarios % size == 0:
            return size
    return scenarios


LANES = 128
SUBLANES = 8
GROUP = 16


def to_tiles(hist):
    scenarios, rows, columns = hist.shape
    high = min(rows, SUBLANES)
    tiles = hist.reshape(scenarios, rows // high, high, columns // LANES, LANES)
    return tiles.transpose(0, 1, 3, 2, 4).reshape(scenarios * rows * (columns // LANES), LANES)


def from_tiles(tiles, shape):
    scenarios, rows, columns = shape
    high = min(rows, SUBLANES)
    parts = tiles.reshape(scenarios, rows // high, columns // LANES, high, LANES)
    return parts.transpose(0, 1, 3, 2, 4).reshape(shape)


def tile_offset(row, lane_tile, rows, lane_tiles):
    high = min(rows, SUBLANES)
    return (row // high * lane_tiles + lane_tile) * high + row % high


def read_row(ref, first_scenario, count, row, rows, columns):
    lane_tiles = columns // LANES
    per = rows * lane_tiles
    return jnp.concatenate(
        [
            ref[pl.ds(first_scenario * per + tile_offset(row, t, rows, lane_tiles), count, stride=per), :]
            for t in range(lane_tiles)
        ],
        axis=1,
    )


def write_row(ref, first_scenario, count, row, rows, columns, values):
    lane_tiles = columns // LANES
    per = rows * lane_tiles
    for t in range(lane_tiles):
        place = pl.ds(first_scenario * per + tile_offset(row, t, rows, lane_tiles), count, stride=per)
        ref[place, :] = values[:, t * LANES : (t + 1) * LANES]


def edge_kernel(rows, size, hist_ref, drift_ref, first_ref, last_ref):
    step = pl.program_id(0)
    columns = drift_ref.shape[2]

    @pl.when(step == 0)
    def _():
        for out, start in ((first_ref, 0), (last_ref, rows - 2)):
            pieces = [
                jnp.concatenate([drift_ref[c, start : start + 1], drift_ref[c, start + 1 : start + 2]], axis=1)
                for c in range(2)
            ]
            exact = jnp.concatenate(pieces, axis=0)
            high = exact.astype(bf16)
            low = (exact - high.astype(f32)).astype(bf16)
            ones = jnp.ones((1, 2 * columns), bf16)
            zeros = jnp.zeros((EXTRA - 5, 2 * columns), bf16)
            out[pl.ds(out.shape[0] - EXTRA, EXTRA), :] = jnp.concatenate([high, low, ones, zeros], axis=0)

    where = pl.ds(pl.multiple_of(step * size, size), size)
    for out, start in ((first_ref, 0), (last_ref, rows - 2)):
        for k in range(2):
            out[where, pl.ds(k * columns, columns)] = read_row(hist_ref, 0, size, start + k, rows, columns).astype(bf16)


def edges(tiles, drift, scenarios):
    rows, columns = drift.shape[1:]
    per = tiles.shape[0] // scenarios
    size = scenario_block(scenarios)
    shape = jax.ShapeDtypeStruct((scenarios + EXTRA, 2 * columns), bf16)
    spec = pl.BlockSpec(shape.shape, lambda i: (0, 0))
    return pl.pallas_call(
        functools.partial(edge_kernel, rows, size),
        grid=(scenarios // size,),
        in_specs=[
            pl.BlockSpec((size * per, LANES), lambda i: (i, 0)),
            pl.BlockSpec(drift.shape, lambda i: (0, 0, 0)),
        ],
        out_specs=[spec, spec],
        out_shape=[shape, shape],
        compiler_params=params(),
        name="edge_rows",
    )(tiles, drift)


def stencil_kernel(rows, size, hist_ref, below_ref, above_ref, alpha_ref, valid_ref, shift_ref, next_ref, inputs_ref):
    columns = alpha_ref.shape[2]
    column = lax.broadcasted_iota(jnp.int32, (GROUP, columns), 1)
    not_first = column > 0
    not_last = column < columns - 1

    def sweep(values, first_row, shift_x, shift_y):
        up, down = [], []
        for k, density in enumerate(values):
            at = first_row + k + 2
            rising = density * (alpha_ref[0, at : at + 1, :] + shift_x)
            up.append(rising)
            down.append(2.0 * diffusion_rate * density - rising)
        results = []
        for k in range(1, len(values) - 1):
            density = values[k]
            at = first_row + k + 2
            rising = density * (alpha_ref[1, at : at + 1, :] + shift_y)
            falling = 2.0 * diffusion_rate * density - rising
            from_left = jnp.where(not_first, pltpu.roll(rising, 1, 1), 0.0)
            from_right = jnp.where(not_last, pltpu.roll(falling, columns - 1, 1), 0.0)
            results.append(
                (1.0 - 4.0 * diffusion_rate) * density + up[k - 1] + down[k + 1] + from_left + from_right
            )
        return results

    def group(g, carry):
        base = pl.multiple_of(g * GROUP, GROUP)
        shifts = shift_ref[pl.ds(base, GROUP), :]
        sh = [jnp.broadcast_to(shifts[:, k : k + 1], (GROUP, columns)) for k in range(4)]
        values = []
        for k in range(2):
            values.append(below_ref[pl.ds(base, GROUP), pl.ds(k * columns, columns)].astype(f32))
        for r in range(rows):
            values.append(read_row(hist_ref, base, GROUP, r, rows, columns))
        for k in range(2):
            values.append(above_ref[pl.ds(base, GROUP), pl.ds(k * columns, columns)].astype(f32))
        middle = sweep(values, -2, sh[0], sh[1])
        middle[0] = middle[0] * valid_ref[0, 0]
        middle[-1] = middle[-1] * valid_ref[0, 1]
        final = sweep(middle, -1, sh[2], sh[3])
        for r in range(rows):
            write_row(next_ref, base, GROUP, r, rows, columns, final[r])
            inputs_ref[pl.ds(base, GROUP), pl.ds(r * columns, columns)] = final[r].astype(bf16)
        return carry

    lax.fori_loop(0, size // GROUP, group, 0)


def stencil(tiles, below, above, alpha, valid, shift):
    scenarios = shift.shape[0]
    rows, columns = alpha.shape[1] - 4, alpha.shape[2]
    per = tiles.shape[0] // scenarios
    size = scenario_block(scenarios)
    block = pl.BlockSpec((size * per, LANES), lambda i: (i, 0))
    halo = pl.BlockSpec((size, 2 * columns), lambda i: (i, 0))
    return pl.pallas_call(
        functools.partial(stencil_kernel, rows, size),
        grid=(scenarios // size,),
        in_specs=[
            block,
            halo,
            halo,
            pl.BlockSpec(alpha.shape, lambda i: (0, 0, 0)),
            pl.BlockSpec(memory_space=pltpu.SMEM),
            pl.BlockSpec((size, 4), lambda i: (i, 0)),
        ],
        out_specs=[block, pl.BlockSpec((size, rows * columns), lambda i: (i, 0))],
        out_shape=[
            jax.ShapeDtypeStruct(tiles.shape, f32),
            jax.ShapeDtypeStruct((scenarios, rows * columns), bf16),
        ],
        compiler_params=params(),
        name="density_steps",
    )(tiles, below, above, alpha, valid, shift)


def middle_kernel(first_ref, mid_ref, head_ref, cot_ref, second_ref, back_ref, head_grad_ref, value_ref):
    parts, scenarios, width = first_ref.shape
    total = jnp.zeros((scenarios, mid_ref.shape[1]), f32)
    for p in range(parts):
        total += jnp.dot(first_ref[p], mid_ref[pl.ds(p * width, width), :], preferred_element_type=f32)
    second = jnp.tanh(total).astype(bf16).astype(f32)
    head = head_ref[...]
    cot = cot_ref[...]
    head_grad_ref[...] = jnp.sum(cot * second, axis=0, keepdims=True)
    value_ref[...] = jnp.sum(second * head, axis=1, keepdims=True)
    back = (cot * head * (1.0 - second * second)).astype(bf16)
    second_ref[...] = back
    for p in range(parts):
        back_ref[p] = lax.dot_general(
            back, mid_ref[pl.ds(p * width, width), :], (((1,), (1,)), ((), ())), preferred_element_type=f32
        ).astype(bf16)


def middle(first3, mid_weight, head, cot):
    parts, scenarios, width = first3.shape
    units = mid_weight.shape[1]
    return pl.pallas_call(
        middle_kernel,
        out_shape=[
            jax.ShapeDtypeStruct((scenarios, units), bf16),
            jax.ShapeDtypeStruct((parts, scenarios, width), bf16),
            jax.ShapeDtypeStruct((1, units), f32),
            jax.ShapeDtypeStruct((scenarios, 1), f32),
        ],
        compiler_params=params(),
        name="value_layers",
    )(first3, mid_weight, head, cot)


def mid_grad_kernel(first_ref, back_ref, out_ref):
    parts, scenarios, width = first_ref.shape
    for p in range(parts):
        out_ref[pl.ds(p * width, width), :] = lax.dot_general(
            first_ref[p], back_ref[...], (((0,), (0,)), ((), ())), preferred_element_type=f32
        ).astype(bf16)


def mid_grad(first3, back):
    parts, scenarios, width = first3.shape
    return pl.pallas_call(
        mid_grad_kernel,
        out_shape=jax.ShapeDtypeStruct((parts * width, back.shape[1]), bf16),
        compiler_params=params(),
        name="mid_gradient",
    )(first3, back)


def first_grad_kernel(inputs_ref, back_ref, out_ref):
    parts, _, width = back_ref.shape
    group = max(1, 256 // width)
    left = inputs_ref[...].T
    for p in range(0, parts, group):
        right = jnp.concatenate([back_ref[p + k] for k in range(group)], axis=1)
        out_ref[:, pl.ds(p * width, group * width)] = jnp.dot(left, right, preferred_element_type=f32).astype(bf16)


def first_grad(inputs, back3):
    scenarios, cells = inputs.shape
    parts, _, width = back3.shape
    size = min(cells, 512)
    return pl.pallas_call(
        first_grad_kernel,
        grid=(cells // size,),
        in_specs=[
            pl.BlockSpec((scenarios, size), lambda i: (0, i)),
            pl.BlockSpec(back3.shape, lambda i: (0, 0, 0)),
        ],
        out_specs=pl.BlockSpec((size, parts * width), lambda i: (i, 0)),
        out_shape=jax.ShapeDtypeStruct((cells, parts * width), bf16),
        compiler_params=params(),
        name="first_gradient",
    )(inputs, back3)


def shock_shift(levels_now, table):
    level_ids = lax.iota(jnp.int32, table.shape[0])
    onehot = (levels_now[:, None] == level_ids[None, :]).astype(f32)
    return jnp.sum(onehot[:, :, None] * table[None, :, :], axis=1)


def local(hist, drift, shocks, shock_table, first_weight, mid_weight, head_weight, cotangent):
    scenarios, rows, columns = hist.shape
    count = lax.axis_size("grid")
    hidden = first_weight.shape[1]
    width = hidden // count
    tiles = to_tiles(hist)

    first_rows, last_rows = edges(tiles, drift, scenarios)
    forward = [(i, i + 1) for i in range(count - 1)]
    backward = [(i + 1, i) for i in range(count - 1)]
    below = lax.ppermute(last_rows, "grid", forward)
    above = lax.ppermute(first_rows, "grid", backward)

    def drift_rows(payload):
        tail = payload[scenarios : scenarios + 4].astype(f32)
        return (tail[:2] + tail[2:]).reshape(2, 2, columns)

    drift_ext = jnp.concatenate([drift_rows(below), drift, drift_rows(above)], axis=1)
    alpha = diffusion_rate + 0.5 * drift_ext
    valid = jnp.stack([below[scenarios + 4, 0], above[scenarios + 4, 0]]).astype(f32).reshape(1, 2)
    shift = jnp.concatenate([0.5 * shock_shift(shocks[:, t], shock_table) for t in range(shocks.shape[1])], axis=1)
    density, inputs = stencil(tiles, below, above, alpha, valid, shift)

    partial = jnp.dot(inputs, first_weight, preferred_element_type=f32).astype(bf16)
    first_pre = lax.psum_scatter(partial, "grid", scatter_dimension=1, tiled=True)
    first_mine = jnp.tanh(first_pre.astype(f32)).astype(bf16)
    first3 = lax.all_gather(first_mine, "grid")
    back_second, back_part, grad_head, value_part = middle(
        first3, mid_weight, head_weight[None, :], cotangent[:, None]
    )
    back_raw = lax.psum_scatter(back_part, "grid", scatter_dimension=0)
    grad_mid = mid_grad(first3, back_second)
    first_f = first_mine.astype(f32)
    back_mine = (back_raw.astype(f32) * (1.0 - first_f * first_f)).astype(bf16)
    value = lax.psum(value_part[:, 0], "grid")
    back3 = lax.all_gather(back_mine, "grid")
    grad_first = first_grad(inputs, back3)
    return from_tiles(density, hist.shape), value, grad_first, grad_mid, grad_head[0]


def solution(mesh):
    in_specs = (
        P("groups", "grid", None),
        P(None, "grid", None),
        P("groups", None),
        P("groups", None),
        P(("groups", "grid"), None),
        P("groups", "grid"),
        P(("groups", "grid")),
        P("groups"),
    )
    out_specs = (
        P("groups", "grid", None),
        P("groups"),
        P(("groups", "grid"), None),
        P("groups", "grid"),
        P(("groups", "grid")),
    )
    return jax.shard_map(local, mesh=mesh, in_specs=in_specs, out_specs=out_specs, check_vma=False)
```

```python
import functools
import jax
import jax.numpy as jnp
from jax import lax
from jax.experimental import pallas as pl
from jax.experimental.pallas import tpu as pltpu
from jax.sharding import PartitionSpec as P

diffusion_rate = 0.24
VMEM_BYTES = 48 * 1024 * 1024
EXTRA = 16
bf16 = jnp.bfloat16
f32 = jnp.float32


def params():
    return pltpu.CompilerParams(vmem_limit_bytes=VMEM_BYTES)


def scenario_block(scenarios):
    for size in (64, 32, 16):
        if scenarios % size == 0:
            return size
    return scenarios


LANES = 128
SUBLANES = 8
GROUP = 16
CHUNKS = 1


def to_tiles(hist):
    scenarios, rows, columns = hist.shape
    high = min(rows, SUBLANES)
    tiles = hist.reshape(scenarios, rows // high, high, columns // LANES, LANES)
    return tiles.transpose(0, 1, 3, 2, 4).reshape(scenarios * rows * (columns // LANES), LANES)


def from_tiles(tiles, shape):
    scenarios, rows, columns = shape
    high = min(rows, SUBLANES)
    parts = tiles.reshape(scenarios, rows // high, columns // LANES, high, LANES)
    return parts.transpose(0, 1, 3, 2, 4).reshape(shape)


def tile_offset(row, lane_tile, rows, lane_tiles):
    high = min(rows, SUBLANES)
    return (row // high * lane_tiles + lane_tile) * high + row % high


def read_row(ref, first_scenario, count, row, rows, columns):
    lane_tiles = columns // LANES
    per = rows * lane_tiles
    return jnp.concatenate(
        [
            ref[pl.ds(first_scenario * per + tile_offset(row, t, rows, lane_tiles), count, stride=per), :]
            for t in range(lane_tiles)
        ],
        axis=1,
    )


def write_row(ref, first_scenario, count, row, rows, columns, values):
    lane_tiles = columns // LANES
    per = rows * lane_tiles
    for t in range(lane_tiles):
        place = pl.ds(first_scenario * per + tile_offset(row, t, rows, lane_tiles), count, stride=per)
        ref[place, :] = values[:, t * LANES : (t + 1) * LANES]


def drift_tail(drift_ref, start):
    pieces = [
        jnp.concatenate([drift_ref[c, start : start + 1], drift_ref[c, start + 1 : start + 2]], axis=1)
        for c in range(2)
    ]
    high, low = two_halves(jnp.concatenate(pieces, axis=0))
    ones = jnp.ones((1, high.shape[1]), bf16)
    zeros = jnp.zeros((EXTRA - 5, high.shape[1]), bf16)
    return jnp.concatenate([high, low, ones, zeros], axis=0)


def half_shifts(levels, table_ref):
    results = []
    for t in range(levels.shape[1]):
        level = jnp.broadcast_to(levels[:, t : t + 1], (levels.shape[0], LANES))
        for c in range(2):
            shift = jnp.zeros(level.shape, f32)
            for n in range(table_ref.shape[0]):
                shift = jnp.where(level == n, 0.5 * table_ref[n, c], shift)
            results.append(shift)
    return results


def sweep_rows(read, coefficient, first, last, shift_x, shift_y, columns):
    lane_tiles = columns // LANES
    wide_x = jnp.concatenate([shift_x] * lane_tiles, axis=1)
    wide_y = jnp.concatenate([shift_y] * lane_tiles, axis=1)
    column = lax.broadcasted_iota(jnp.int32, wide_x.shape, 1)
    twice = 2.0 * diffusion_rate
    before = now = None
    for row in range(first, last + 1):
        density = read(row)
        up = density * (coefficient(0, row) + wide_x)
        coming = (density, up, twice * density - up)
        if before is not None:
            middle = now[0]
            rising = middle * (coefficient(1, row - 1) + wide_y)
            falling = twice * middle - rising
            from_left = jnp.where(column > 0, pltpu.roll(rising, 1, 1), 0.0)
            from_right = jnp.where(column < columns - 1, pltpu.roll(falling, columns - 1, 1), 0.0)
            result = (1.0 - 2.0 * twice) * middle + (before[1] + coming[2]) + (from_left + from_right)
            yield row - 1, result
        before, now = now, coming


def two_steps(read, coefficient, edge, first, last, shifts, columns, write):
    middle = sweep_rows(read, coefficient, first - 2, last + 2, shifts[0], shifts[1], columns)

    def read_middle(row):
        at, density = next(middle)
        assert at == row
        return edge(row, density)

    for row, density in sweep_rows(read_middle, coefficient, first - 1, last + 1, shifts[2], shifts[3], columns):
        write(row, density)


def inner_kernel(
    rows, size, hist_ref, drift_ref, levels_ref, table_ref, first_ref, next_ref, prev_ref, last_ref, inner_ref, work
):
    step = pl.program_id(0)
    columns = drift_ref.shape[2]

    @pl.when(step == 0)
    def _():
        for out, start in ((first_ref, 0), (last_ref, rows - 2)):
            out[pl.ds(out.shape[0] - EXTRA, EXTRA), :] = drift_tail(drift_ref, start)

    where = pl.ds(pl.multiple_of(step * size, size), size)
    for out, start in ((first_ref, 0), (next_ref, 2), (prev_ref, rows - 4), (last_ref, rows - 2)):
        for k in range(2):
            out[where, pl.ds(k * columns, columns)] = read_row(hist_ref, 0, size, start + k, rows, columns).astype(bf16)
    if rows <= 4:
        return

    def coefficient(c, row):
        return diffusion_rate + 0.5 * drift_ref[c, row : row + 1, :]

    def group(g, carry):
        base = pl.multiple_of(g * GROUP, GROUP)
        for half in range(GROUP // SUBLANES):
            at = base + half * SUBLANES
            shifts = half_shifts(levels_ref[pl.ds(pl.multiple_of(at, SUBLANES), SUBLANES), :], table_ref)

            def write(row, density):
                work[pl.ds(half * SUBLANES, SUBLANES), pl.ds((row - 2) * columns, columns)] = density

            two_steps(
                lambda row: read_row(hist_ref, at, SUBLANES, row, rows, columns),
                coefficient,
                lambda row, density: density,
                2,
                rows - 3,
                shifts,
                columns,
                write,
            )
        inner_ref[pl.ds(base, GROUP), :] = work[...].astype(bf16)
        return carry

    lax.fori_loop(0, size // GROUP, group, 0)


def inner_steps(tiles, drift, shocks, table):
    scenarios = shocks.shape[0]
    rows, columns = drift.shape[1:]
    per = tiles.shape[0] // scenarios
    size = scenario_block(scenarios)
    inner = max(rows - 4, 1) * columns
    edge = jax.ShapeDtypeStruct((scenarios, 2 * columns), bf16)
    sent = jax.ShapeDtypeStruct((scenarios + EXTRA, 2 * columns), bf16)
    whole = [pl.BlockSpec(shape.shape, lambda i: (0, 0)) for shape in (sent, edge, edge, sent)]
    return pl.pallas_call(
        functools.partial(inner_kernel, rows, size),
        grid=(scenarios // size,),
        in_specs=[
            pl.BlockSpec((size * per, LANES), lambda i: (i, 0)),
            pl.BlockSpec(drift.shape, lambda i: (0, 0, 0)),
            pl.BlockSpec((size, shocks.shape[1]), lambda i: (i, 0)),
            smem(),
        ],
        out_specs=whole + [pl.BlockSpec((size, inner), lambda i: (i, 0))],
        out_shape=[sent, edge, edge, sent, jax.ShapeDtypeStruct((scenarios, inner), bf16)],
        scratch_shapes=[pltpu.VMEM((GROUP, inner), f32)],
        compiler_params=params(),
        cost_estimate=pl.CostEstimate(flops=1, bytes_accessed=1, transcendentals=0),
        name="inner_density_steps",
    )(tiles, drift, shocks, table)


def halo_drift(ref, columns):
    tail = ref[pl.ds(ref.shape[0] - EXTRA, EXTRA), :].astype(f32)
    rows = [[tail[c : c + 1, k * columns : (k + 1) * columns] + tail[2 + c : 3 + c, k * columns : (k + 1) * columns] for k in range(2)] for c in range(2)]
    return rows, tail[4:5, :columns]


def coefficients(drift_ref, below, above, rows):
    def coefficient(c, row):
        if row < 0:
            drift = below[c][row + 2]
        elif row >= rows:
            drift = above[c][row - rows]
        else:
            drift = drift_ref[c, row : row + 1, :]
        return diffusion_rate + 0.5 * drift

    return coefficient


def edge_kernel(
    size, drift_ref, levels_ref, table_ref, first_ref, next_ref, prev_ref, last_ref, below_ref, above_ref, *refs
):
    low_ref, high_ref, work = refs[-3:]
    step = pl.program_id(0)
    rows, columns = drift_ref.shape[1:]
    below, below_valid = halo_drift(below_ref, columns)
    above, above_valid = halo_drift(above_ref, columns)
    coefficient = coefficients(drift_ref, below, above, rows)

    def edge(row, density):
        if row < 0:
            return density * below_valid
        if row >= rows:
            return density * above_valid
        return density

    start = pl.multiple_of(step * size, size)

    def group(g, carry):
        base = pl.multiple_of(g * GROUP, GROUP)
        every = pl.ds(pl.multiple_of(start + base, GROUP), GROUP)
        for out, refs, first in (
            (low_ref, (below_ref, first_ref, next_ref), 0),
            (high_ref, (prev_ref, last_ref, above_ref), rows - 2),
        ):
            wide = [ref[every, :].astype(f32) for ref in refs]
            for half in range(GROUP // SUBLANES):
                part = slice(half * SUBLANES, (half + 1) * SUBLANES)
                levels = levels_ref[pl.ds(pl.multiple_of(base + half * SUBLANES, SUBLANES), SUBLANES), :]

                def read(row):
                    at = row - (first - 2)
                    return wide[at // 2][part, at % 2 * columns : (at % 2 + 1) * columns]

                def write(row, density):
                    work[part, pl.ds((row - first) * columns, columns)] = density

                two_steps(
                    read, coefficient, edge, first, first + 1, half_shifts(levels, table_ref), columns, write
                )
            out[pl.ds(base, GROUP), :] = work[...].astype(bf16)
        return carry

    lax.fori_loop(0, size // GROUP, group, 0)


def edge_steps(drift, shocks, table, own, below, above, deps):
    scenarios = shocks.shape[0]
    columns = drift.shape[2]
    size = scenario_block(scenarios)
    edge = jax.ShapeDtypeStruct((scenarios, 2 * columns), bf16)
    spec = pl.BlockSpec((size, 2 * columns), lambda i: (i, 0))
    return pl.pallas_call(
        functools.partial(edge_kernel, size),
        grid=(scenarios // size,),
        in_specs=[
            pl.BlockSpec(drift.shape, lambda i: (0, 0, 0)),
            pl.BlockSpec((size, shocks.shape[1]), lambda i: (i, 0)),
            smem(),
        ]
        + [pl.BlockSpec(ref.shape, lambda i: (0, 0)) for ref in (*own, below, above)]
        + any_specs(deps),
        out_specs=[spec, spec],
        out_shape=[edge, edge],
        scratch_shapes=[pltpu.VMEM((GROUP, 2 * columns), f32)],
        compiler_params=params(),
        cost_estimate=pl.CostEstimate(flops=1, bytes_accessed=1, transcendentals=0),
        name="edge_density_steps",
    )(drift, shocks, table, *own, below, above, *deps)


def density_kernel(
    rows, size, first_step, hist_ref, drift_ref, levels_ref, table_ref, below_ref, above_ref, dep_ref, *refs
):
    next_ref = refs[-1]
    columns = drift_ref.shape[2]
    below, below_valid = halo_drift(below_ref, columns)
    above, above_valid = halo_drift(above_ref, columns)
    coefficient = coefficients(drift_ref, below, above, rows)
    start = (first_step + pl.program_id(0)) * size

    def edge(row, density):
        if row < 0:
            return density * below_valid
        if row >= rows:
            return density * above_valid
        return density

    def group(g, carry):
        base = pl.multiple_of(g * GROUP, GROUP)
        every = pl.ds(pl.multiple_of(start + base, GROUP), GROUP)
        wide = [ref[every, :].astype(f32) for ref in (below_ref, above_ref)]
        for half in range(GROUP // SUBLANES):
            part = slice(half * SUBLANES, (half + 1) * SUBLANES)
            at = pl.multiple_of(base + half * SUBLANES, SUBLANES)

            def read(row):
                if row < 0:
                    return wide[0][part, (row + 2) * columns : (row + 3) * columns]
                if row >= rows:
                    return wide[1][part, (row - rows) * columns : (row - rows + 1) * columns]
                return read_row(hist_ref, at, SUBLANES, row, rows, columns)

            shifts = half_shifts(levels_ref[pl.ds(at, SUBLANES), :], table_ref)
            two_steps(
                read,
                coefficient,
                edge,
                0,
                rows - 1,
                shifts,
                columns,
                lambda row, density: write_row(next_ref, at, SUBLANES, row, rows, columns, density),
            )
        return carry

    lax.fori_loop(0, size // GROUP, group, 0)


def density_steps(tiles, drift, shocks, table, below, above, dep, so_far, turn, turns):
    scenarios = shocks.shape[0]
    rows, columns = drift.shape[1:]
    per = tiles.shape[0] // scenarios
    size = GROUP * 2 if scenarios % (turns * GROUP * 2) == 0 else GROUP
    steps = scenarios // size // turns
    first = turn * steps
    block = pl.BlockSpec((size * per, LANES), lambda i: (first + i, 0))
    hidden = pl.BlockSpec(memory_space=pl.ANY)
    args = [tiles, drift, shocks, table, below, above, dep]
    in_specs = [
        block,
        pl.BlockSpec(drift.shape, lambda i: (0, 0, 0)),
        pl.BlockSpec((size, shocks.shape[1]), lambda i: (first + i, 0)),
        smem(),
        pl.BlockSpec(below.shape, lambda i: (0, 0)),
        pl.BlockSpec(above.shape, lambda i: (0, 0)),
        hidden,
    ]
    aliases = {}
    if so_far is not None:
        args.append(so_far)
        in_specs.append(hidden)
        aliases = {7: 0}
    return pl.pallas_call(
        functools.partial(density_kernel, rows, size, first),
        grid=(steps,),
        in_specs=in_specs,
        out_specs=block,
        out_shape=jax.ShapeDtypeStruct(tiles.shape, f32),
        input_output_aliases=aliases,
        compiler_params=params(),
        cost_estimate=pl.CostEstimate(flops=1, bytes_accessed=1, transcendentals=0),
        name="density_steps",
    )(*args)


def smem():
    return pl.BlockSpec(memory_space=pltpu.SMEM)


def swap(values, count, flip):
    return lax.ppermute(values, "grid", [(i, i ^ flip) for i in range(count)])


def inner_product_kernel(count, dep_count, *refs):
    inputs_ref = refs[0]
    weights = refs[1 : 1 + count]
    weight = jnp.concatenate([ref[...] for ref in weights], axis=0)
    refs[-1][0] = jnp.dot(inputs_ref[...], weight, preferred_element_type=f32)


def inner_product(inner, weight, width, deps):
    scenarios, cells = inner.shape
    total, hidden = weight.shape
    size = (total - cells) // 2
    count = cells // size
    hidden_spec = pl.BlockSpec(memory_space=pl.ANY)

    def spec(k):
        return pl.BlockSpec((size, width), lambda n: (1 + k, n))

    return pl.pallas_call(
        functools.partial(inner_product_kernel, count, len(deps)),
        grid=(hidden // width,),
        in_specs=[pl.BlockSpec(inner.shape, lambda n: (0, 0))]
        + [spec(k) for k in range(count)]
        + [hidden_spec] * len(deps),
        out_specs=pl.BlockSpec((1, scenarios, width), lambda n: (n, 0, 0)),
        out_shape=jax.ShapeDtypeStruct((hidden // width, scenarios, width), f32),
        compiler_params=params(),
        cost_estimate=pl.CostEstimate(flops=1, bytes_accessed=1, transcendentals=0),
        name="inner_product",
    )(inner, *([weight] * count), *deps)


def edge_product_kernel(block, with_inner, place_ref, low_ref, high_ref, top_ref, bottom_ref, *refs):
    keep_ref, send_ref, total = refs[-3:]
    left = jnp.concatenate([low_ref[...], high_ref[...]], axis=1)
    weight = jnp.concatenate([top_ref[...], bottom_ref[...]], axis=0)
    product = jnp.dot(left, weight, preferred_element_type=f32)
    total[...] = product + refs[0][0] if with_inner else product
    core = place_ref[0]
    for out, half in ((keep_ref, core), (send_ref, 1 - core)):
        for side in range(2):
            start = pl.multiple_of((2 * half + side) * block, block)
            out[side, 0] = total[pl.ds(start, block), :].astype(out.dtype)


def edge_product(place, low, high, weight, inner, parts, width, chunk):
    scenarios, size = low.shape
    block = scenarios // 4
    last = weight.shape[0] // size - 1
    shape = (2, parts, block, width)
    spec = pl.BlockSpec((2, 1, block, width), lambda n: (0, n, 0, 0))
    in_specs = [
        smem(),
        pl.BlockSpec(low.shape, lambda n: (0, 0)),
        pl.BlockSpec(low.shape, lambda n: (0, 0)),
        pl.BlockSpec((size, width), lambda n: (0, chunk * parts + n)),
        pl.BlockSpec((size, width), lambda n: (last, chunk * parts + n)),
    ]
    args = [place, low, high, weight, weight]
    if inner is not None:
        in_specs.append(pl.BlockSpec((1, scenarios, width), lambda n: (chunk * parts + n, 0, 0)))
        args.append(inner)
    return pl.pallas_call(
        functools.partial(edge_product_kernel, block, inner is not None),
        grid=(parts,),
        in_specs=in_specs,
        out_specs=[spec, spec],
        out_shape=[jax.ShapeDtypeStruct(shape, f32), jax.ShapeDtypeStruct(shape, bf16)],
        scratch_shapes=[pltpu.VMEM((scenarios, width), f32)],
        compiler_params=params(),
        cost_estimate=pl.CostEstimate(flops=1, bytes_accessed=1, transcendentals=0),
        name="edge_product",
    )(*args)


def add_side_kernel(place_ref, mine_ref, other_ref, *refs):
    keep_ref, send_ref = refs[-2:]
    side = place_ref[1]
    keep_ref[...] = mine_ref[side] + other_ref[side].astype(f32)
    send_ref[...] = (mine_ref[1 - side] + other_ref[1 - side].astype(f32)).astype(bf16)


def any_specs(deps):
    return [pl.BlockSpec(memory_space=pl.ANY)] * len(deps)


def add_side(place, mine, other, deps=()):
    shape = mine.shape[1:]
    return pl.pallas_call(
        add_side_kernel,
        in_specs=[smem()] + [pl.BlockSpec(memory_space=pltpu.VMEM)] * 2 + any_specs(deps),
        out_shape=[jax.ShapeDtypeStruct(shape, f32), jax.ShapeDtypeStruct(shape, bf16)],
        compiler_params=params(),
        cost_estimate=pl.CostEstimate(flops=1, bytes_accessed=1, transcendentals=0),
        name="add_side",
    )(place, mine, other, *deps)


def add_parts_kernel(dep_count, place_ref, mine_ref, other_ref, *refs):
    own_ref, *send_refs = refs[dep_count:]
    part = place_ref[2]
    own_ref[...] = mine_ref[part] + other_ref[part].astype(f32)
    for k, out in enumerate(send_refs):
        at = part ^ (k + 1)
        out[...] = (mine_ref[at] + other_ref[at].astype(f32)).astype(bf16)


def add_parts(place, mine, other, deps=()):
    parts = mine.shape[0]
    vmem = pl.BlockSpec(memory_space=pltpu.VMEM)
    return pl.pallas_call(
        functools.partial(add_parts_kernel, len(deps)),
        in_specs=[smem(), vmem, vmem] + any_specs(deps),
        out_shape=[jax.ShapeDtypeStruct(mine.shape[1:], f32)]
        + [jax.ShapeDtypeStruct(mine.shape[1:], bf16)] * (parts - 1),
        compiler_params=params(),
        cost_estimate=pl.CostEstimate(flops=1, bytes_accessed=1, transcendentals=0),
        name="add_parts",
    )(place, mine, other, *deps)


def activate_kernel(count, *refs):
    total = refs[0][...]
    for ref in refs[1 : 1 + count]:
        total = total + ref[...].astype(f32)
    refs[-1][...] = jnp.tanh(total).astype(bf16)


def activate(own, received, deps=()):
    return pl.pallas_call(
        functools.partial(activate_kernel, len(received)),
        in_specs=[pl.BlockSpec(memory_space=pltpu.VMEM)] * (1 + len(received)) + any_specs(deps),
        out_shape=jax.ShapeDtypeStruct(own.shape, bf16),
        compiler_params=params(),
        cost_estimate=pl.CostEstimate(flops=1, bytes_accessed=1, transcendentals=0),
        name="first_activation",
    )(own, *received, *deps)


def two_halves(exact):
    high = exact.astype(bf16)
    low = (exact - high.astype(f32)).astype(bf16)
    return high, low


def tail_rows(exact):
    high, low = two_halves(exact)
    zeros = jnp.zeros((EXTRA - 2, exact.shape[1]), bf16)
    return jnp.concatenate([high, low, zeros], axis=0)


def middle_kernel(chunks, parts, width, *refs):
    pieces = chunks * parts
    place_ref, cot_ref = refs[0], refs[1]
    first_refs = refs[2 : 2 + pieces]
    mid_refs = refs[2 + pieces : 6 + pieces]
    weight_refs = refs[6 + pieces : 10 + pieces]
    outs = refs[-(3 + parts) :]
    back_ref, own_ref, value_ref, head_ref = outs[:4]
    send_refs = outs[4:]
    part = place_ref[2]
    block = cot_ref.shape[0]

    def mid_rows(start):
        return jnp.concatenate([ref[pl.ds(start, width), :] for ref in mid_refs], axis=1)

    def start_of(c, k):
        return pl.multiple_of((c * parts + (part ^ k)) * width, width)

    total = None
    for c in range(chunks):
        for k in range(parts):
            term = jnp.dot(first_refs[c * parts + k][...], mid_rows(start_of(c, k)), preferred_element_type=f32)
            total = term if total is None else total + term
    second_low = jnp.tanh(total).astype(bf16)
    second = second_low.astype(f32)
    head = jnp.concatenate([ref[...] for ref in weight_refs], axis=1)
    heads = tail_rows(head)
    rows = lax.dot_general(heads, second_low, (((1,), (1,)), ((), ())), preferred_element_type=f32)
    value = rows[0:1] + rows[1:2]
    if width > block:
        value = jnp.concatenate([value, jnp.zeros((1, width - block), f32)], axis=1)
    value_ref[...] = value
    cot = cot_ref[...]
    head_ref[...] = jnp.sum(cot * second, axis=0, keepdims=True)
    back = (cot * head * (1.0 - second * second)).astype(bf16)
    back_ref[...] = back
    for k in range(parts):
        for c in range(chunks):
            piece = lax.dot_general(
                back, mid_rows(start_of(c, k)), (((1,), (1,)), ((), ())), preferred_element_type=f32
            )
            if k == 0:
                own_ref[pl.ds(c * block, block), :] = piece
            else:
                send_refs[k - 1][pl.ds(c * block, block), :] = piece.astype(bf16)
        if k > 0:
            send_refs[k - 1][pl.ds(chunks * block, EXTRA), :] = tail_rows(value)


def middle(place, cot, firsts, mids, heads, chunks, parts, width, deps=()):
    block = cot.shape[0]
    units = 4 * mids[0].shape[1]
    vmem = pl.BlockSpec(memory_space=pltpu.VMEM)
    return pl.pallas_call(
        functools.partial(middle_kernel, chunks, parts, width),
        in_specs=[smem()] + [vmem] * (1 + len(firsts) + 8) + any_specs(deps),
        out_shape=[
            jax.ShapeDtypeStruct((block, units), bf16),
            jax.ShapeDtypeStruct((chunks * block, width), f32),
            jax.ShapeDtypeStruct((1, width), f32),
            jax.ShapeDtypeStruct((1, units), f32),
        ]
        + [jax.ShapeDtypeStruct((chunks * block + EXTRA, width), bf16)] * (parts - 1),
        compiler_params=params(),
        cost_estimate=pl.CostEstimate(flops=1, bytes_accessed=1, transcendentals=0),
        name="value_layers",
    )(place, cot, *firsts, *mids, *heads, *deps)


def mid_grad_kernel(chunks, parts, width, *refs):
    pieces = chunks * parts
    place_ref, back_ref, head_ref = refs[:3]
    first_refs = refs[3 : 3 + pieces]
    keep_ref, send_ref = refs[-2:]
    part = place_ref[2]
    units = back_ref.shape[1] // 4
    for c in range(chunks):
        for k in range(parts):
            start = pl.multiple_of((c * parts + (part ^ k)) * width, width)
            product = lax.dot_general(
                first_refs[c * parts + k][...],
                back_ref[...],
                (((0,), (0,)), ((), ())),
                preferred_element_type=f32,
            ).astype(bf16)
            for p in range(4):
                out = (keep_ref, send_ref)[p % 2]
                out[p // 2, pl.ds(start, width), :] = product[:, p * units : (p + 1) * units]
    for p in range(4):
        out = (keep_ref, send_ref)[p % 2]
        out[p // 2, pl.ds(pieces * width, EXTRA), :] = tail_rows(head_ref[:, p * units : (p + 1) * units])


def mid_grad(place, back, head, firsts, chunks, parts, width, deps=()):
    units = back.shape[1] // 4
    vmem = pl.BlockSpec(memory_space=pltpu.VMEM)
    shape = jax.ShapeDtypeStruct((2, chunks * parts * width + EXTRA, units), bf16)
    return pl.pallas_call(
        functools.partial(mid_grad_kernel, chunks, parts, width),
        in_specs=[smem()] + [vmem] * (2 + len(firsts)) + any_specs(deps),
        out_shape=[shape, shape],
        compiler_params=params(),
        cost_estimate=pl.CostEstimate(flops=1, bytes_accessed=1, transcendentals=0),
        name="mid_gradient",
    )(place, back, head, *firsts, *deps)


def add_tail(left, right, hidden):
    body = left[:hidden].astype(f32) + right[:hidden].astype(f32)
    tails = left[hidden:].astype(f32) + right[hidden:].astype(f32)
    return body.astype(bf16), tails[0:1] + tails[1:2]


def mid_add_kernel(keep_ref, other_ref, *refs):
    own_ref, send_ref = refs[-2:]
    hidden = own_ref.shape[0] - EXTRA
    for at, out in enumerate((own_ref, send_ref)):
        body, tail = add_tail(keep_ref[at], other_ref[at], hidden)
        out[pl.ds(0, hidden), :] = body
        out[pl.ds(hidden, EXTRA), :] = tail_rows(tail)


def mid_add(keep, other, deps=()):
    shape = jax.ShapeDtypeStruct(keep.shape[1:], bf16)
    return pl.pallas_call(
        mid_add_kernel,
        in_specs=[pl.BlockSpec(memory_space=pltpu.VMEM)] * 2 + any_specs(deps),
        out_shape=[shape, shape],
        compiler_params=params(),
        cost_estimate=pl.CostEstimate(flops=1, bytes_accessed=1, transcendentals=0),
        name="mid_gradient_add",
    )(keep, other, *deps)


def mid_final_kernel(own_ref, other_ref, out_ref, head_ref):
    body, tail = add_tail(own_ref[...], other_ref[...], out_ref.shape[0])
    out_ref[...] = body
    head_ref[...] = tail


def mid_final(own, other):
    hidden = own.shape[0] - EXTRA
    return pl.pallas_call(
        mid_final_kernel,
        out_shape=[
            jax.ShapeDtypeStruct((hidden, own.shape[1]), bf16),
            jax.ShapeDtypeStruct((1, own.shape[1]), f32),
        ],
        compiler_params=params(),
        cost_estimate=pl.CostEstimate(flops=1, bytes_accessed=1, transcendentals=0),
        name="mid_gradient_final",
    )(own, other)


def back_first_kernel(chunks, count, *refs):
    own_ref, value_ref = refs[:2]
    received = refs[2 : 2 + count]
    first_refs = refs[2 + count : 2 + count + chunks]
    out_refs = refs[-1 - chunks : -1]
    tail_ref = refs[-1]
    block = first_refs[0].shape[0]
    value = value_ref[...]
    for ref in received:
        tail = ref[pl.ds(chunks * block, EXTRA), :].astype(f32)
        value = value + (tail[0:1] + tail[1:2])
    tail_ref[...] = tail_rows(value)
    for c in range(chunks):
        total = own_ref[pl.ds(c * block, block), :]
        for ref in received:
            total = total + ref[pl.ds(c * block, block), :].astype(f32)
        first = first_refs[c][...].astype(f32)
        out_refs[c][...] = (total * (1.0 - first * first)).astype(bf16)


def back_first(own, value, received, firsts, deps=()):
    chunks = len(firsts)
    shape = firsts[0].shape
    return pl.pallas_call(
        functools.partial(back_first_kernel, chunks, len(received)),
        in_specs=[pl.BlockSpec(memory_space=pltpu.VMEM)] * (2 + len(received) + chunks) + any_specs(deps),
        out_shape=[jax.ShapeDtypeStruct(shape, bf16)] * chunks
        + [jax.ShapeDtypeStruct((EXTRA, shape[1]), bf16)],
        compiler_params=params(),
        cost_estimate=pl.CostEstimate(flops=1, bytes_accessed=1, transcendentals=0),
        name="back_first",
    )(own, value, *received, *firsts, *deps)


def stack_kernel(count, *refs):
    at = 0
    for ref in refs[:count]:
        refs[-1][pl.ds(at, ref.shape[0]), :] = ref[...]
        at += ref.shape[0]


def stack(pieces, deps=()):
    rows = sum(piece.shape[0] for piece in pieces)
    return pl.pallas_call(
        functools.partial(stack_kernel, len(pieces)),
        in_specs=[pl.BlockSpec(memory_space=pltpu.VMEM)] * len(pieces) + any_specs(deps),
        out_shape=jax.ShapeDtypeStruct((rows, pieces[0].shape[1]), bf16),
        compiler_params=params(),
        cost_estimate=pl.CostEstimate(flops=1, bytes_accessed=1, transcendentals=0),
        name="stack_parts",
    )(*pieces, *deps)


def first_grad_kernel(parts, block, with_inner, with_value, with_output, *refs):
    place_ref, low_ref, high_ref = refs[:3]
    stacks = refs[3 + with_inner : 7 + with_inner]
    out_ref = refs[7 + with_inner + with_output]
    whole = refs[-1]
    width = stacks[0].shape[1]
    step = pl.program_id(0)

    @pl.when(step == 0)
    def _():
        part, mine = place_ref[2], place_ref[3]
        for t, ref in enumerate(stacks):
            at = mine ^ (2 * (t % 2) + t // 2)
            for k in range(parts):
                column = pl.multiple_of((part ^ k) * width, width)
                whole[pl.ds(pl.multiple_of(at * block, block), block), pl.ds(column, width)] = ref[
                    pl.ds(k * block, block), :
                ]
            if with_value:
                tail = ref[pl.ds(parts * block, EXTRA), :].astype(f32)
                refs[8 + with_inner + with_output][pl.ds(at, 1), :] = tail[0:1] + tail[1:2]

    def product(ref):
        out_ref[...] = jnp.dot(ref[...].T, whole[...], preferred_element_type=f32).astype(bf16)

    @pl.when(step == 0)
    def _():
        product(low_ref)

    if with_inner:

        @pl.when((step > 0) & (step < pl.num_programs(0) - 1))
        def _():
            product(refs[3])

    @pl.when(step == pl.num_programs(0) - 1)
    def _():
        product(high_ref)


def first_grad(place, low, inner, high, stacks, so_far, hidden, parts, block, chunk):
    scenarios, size = low.shape
    inner_steps = 0 if inner is None else inner.shape[1] // size
    cells = (inner_steps + 2) * size
    width = stacks[0].shape[1]
    with_value = chunk == 0
    with_output = so_far is not None
    in_specs = [smem()] + [pl.BlockSpec(low.shape, lambda i: (0, 0))] * 2
    args = [place, low, high]
    if inner is not None:
        in_specs.append(pl.BlockSpec((scenarios, size), lambda i: (0, jnp.clip(i - 1, 0, inner_steps - 1))))
        args.append(inner)
    in_specs += [pl.BlockSpec(ref.shape, lambda i: (0, 0)) for ref in stacks]
    args += stacks
    aliases = {}
    if with_output:
        aliases = {len(args): 0}
        in_specs.append(pl.BlockSpec(memory_space=pl.ANY))
        args.append(so_far)
    out_specs = [pl.BlockSpec((size, parts * width), lambda i: (i, chunk))]
    out_shape = [jax.ShapeDtypeStruct((cells, hidden), bf16)]
    if with_value:
        out_specs.append(pl.BlockSpec((4, width), lambda i: (0, 0)))
        out_shape.append(jax.ShapeDtypeStruct((4, width), f32))
    return pl.pallas_call(
        functools.partial(first_grad_kernel, parts, block, inner is not None, with_value, with_output),
        grid=(inner_steps + 2,),
        in_specs=in_specs,
        out_specs=out_specs,
        out_shape=out_shape,
        input_output_aliases=aliases,
        scratch_shapes=[pltpu.VMEM((scenarios, parts * width), bf16)],
        compiler_params=params(),
        cost_estimate=pl.CostEstimate(flops=1, bytes_accessed=1, transcendentals=0),
        name="first_gradient",
    )(*args)


def local(hist, drift, shocks, shock_table, first_weight, mid_weight, head_weight, cotangent):
    scenarios, rows, columns = hist.shape
    count = lax.axis_size("grid")
    hidden = first_weight.shape[1]
    units = mid_weight.shape[1]
    parts = count // 4
    chunks = CHUNKS if hidden % (parts * CHUNKS * LANES) == 0 else 1
    width = hidden // (parts * chunks)
    block = scenarios // 4
    index = lax.axis_index("grid")
    core, side, part = index % 2, index // 2 % 2, index // 4
    mine = 2 * core + side
    tiles = to_tiles(hist)

    place = jnp.stack([core, side, part, mine])
    cot = lax.dynamic_slice_in_dim(cotangent, mine * block, block)[:, None]
    heads = [head_weight[None, :]]
    mids = [mid_weight]

    *own_rows, inner = inner_steps(tiles, drift, shocks, shock_table)
    inner = inner if rows > 4 else None
    forward = [(i, i + 1) for i in range(count - 1)]
    backward = [(i + 1, i) for i in range(count - 1)]
    below = lax.ppermute(own_rows[3], "grid", forward)
    above = lax.ppermute(own_rows[0], "grid", backward)
    mids.append(swap(mids[0], count, 1))
    mids.append(swap(mids[0], count, 2))
    product = None if inner is None else inner_product(inner, first_weight, width, mids[1:])
    mids.append(swap(mids[2], count, 1))
    low, high = edge_steps(drift, shocks, shock_table, own_rows, below, above, [] if product is None else [product])

    def density_turn(turn, dep, so_far):
        return density_steps(tiles, drift, shocks, shock_table, below, above, dep, so_far, turn, 4)

    owned, firsts, density = [], [], None
    products = [edge_product(place, low, high, first_weight, product, parts, width, c) for c in range(chunks)]
    sums = []
    for c, (keep, send) in enumerate(products):
        keep, send = add_side(place, keep, swap(send, count, 1), [mids[3]])
        sums.append((keep, send, swap(send, count, 2)))
    density = density_turn(0, sums[-1][1], density)
    for c, (keep, send, other) in enumerate(sums):
        own, *sends = add_parts(place, keep, other, [density])
        received = [swap(piece, count, 4 * (k + 1)) for k, piece in enumerate(sends)]
        if c == chunks - 1:
            density = density_turn(1, sends[-1], density)
        owned.append(activate(own, received, [density]))
    for first in owned:
        firsts.append(first)
        firsts += [swap(first, count, 4 * k) for k in range(1, parts)]
    heads += [swap(heads[0], count, k) for k in range(1, 4)]
    density = density_turn(2, owned[-1], density)
    back_second, own, value, head_part, *sends = middle(
        place, cot, firsts, mids, heads, chunks, parts, width, [density]
    )
    received = [swap(piece, count, 4 * (k + 1)) for k, piece in enumerate(sends)]
    density = density_turn(3, received[0], density)
    keep, send = mid_grad(place, back_second, head_part, firsts, chunks, parts, width, [density])
    *backs, tail = back_first(own, value, received, owned, [density])
    keep, send = mid_add(keep, swap(send, count, 1), [received[-1]])
    grad_mid, grad_head = mid_final(keep, swap(send, count, 2))
    grad_first = None
    for c in range(chunks):
        pieces = [backs[c]] + [swap(backs[c], count, 4 * k) for k in range(1, parts)]
        mine_stack = stack(pieces + [tail] if c == 0 else pieces, [grad_mid])
        stacks = [mine_stack, swap(mine_stack, count, 1), swap(mine_stack, count, 2)]
        stacks.append(swap(stacks[2], count, 1))
        results = first_grad(place, low, inner, high, stacks, grad_first, hidden, parts, block, c)
        grad_first = results[0]
        if c == 0:
            value = results[1][:, :block].reshape(scenarios)
    return from_tiles(density, hist.shape), value, grad_first, grad_mid, grad_head[0]


def solution(mesh):
    in_specs = (
        P("groups", "grid", None),
        P(None, "grid", None),
        P("groups", None),
        P("groups", None),
        P(("groups", "grid"), None),
        P("groups", "grid"),
        P(("groups", "grid")),
        P("groups"),
    )
    out_specs = (
        P("groups", "grid", None),
        P("groups"),
        P(("groups", "grid"), None),
        P("groups", "grid"),
        P(("groups", "grid")),
    )
    return jax.shard_map(local, mesh=mesh, in_specs=in_specs, out_specs=out_specs, check_vma=False)
```

```python
import functools
import jax
import jax.numpy as jnp
import numpy as np
from jax import lax
from jax.experimental import pallas as pl
from jax.experimental.pallas import tpu as pltpu
from jax.sharding import PartitionSpec as P

diffusion_rate = 0.24
VMEM_BYTES = 48 * 1024 * 1024
EXTRA = 16
bf16 = jnp.bfloat16
f32 = jnp.float32


def params():
    return pltpu.CompilerParams(vmem_limit_bytes=VMEM_BYTES)


def scenario_block(scenarios):
    for size in (64, 32, 16):
        if scenarios % size == 0:
            return size
    return scenarios


LANES = 128
SUBLANES = 8
GROUP = 16
CHUNKS = 1


def to_tiles(hist):
    scenarios, rows, columns = hist.shape
    high = min(rows, SUBLANES)
    tiles = hist.reshape(scenarios, rows // high, high, columns // LANES, LANES)
    return tiles.transpose(0, 1, 3, 2, 4).reshape(scenarios * rows * (columns // LANES), LANES)


def from_tiles(tiles, shape):
    scenarios, rows, columns = shape
    high = min(rows, SUBLANES)
    parts = tiles.reshape(scenarios, rows // high, columns // LANES, high, LANES)
    return parts.transpose(0, 1, 3, 2, 4).reshape(shape)


def tile_offset(row, lane_tile, rows, lane_tiles):
    high = min(rows, SUBLANES)
    return (row // high * lane_tiles + lane_tile) * high + row % high


def read_row(ref, first_scenario, count, row, rows, columns):
    lane_tiles = columns // LANES
    per = rows * lane_tiles
    return jnp.concatenate(
        [
            ref[pl.ds(first_scenario * per + tile_offset(row, t, rows, lane_tiles), count, stride=per), :]
            for t in range(lane_tiles)
        ],
        axis=1,
    )


def write_row(ref, first_scenario, count, row, rows, columns, values):
    lane_tiles = columns // LANES
    per = rows * lane_tiles
    for t in range(lane_tiles):
        place = pl.ds(first_scenario * per + tile_offset(row, t, rows, lane_tiles), count, stride=per)
        ref[place, :] = values[:, t * LANES : (t + 1) * LANES]


def drift_tail(drift_ref, start):
    pieces = [
        jnp.concatenate([drift_ref[c, start : start + 1], drift_ref[c, start + 1 : start + 2]], axis=1)
        for c in range(2)
    ]
    high, low = two_halves(jnp.concatenate(pieces, axis=0))
    ones = jnp.ones((1, high.shape[1]), bf16)
    zeros = jnp.zeros((EXTRA - 5, high.shape[1]), bf16)
    return jnp.concatenate([high, low, ones, zeros], axis=0)


def band_matrix(columns):
    beside = np.eye(columns, k=1) + np.eye(columns, k=-1)
    flux = np.eye(columns, k=1) - np.eye(columns, k=-1)
    centre = (1.0 - 4.0 * diffusion_rate) * np.eye(columns) + diffusion_rate * beside
    return jnp.asarray(np.concatenate([centre, flux], axis=0), dtype=bf16)


def half_shifts(levels_ref, table_ref, shift_ref):
    scenarios = levels_ref.shape[1]
    for t in range(levels_ref.shape[0]):
        level = jnp.broadcast_to(levels_ref[t : t + 1, :].astype(f32), (LANES, scenarios)).T
        for c in range(2):
            shift = jnp.zeros(level.shape, f32)
            for n in range(table_ref.shape[1]):
                shift = jnp.where(level == n, 0.5 * table_ref[c, n], shift)
            shift_ref[2 * t + c] = shift


def wide(values, columns):
    return jnp.concatenate([values] * (columns // LANES), axis=1)


def one_step(segments, read, half_drift, band, shift_x, shift_y, pairs, terms, write):
    size, columns = shift_x.shape
    places = [row for first, last in segments for row in range(first + 1, last)]
    for k, row in enumerate(places):
        density = read(row)
        pairs[pl.ds(k * size, size), pl.ds(0, columns)] = density.astype(bf16)
        flux = (half_drift(1, row) + shift_y) * density
        pairs[pl.ds(k * size, size), pl.ds(columns, columns)] = flux.astype(bf16)
    count = len(places) * size
    terms[pl.ds(0, count), :] = jnp.dot(pairs[pl.ds(0, count), :], band, preferred_element_type=f32)
    for k, row in enumerate(places):
        low = read(row - 1) * ((diffusion_rate + half_drift(0, row - 1)) + shift_x)
        high = read(row + 1) * ((diffusion_rate - half_drift(0, row + 1)) - shift_x)
        write(row, terms[pl.ds(k * size, size), :] + low + high)


def two_steps(segments, read, half_drift, edge, band, shifts, scratch, write):
    pairs, terms, middle = scratch
    size, columns = shifts[0].shape
    before = [(first - 2, last + 2) for first, last in segments]
    between = [(first - 1, last + 1) for first, last in segments]
    places = [row for first, last in between for row in range(first, last + 1)]

    def write_middle(row, density):
        middle[pl.ds(places.index(row) * size, size), :] = edge(row, density).astype(bf16)

    def read_middle(row):
        return middle[pl.ds(places.index(row) * size, size), :].astype(f32)

    one_step(before, read, half_drift, band, shifts[0], shifts[1], pairs, terms, write_middle)
    one_step(between, read_middle, half_drift, band, shifts[2], shifts[3], pairs, terms, write)


def step_scratch(rows, size, columns):
    return [
        pltpu.VMEM((rows * size, 2 * columns), bf16),
        pltpu.VMEM((rows * size, columns), f32),
        pltpu.VMEM((rows * size, columns), bf16),
    ]


def inner_kernel(
    rows, size, hist_ref, drift_ref, levels_ref, table_ref, band_ref,
    first_ref, next_ref, prev_ref, last_ref, shift_ref, inner_ref, *scratch,
):
    step = pl.program_id(0)
    columns = drift_ref.shape[2]

    @pl.when(step == 0)
    def _():
        half_shifts(levels_ref, table_ref, shift_ref)
        for out, start in ((first_ref, 0), (last_ref, rows - 2)):
            out[pl.ds(out.shape[0] - EXTRA, EXTRA), :] = drift_tail(drift_ref, start)

    where = pl.ds(pl.multiple_of(step * size, size), size)
    for out, start in ((first_ref, 0), (next_ref, 2), (prev_ref, rows - 4), (last_ref, rows - 2)):
        for k in range(2):
            out[where, pl.ds(k * columns, columns)] = read_row(hist_ref, 0, size, start + k, rows, columns).astype(bf16)
    if rows <= 4:
        return

    def write(row, density):
        inner_ref[:, pl.ds((row - 2) * columns, columns)] = density.astype(bf16)

    two_steps(
        [(2, rows - 3)],
        lambda row: read_row(hist_ref, 0, size, row, rows, columns),
        lambda c, row: 0.5 * drift_ref[c, row : row + 1, :],
        lambda row, density: density,
        band_ref[...],
        [wide(shift_ref[n, where, :], columns) for n in range(4)],
        scratch,
        write,
    )


def inner_steps(tiles, drift, levels, table, band):
    scenarios = levels.shape[1]
    rows, columns = drift.shape[1:]
    per = tiles.shape[0] // scenarios
    size = scenario_block(scenarios)
    inner = max(rows - 4, 1) * columns
    edge = jax.ShapeDtypeStruct((scenarios, 2 * columns), bf16)
    sent = jax.ShapeDtypeStruct((scenarios + EXTRA, 2 * columns), bf16)
    shifts = jax.ShapeDtypeStruct((4, scenarios, LANES), f32)
    return pl.pallas_call(
        functools.partial(inner_kernel, rows, size),
        grid=(scenarios // size,),
        in_specs=[
            pl.BlockSpec((size * per, LANES), lambda i: (i, 0)),
            pl.BlockSpec(drift.shape, lambda i: (0, 0, 0)),
            pl.BlockSpec(levels.shape, lambda i: (0, 0)),
            smem(),
            pl.BlockSpec(band.shape, lambda i: (0, 0)),
        ],
        out_specs=[pl.BlockSpec(shape.shape, lambda i: (0, 0)) for shape in (sent, edge, edge, sent)]
        + [pl.BlockSpec(shifts.shape, lambda i: (0, 0, 0)), pl.BlockSpec((size, inner), lambda i: (i, 0))],
        out_shape=[sent, edge, edge, sent, shifts, jax.ShapeDtypeStruct((scenarios, inner), bf16)],
        scratch_shapes=step_scratch(max(rows - 2, 1), size, columns),
        compiler_params=params(),
        cost_estimate=pl.CostEstimate(flops=1, bytes_accessed=1, transcendentals=0),
        name="inner_density_steps",
    )(tiles, drift, levels, table, band)


def halo_drift(ref, columns):
    tail = ref[pl.ds(ref.shape[0] - EXTRA, EXTRA), :].astype(f32)
    both = 0.5 * (tail[0:2] + tail[2:4])
    rows = [[both[c : c + 1, k * columns : (k + 1) * columns] for k in range(2)] for c in range(2)]
    return rows, tail[4:5, :columns]


def with_halo(drift_ref, below_ref, above_ref):
    rows, columns = drift_ref.shape[1:]
    below, below_valid = halo_drift(below_ref, columns)
    above, above_valid = halo_drift(above_ref, columns)

    def half_drift(c, row):
        if row < 0:
            return below[c][row + 2]
        if row >= rows:
            return above[c][row - rows]
        return 0.5 * drift_ref[c, row : row + 1, :]

    def edge(row, density):
        if row < 0:
            return density * below_valid
        if row >= rows:
            return density * above_valid
        return density

    return half_drift, edge


def edge_kernel(
    size, drift_ref, shift_ref, band_ref, first_ref, next_ref, prev_ref, last_ref, below_ref, above_ref, *refs
):
    low_ref, high_ref, *scratch = refs[-5:]
    rows, columns = drift_ref.shape[1:]
    half_drift, edge = with_halo(drift_ref, below_ref, above_ref)
    where = pl.ds(pl.multiple_of(pl.program_id(0) * size, size), size)
    shifts = [wide(shift_ref[n, where, :], columns) for n in range(4)]
    for out, refs, first in (
        (low_ref, (below_ref, first_ref, next_ref), 0),
        (high_ref, (prev_ref, last_ref, above_ref), rows - 2),
    ):

        def read(row):
            at = row - (first - 2)
            return refs[at // 2][where, pl.ds(at % 2 * columns, columns)].astype(f32)

        def write(row, density):
            out[:, pl.ds((row - first) * columns, columns)] = density.astype(bf16)

        two_steps([(first, first + 1)], read, half_drift, edge, band_ref[...], shifts, scratch, write)


def edge_steps(drift, shifts, band, own, below, above, deps):
    scenarios = shifts.shape[1]
    columns = drift.shape[2]
    size = scenario_block(scenarios)
    edge = jax.ShapeDtypeStruct((scenarios, 2 * columns), bf16)
    spec = pl.BlockSpec((size, 2 * columns), lambda i: (i, 0))
    return pl.pallas_call(
        functools.partial(edge_kernel, size),
        grid=(scenarios // size,),
        in_specs=[
            pl.BlockSpec(drift.shape, lambda i: (0, 0, 0)),
            pl.BlockSpec(shifts.shape, lambda i: (0, 0, 0)),
            pl.BlockSpec(band.shape, lambda i: (0, 0)),
        ]
        + [pl.BlockSpec(ref.shape, lambda i: (0, 0)) for ref in (*own, below, above)]
        + any_specs(deps),
        out_specs=[spec, spec],
        out_shape=[edge, edge],
        scratch_shapes=step_scratch(4, size, columns),
        compiler_params=params(),
        cost_estimate=pl.CostEstimate(flops=1, bytes_accessed=1, transcendentals=0),
        name="edge_density_steps",
    )(drift, shifts, band, *own, below, above, *deps)


def density_kernel(
    rows, size, first_step, hist_ref, drift_ref, shift_ref, band_ref, below_ref, above_ref, dep_ref, *refs
):
    next_ref, *scratch = refs[-4:]
    columns = drift_ref.shape[2]
    half_drift, edge = with_halo(drift_ref, below_ref, above_ref)
    where = pl.ds(pl.multiple_of((first_step + pl.program_id(0)) * size, size), size)

    def read(row):
        if row < 0:
            return below_ref[where, pl.ds((row + 2) * columns, columns)].astype(f32)
        if row >= rows:
            return above_ref[where, pl.ds((row - rows) * columns, columns)].astype(f32)
        return read_row(hist_ref, 0, size, row, rows, columns)

    two_steps(
        [(0, rows - 1)],
        read,
        half_drift,
        edge,
        band_ref[...],
        [wide(shift_ref[n, where, :], columns) for n in range(4)],
        scratch,
        lambda row, density: write_row(next_ref, 0, size, row, rows, columns, density),
    )


def density_steps(tiles, drift, shifts, band, below, above, dep, so_far, turn, turns):
    scenarios = shifts.shape[1]
    rows, columns = drift.shape[1:]
    per = tiles.shape[0] // scenarios
    size = 3 * GROUP if scenarios % (turns * GROUP * 3) == 0 else GROUP
    steps = scenarios // size // turns
    first = turn * steps
    block = pl.BlockSpec((size * per, LANES), lambda i: (first + i, 0))
    hidden = pl.BlockSpec(memory_space=pl.ANY)
    args = [tiles, drift, shifts, band, below, above, dep]
    in_specs = [
        block,
        pl.BlockSpec(drift.shape, lambda i: (0, 0, 0)),
        pl.BlockSpec(shifts.shape, lambda i: (0, 0, 0)),
        pl.BlockSpec(band.shape, lambda i: (0, 0)),
        pl.BlockSpec(below.shape, lambda i: (0, 0)),
        pl.BlockSpec(above.shape, lambda i: (0, 0)),
        hidden,
    ]
    aliases = {}
    if so_far is not None:
        args.append(so_far)
        in_specs.append(hidden)
        aliases = {7: 0}
    return pl.pallas_call(
        functools.partial(density_kernel, rows, size, first),
        grid=(steps,),
        in_specs=in_specs,
        out_specs=block,
        out_shape=jax.ShapeDtypeStruct(tiles.shape, f32),
        input_output_aliases=aliases,
        scratch_shapes=step_scratch(rows + 2, size, columns),
        compiler_params=params(),
        cost_estimate=pl.CostEstimate(flops=1, bytes_accessed=1, transcendentals=0),
        name="density_steps",
    )(*args)


def smem():
    return pl.BlockSpec(memory_space=pltpu.SMEM)


def swap(values, count, flip):
    return lax.ppermute(values, "grid", [(i, i ^ flip) for i in range(count)])


def inner_product_kernel(count, dep_count, *refs):
    inputs_ref = refs[0]
    weights = refs[1 : 1 + count]
    weight = jnp.concatenate([ref[...] for ref in weights], axis=0)
    refs[-1][0] = jnp.dot(inputs_ref[...], weight, preferred_element_type=f32)


def inner_product(inner, weight, width, deps):
    scenarios, cells = inner.shape
    total, hidden = weight.shape
    size = (total - cells) // 2
    count = cells // size
    hidden_spec = pl.BlockSpec(memory_space=pl.ANY)

    def spec(k):
        return pl.BlockSpec((size, width), lambda n: (1 + k, n))

    return pl.pallas_call(
        functools.partial(inner_product_kernel, count, len(deps)),
        grid=(hidden // width,),
        in_specs=[pl.BlockSpec(inner.shape, lambda n: (0, 0))]
        + [spec(k) for k in range(count)]
        + [hidden_spec] * len(deps),
        out_specs=pl.BlockSpec((1, scenarios, width), lambda n: (n, 0, 0)),
        out_shape=jax.ShapeDtypeStruct((hidden // width, scenarios, width), f32),
        compiler_params=params(),
        cost_estimate=pl.CostEstimate(flops=1, bytes_accessed=1, transcendentals=0),
        name="inner_product",
    )(inner, *([weight] * count), *deps)


def edge_product_kernel(block, with_inner, place_ref, low_ref, high_ref, top_ref, bottom_ref, *refs):
    keep_ref, send_ref, total = refs[-3:]
    left = jnp.concatenate([low_ref[...], high_ref[...]], axis=1)
    weight = jnp.concatenate([top_ref[...], bottom_ref[...]], axis=0)
    product = jnp.dot(left, weight, preferred_element_type=f32)
    total[...] = product + refs[0][0] if with_inner else product
    core = place_ref[0]
    for out, half in ((keep_ref, core), (send_ref, 1 - core)):
        for side in range(2):
            start = pl.multiple_of((2 * half + side) * block, block)
            out[side, 0] = total[pl.ds(start, block), :].astype(out.dtype)


def edge_product(place, low, high, weight, inner, parts, width, chunk):
    scenarios, size = low.shape
    block = scenarios // 4
    last = weight.shape[0] // size - 1
    shape = (2, parts, block, width)
    spec = pl.BlockSpec((2, 1, block, width), lambda n: (0, n, 0, 0))
    in_specs = [
        smem(),
        pl.BlockSpec(low.shape, lambda n: (0, 0)),
        pl.BlockSpec(low.shape, lambda n: (0, 0)),
        pl.BlockSpec((size, width), lambda n: (0, chunk * parts + n)),
        pl.BlockSpec((size, width), lambda n: (last, chunk * parts + n)),
    ]
    args = [place, low, high, weight, weight]
    if inner is not None:
        in_specs.append(pl.BlockSpec((1, scenarios, width), lambda n: (chunk * parts + n, 0, 0)))
        args.append(inner)
    return pl.pallas_call(
        functools.partial(edge_product_kernel, block, inner is not None),
        grid=(parts,),
        in_specs=in_specs,
        out_specs=[spec, spec],
        out_shape=[jax.ShapeDtypeStruct(shape, f32), jax.ShapeDtypeStruct(shape, bf16)],
        scratch_shapes=[pltpu.VMEM((scenarios, width), f32)],
        compiler_params=params(),
        cost_estimate=pl.CostEstimate(flops=1, bytes_accessed=1, transcendentals=0),
        name="edge_product",
    )(*args)


def add_side_kernel(place_ref, mine_ref, other_ref, *refs):
    keep_ref, send_ref = refs[-2:]
    side = place_ref[1]
    keep_ref[...] = mine_ref[side] + other_ref[side].astype(f32)
    send_ref[...] = (mine_ref[1 - side] + other_ref[1 - side].astype(f32)).astype(bf16)


def any_specs(deps):
    return [pl.BlockSpec(memory_space=pl.ANY)] * len(deps)


def add_side(place, mine, other, deps=()):
    shape = mine.shape[1:]
    return pl.pallas_call(
        add_side_kernel,
        in_specs=[smem()] + [pl.BlockSpec(memory_space=pltpu.VMEM)] * 2 + any_specs(deps),
        out_shape=[jax.ShapeDtypeStruct(shape, f32), jax.ShapeDtypeStruct(shape, bf16)],
        compiler_params=params(),
        cost_estimate=pl.CostEstimate(flops=1, bytes_accessed=1, transcendentals=0),
        name="add_side",
    )(place, mine, other, *deps)


def add_parts_kernel(dep_count, place_ref, mine_ref, other_ref, *refs):
    own_ref, *send_refs = refs[dep_count:]
    part = place_ref[2]
    own_ref[...] = mine_ref[part] + other_ref[part].astype(f32)
    for k, out in enumerate(send_refs):
        at = part ^ (k + 1)
        out[...] = (mine_ref[at] + other_ref[at].astype(f32)).astype(bf16)


def add_parts(place, mine, other, deps=()):
    parts = mine.shape[0]
    vmem = pl.BlockSpec(memory_space=pltpu.VMEM)
    return pl.pallas_call(
        functools.partial(add_parts_kernel, len(deps)),
        in_specs=[smem(), vmem, vmem] + any_specs(deps),
        out_shape=[jax.ShapeDtypeStruct(mine.shape[1:], f32)]
        + [jax.ShapeDtypeStruct(mine.shape[1:], bf16)] * (parts - 1),
        compiler_params=params(),
        cost_estimate=pl.CostEstimate(flops=1, bytes_accessed=1, transcendentals=0),
        name="add_parts",
    )(place, mine, other, *deps)


def activate_kernel(count, *refs):
    total = refs[0][...]
    for ref in refs[1 : 1 + count]:
        total = total + ref[...].astype(f32)
    refs[-1][...] = jnp.tanh(total).astype(bf16)


def activate(own, received, deps=()):
    return pl.pallas_call(
        functools.partial(activate_kernel, len(received)),
        in_specs=[pl.BlockSpec(memory_space=pltpu.VMEM)] * (1 + len(received)) + any_specs(deps),
        out_shape=jax.ShapeDtypeStruct(own.shape, bf16),
        compiler_params=params(),
        cost_estimate=pl.CostEstimate(flops=1, bytes_accessed=1, transcendentals=0),
        name="first_activation",
    )(own, *received, *deps)


def two_halves(exact):
    high = exact.astype(bf16)
    low = (exact - high.astype(f32)).astype(bf16)
    return high, low


def tail_rows(exact):
    high, low = two_halves(exact)
    zeros = jnp.zeros((EXTRA - 2, exact.shape[1]), bf16)
    return jnp.concatenate([high, low, zeros], axis=0)


def middle_kernel(chunks, parts, width, *refs):
    pieces = chunks * parts
    place_ref, cot_ref = refs[0], refs[1]
    first_refs = refs[2 : 2 + pieces]
    mid_refs = refs[2 + pieces : 6 + pieces]
    weight_refs = refs[6 + pieces : 10 + pieces]
    outs = refs[-(3 + parts) :]
    own_ref, value_ref, mid_keep_ref, mid_send_ref = outs[:4]
    send_refs = outs[4:]
    part = place_ref[2]
    block = cot_ref.shape[0]

    def mid_rows(start):
        return jnp.concatenate([ref[pl.ds(start, width), :] for ref in mid_refs], axis=1)

    def start_of(c, k):
        return pl.multiple_of((c * parts + (part ^ k)) * width, width)

    total = None
    for c in range(chunks):
        for k in range(parts):
            term = jnp.dot(first_refs[c * parts + k][...], mid_rows(start_of(c, k)), preferred_element_type=f32)
            total = term if total is None else total + term
    second_low = jnp.tanh(total).astype(bf16)
    second = second_low.astype(f32)
    head = jnp.concatenate([ref[...] for ref in weight_refs], axis=1)
    heads = tail_rows(head)
    rows = lax.dot_general(heads, second_low, (((1,), (1,)), ((), ())), preferred_element_type=f32)
    value = rows[0:1] + rows[1:2]
    if width > block:
        value = jnp.concatenate([value, jnp.zeros((1, width - block), f32)], axis=1)
    value_ref[...] = value
    cot = cot_ref[...]
    head_part = jnp.sum(cot * second, axis=0, keepdims=True)
    back = (cot * head * (1.0 - second * second)).astype(bf16)
    units = mid_refs[0].shape[1]
    for k in range(parts):
        for c in range(chunks):
            piece = lax.dot_general(
                back, mid_rows(start_of(c, k)), (((1,), (1,)), ((), ())), preferred_element_type=f32
            )
            if k == 0:
                own_ref[pl.ds(c * block, block), :] = piece
            else:
                send_refs[k - 1][pl.ds(c * block, block), :] = piece.astype(bf16)
        if k > 0:
            send_refs[k - 1][pl.ds(chunks * block, EXTRA), :] = tail_rows(value)
    for c in range(chunks):
        for k in range(parts):
            product = lax.dot_general(
                first_refs[c * parts + k][...], back, (((0,), (0,)), ((), ())), preferred_element_type=f32
            ).astype(bf16)
            for p in range(4):
                out = (mid_keep_ref, mid_send_ref)[p % 2]
                out[p // 2, pl.ds(start_of(c, k), width), :] = product[:, p * units : (p + 1) * units]
    for p in range(4):
        out = (mid_keep_ref, mid_send_ref)[p % 2]
        out[p // 2, pl.ds(pieces * width, EXTRA), :] = tail_rows(head_part[:, p * units : (p + 1) * units])


def middle(place, cot, firsts, mids, heads, chunks, parts, width, deps=()):
    block = cot.shape[0]
    hidden, units = mids[0].shape
    partial = jax.ShapeDtypeStruct((2, hidden + EXTRA, units), bf16)
    vmem = pl.BlockSpec(memory_space=pltpu.VMEM)
    return pl.pallas_call(
        functools.partial(middle_kernel, chunks, parts, width),
        in_specs=[smem()] + [vmem] * (1 + len(firsts) + 8) + any_specs(deps),
        out_shape=[
            jax.ShapeDtypeStruct((chunks * block, width), f32),
            jax.ShapeDtypeStruct((1, width), f32),
            partial,
            partial,
        ]
        + [jax.ShapeDtypeStruct((chunks * block + EXTRA, width), bf16)] * (parts - 1),
        compiler_params=params(),
        cost_estimate=pl.CostEstimate(flops=1, bytes_accessed=1, transcendentals=0),
        name="value_layers",
    )(place, cot, *firsts, *mids, *heads, *deps)


def add_tail(left, right, hidden):
    body = left[:hidden].astype(f32) + right[:hidden].astype(f32)
    tails = left[hidden:].astype(f32) + right[hidden:].astype(f32)
    return body.astype(bf16), tails[0:1] + tails[1:2]


def mid_add_kernel(keep_ref, other_ref, *refs):
    own_ref, send_ref = refs[-2:]
    hidden = own_ref.shape[0] - EXTRA
    for at, out in enumerate((own_ref, send_ref)):
        body, tail = add_tail(keep_ref[at], other_ref[at], hidden)
        out[pl.ds(0, hidden), :] = body
        out[pl.ds(hidden, EXTRA), :] = tail_rows(tail)


def mid_add(keep, other, deps=()):
    shape = jax.ShapeDtypeStruct(keep.shape[1:], bf16)
    return pl.pallas_call(
        mid_add_kernel,
        in_specs=[pl.BlockSpec(memory_space=pltpu.VMEM)] * 2 + any_specs(deps),
        out_shape=[shape, shape],
        compiler_params=params(),
        cost_estimate=pl.CostEstimate(flops=1, bytes_accessed=1, transcendentals=0),
        name="mid_gradient_add",
    )(keep, other, *deps)


def mid_final_kernel(own_ref, other_ref, out_ref, head_ref):
    body, tail = add_tail(own_ref[...], other_ref[...], out_ref.shape[0])
    out_ref[...] = body
    head_ref[...] = tail


def mid_final(own, other):
    hidden = own.shape[0] - EXTRA
    return pl.pallas_call(
        mid_final_kernel,
        out_shape=[
            jax.ShapeDtypeStruct((hidden, own.shape[1]), bf16),
            jax.ShapeDtypeStruct((1, own.shape[1]), f32),
        ],
        compiler_params=params(),
        cost_estimate=pl.CostEstimate(flops=1, bytes_accessed=1, transcendentals=0),
        name="mid_gradient_final",
    )(own, other)


def back_first_kernel(chunks, count, *refs):
    own_ref, value_ref = refs[:2]
    received = refs[2 : 2 + count]
    first_refs = refs[2 + count : 2 + count + chunks]
    out_refs = refs[-1 - chunks : -1]
    tail_ref = refs[-1]
    block = first_refs[0].shape[0]
    value = value_ref[...]
    for ref in received:
        tail = ref[pl.ds(chunks * block, EXTRA), :].astype(f32)
        value = value + (tail[0:1] + tail[1:2])
    tail_ref[...] = tail_rows(value)
    for c in range(chunks):
        total = own_ref[pl.ds(c * block, block), :]
        for ref in received:
            total = total + ref[pl.ds(c * block, block), :].astype(f32)
        first = first_refs[c][...].astype(f32)
        out_refs[c][...] = (total * (1.0 - first * first)).astype(bf16)


def back_first(own, value, received, firsts, deps=()):
    chunks = len(firsts)
    shape = firsts[0].shape
    return pl.pallas_call(
        functools.partial(back_first_kernel, chunks, len(received)),
        in_specs=[pl.BlockSpec(memory_space=pltpu.VMEM)] * (2 + len(received) + chunks) + any_specs(deps),
        out_shape=[jax.ShapeDtypeStruct(shape, bf16)] * chunks
        + [jax.ShapeDtypeStruct((EXTRA, shape[1]), bf16)],
        compiler_params=params(),
        cost_estimate=pl.CostEstimate(flops=1, bytes_accessed=1, transcendentals=0),
        name="back_first",
    )(own, value, *received, *firsts, *deps)


def stack_kernel(count, *refs):
    at = 0
    for ref in refs[:count]:
        refs[-1][pl.ds(at, ref.shape[0]), :] = ref[...]
        at += ref.shape[0]


def stack(pieces, deps=()):
    rows = sum(piece.shape[0] for piece in pieces)
    return pl.pallas_call(
        functools.partial(stack_kernel, len(pieces)),
        in_specs=[pl.BlockSpec(memory_space=pltpu.VMEM)] * len(pieces) + any_specs(deps),
        out_shape=jax.ShapeDtypeStruct((rows, pieces[0].shape[1]), bf16),
        compiler_params=params(),
        cost_estimate=pl.CostEstimate(flops=1, bytes_accessed=1, transcendentals=0),
        name="stack_parts",
    )(*pieces, *deps)


def turn_kernel(count, *refs):
    for ref, out in zip(refs[:count], refs[-count:]):
        out[...] = ref[...].T


def transposed(arrays, deps):
    vmem = pl.BlockSpec(memory_space=pltpu.VMEM)
    return pl.pallas_call(
        functools.partial(turn_kernel, len(arrays)),
        in_specs=[vmem] * len(arrays) + any_specs(deps),
        out_shape=[jax.ShapeDtypeStruct(array.shape[::-1], array.dtype) for array in arrays],
        compiler_params=params(),
        cost_estimate=pl.CostEstimate(flops=1, bytes_accessed=1, transcendentals=0),
        name="transposed_inputs",
    )(*arrays, *deps)


def first_grad_kernel(parts, block, count, tile, with_value, with_output, *refs):
    place_ref = refs[0]
    lefts = refs[1 : 1 + count]
    stacks = refs[1 + count : 5 + count]
    out_ref = refs[5 + count + with_output]
    whole = refs[-1]
    width = stacks[0].shape[1]
    step = pl.program_id(0)
    part, mine = place_ref[2], place_ref[3]

    if with_value:

        @pl.when(step == 0)
        def _():
            for t, ref in enumerate(stacks):
                at = mine ^ (2 * (t % 2) + t // 2)
                tail = ref[pl.ds(parts * block, EXTRA), :].astype(f32)
                refs[6 + count + with_output][pl.ds(at, 1), :] = tail[0:1] + tail[1:2]

    tiles = width // tile
    piece = step // tiles ^ part
    column = pl.ds(pl.multiple_of(step % tiles * tile, tile), tile)
    for t, ref in enumerate(stacks):
        at = mine ^ (2 * (t % 2) + t // 2)
        whole[pl.ds(pl.multiple_of(at * block, block), block), :] = ref[
            pl.ds(pl.multiple_of(piece * block, block), block), column
        ]
    start = 0
    for ref in lefts:
        cells = ref.shape[0]
        out_ref[pl.ds(start, cells), :] = jnp.dot(ref[...], whole[...], preferred_element_type=f32).astype(bf16)
        start += cells


def first_grad(place, lefts, stacks, so_far, hidden, parts, block, chunk):
    scenarios = lefts[0].shape[1]
    cells = sum(left.shape[0] for left in lefts)
    width = stacks[0].shape[1]
    tile = min(width, 256)
    steps = parts * width // tile
    with_value = chunk == 0
    with_output = so_far is not None
    in_specs = [smem()] + [pl.BlockSpec(ref.shape, lambda i: (0, 0)) for ref in (*lefts, *stacks)]
    args = [place, *lefts, *stacks]
    aliases = {}
    if with_output:
        aliases = {len(args): 0}
        in_specs.append(pl.BlockSpec(memory_space=pl.ANY))
        args.append(so_far)
    out_specs = [pl.BlockSpec((cells, tile), lambda i: (0, chunk * steps + i))]
    out_shape = [jax.ShapeDtypeStruct((cells, hidden), bf16)]
    if with_value:
        out_specs.append(pl.BlockSpec((4, width), lambda i: (0, 0)))
        out_shape.append(jax.ShapeDtypeStruct((4, width), f32))
    return pl.pallas_call(
        functools.partial(first_grad_kernel, parts, block, len(lefts), tile, with_value, with_output),
        grid=(steps,),
        in_specs=in_specs,
        out_specs=out_specs,
        out_shape=out_shape,
        input_output_aliases=aliases,
        scratch_shapes=[pltpu.VMEM((scenarios, tile), bf16)],
        compiler_params=params(),
        cost_estimate=pl.CostEstimate(flops=1, bytes_accessed=1, transcendentals=0),
        name="first_gradient",
    )(*args)


def local(hist, drift, shocks, shock_table, first_weight, mid_weight, head_weight, cotangent):
    scenarios, rows, columns = hist.shape
    count = lax.axis_size("grid")
    hidden = first_weight.shape[1]
    units = mid_weight.shape[1]
    parts = count // 4
    chunks = CHUNKS if hidden % (parts * CHUNKS * LANES) == 0 else 1
    width = hidden // (parts * chunks)
    block = scenarios // 4
    index = lax.axis_index("grid")
    core, side, part = index % 2, index // 2 % 2, index // 4
    mine = 2 * core + side
    tiles = to_tiles(hist)

    place = jnp.stack([core, side, part, mine])
    cot = lax.dynamic_slice_in_dim(cotangent, mine * block, block)[:, None]
    heads = [head_weight[None, :]]
    mids = [mid_weight]

    band = band_matrix(columns)
    *own_rows, shifts, inner = inner_steps(tiles, drift, shocks.T, shock_table.T, band)
    inner = inner if rows > 4 else None
    forward = [(i, i + 1) for i in range(count - 1)]
    backward = [(i + 1, i) for i in range(count - 1)]
    below = lax.ppermute(own_rows[3], "grid", forward)
    above = lax.ppermute(own_rows[0], "grid", backward)
    mids.append(swap(mids[0], count, 1))
    mids.append(swap(mids[0], count, 2))
    product = None if inner is None else inner_product(inner, first_weight, width, mids[1:])
    mids.append(swap(mids[2], count, 1))
    low, high = edge_steps(drift, shifts, band, own_rows, below, above, [] if product is None else [product])

    def density_turn(turn, dep, so_far):
        return density_steps(tiles, drift, shifts, band, below, above, dep, so_far, turn, 4)

    owned, firsts, density = [], [], None
    products = [edge_product(place, low, high, first_weight, product, parts, width, c) for c in range(chunks)]
    sums = []
    for c, (keep, send) in enumerate(products):
        keep, send = add_side(place, keep, swap(send, count, 1), [mids[3]])
        sums.append((keep, send, swap(send, count, 2)))
    density = density_turn(0, sums[-1][1], density)
    for c, (keep, send, other) in enumerate(sums):
        own, *sends = add_parts(place, keep, other, [density])
        received = [swap(piece, count, 4 * (k + 1)) for k, piece in enumerate(sends)]
        if c == chunks - 1:
            density = density_turn(1, sends[-1], density)
        owned.append(activate(own, received, [density]))
    for first in owned:
        firsts.append(first)
        firsts += [swap(first, count, 4 * k) for k in range(1, parts)]
    heads += [swap(heads[0], count, k) for k in range(1, 4)]
    density = density_turn(2, owned[-1], density)
    own, value, mid_keep, mid_send, *sends = middle(
        place, cot, firsts, mids, heads, chunks, parts, width, [density]
    )
    received = [swap(piece, count, 4 * (k + 1)) for k, piece in enumerate(sends)]
    *backs, tail = back_first(own, value, received, owned)
    mid_keep, mid_send = mid_add(mid_keep, swap(mid_send, count, 1), [backs[-1]])
    density = density_turn(3, backs[-1], density)
    lefts = transposed([low, high] if inner is None else [low, inner, high], [density])
    grad_mid, grad_head = mid_final(mid_keep, swap(mid_send, count, 2))
    grad_first = None
    for c in range(chunks):
        pieces = [backs[c]] + [swap(backs[c], count, 4 * k) for k in range(1, parts)]
        mine_stack = stack(pieces + [tail] if c == 0 else pieces, [grad_mid, lefts[0]])
        stacks = [mine_stack, swap(mine_stack, count, 1), swap(mine_stack, count, 2)]
        stacks.append(swap(stacks[2], count, 1))
        results = first_grad(place, lefts, stacks, grad_first, hidden, parts, block, c)
        grad_first = results[0]
        if c == 0:
            value = results[1][:, :block].reshape(scenarios)
    return from_tiles(density, hist.shape), value, grad_first, grad_mid, grad_head[0]


def solution(mesh):
    in_specs = (
        P("groups", "grid", None),
        P(None, "grid", None),
        P("groups", None),
        P("groups", None),
        P(("groups", "grid"), None),
        P("groups", "grid"),
        P(("groups", "grid")),
        P("groups"),
    )
    out_specs = (
        P("groups", "grid", None),
        P("groups"),
        P(("groups", "grid"), None),
        P("groups", "grid"),
        P(("groups", "grid")),
    )
    return jax.shard_map(local, mesh=mesh, in_specs=in_specs, out_specs=out_specs, check_vma=False)
```

```python
import functools
import jax
import jax.numpy as jnp
from jax import lax
from jax.experimental import pallas as pl
from jax.experimental.pallas import tpu as pltpu
from jax.sharding import PartitionSpec as P

diffusion_rate = 0.24
VMEM_BYTES = 40 * 1024 * 1024
EXTRA = 16
bf16 = jnp.bfloat16
f32 = jnp.float32


def params():
    return pltpu.CompilerParams(vmem_limit_bytes=VMEM_BYTES)


def scenario_block(scenarios):
    for size in (64, 32, 16):
        if scenarios % size == 0:
            return size
    return scenarios


LANES = 128
SUBLANES = 8
GROUP = 16
CHUNKS = 2


def to_tiles(hist):
    scenarios, rows, columns = hist.shape
    high = min(rows, SUBLANES)
    tiles = hist.reshape(scenarios, rows // high, high, columns // LANES, LANES)
    return tiles.transpose(0, 1, 3, 2, 4).reshape(scenarios * rows * (columns // LANES), LANES)


def from_tiles(tiles, shape):
    scenarios, rows, columns = shape
    high = min(rows, SUBLANES)
    parts = tiles.reshape(scenarios, rows // high, columns // LANES, high, LANES)
    return parts.transpose(0, 1, 3, 2, 4).reshape(shape)


def tile_offset(row, lane_tile, rows, lane_tiles):
    high = min(rows, SUBLANES)
    return (row // high * lane_tiles + lane_tile) * high + row % high


def read_row(ref, first_scenario, count, row, rows, columns):
    lane_tiles = columns // LANES
    per = rows * lane_tiles
    return jnp.concatenate(
        [
            ref[pl.ds(first_scenario * per + tile_offset(row, t, rows, lane_tiles), count, stride=per), :]
            for t in range(lane_tiles)
        ],
        axis=1,
    )


def write_row(ref, first_scenario, count, row, rows, columns, values):
    lane_tiles = columns // LANES
    per = rows * lane_tiles
    for t in range(lane_tiles):
        place = pl.ds(first_scenario * per + tile_offset(row, t, rows, lane_tiles), count, stride=per)
        ref[place, :] = values[:, t * LANES : (t + 1) * LANES]


def drift_tail(drift_ref, start):
    pieces = [
        jnp.concatenate([drift_ref[c, start : start + 1], drift_ref[c, start + 1 : start + 2]], axis=1)
        for c in range(2)
    ]
    high, low = two_halves(jnp.concatenate(pieces, axis=0))
    ones = jnp.ones((1, high.shape[1]), bf16)
    zeros = jnp.zeros((EXTRA - 5, high.shape[1]), bf16)
    return jnp.concatenate([high, low, ones, zeros], axis=0)


def band_matrix(columns):
    row = lax.broadcasted_iota(jnp.int32, (columns, columns), 0)
    column = lax.broadcasted_iota(jnp.int32, (columns, columns), 1)
    right = jnp.where(column == row + 1, 1.0, 0.0)
    left = jnp.where(column == row - 1, 1.0, 0.0)
    centre = jnp.where(column == row, 1.0 - 4.0 * diffusion_rate, diffusion_rate * (right + left))
    return centre.astype(bf16), (right - left).astype(bf16)


def half_shifts(levels_ref, table_ref, shift_ref):
    scenarios = levels_ref.shape[1]
    for t in range(levels_ref.shape[0]):
        level = jnp.broadcast_to(levels_ref[t : t + 1, :].astype(f32), (LANES, scenarios)).T
        for c in range(2):
            shift = jnp.zeros(level.shape, f32)
            for n in range(table_ref.shape[1]):
                shift = jnp.where(level == n, 0.5 * table_ref[c : c + 1, n : n + 1], shift)
            shift_ref[2 * t + c] = shift


def wide(values, columns):
    return jnp.concatenate([values] * (columns // LANES), axis=1)


def one_step(rows_of, places, half_drift, band, shift_x, shift_y, pairs, terms, write):
    size, columns = shift_x.shape
    whole = pl.ds(0, columns)

    def density(row):
        return pairs[pl.ds(rows_of[row] * size, size), whole].astype(f32)

    for row in places:
        flux = (half_drift(1, row) + shift_y) * density(row)
        pairs[pl.ds(rows_of[row] * size, size), pl.ds(columns, columns)] = flux.astype(bf16)
    runs = []
    for row in places:
        at = rows_of[row]
        if runs and runs[-1][0] + runs[-1][1] == at:
            runs[-1][1] += 1
        else:
            runs.append([at, 1])
    for at, count in runs:
        where = pl.ds(at * size, count * size)
        terms[where, :] = jnp.dot(pairs[where, :], band, preferred_element_type=f32)
    for row in places:
        low = density(row - 1) * ((diffusion_rate + half_drift(0, row - 1)) + shift_x)
        high = density(row + 1) * ((diffusion_rate - half_drift(0, row + 1)) - shift_x)
        write(row, terms[pl.ds(rows_of[row] * size, size), :] + low + high)


def two_steps(first, last, read, half_drift, edge, band, shifts, scratch, write):
    pairs, later, terms = scratch
    size, columns = shifts[0].shape
    rows_of = {row: k for k, row in enumerate(range(first - 2, last + 3))}
    for row, k in rows_of.items():
        pairs[pl.ds(k * size, size), pl.ds(0, columns)] = read(row).astype(bf16)

    def write_later(row, density):
        later[pl.ds(rows_of[row] * size, size), pl.ds(0, columns)] = edge(row, density).astype(bf16)

    one_step(
        rows_of, range(first - 1, last + 2), half_drift, band, shifts[0], shifts[1], pairs, terms, write_later
    )
    one_step(rows_of, range(first, last + 1), half_drift, band, shifts[2], shifts[3], later, terms, write)


def step_scratch(rows, size, columns):
    pairs = pltpu.VMEM(((rows + 4) * size, 2 * columns), bf16)
    return [pairs, pairs, pltpu.VMEM(((rows + 4) * size, columns), f32)]


def inner_kernel(
    rows, size, hist_ref, drift_hbm, levels_hbm, table_hbm,
    first_ref, next_ref, prev_ref, last_ref, shift_ref, band_ref, inner_ref,
    drift_ref, levels_ref, table_ref, arrived, *scratch,
):
    step = pl.program_id(0)
    columns = drift_ref.shape[2]

    @pl.when(step == 0)
    def _():
        sources = ((drift_hbm, drift_ref), (levels_hbm, levels_ref), (table_hbm, table_ref))
        copies = [pltpu.make_async_copy(*pair, arrived.at[n]) for n, pair in enumerate(sources)]
        for copy in copies:
            copy.start()
        centre, flux = band_matrix(columns)
        band_ref[pl.ds(0, columns), :] = centre
        band_ref[pl.ds(columns, columns), :] = flux
        for copy in copies:
            copy.wait()
        half_shifts(levels_ref, table_ref, shift_ref)
        for out, start in ((first_ref, 0), (last_ref, rows - 2)):
            out[pl.ds(out.shape[0] - EXTRA, EXTRA), :] = drift_tail(drift_ref, start)

    where = pl.ds(pl.multiple_of(step * size, size), size)
    edges = {}
    for out, start in ((first_ref, 0), (next_ref, 2), (prev_ref, rows - 4), (last_ref, rows - 2)):
        for k in range(2):
            edges.setdefault(start + k, []).append((out, k))

    def read(row):
        density = read_row(hist_ref, 0, size, row, rows, columns)
        for out, k in edges.get(row, []):
            out[where, pl.ds(k * columns, columns)] = density.astype(bf16)
        return density

    if rows <= 4:
        for row in range(rows):
            read(row)
        return

    def write(row, density):
        inner_ref[:, pl.ds((row - 2) * columns, columns)] = density.astype(bf16)

    two_steps(
        2,
        rows - 3,
        read,
        lambda c, row: 0.5 * drift_ref[c, row : row + 1, :],
        lambda row, density: density,
        band_ref[...],
        [wide(shift_ref[n, where, :], columns) for n in range(4)],
        scratch,
        write,
    )


def inner_steps(tiles, drift, levels, table):
    scenarios = levels.shape[1]
    rows, columns = drift.shape[1:]
    per = tiles.shape[0] // scenarios
    size = scenario_block(scenarios)
    inner = max(rows - 4, 1) * columns
    edge = jax.ShapeDtypeStruct((scenarios, 2 * columns), bf16)
    sent = jax.ShapeDtypeStruct((scenarios + EXTRA, 2 * columns), bf16)
    shifts = jax.ShapeDtypeStruct((4, scenarios, LANES), f32)
    band = jax.ShapeDtypeStruct((2 * columns, columns), bf16)
    return pl.pallas_call(
        functools.partial(inner_kernel, rows, size),
        grid=(scenarios // size,),
        in_specs=[pl.BlockSpec((size * per, LANES), lambda i: (i, 0))] + [pl.BlockSpec(memory_space=pltpu.HBM)] * 3,
        out_specs=[pl.BlockSpec(shape.shape, lambda i: (0, 0)) for shape in (sent, edge, edge, sent)]
        + [
            pl.BlockSpec(shifts.shape, lambda i: (0, 0, 0)),
            pl.BlockSpec(band.shape, lambda i: (0, 0)),
            pl.BlockSpec((size, inner), lambda i: (i, 0)),
        ],
        out_shape=[sent, edge, edge, sent, shifts, band, jax.ShapeDtypeStruct((scenarios, inner), bf16)],
        scratch_shapes=[
            pltpu.VMEM(drift.shape, f32),
            pltpu.VMEM(levels.shape, levels.dtype),
            pltpu.VMEM(table.shape, f32),
            pltpu.SemaphoreType.DMA((3,)),
        ]
        + step_scratch(max(rows - 4, 1), size, columns),
        compiler_params=params(),
        cost_estimate=pl.CostEstimate(flops=1, bytes_accessed=1, transcendentals=0),
        name="inner_density_steps",
    )(tiles, drift, levels, table)


def halo_drift(ref, columns):
    tail = ref[pl.ds(ref.shape[0] - EXTRA, EXTRA), :].astype(f32)
    both = 0.5 * (tail[0:2] + tail[2:4])
    rows = [[both[c : c + 1, k * columns : (k + 1) * columns] for k in range(2)] for c in range(2)]
    return rows, tail[4:5, :columns]


def with_halo(drift_ref, below_ref, above_ref):
    rows, columns = drift_ref.shape[1:]
    below, below_valid = halo_drift(below_ref, columns)
    above, above_valid = halo_drift(above_ref, columns)

    def half_drift(c, row):
        if row < 0:
            return below[c][row + 2]
        if row >= rows:
            return above[c][row - rows]
        return 0.5 * drift_ref[c, row : row + 1, :]

    def edge(row, density):
        if row < 0:
            return density * below_valid
        if row >= rows:
            return density * above_valid
        return density

    return half_drift, edge


def edge_kernel(
    size, drift_ref, shift_ref, band_ref, first_ref, next_ref, prev_ref, last_ref, below_ref, above_ref, *refs
):
    low_ref, high_ref, *scratch = refs[-5:]
    rows, columns = drift_ref.shape[1:]
    half_drift, edge = with_halo(drift_ref, below_ref, above_ref)
    where = pl.ds(pl.multiple_of(pl.program_id(0) * size, size), size)
    shifts = [wide(shift_ref[n, where, :], columns) for n in range(4)]
    for out, refs, first in (
        (low_ref, (below_ref, first_ref, next_ref), 0),
        (high_ref, (prev_ref, last_ref, above_ref), rows - 2),
    ):

        def read(row):
            at = row - (first - 2)
            return refs[at // 2][where, pl.ds(at % 2 * columns, columns)].astype(f32)

        def write(row, density):
            out[:, pl.ds((row - first) * columns, columns)] = density.astype(bf16)

        two_steps(first, first + 1, read, half_drift, edge, band_ref[...], shifts, scratch, write)


def edge_steps(drift, shifts, band, own, below, above, deps):
    scenarios = shifts.shape[1]
    columns = drift.shape[2]
    size = scenario_block(scenarios)
    edge = jax.ShapeDtypeStruct((scenarios, 2 * columns), bf16)
    spec = pl.BlockSpec((size, 2 * columns), lambda i: (i, 0))
    return pl.pallas_call(
        functools.partial(edge_kernel, size),
        grid=(scenarios // size,),
        in_specs=[
            pl.BlockSpec(drift.shape, lambda i: (0, 0, 0)),
            pl.BlockSpec(shifts.shape, lambda i: (0, 0, 0)),
            pl.BlockSpec(band.shape, lambda i: (0, 0)),
        ]
        + [pl.BlockSpec(ref.shape, lambda i: (0, 0)) for ref in (*own, below, above)]
        + any_specs(deps),
        out_specs=[spec, spec],
        out_shape=[edge, edge],
        scratch_shapes=step_scratch(2, size, columns),
        compiler_params=params(),
        cost_estimate=pl.CostEstimate(flops=1, bytes_accessed=1, transcendentals=0),
        name="edge_density_steps",
    )(drift, shifts, band, *own, below, above, *deps)


def density_kernel(
    rows, size, first_step, hist_ref, drift_ref, shift_ref, band_ref, below_ref, above_ref, dep_ref, *refs
):
    next_ref, token_ref, *scratch = refs[-5:]
    token_ref[...] = jnp.zeros(token_ref.shape, f32)
    columns = drift_ref.shape[2]
    half_drift, edge = with_halo(drift_ref, below_ref, above_ref)
    where = pl.ds(pl.multiple_of((first_step + pl.program_id(0)) * size, size), size)

    def read(row):
        if row < 0:
            return below_ref[where, pl.ds((row + 2) * columns, columns)].astype(f32)
        if row >= rows:
            return above_ref[where, pl.ds((row - rows) * columns, columns)].astype(f32)
        return read_row(hist_ref, 0, size, row, rows, columns)

    two_steps(
        0,
        rows - 1,
        read,
        half_drift,
        edge,
        band_ref[...],
        [wide(shift_ref[n, where, :], columns) for n in range(4)],
        scratch,
        lambda row, density: write_row(next_ref, 0, size, row, rows, columns, density),
    )


def density_steps(tiles, drift, shifts, band, below, above, dep, so_far, turn, turns):
    scenarios = shifts.shape[1]
    rows, columns = drift.shape[1:]
    per = tiles.shape[0] // scenarios
    size = 3 * GROUP if scenarios % (turns * GROUP * 3) == 0 else GROUP
    steps = scenarios // size // turns
    first = turn * steps
    block = pl.BlockSpec((size * per, LANES), lambda i: (first + i, 0))
    hidden = pl.BlockSpec(memory_space=pltpu.HBM)
    args = [tiles, drift, shifts, band, below, above, dep]
    in_specs = [
        block,
        pl.BlockSpec(drift.shape, lambda i: (0, 0, 0)),
        pl.BlockSpec(shifts.shape, lambda i: (0, 0, 0)),
        pl.BlockSpec(band.shape, lambda i: (0, 0)),
        pl.BlockSpec(below.shape, lambda i: (0, 0)),
        pl.BlockSpec(above.shape, lambda i: (0, 0)),
        hidden,
    ]
    aliases = {}
    if so_far is not None:
        args.append(so_far)
        in_specs.append(hidden)
        aliases = {7: 0}
    return pl.pallas_call(
        functools.partial(density_kernel, rows, size, first),
        grid=(steps,),
        in_specs=in_specs,
        out_specs=[block, pl.BlockSpec((SUBLANES, LANES), lambda i: (0, 0))],
        out_shape=[pltpu.HBM(tiles.shape, f32), jax.ShapeDtypeStruct((SUBLANES, LANES), f32)],
        input_output_aliases=aliases,
        scratch_shapes=step_scratch(rows, size, columns),
        compiler_params=params(),
        cost_estimate=pl.CostEstimate(flops=1, bytes_accessed=1, transcendentals=0),
        name="density_steps",
    )(*args)


def smem():
    return pl.BlockSpec(memory_space=pltpu.SMEM)


def swap(values, count, flip):
    return lax.ppermute(values, "grid", [(i, i ^ flip) for i in range(count)])


def inner_product_kernel(count, dep_count, *refs):
    inputs_ref = refs[0]
    weights = refs[1 : 1 + count]
    weight = jnp.concatenate([ref[...] for ref in weights], axis=0)
    refs[-1][0] = jnp.dot(inputs_ref[...], weight, preferred_element_type=f32)


def inner_product(inner, weight, width, deps):
    scenarios, cells = inner.shape
    total, hidden = weight.shape
    size = (total - cells) // 2
    count = cells // size
    hidden_spec = pl.BlockSpec(memory_space=pl.ANY)

    def spec(k):
        return pl.BlockSpec((size, width), lambda n: (1 + k, n))

    return pl.pallas_call(
        functools.partial(inner_product_kernel, count, len(deps)),
        grid=(hidden // width,),
        in_specs=[pl.BlockSpec(inner.shape, lambda n: (0, 0))]
        + [spec(k) for k in range(count)]
        + [hidden_spec] * len(deps),
        out_specs=pl.BlockSpec((1, scenarios, width), lambda n: (n, 0, 0)),
        out_shape=jax.ShapeDtypeStruct((hidden // width, scenarios, width), f32),
        compiler_params=params(),
        cost_estimate=pl.CostEstimate(flops=1, bytes_accessed=1, transcendentals=0),
        name="inner_product",
    )(inner, *([weight] * count), *deps)


def edge_product_kernel(block, with_inner, place_ref, low_ref, high_ref, top_ref, bottom_ref, *refs):
    keep_ref, send_ref, total = refs[-3:]
    left = jnp.concatenate([low_ref[...], high_ref[...]], axis=1)
    weight = jnp.concatenate([top_ref[...], bottom_ref[...]], axis=0)
    product = jnp.dot(left, weight, preferred_element_type=f32)
    total[...] = product + refs[0][0] if with_inner else product
    core = place_ref[0]
    for out, half in ((keep_ref, core), (send_ref, 1 - core)):
        for side in range(2):
            start = pl.multiple_of((2 * half + side) * block, block)
            out[side, 0] = total[pl.ds(start, block), :].astype(out.dtype)


def edge_product(place, low, high, weight, inner, parts, width, chunk):
    scenarios, size = low.shape
    block = scenarios // 4
    last = weight.shape[0] // size - 1
    shape = (2, parts, block, width)
    spec = pl.BlockSpec((2, 1, block, width), lambda n: (0, n, 0, 0))
    in_specs = [
        smem(),
        pl.BlockSpec(low.shape, lambda n: (0, 0)),
        pl.BlockSpec(low.shape, lambda n: (0, 0)),
        pl.BlockSpec((size, width), lambda n: (0, chunk * parts + n)),
        pl.BlockSpec((size, width), lambda n: (last, chunk * parts + n)),
    ]
    args = [place, low, high, weight, weight]
    if inner is not None:
        in_specs.append(pl.BlockSpec((1, scenarios, width), lambda n: (chunk * parts + n, 0, 0)))
        args.append(inner)
    return pl.pallas_call(
        functools.partial(edge_product_kernel, block, inner is not None),
        grid=(parts,),
        in_specs=in_specs,
        out_specs=[spec, spec],
        out_shape=[jax.ShapeDtypeStruct(shape, f32), jax.ShapeDtypeStruct(shape, bf16)],
        scratch_shapes=[pltpu.VMEM((scenarios, width), f32)],
        compiler_params=params(),
        cost_estimate=pl.CostEstimate(flops=1, bytes_accessed=1, transcendentals=0),
        name="edge_product",
    )(*args)


def add_side_kernel(place_ref, mine_ref, other_ref, *refs):
    keep_ref, send_ref = refs[-2:]
    side = place_ref[1]
    keep_ref[...] = mine_ref[side] + other_ref[side].astype(f32)
    send_ref[...] = (mine_ref[1 - side] + other_ref[1 - side].astype(f32)).astype(bf16)


def any_specs(deps):
    return [pl.BlockSpec(memory_space=pl.ANY)] * len(deps)


def add_side(place, mine, other, deps=()):
    shape = mine.shape[1:]
    return pl.pallas_call(
        add_side_kernel,
        in_specs=[smem()] + [pl.BlockSpec(memory_space=pltpu.VMEM)] * 2 + any_specs(deps),
        out_shape=[jax.ShapeDtypeStruct(shape, f32), jax.ShapeDtypeStruct(shape, bf16)],
        compiler_params=params(),
        cost_estimate=pl.CostEstimate(flops=1, bytes_accessed=1, transcendentals=0),
        name="add_side",
    )(place, mine, other, *deps)


def add_parts_kernel(dep_count, place_ref, mine_ref, other_ref, *refs):
    own_ref, *send_refs = refs[dep_count:]
    part = place_ref[2]
    own_ref[...] = mine_ref[part] + other_ref[part].astype(f32)
    for k, out in enumerate(send_refs):
        at = part ^ (k + 1)
        out[...] = (mine_ref[at] + other_ref[at].astype(f32)).astype(bf16)


def add_parts(place, mine, other, deps=()):
    parts = mine.shape[0]
    vmem = pl.BlockSpec(memory_space=pltpu.VMEM)
    return pl.pallas_call(
        functools.partial(add_parts_kernel, len(deps)),
        in_specs=[smem(), vmem, vmem] + any_specs(deps),
        out_shape=[jax.ShapeDtypeStruct(mine.shape[1:], f32)]
        + [jax.ShapeDtypeStruct(mine.shape[1:], bf16)] * (parts - 1),
        compiler_params=params(),
        cost_estimate=pl.CostEstimate(flops=1, bytes_accessed=1, transcendentals=0),
        name="add_parts",
    )(place, mine, other, *deps)


def activate_kernel(count, *refs):
    total = refs[0][...]
    for ref in refs[1 : 1 + count]:
        total = total + ref[...].astype(f32)
    refs[-1][...] = jnp.tanh(total).astype(bf16)


def activate(own, received, deps=()):
    return pl.pallas_call(
        functools.partial(activate_kernel, len(received)),
        in_specs=[pl.BlockSpec(memory_space=pltpu.VMEM)] * (1 + len(received)) + any_specs(deps),
        out_shape=jax.ShapeDtypeStruct(own.shape, bf16),
        compiler_params=params(),
        cost_estimate=pl.CostEstimate(flops=1, bytes_accessed=1, transcendentals=0),
        name="first_activation",
    )(own, *received, *deps)


def two_halves(exact):
    high = exact.astype(bf16)
    low = (exact - high.astype(f32)).astype(bf16)
    return high, low


def tail_rows(exact):
    high, low = two_halves(exact)
    zeros = jnp.zeros((EXTRA - 2, exact.shape[1]), bf16)
    return jnp.concatenate([high, low, zeros], axis=0)


def middle_kernel(chunks, parts, width, *refs):
    pieces = chunks * parts
    place_ref, cot_ref = refs[0], refs[1]
    first_refs = refs[2 : 2 + pieces]
    mid_refs = refs[2 + pieces : 6 + pieces]
    weight_refs = refs[6 + pieces : 10 + pieces]
    outs = refs[-(3 + parts) :]
    own_ref, value_ref, mid_keep_ref, mid_send_ref = outs[:4]
    send_refs = outs[4:]
    part = place_ref[2]
    block = cot_ref.shape[0]

    def mid_rows(start):
        return jnp.concatenate([ref[pl.ds(start, width), :] for ref in mid_refs], axis=1)

    def start_of(c, k):
        return pl.multiple_of((c * parts + (part ^ k)) * width, width)

    total = None
    for c in range(chunks):
        for k in range(parts):
            term = jnp.dot(first_refs[c * parts + k][...], mid_rows(start_of(c, k)), preferred_element_type=f32)
            total = term if total is None else total + term
    second_low = jnp.tanh(total).astype(bf16)
    second = second_low.astype(f32)
    head = jnp.concatenate([ref[...] for ref in weight_refs], axis=1)
    heads = tail_rows(head)
    rows = lax.dot_general(heads, second_low, (((1,), (1,)), ((), ())), preferred_element_type=f32)
    value = rows[0:1] + rows[1:2]
    if width > block:
        value = jnp.concatenate([value, jnp.zeros((1, width - block), f32)], axis=1)
    value_ref[...] = value
    cot = cot_ref[...]
    head_part = jnp.sum(cot * second, axis=0, keepdims=True)
    back = (cot * head * (1.0 - second * second)).astype(bf16)
    units = mid_refs[0].shape[1]
    for k in range(parts):
        for c in range(chunks):
            piece = lax.dot_general(
                back, mid_rows(start_of(c, k)), (((1,), (1,)), ((), ())), preferred_element_type=f32
            )
            if k == 0:
                own_ref[pl.ds(c * block, block), :] = piece
            else:
                send_refs[k - 1][pl.ds(c * block, block), :] = piece.astype(bf16)
        if k > 0:
            send_refs[k - 1][pl.ds(chunks * block, EXTRA), :] = tail_rows(value)
    for c in range(chunks):
        for k in range(parts):
            product = lax.dot_general(
                first_refs[c * parts + k][...], back, (((0,), (0,)), ((), ())), preferred_element_type=f32
            ).astype(bf16)
            for p in range(4):
                out = (mid_keep_ref, mid_send_ref)[p % 2]
                out[p // 2, pl.ds(start_of(c, k), width), :] = product[:, p * units : (p + 1) * units]
    for p in range(4):
        out = (mid_keep_ref, mid_send_ref)[p % 2]
        out[p // 2, pl.ds(pieces * width, EXTRA), :] = tail_rows(head_part[:, p * units : (p + 1) * units])


def middle(place, cot, firsts, mids, heads, chunks, parts, width, deps=()):
    block = cot.shape[0]
    hidden, units = mids[0].shape
    partial = jax.ShapeDtypeStruct((2, hidden + EXTRA, units), bf16)
    vmem = pl.BlockSpec(memory_space=pltpu.VMEM)
    return pl.pallas_call(
        functools.partial(middle_kernel, chunks, parts, width),
        in_specs=[smem()] + [vmem] * (1 + len(firsts) + 8) + any_specs(deps),
        out_shape=[
            jax.ShapeDtypeStruct((chunks * block, width), f32),
            jax.ShapeDtypeStruct((1, width), f32),
            partial,
            partial,
        ]
        + [jax.ShapeDtypeStruct((chunks * block + EXTRA, width), bf16)] * (parts - 1),
        compiler_params=params(),
        cost_estimate=pl.CostEstimate(flops=1, bytes_accessed=1, transcendentals=0),
        name="value_layers",
    )(place, cot, *firsts, *mids, *heads, *deps)


def add_tail(left, right, hidden):
    body = left[:hidden].astype(f32) + right[:hidden].astype(f32)
    tails = left[hidden:].astype(f32) + right[hidden:].astype(f32)
    return body.astype(bf16), tails[0:1] + tails[1:2]


def mid_add_kernel(keep_ref, other_ref, *refs):
    own_ref, send_ref = refs[-2:]
    hidden = own_ref.shape[0] - EXTRA
    for at, out in enumerate((own_ref, send_ref)):
        body, tail = add_tail(keep_ref[at], other_ref[at], hidden)
        out[pl.ds(0, hidden), :] = body
        out[pl.ds(hidden, EXTRA), :] = tail_rows(tail)


def mid_add(keep, other, deps=()):
    shape = jax.ShapeDtypeStruct(keep.shape[1:], bf16)
    return pl.pallas_call(
        mid_add_kernel,
        in_specs=[pl.BlockSpec(memory_space=pltpu.VMEM)] * 2 + any_specs(deps),
        out_shape=[shape, shape],
        compiler_params=params(),
        cost_estimate=pl.CostEstimate(flops=1, bytes_accessed=1, transcendentals=0),
        name="mid_gradient_add",
    )(keep, other, *deps)


def mid_final_kernel(own_ref, other_ref, out_ref, head_ref):
    body, tail = add_tail(own_ref[...], other_ref[...], out_ref.shape[0])
    out_ref[...] = body
    head_ref[...] = tail


def mid_final(own, other):
    hidden = own.shape[0] - EXTRA
    return pl.pallas_call(
        mid_final_kernel,
        out_shape=[
            jax.ShapeDtypeStruct((hidden, own.shape[1]), bf16),
            jax.ShapeDtypeStruct((1, own.shape[1]), f32),
        ],
        compiler_params=params(),
        cost_estimate=pl.CostEstimate(flops=1, bytes_accessed=1, transcendentals=0),
        name="mid_gradient_final",
    )(own, other)


def back_first_kernel(chunks, count, *refs):
    own_ref, value_ref = refs[:2]
    received = refs[2 : 2 + count]
    first_refs = refs[2 + count : 2 + count + chunks]
    out_refs = refs[-1 - chunks : -1]
    tail_ref = refs[-1]
    block = first_refs[0].shape[0]
    value = value_ref[...]
    for ref in received:
        tail = ref[pl.ds(chunks * block, EXTRA), :].astype(f32)
        value = value + (tail[0:1] + tail[1:2])
    tail_ref[...] = tail_rows(value)
    for c in range(chunks):
        total = own_ref[pl.ds(c * block, block), :]
        for ref in received:
            total = total + ref[pl.ds(c * block, block), :].astype(f32)
        first = first_refs[c][...].astype(f32)
        out_refs[c][...] = (total * (1.0 - first * first)).astype(bf16)


def back_first(own, value, received, firsts, deps=()):
    chunks = len(firsts)
    shape = firsts[0].shape
    return pl.pallas_call(
        functools.partial(back_first_kernel, chunks, len(received)),
        in_specs=[pl.BlockSpec(memory_space=pltpu.VMEM)] * (2 + len(received) + chunks) + any_specs(deps),
        out_shape=[jax.ShapeDtypeStruct(shape, bf16)] * chunks
        + [jax.ShapeDtypeStruct((EXTRA, shape[1]), bf16)],
        compiler_params=params(),
        cost_estimate=pl.CostEstimate(flops=1, bytes_accessed=1, transcendentals=0),
        name="back_first",
    )(own, value, *received, *firsts, *deps)


def stack_kernel(count, *refs):
    at = 0
    for ref in refs[:count]:
        refs[-1][pl.ds(at, ref.shape[0]), :] = ref[...]
        at += ref.shape[0]


def stack(pieces, deps=()):
    rows = sum(piece.shape[0] for piece in pieces)
    return pl.pallas_call(
        functools.partial(stack_kernel, len(pieces)),
        in_specs=[pl.BlockSpec(memory_space=pltpu.VMEM)] * len(pieces) + any_specs(deps),
        out_shape=jax.ShapeDtypeStruct((rows, pieces[0].shape[1]), bf16),
        compiler_params=params(),
        cost_estimate=pl.CostEstimate(flops=1, bytes_accessed=1, transcendentals=0),
        name="stack_parts",
    )(*pieces, *deps)


def turn_kernel(count, *refs):
    for ref, out in zip(refs[:count], refs[-count:]):
        out[...] = ref[...].T


def transposed(arrays, deps):
    vmem = pl.BlockSpec(memory_space=pltpu.VMEM)
    return pl.pallas_call(
        functools.partial(turn_kernel, len(arrays)),
        in_specs=[vmem] * len(arrays) + any_specs(deps),
        out_shape=[jax.ShapeDtypeStruct(array.shape[::-1], array.dtype) for array in arrays],
        compiler_params=params(),
        cost_estimate=pl.CostEstimate(flops=1, bytes_accessed=1, transcendentals=0),
        name="transposed_inputs",
    )(*arrays, *deps)


def first_grad_kernel(parts, block, count, tile, with_value, with_output, *refs):
    place_ref = refs[0]
    lefts = refs[1 : 1 + count]
    stacks = refs[1 + count : 5 + count]
    out_ref = refs[5 + count + with_output]
    whole = refs[-1]
    width = stacks[0].shape[1]
    step = pl.program_id(0)
    part, mine = place_ref[2], place_ref[3]

    if with_value:

        @pl.when(step == 0)
        def _():
            for t, ref in enumerate(stacks):
                at = mine ^ (2 * (t % 2) + t // 2)
                tail = ref[pl.ds(parts * block, EXTRA), :].astype(f32)
                refs[6 + count + with_output][pl.ds(at, 1), :] = tail[0:1] + tail[1:2]

    tiles = width // tile
    piece = step // tiles ^ part
    column = pl.ds(pl.multiple_of(step % tiles * tile, tile), tile)
    for t, ref in enumerate(stacks):
        at = mine ^ (2 * (t % 2) + t // 2)
        whole[pl.ds(pl.multiple_of(at * block, block), block), :] = ref[
            pl.ds(pl.multiple_of(piece * block, block), block), column
        ]
    start = 0
    for ref in lefts:
        cells = ref.shape[0]
        out_ref[pl.ds(start, cells), :] = jnp.dot(ref[...], whole[...], preferred_element_type=f32).astype(bf16)
        start += cells


def first_grad(place, lefts, stacks, so_far, hidden, parts, block, chunk):
    scenarios = lefts[0].shape[1]
    cells = sum(left.shape[0] for left in lefts)
    width = stacks[0].shape[1]
    tile = min(width, 256)
    steps = parts * width // tile
    with_value = chunk == 0
    with_output = so_far is not None
    in_specs = [smem()] + [pl.BlockSpec(ref.shape, lambda i: (0, 0)) for ref in (*lefts, *stacks)]
    args = [place, *lefts, *stacks]
    aliases = {}
    if with_output:
        aliases = {len(args): 0}
        in_specs.append(pl.BlockSpec(memory_space=pl.ANY))
        args.append(so_far)
    out_specs = [pl.BlockSpec((cells, tile), lambda i: (0, chunk * steps + i))]
    out_shape = [jax.ShapeDtypeStruct((cells, hidden), bf16)]
    if with_value:
        out_specs.append(pl.BlockSpec((4, width), lambda i: (0, 0)))
        out_shape.append(jax.ShapeDtypeStruct((4, width), f32))
    return pl.pallas_call(
        functools.partial(first_grad_kernel, parts, block, len(lefts), tile, with_value, with_output),
        grid=(steps,),
        in_specs=in_specs,
        out_specs=out_specs,
        out_shape=out_shape,
        input_output_aliases=aliases,
        scratch_shapes=[pltpu.VMEM((scenarios, tile), bf16)],
        compiler_params=params(),
        cost_estimate=pl.CostEstimate(flops=1, bytes_accessed=1, transcendentals=0),
        name="first_gradient",
    )(*args)


def local(hist, drift, shocks, shock_table, first_weight, mid_weight, head_weight, cotangent):
    scenarios, rows, columns = hist.shape
    count = lax.axis_size("grid")
    hidden = first_weight.shape[1]
    units = mid_weight.shape[1]
    parts = count // 4
    chunks = CHUNKS if hidden % (parts * CHUNKS * LANES) == 0 else 1
    width = hidden // (parts * chunks)
    block = scenarios // 4
    index = lax.axis_index("grid")
    core, side, part = index % 2, index // 2 % 2, index // 4
    mine = 2 * core + side
    tiles = pltpu.with_memory_space_constraint(to_tiles(hist), pltpu.HBM)

    place = jnp.stack([core, side, part, mine])
    cot = lax.dynamic_slice_in_dim(cotangent, mine * block, block)[:, None]
    heads = [head_weight[None, :]]
    mids = [mid_weight]

    *own_rows, shifts, band, inner = inner_steps(tiles, drift, shocks.T, shock_table.T)
    inner = inner if rows > 4 else None
    forward = [(i, i + 1) for i in range(count - 1)]
    backward = [(i + 1, i) for i in range(count - 1)]
    below = lax.ppermute(own_rows[3], "grid", forward)
    above = lax.ppermute(own_rows[0], "grid", backward)
    product = None if inner is None else inner_product(inner, first_weight, width, [])
    low, high = edge_steps(drift, shifts, band, own_rows, below, above, [] if product is None else [product])

    def density_turn(turn, dep, so_far):
        return density_steps(tiles, drift, shifts, band, below, above, dep, so_far, turn, 4)

    owned, firsts, density = [], [], None
    products = [edge_product(place, low, high, first_weight, product, parts, width, c) for c in range(chunks)]
    sums = []
    for c, (keep, send) in enumerate(products):
        keep, send = add_side(place, keep, swap(send, count, 1))
        sums.append((keep, send, swap(send, count, 2)))
    density, token = density_turn(0, sums[-1][1], density)
    mids.append(swap(mids[0], count, 1))
    mids.append(swap(mids[0], count, 2))
    mids.append(swap(mids[2], count, 1))
    for c, (keep, send, other) in enumerate(sums):
        own, *sends = add_parts(place, keep, other, [token])
        received = [swap(piece, count, 4 * (k + 1)) for k, piece in enumerate(sends)]
        if c == chunks - 1:
            density, token = density_turn(1, sends[-1], density)
        owned.append(activate(own, received, [token, mids[2]] if c == chunks - 1 else []))
    for first in owned:
        firsts.append(first)
        firsts += [swap(first, count, 4 * k) for k in range(1, parts)]
    heads += [swap(heads[0], count, k) for k in range(1, 4)]
    density, token = density_turn(2, owned[-1], density)
    own, value, mid_keep, mid_send, *sends = middle(
        place, cot, firsts, mids, heads, chunks, parts, width, [token]
    )
    received = [swap(piece, count, 4 * (k + 1)) for k, piece in enumerate(sends)]
    *backs, tail = back_first(own, value, received, owned)
    mid_keep, mid_send = mid_add(mid_keep, swap(mid_send, count, 1), [backs[-1]])
    density, token = density_turn(3, backs[-1], density)
    lefts = transposed([low, high] if inner is None else [low, inner, high], [token])
    grad_mid, grad_head = mid_final(mid_keep, swap(mid_send, count, 2))
    grad_first = None
    for c in range(chunks):
        pieces = [backs[c]] + [swap(backs[c], count, 4 * k) for k in range(1, parts)]
        mine_stack = stack(pieces + [tail] if c == 0 else pieces, [grad_mid, lefts[0]])
        stacks = [mine_stack, swap(mine_stack, count, 1), swap(mine_stack, count, 2)]
        stacks.append(swap(stacks[2], count, 1))
        results = first_grad(place, lefts, stacks, grad_first, hidden, parts, block, c)
        grad_first = results[0]
        if c == 0:
            value = results[1][:, :block].reshape(scenarios)
    return from_tiles(density, hist.shape), value, grad_first, grad_mid, grad_head[0]


def solution(mesh):
    in_specs = (
        P("groups", "grid", None),
        P(None, "grid", None),
        P("groups", None),
        P("groups", None),
        P(("groups", "grid"), None),
        P("groups", "grid"),
        P(("groups", "grid")),
        P("groups"),
    )
    out_specs = (
        P("groups", "grid", None),
        P("groups"),
        P(("groups", "grid"), None),
        P("groups", "grid"),
        P(("groups", "grid")),
    )
    return jax.shard_map(local, mesh=mesh, in_specs=in_specs, out_specs=out_specs, check_vma=False)
```

```python
import functools
import jax
import jax.numpy as jnp
from jax import lax
from jax.experimental import pallas as pl
from jax.experimental.pallas import tpu as pltpu
from jax.sharding import PartitionSpec as P

diffusion_rate = 0.24
VMEM_BYTES = 40 * 1024 * 1024
EXTRA = 16
bf16 = jnp.bfloat16
f32 = jnp.float32


def params():
    return pltpu.CompilerParams(vmem_limit_bytes=VMEM_BYTES)


def scenario_block(scenarios):
    for size in (64, 32, 16):
        if scenarios % size == 0:
            return size
    return scenarios


LANES = 128
SUBLANES = 8
GROUP = 16


def to_tiles(hist):
    scenarios, rows, columns = hist.shape
    high = min(rows, SUBLANES)
    tiles = hist.reshape(scenarios, rows // high, high, columns // LANES, LANES)
    return tiles.transpose(0, 1, 3, 2, 4).reshape(scenarios * rows * (columns // LANES), LANES)


def from_tiles(tiles, shape):
    scenarios, rows, columns = shape
    high = min(rows, SUBLANES)
    parts = tiles.reshape(scenarios, rows // high, columns // LANES, high, LANES)
    return parts.transpose(0, 1, 3, 2, 4).reshape(shape)


def tile_offset(row, lane_tile, rows, lane_tiles):
    high = min(rows, SUBLANES)
    return (row // high * lane_tiles + lane_tile) * high + row % high


def read_row(ref, first_scenario, count, row, rows, columns):
    lane_tiles = columns // LANES
    per = rows * lane_tiles
    return jnp.concatenate(
        [
            ref[pl.ds(first_scenario * per + tile_offset(row, t, rows, lane_tiles), count, stride=per), :]
            for t in range(lane_tiles)
        ],
        axis=1,
    )


def write_row(ref, first_scenario, count, row, rows, columns, values):
    lane_tiles = columns // LANES
    per = rows * lane_tiles
    for t in range(lane_tiles):
        place = pl.ds(first_scenario * per + tile_offset(row, t, rows, lane_tiles), count, stride=per)
        ref[place, :] = values[:, t * LANES : (t + 1) * LANES]


def drift_tail(drift_ref, start):
    pieces = [
        jnp.concatenate([drift_ref[c, start : start + 1], drift_ref[c, start + 1 : start + 2]], axis=1)
        for c in range(2)
    ]
    high, low = two_halves(jnp.concatenate(pieces, axis=0))
    ones = jnp.ones((1, high.shape[1]), bf16)
    zeros = jnp.zeros((EXTRA - 5, high.shape[1]), bf16)
    return jnp.concatenate([high, low, ones, zeros], axis=0)


def band_matrix(columns):
    row = lax.broadcasted_iota(jnp.int32, (columns, columns), 0)
    column = lax.broadcasted_iota(jnp.int32, (columns, columns), 1)
    right = jnp.where(column == row + 1, 1.0, 0.0)
    left = jnp.where(column == row - 1, 1.0, 0.0)
    centre = jnp.where(column == row, 1.0 - 4.0 * diffusion_rate, diffusion_rate * (right + left))
    return centre.astype(bf16), (right - left).astype(bf16)


def half_shifts(levels_ref, table_ref, shift_ref):
    scenarios = levels_ref.shape[1]
    for t in range(levels_ref.shape[0]):
        level = jnp.broadcast_to(levels_ref[t : t + 1, :].astype(f32), (LANES, scenarios)).T
        for c in range(2):
            shift = jnp.zeros(level.shape, f32)
            for n in range(table_ref.shape[1]):
                shift = jnp.where(level == n, 0.5 * table_ref[c : c + 1, n : n + 1], shift)
            shift_ref[2 * t + c] = shift


def wide(values, columns):
    return jnp.concatenate([values] * (columns // LANES), axis=1)


def one_step(rows_of, places, half_drift, band, shift_x, shift_y, pairs, terms, write):
    size, columns = shift_x.shape
    whole = pl.ds(0, columns)

    def density(row):
        return pairs[pl.ds(rows_of[row] * size, size), whole].astype(f32)

    for row in places:
        flux = (half_drift(1, row) + shift_y) * density(row)
        pairs[pl.ds(rows_of[row] * size, size), pl.ds(columns, columns)] = flux.astype(bf16)
    start = rows_of[places[0]] * size
    count = (rows_of[places[-1]] + 1) * size - start
    terms[pl.ds(start, count), :] = jnp.dot(pairs[pl.ds(start, count), :], band, preferred_element_type=f32)
    for row in places:
        low = density(row - 1) * ((diffusion_rate + half_drift(0, row - 1)) + shift_x)
        high = density(row + 1) * ((diffusion_rate - half_drift(0, row + 1)) - shift_x)
        write(row, terms[pl.ds(rows_of[row] * size, size), :] + low + high)


def two_steps(segments, read, half_drift, edge, band, shifts, scratch, write):
    pairs, later, terms = scratch
    size, columns = shifts[0].shape
    before, between, after = [
        [row for first, last in segments for row in range(first - more, last + more + 1)] for more in (2, 1, 0)
    ]
    rows_of = {row: k for k, row in enumerate(before)}
    for row, k in rows_of.items():
        pairs[pl.ds(k * size, size), pl.ds(0, columns)] = read(row)

    def write_later(row, density):
        later[pl.ds(rows_of[row] * size, size), pl.ds(0, columns)] = edge(row, density).astype(bf16)

    one_step(rows_of, between, half_drift, band, shifts[0], shifts[1], pairs, terms, write_later)
    one_step(rows_of, after, half_drift, band, shifts[2], shifts[3], later, terms, write)


def step_scratch(segments, size, columns):
    rows = sum(last - first + 5 for first, last in segments)
    pairs = pltpu.VMEM((rows * size, 2 * columns), bf16)
    return [pairs, pairs, pltpu.VMEM((rows * size, columns), f32)]


def edge_segments(rows):
    return [(0, 1), (rows - 2, rows - 1)] if rows >= 8 else [(0, rows - 1)]


def inner_kernel(
    rows, size, hist_ref, drift_hbm, levels_hbm, table_hbm,
    first_ref, last_ref, shift_ref, band_ref, rows_ref, inner_ref,
    drift_ref, levels_ref, table_ref, arrived, all_shifts, *scratch,
):
    step = pl.program_id(0)
    columns = drift_ref.shape[2]

    @pl.when(step == 0)
    def _():
        sources = ((drift_hbm, drift_ref), (levels_hbm, levels_ref), (table_hbm, table_ref))
        copies = [pltpu.make_async_copy(*pair, arrived.at[n]) for n, pair in enumerate(sources)]
        for copy in copies:
            copy.start()
        centre, flux = band_matrix(columns)
        band_ref[pl.ds(0, columns), :] = centre
        band_ref[pl.ds(columns, columns), :] = flux
        for copy in copies:
            copy.wait()
        half_shifts(levels_ref, table_ref, all_shifts)
        for out, start in ((first_ref, 0), (last_ref, rows - 2)):
            out[pl.ds(out.shape[0] - EXTRA, EXTRA), :] = drift_tail(drift_ref, start)

    where = pl.ds(pl.multiple_of(step * size, size), size)
    for n in range(4):
        shift_ref[n] = all_shifts[n, where, :]
    for row in range(rows):
        density = read_row(hist_ref, 0, size, row, rows, columns).astype(bf16)
        rows_ref[:, pl.ds(row * columns, columns)] = density
        if row < 2:
            first_ref[where, pl.ds(row * columns, columns)] = density
        if row >= rows - 2:
            last_ref[where, pl.ds((row - rows + 2) * columns, columns)] = density
    if rows <= 4:
        return

    def write(row, density):
        inner_ref[:, pl.ds((row - 2) * columns, columns)] = density.astype(bf16)

    two_steps(
        [(2, rows - 3)],
        lambda row: rows_ref[:, pl.ds(row * columns, columns)],
        lambda c, row: 0.5 * drift_ref[c, row : row + 1, :],
        lambda row, density: density,
        band_ref[...],
        [wide(shift_ref[n], columns) for n in range(4)],
        scratch,
        write,
    )


def inner_steps(tiles, drift, levels, table):
    scenarios = levels.shape[1]
    rows, columns = drift.shape[1:]
    per = tiles.shape[0] // scenarios
    size = scenario_block(scenarios)
    inner = max(rows - 4, 1) * columns
    sent = jax.ShapeDtypeStruct((scenarios + EXTRA, 2 * columns), bf16)
    shifts = jax.ShapeDtypeStruct((4, scenarios, LANES), f32)
    band = jax.ShapeDtypeStruct((2 * columns, columns), bf16)
    return pl.pallas_call(
        functools.partial(inner_kernel, rows, size),
        grid=(scenarios // size,),
        in_specs=[pl.BlockSpec((size * per, LANES), lambda i: (i, 0))] + [pl.BlockSpec(memory_space=pltpu.HBM)] * 3,
        out_specs=[pl.BlockSpec(sent.shape, lambda i: (0, 0))] * 2
        + [
            pl.BlockSpec((4, size, LANES), lambda i: (0, i, 0)),
            pl.BlockSpec(band.shape, lambda i: (0, 0)),
            pl.BlockSpec((size, rows * columns), lambda i: (i, 0)),
            pl.BlockSpec((size, inner), lambda i: (i, 0)),
        ],
        out_shape=[
            sent,
            sent,
            shifts,
            band,
            jax.ShapeDtypeStruct((scenarios, rows * columns), bf16),
            jax.ShapeDtypeStruct((scenarios, inner), bf16),
        ],
        scratch_shapes=[
            pltpu.VMEM(drift.shape, f32),
            pltpu.VMEM(levels.shape, levels.dtype),
            pltpu.VMEM(table.shape, f32),
            pltpu.SemaphoreType.DMA((3,)),
            pltpu.VMEM(shifts.shape, f32),
        ]
        + step_scratch([(2, max(rows - 3, 2))], size, columns),
        compiler_params=params(),
        cost_estimate=pl.CostEstimate(flops=1, bytes_accessed=1, transcendentals=0),
        name="inner_density_steps",
    )(tiles, drift, levels, table)


def halo_drift(ref, columns):
    tail = ref[...].astype(f32)
    both = 0.5 * (tail[0:2] + tail[2:4])
    rows = [[both[c : c + 1, k * columns : (k + 1) * columns] for k in range(2)] for c in range(2)]
    return rows, tail[4:5, :columns]


def with_halo(drift_ref, below_tail, above_tail):
    rows, columns = drift_ref.shape[1:]
    below, below_valid = halo_drift(below_tail, columns)
    above, above_valid = halo_drift(above_tail, columns)

    def half_drift(c, row):
        if row < 0:
            return below[c][row + 2]
        if row >= rows:
            return above[c][row - rows]
        return 0.5 * drift_ref[c, row : row + 1, :]

    def edge(row, density):
        if row < 0:
            return density * below_valid
        if row >= rows:
            return density * above_valid
        return density

    return half_drift, edge


def density_kernel(segments, drift_ref, shift_ref, band_ref, rows_ref, below_ref, above_ref, below_tail, above_tail, dep_ref, *refs):
    scratch = refs[-3:]
    rows, columns = drift_ref.shape[1:]
    size = shift_ref.shape[1]
    half_drift, edge = with_halo(drift_ref, below_tail, above_tail)

    def read(row):
        if row < 0:
            return below_ref[:, pl.ds((row + 2) * columns, columns)]
        if row >= rows:
            return above_ref[:, pl.ds((row - rows) * columns, columns)]
        return rows_ref[:, pl.ds(row * columns, columns)]

    if segments is None:
        next_ref, token_ref = refs[-5:-3]
        token_ref[...] = jnp.zeros(token_ref.shape, f32)

        def write(row, density):
            write_row(next_ref, 0, size, row, rows, columns, density)

    else:
        low_ref, high_ref = refs[-5:-3]

        def write(row, density):
            if row < 2:
                low_ref[:, pl.ds(row * columns, columns)] = density.astype(bf16)
            else:
                high_ref[:, pl.ds((row - rows + 2) * columns, columns)] = density.astype(bf16)

    shifts = [wide(shift_ref[n], columns) for n in range(4)]
    two_steps(segments or [(0, rows - 1)], read, half_drift, edge, band_ref[...], shifts, scratch, write)


def density_specs(drift, shifts, band, own, below, size, first):
    columns = drift.shape[2]
    scenarios = shifts.shape[1]
    halo = pl.BlockSpec((size, 2 * columns), lambda i: (first + i, 0))
    tail = pl.BlockSpec((EXTRA, 2 * columns), lambda i: (scenarios // EXTRA, 0))
    return [
        pl.BlockSpec(drift.shape, lambda i: (0, 0, 0)),
        pl.BlockSpec((4, size, LANES), lambda i: (0, first + i, 0)),
        pl.BlockSpec(band.shape, lambda i: (0, 0)),
        pl.BlockSpec((size, own.shape[1]), lambda i: (first + i, 0)),
        halo,
        halo,
        tail,
        tail,
        pl.BlockSpec(memory_space=pl.ANY),
    ]


def edge_steps(drift, shifts, band, own, below, above, dep):
    scenarios = shifts.shape[1]
    rows, columns = drift.shape[1:]
    size = 2 * scenario_block(scenarios)
    size = size if scenarios % size == 0 else size // 2
    edge = jax.ShapeDtypeStruct((scenarios, 2 * columns), bf16)
    spec = pl.BlockSpec((size, 2 * columns), lambda i: (i, 0))
    segments = edge_segments(rows)
    return pl.pallas_call(
        functools.partial(density_kernel, segments),
        grid=(scenarios // size,),
        in_specs=density_specs(drift, shifts, band, own, below, size, 0),
        out_specs=[spec, spec],
        out_shape=[edge, edge],
        scratch_shapes=step_scratch(segments, size, columns),
        compiler_params=params(),
        cost_estimate=pl.CostEstimate(flops=1, bytes_accessed=1, transcendentals=0),
        name="edge_density_steps",
    )(drift, shifts, band, own, below, above, below, above, dep)


def density_steps(drift, shifts, band, own, below, above, dep, so_far, turn, turns):
    scenarios = shifts.shape[1]
    rows, columns = drift.shape[1:]
    per = rows * (columns // LANES)
    size = 3 * GROUP if scenarios % (turns * GROUP * 3) == 0 else GROUP
    steps = scenarios // size // turns
    first = turn * steps
    args = [drift, shifts, band, own, below, above, below, above, dep]
    in_specs = density_specs(drift, shifts, band, own, below, size, first)
    aliases = {}
    if so_far is not None:
        aliases = {len(args): 0}
        args.append(so_far)
        in_specs.append(pl.BlockSpec(memory_space=pltpu.HBM))
    return pl.pallas_call(
        functools.partial(density_kernel, None),
        grid=(steps,),
        in_specs=in_specs,
        out_specs=[
            pl.BlockSpec((size * per, LANES), lambda i: (first + i, 0)),
            pl.BlockSpec((SUBLANES, LANES), lambda i: (0, 0)),
        ],
        out_shape=[pltpu.HBM((scenarios * per, LANES), f32), jax.ShapeDtypeStruct((SUBLANES, LANES), f32)],
        input_output_aliases=aliases,
        scratch_shapes=step_scratch([(0, rows - 1)], size, columns),
        compiler_params=params(),
        cost_estimate=pl.CostEstimate(flops=1, bytes_accessed=1, transcendentals=0),
        name="density_steps",
    )(*args)


def smem():
    return pl.BlockSpec(memory_space=pltpu.SMEM)


def vmem():
    return pl.BlockSpec(memory_space=pltpu.VMEM)


def swap(values, count, flip):
    return lax.ppermute(values, "grid", [(i, i ^ flip) for i in range(count)])


def inner_product_kernel(count, inputs_ref, *refs):
    weight = jnp.concatenate([ref[...] for ref in refs[:count]], axis=0)
    refs[-1][pl.program_id(0)] = jnp.dot(inputs_ref[...], weight, preferred_element_type=f32)


def inner_product(inner, weight, width):
    scenarios, cells = inner.shape
    total, hidden = weight.shape
    size = (total - cells) // 2
    count = cells // size

    def spec(k):
        return pl.BlockSpec((size, width), lambda n: (1 + k, n))

    return pl.pallas_call(
        functools.partial(inner_product_kernel, count),
        grid=(hidden // width,),
        in_specs=[vmem()] + [spec(k) for k in range(count)],
        out_specs=vmem(),
        out_shape=jax.ShapeDtypeStruct((hidden // width, scenarios, width), f32),
        compiler_params=params(),
        cost_estimate=pl.CostEstimate(flops=1, bytes_accessed=1, transcendentals=0),
        name="inner_product",
    )(inner, *([weight] * count))


def edge_product_kernel(block, with_inner, place_ref, low_ref, high_ref, top_ref, bottom_ref, *refs):
    keep_ref, send_ref, total = refs[-3:]
    step = pl.program_id(0)
    left = jnp.concatenate([low_ref[...], high_ref[...]], axis=1)
    weight = jnp.concatenate([top_ref[...], bottom_ref[...]], axis=0)
    product = jnp.dot(left, weight, preferred_element_type=f32)
    total[...] = product + refs[0][step] if with_inner else product
    core = place_ref[0]
    for out, half in ((keep_ref, core), (send_ref, 1 - core)):
        for side in range(2):
            start = pl.multiple_of((2 * half + side) * block, block)
            out[side, step] = total[pl.ds(start, block), :].astype(out.dtype)


def edge_product(place, low, high, weight, inner, parts, width):
    scenarios, size = low.shape
    block = scenarios // 4
    last = weight.shape[0] // size - 1
    shape = (2, parts, block, width)
    in_specs = [
        smem(),
        vmem(),
        vmem(),
        pl.BlockSpec((size, width), lambda n: (0, n)),
        pl.BlockSpec((size, width), lambda n: (last, n)),
    ]
    args = [place, low, high, weight, weight]
    if inner is not None:
        in_specs.append(vmem())
        args.append(inner)
    return pl.pallas_call(
        functools.partial(edge_product_kernel, block, inner is not None),
        grid=(parts,),
        in_specs=in_specs,
        out_specs=[vmem(), vmem()],
        out_shape=[jax.ShapeDtypeStruct(shape, f32), jax.ShapeDtypeStruct(shape, bf16)],
        scratch_shapes=[pltpu.VMEM((scenarios, width), f32)],
        compiler_params=params(),
        cost_estimate=pl.CostEstimate(flops=1, bytes_accessed=1, transcendentals=0),
        name="edge_product",
    )(*args)


def add_side_kernel(place_ref, mine_ref, other_ref, *refs):
    keep_ref, send_ref = refs[-2:]
    side = place_ref[1]
    keep_ref[...] = mine_ref[side] + other_ref[side].astype(f32)
    send_ref[...] = (mine_ref[1 - side] + other_ref[1 - side].astype(f32)).astype(bf16)


def any_specs(deps):
    return [pl.BlockSpec(memory_space=pl.ANY)] * len(deps)


def add_side(place, mine, other, deps=()):
    shape = mine.shape[1:]
    return pl.pallas_call(
        add_side_kernel,
        in_specs=[smem()] + [vmem()] * 2 + any_specs(deps),
        out_shape=[jax.ShapeDtypeStruct(shape, f32), jax.ShapeDtypeStruct(shape, bf16)],
        compiler_params=params(),
        cost_estimate=pl.CostEstimate(flops=1, bytes_accessed=1, transcendentals=0),
        name="add_side",
    )(place, mine, other, *deps)


def add_parts_kernel(dep_count, place_ref, mine_ref, other_ref, *refs):
    own_ref, *send_refs = refs[dep_count:]
    part = place_ref[2]
    own_ref[...] = mine_ref[part] + other_ref[part].astype(f32)
    for k, out in enumerate(send_refs):
        at = part ^ (k + 1)
        out[...] = (mine_ref[at] + other_ref[at].astype(f32)).astype(bf16)


def add_parts(place, mine, other, deps=()):
    parts = mine.shape[0]
    return pl.pallas_call(
        functools.partial(add_parts_kernel, len(deps)),
        in_specs=[smem(), vmem(), vmem()] + any_specs(deps),
        out_shape=[jax.ShapeDtypeStruct(mine.shape[1:], f32)]
        + [jax.ShapeDtypeStruct(mine.shape[1:], bf16)] * (parts - 1),
        compiler_params=params(),
        cost_estimate=pl.CostEstimate(flops=1, bytes_accessed=1, transcendentals=0),
        name="add_parts",
    )(place, mine, other, *deps)


def activate_kernel(count, *refs):
    total = refs[0][...]
    for ref in refs[1 : 1 + count]:
        total = total + ref[...].astype(f32)
    refs[-1][...] = jnp.tanh(total).astype(bf16)


def activate(own, received, deps=()):
    return pl.pallas_call(
        functools.partial(activate_kernel, len(received)),
        in_specs=[vmem()] * (1 + len(received)) + any_specs(deps),
        out_shape=jax.ShapeDtypeStruct(own.shape, bf16),
        compiler_params=params(),
        cost_estimate=pl.CostEstimate(flops=1, bytes_accessed=1, transcendentals=0),
        name="first_activation",
    )(own, *received, *deps)


def pack_kernel(mid_ref, head_ref, *refs):
    out_ref = refs[-1]
    hidden = mid_ref.shape[0]
    out_ref[pl.ds(0, hidden), :] = mid_ref[...]
    out_ref[pl.ds(hidden, EXTRA), :] = tail_rows(head_ref[...])


def pack(mid_weight, head, deps):
    hidden, units = mid_weight.shape
    return pl.pallas_call(
        pack_kernel,
        in_specs=[vmem()] * 2 + any_specs(deps),
        out_shape=jax.ShapeDtypeStruct((hidden + EXTRA, units), bf16),
        compiler_params=params(),
        cost_estimate=pl.CostEstimate(flops=1, bytes_accessed=1, transcendentals=0),
        name="mid_with_head",
    )(mid_weight, head, *deps)


def two_halves(exact):
    high = exact.astype(bf16)
    low = (exact - high.astype(f32)).astype(bf16)
    return high, low


def tail_rows(exact):
    high, low = two_halves(exact)
    zeros = jnp.zeros((EXTRA - 2, exact.shape[1]), bf16)
    return jnp.concatenate([high, low, zeros], axis=0)


def middle_kernel(chunks, parts, width, *refs):
    pieces = chunks * parts
    place_ref, cot_ref = refs[0], refs[1]
    first_refs = refs[2 : 2 + pieces]
    mid_refs = refs[2 + pieces : 6 + pieces]
    outs = refs[-(3 + parts) :]
    own_ref, value_ref, mid_keep_ref, mid_send_ref = outs[:4]
    send_refs = outs[4:]
    part = place_ref[2]
    block = cot_ref.shape[0]

    def mid_rows(start):
        return jnp.concatenate([ref[pl.ds(start, width), :] for ref in mid_refs], axis=1)

    def start_of(c, k):
        return pl.multiple_of((c * parts + (part ^ k)) * width, width)

    total = None
    for c in range(chunks):
        for k in range(parts):
            term = jnp.dot(first_refs[c * parts + k][...], mid_rows(start_of(c, k)), preferred_element_type=f32)
            total = term if total is None else total + term
    second_low = jnp.tanh(total).astype(bf16)
    second = second_low.astype(f32)
    heads = jnp.concatenate([ref[pl.ds(pieces * width, EXTRA), :] for ref in mid_refs], axis=1)
    head = heads[0:1].astype(f32) + heads[1:2].astype(f32)
    rows = lax.dot_general(heads, second_low, (((1,), (1,)), ((), ())), preferred_element_type=f32)
    value = rows[0:1] + rows[1:2]
    if width > block:
        value = jnp.concatenate([value, jnp.zeros((1, width - block), f32)], axis=1)
    value_ref[...] = value
    cot = cot_ref[...]
    head_part = jnp.sum(cot * second, axis=0, keepdims=True)
    back = (cot * head * (1.0 - second * second)).astype(bf16)
    units = mid_refs[0].shape[1]
    for k in range(parts):
        for c in range(chunks):
            piece = lax.dot_general(
                back, mid_rows(start_of(c, k)), (((1,), (1,)), ((), ())), preferred_element_type=f32
            )
            if k == 0:
                own_ref[pl.ds(c * block, block), :] = piece
            else:
                send_refs[k - 1][pl.ds(c * block, block), :] = piece.astype(bf16)
        if k > 0:
            send_refs[k - 1][pl.ds(chunks * block, EXTRA), :] = tail_rows(value)
    for c in range(chunks):
        for k in range(parts):
            product = lax.dot_general(
                first_refs[c * parts + k][...], back, (((0,), (0,)), ((), ())), preferred_element_type=f32
            ).astype(bf16)
            for p in range(4):
                out = (mid_keep_ref, mid_send_ref)[p % 2]
                out[p // 2, pl.ds(start_of(c, k), width), :] = product[:, p * units : (p + 1) * units]
    for p in range(4):
        out = (mid_keep_ref, mid_send_ref)[p % 2]
        out[p // 2, pl.ds(pieces * width, EXTRA), :] = tail_rows(head_part[:, p * units : (p + 1) * units])


def middle(place, cot, firsts, mids, chunks, parts, width, deps=()):
    block = cot.shape[0]
    partial = jax.ShapeDtypeStruct((2, *mids[0].shape), bf16)
    return pl.pallas_call(
        functools.partial(middle_kernel, chunks, parts, width),
        in_specs=[smem()] + [vmem()] * (1 + len(firsts) + 4) + any_specs(deps),
        out_shape=[
            jax.ShapeDtypeStruct((chunks * block, width), f32),
            jax.ShapeDtypeStruct((1, width), f32),
            partial,
            partial,
        ]
        + [jax.ShapeDtypeStruct((chunks * block + EXTRA, width), bf16)] * (parts - 1),
        compiler_params=params(),
        cost_estimate=pl.CostEstimate(flops=1, bytes_accessed=1, transcendentals=0),
        name="value_layers",
    )(place, cot, *firsts, *mids, *deps)


def add_tail(left, right, hidden):
    body = left[:hidden].astype(f32) + right[:hidden].astype(f32)
    tails = left[hidden:].astype(f32) + right[hidden:].astype(f32)
    return body.astype(bf16), tails[0:1] + tails[1:2]


def mid_add_kernel(keep_ref, other_ref, *refs):
    own_ref, send_ref = refs[-2:]
    hidden = own_ref.shape[0] - EXTRA
    for at, out in enumerate((own_ref, send_ref)):
        body, tail = add_tail(keep_ref[at], other_ref[at], hidden)
        out[pl.ds(0, hidden), :] = body
        out[pl.ds(hidden, EXTRA), :] = tail_rows(tail)


def mid_add(keep, other, deps=()):
    shape = jax.ShapeDtypeStruct(keep.shape[1:], bf16)
    return pl.pallas_call(
        mid_add_kernel,
        in_specs=[vmem()] * 2 + any_specs(deps),
        out_shape=[shape, shape],
        compiler_params=params(),
        cost_estimate=pl.CostEstimate(flops=1, bytes_accessed=1, transcendentals=0),
        name="mid_gradient_add",
    )(keep, other, *deps)


def mid_final_kernel(own_ref, other_ref, *refs):
    out_ref, head_ref = refs[-2:]
    body, tail = add_tail(own_ref[...], other_ref[...], out_ref.shape[0])
    out_ref[...] = body
    head_ref[...] = tail


def mid_final(own, other, deps=()):
    hidden = own.shape[0] - EXTRA
    return pl.pallas_call(
        mid_final_kernel,
        in_specs=[vmem()] * 2 + any_specs(deps),
        out_shape=[
            jax.ShapeDtypeStruct((hidden, own.shape[1]), bf16),
            jax.ShapeDtypeStruct((1, own.shape[1]), f32),
        ],
        compiler_params=params(),
        cost_estimate=pl.CostEstimate(flops=1, bytes_accessed=1, transcendentals=0),
        name="mid_gradient_final",
    )(own, other, *deps)


def back_first_kernel(chunks, count, *refs):
    own_ref, value_ref = refs[:2]
    received = refs[2 : 2 + count]
    first_refs = refs[2 + count : 2 + count + chunks]
    out_refs = refs[-1 - chunks : -1]
    tail_ref = refs[-1]
    block = first_refs[0].shape[0]
    value = value_ref[...]
    for ref in received:
        tail = ref[pl.ds(chunks * block, EXTRA), :].astype(f32)
        value = value + (tail[0:1] + tail[1:2])
    tail_ref[...] = tail_rows(value)
    for c in range(chunks):
        total = own_ref[pl.ds(c * block, block), :]
        for ref in received:
            total = total + ref[pl.ds(c * block, block), :].astype(f32)
        first = first_refs[c][...].astype(f32)
        out_refs[c][...] = (total * (1.0 - first * first)).astype(bf16)


def back_first(own, value, received, firsts, deps=()):
    chunks = len(firsts)
    shape = firsts[0].shape
    return pl.pallas_call(
        functools.partial(back_first_kernel, chunks, len(received)),
        in_specs=[vmem()] * (2 + len(received) + chunks) + any_specs(deps),
        out_shape=[jax.ShapeDtypeStruct(shape, bf16)] * chunks
        + [jax.ShapeDtypeStruct((EXTRA, shape[1]), bf16)],
        compiler_params=params(),
        cost_estimate=pl.CostEstimate(flops=1, bytes_accessed=1, transcendentals=0),
        name="back_first",
    )(own, value, *received, *firsts, *deps)


def stack_kernel(count, halves, *refs):
    outs = refs[-halves:]
    width = outs[0].shape[1]
    at = 0
    for ref in refs[:count]:
        for n, out in enumerate(outs):
            out[pl.ds(at, ref.shape[0]), :] = ref[:, pl.ds(n * width, width)]
        at += ref.shape[0]


def stack(pieces, halves, deps=()):
    rows = sum(piece.shape[0] for piece in pieces)
    shape = jax.ShapeDtypeStruct((rows, pieces[0].shape[1] // halves), bf16)
    return pl.pallas_call(
        functools.partial(stack_kernel, len(pieces), halves),
        in_specs=[vmem()] * len(pieces) + any_specs(deps),
        out_shape=[shape] * halves,
        compiler_params=params(),
        cost_estimate=pl.CostEstimate(flops=1, bytes_accessed=1, transcendentals=0),
        name="stack_parts",
    )(*pieces, *deps)


def turn_kernel(count, *refs):
    for ref, out in zip(refs[:count], refs[-count:]):
        out[...] = ref[...].T


def transposed(arrays, deps):
    return pl.pallas_call(
        functools.partial(turn_kernel, len(arrays)),
        in_specs=[vmem()] * len(arrays) + any_specs(deps),
        out_shape=[jax.ShapeDtypeStruct(array.shape[::-1], array.dtype) for array in arrays],
        compiler_params=params(),
        cost_estimate=pl.CostEstimate(flops=1, bytes_accessed=1, transcendentals=0),
        name="transposed_inputs",
    )(*arrays, *deps)


def first_grad_kernel(parts, block, count, with_value, *refs):
    place_ref = refs[0]
    lefts = refs[1 : 1 + count]
    stacks = refs[1 + count : 5 + count]
    outs = refs[-3:-1] if with_value else refs[-2:-1]
    whole = refs[-1]
    step = pl.program_id(0)
    mine = place_ref[3]
    for t, ref in enumerate(stacks):
        at = mine ^ (2 * (t % 2) + t // 2)
        piece = step ^ place_ref[2]
        whole[pl.ds(pl.multiple_of(at * block, block), block), :] = ref[
            pl.ds(pl.multiple_of(piece * block, block), block), :
        ]
        if with_value:
            tail = ref[pl.ds(parts * block, EXTRA), :].astype(f32)
            outs[1][pl.ds(at, 1), :] = tail[0:1] + tail[1:2]
    start = 0
    for ref in lefts:
        cells = ref.shape[0]
        outs[0][pl.ds(start, cells), :] = jnp.dot(ref[...], whole[...], preferred_element_type=f32).astype(bf16)
        start += cells


def first_grad(place, lefts, stacks, so_far, hidden, parts, block, half, halves, deps):
    scenarios = lefts[0].shape[1]
    cells = sum(left.shape[0] for left in lefts)
    width = stacks[0].shape[1]
    with_value = half == 0
    in_specs = [smem()] + [vmem()] * (len(lefts) + 4) + any_specs(deps)
    args = [place, *lefts, *stacks, *deps]
    aliases = {}
    if so_far is not None:
        aliases = {len(args): 0}
        in_specs.append(pl.BlockSpec(memory_space=pltpu.HBM))
        args.append(so_far)
    out_specs = [pl.BlockSpec((cells, width), lambda i: (0, i * halves + half))]
    out_shape = [pltpu.HBM((cells, hidden), bf16)]
    if with_value:
        out_specs.append(pl.BlockSpec((4, width), lambda i: (0, 0)))
        out_shape.append(jax.ShapeDtypeStruct((4, width), f32))
    return pl.pallas_call(
        functools.partial(first_grad_kernel, parts, block, len(lefts), with_value),
        grid=(parts,),
        in_specs=in_specs,
        out_specs=out_specs,
        out_shape=out_shape,
        input_output_aliases=aliases,
        scratch_shapes=[pltpu.VMEM((scenarios, width), bf16)],
        compiler_params=params(),
        cost_estimate=pl.CostEstimate(flops=1, bytes_accessed=1, transcendentals=0),
        name="first_gradient",
    )(*args)


def local(hist, drift, shocks, shock_table, first_weight, mid_weight, head_weight, cotangent):
    scenarios, rows, columns = hist.shape
    count = lax.axis_size("grid")
    hidden = first_weight.shape[1]
    units = mid_weight.shape[1]
    parts = count // 4
    width = hidden // parts
    block = scenarios // 4
    index = lax.axis_index("grid")
    core, side, part = index % 2, index // 2 % 2, index // 4
    mine = 2 * core + side
    tiles = pltpu.with_memory_space_constraint(to_tiles(hist), pltpu.HBM)

    place = jnp.stack([core, side, part, mine])
    cot = lax.dynamic_slice_in_dim(cotangent, mine * block, block)[:, None]
    halves = 2 if width % 256 == 0 else 1

    small = [pltpu.with_memory_space_constraint(array, pltpu.HBM) for array in (drift, shocks.T, shock_table.T)]
    first_rows, last_rows, shifts, band, own_rows, inner = inner_steps(tiles, *small)
    inner = inner if rows > 4 else None
    forward = [(i, i + 1) for i in range(count - 1)]
    backward = [(i + 1, i) for i in range(count - 1)]
    below = lax.ppermute(last_rows, "grid", forward)
    above = lax.ppermute(first_rows, "grid", backward)
    product = None if inner is None else inner_product(inner, first_weight, width)
    low, high = edge_steps(drift, shifts, band, own_rows, below, above, own_rows if product is None else product)

    def density_turn(turn, dep, so_far):
        return density_steps(drift, shifts, band, own_rows, below, above, dep, so_far, turn, 2)

    keep, send = edge_product(place, low, high, first_weight, product, parts, width)
    mids = [pack(mid_weight, head_weight[None, :], [send])]
    keep, send = add_side(place, keep, swap(send, count, 1), mids)
    other = swap(send, count, 2)
    density, token = density_turn(0, send, None)
    own, *sends = add_parts(place, keep, other, [token])
    received = [swap(piece, count, 4 * (k + 1)) for k, piece in enumerate(sends)]
    mids.append(swap(mids[0], count, 1))
    mids.append(swap(mids[0], count, 2))
    mids.append(swap(mids[2], count, 1))
    first = activate(own, received, [mids[2]])
    firsts = [first] + [swap(first, count, 4 * k) for k in range(1, parts)]
    density, token = density_turn(1, first, density)
    own, value, mid_keep, mid_send, *sends = middle(place, cot, firsts, mids, 1, parts, width, [token])
    received = [swap(piece, count, 4 * (k + 1)) for k, piece in enumerate(sends)]
    back, tail = back_first(own, value, received, [first])
    mid_keep, mid_send = mid_add(mid_keep, swap(mid_send, count, 1), [back])
    lefts = transposed([low, high] if inner is None else [low, inner, high], [back])
    pieces = [back] + [swap(back, count, 4 * k) for k in range(1, parts)]
    stacks = stack(pieces + [tail], halves, [lefts[0]])
    grad_mid, grad_head = mid_final(mid_keep, swap(mid_send, count, 2), stacks[:1])
    grad_first = None
    for half, own_stack in enumerate(stacks):
        gathered = [own_stack, swap(own_stack, count, 1), swap(own_stack, count, 2)]
        gathered.append(swap(gathered[2], count, 1))
        results = first_grad(
            place, lefts, gathered, grad_first, hidden, parts, block, half, halves, [grad_head]
        )
        grad_first = results[0]
        if half == 0:
            value = results[1][:, :block].reshape(scenarios)
    return from_tiles(density, hist.shape), value, grad_first, grad_mid, grad_head[0]


def solution(mesh):
    in_specs = (
        P("groups", "grid", None),
        P(None, "grid", None),
        P("groups", None),
        P("groups", None),
        P(("groups", "grid"), None),
        P("groups", "grid"),
        P(("groups", "grid")),
        P("groups"),
    )
    out_specs = (
        P("groups", "grid", None),
        P("groups"),
        P(("groups", "grid"), None),
        P("groups", "grid"),
        P(("groups", "grid")),
    )
    return jax.shard_map(local, mesh=mesh, in_specs=in_specs, out_specs=out_specs, check_vma=False)
```

```python
import functools
import jax
import jax.numpy as jnp
from jax import lax
from jax.experimental import pallas as pl
from jax.experimental.pallas import tpu as pltpu
from jax.sharding import PartitionSpec as P

diffusion_rate = 0.24
VMEM_BYTES = 24 * 1024 * 1024
EXTRA = 16
bf16 = jnp.bfloat16
f32 = jnp.float32


def params():
    return pltpu.CompilerParams(vmem_limit_bytes=VMEM_BYTES)


def scenario_block(scenarios):
    for size in (64, 32, 16):
        if scenarios % size == 0:
            return size
    return scenarios


LANES = 128
SUBLANES = 8
GROUP = 16


def to_tiles(hist):
    scenarios, rows, columns = hist.shape
    high = min(rows, SUBLANES)
    tiles = hist.reshape(scenarios, rows // high, high, columns // LANES, LANES)
    return tiles.transpose(0, 1, 3, 2, 4).reshape(scenarios * rows * (columns // LANES), LANES)


def from_tiles(tiles, shape):
    scenarios, rows, columns = shape
    high = min(rows, SUBLANES)
    parts = tiles.reshape(scenarios, rows // high, columns // LANES, high, LANES)
    return parts.transpose(0, 1, 3, 2, 4).reshape(shape)


def tile_offset(row, lane_tile, rows, lane_tiles):
    high = min(rows, SUBLANES)
    return (row // high * lane_tiles + lane_tile) * high + row % high


def read_row(ref, first_scenario, count, row, rows, columns):
    lane_tiles = columns // LANES
    per = rows * lane_tiles
    return jnp.concatenate(
        [
            ref[pl.ds(first_scenario * per + tile_offset(row, t, rows, lane_tiles), count, stride=per), :]
            for t in range(lane_tiles)
        ],
        axis=1,
    )


def write_row(ref, first_scenario, count, row, rows, columns, values):
    lane_tiles = columns // LANES
    per = rows * lane_tiles
    for t in range(lane_tiles):
        place = pl.ds(first_scenario * per + tile_offset(row, t, rows, lane_tiles), count, stride=per)
        ref[place, :] = values[:, t * LANES : (t + 1) * LANES]


def drift_tail(drift_ref, start):
    pieces = [
        jnp.concatenate([drift_ref[c, start : start + 1], drift_ref[c, start + 1 : start + 2]], axis=1)
        for c in range(2)
    ]
    high, low = two_halves(jnp.concatenate(pieces, axis=0))
    ones = jnp.ones((1, high.shape[1]), bf16)
    zeros = jnp.zeros((EXTRA - 5, high.shape[1]), bf16)
    return jnp.concatenate([high, low, ones, zeros], axis=0)


def band_matrix(columns):
    row = lax.broadcasted_iota(jnp.int32, (columns, columns), 0)
    column = lax.broadcasted_iota(jnp.int32, (columns, columns), 1)
    right = jnp.where(column == row + 1, 1.0, 0.0)
    left = jnp.where(column == row - 1, 1.0, 0.0)
    centre = jnp.where(column == row, 1.0 - 4.0 * diffusion_rate, diffusion_rate * (right + left))
    return centre.astype(bf16), (right - left).astype(bf16)


def half_shifts(levels_ref, table_ref, shift_ref):
    scenarios = levels_ref.shape[1]
    for t in range(levels_ref.shape[0]):
        level = jnp.broadcast_to(levels_ref[t : t + 1, :].astype(f32), (LANES, scenarios)).T
        for c in range(2):
            shift = jnp.zeros(level.shape, f32)
            for n in range(table_ref.shape[1]):
                shift = jnp.where(level == n, 0.5 * table_ref[c : c + 1, n : n + 1], shift)
            shift_ref[2 * t + c] = shift


def wide(values, columns):
    return jnp.concatenate([values] * (columns // LANES), axis=1)


def one_step(rows_of, places, half_drift, band, shift_x, shift_y, pairs, terms, write):
    size, columns = shift_x.shape
    whole = pl.ds(0, columns)

    def density(row):
        return pairs[pl.ds(rows_of[row] * size, size), whole].astype(f32)

    for row in places:
        flux = (half_drift(1, row) + shift_y) * density(row)
        pairs[pl.ds(rows_of[row] * size, size), pl.ds(columns, columns)] = flux.astype(bf16)
    start = rows_of[places[0]] * size
    count = (rows_of[places[-1]] + 1) * size - start
    terms[pl.ds(start, count), :] = jnp.dot(pairs[pl.ds(start, count), :], band, preferred_element_type=f32)
    for row in places:
        low = density(row - 1) * ((diffusion_rate + half_drift(0, row - 1)) + shift_x)
        high = density(row + 1) * ((diffusion_rate - half_drift(0, row + 1)) - shift_x)
        write(row, terms[pl.ds(rows_of[row] * size, size), :] + low + high)


def two_steps(segments, read, half_drift, edge, band, shifts, scratch, write):
    pairs, later, terms = scratch
    size, columns = shifts[0].shape
    before, between, after = [
        [row for first, last in segments for row in range(first - more, last + more + 1)] for more in (2, 1, 0)
    ]
    rows_of = {row: k for k, row in enumerate(before)}
    for row, k in rows_of.items():
        pairs[pl.ds(k * size, size), pl.ds(0, columns)] = read(row)

    def write_later(row, density):
        later[pl.ds(rows_of[row] * size, size), pl.ds(0, columns)] = edge(row, density).astype(bf16)

    one_step(rows_of, between, half_drift, band, shifts[0], shifts[1], pairs, terms, write_later)
    one_step(rows_of, after, half_drift, band, shifts[2], shifts[3], later, terms, write)


def step_scratch(segments, size, columns):
    rows = sum(last - first + 5 for first, last in segments)
    pairs = pltpu.VMEM((rows * size, 2 * columns), bf16)
    return [pairs, pairs, pltpu.VMEM((rows * size, columns), f32)]


def edge_segments(rows):
    return [(0, 1), (rows - 2, rows - 1)] if rows >= 8 else [(0, rows - 1)]


def inner_kernel(
    rows, size, hist_ref, drift_hbm, levels_hbm, table_hbm,
    first_ref, last_ref, shift_ref, band_ref, rows_ref, inner_ref,
    drift_ref, levels_ref, table_ref, arrived, all_shifts, *scratch,
):
    step = pl.program_id(0)
    columns = drift_ref.shape[2]

    @pl.when(step == 0)
    def _():
        sources = ((drift_hbm, drift_ref), (levels_hbm, levels_ref), (table_hbm, table_ref))
        copies = [pltpu.make_async_copy(*pair, arrived.at[n]) for n, pair in enumerate(sources)]
        for copy in copies:
            copy.start()
        centre, flux = band_matrix(columns)
        band_ref[pl.ds(0, columns), :] = centre
        band_ref[pl.ds(columns, columns), :] = flux
        for copy in copies:
            copy.wait()
        half_shifts(levels_ref, table_ref, all_shifts)
        for out, start in ((first_ref, 0), (last_ref, rows - 2)):
            out[pl.ds(out.shape[0] - EXTRA, EXTRA), :] = drift_tail(drift_ref, start)

    where = pl.ds(pl.multiple_of(step * size, size), size)
    for n in range(4):
        shift_ref[n] = all_shifts[n, where, :]
    for row in range(rows):
        density = read_row(hist_ref, 0, size, row, rows, columns).astype(bf16)
        rows_ref[:, pl.ds(row * columns, columns)] = density
        if row < 2:
            first_ref[where, pl.ds(row * columns, columns)] = density
        if row >= rows - 2:
            last_ref[where, pl.ds((row - rows + 2) * columns, columns)] = density
    if rows <= 4:
        return

    def write(row, density):
        inner_ref[:, pl.ds((row - 2) * columns, columns)] = density.astype(bf16)

    two_steps(
        [(2, rows - 3)],
        lambda row: rows_ref[:, pl.ds(row * columns, columns)],
        lambda c, row: 0.5 * drift_ref[c, row : row + 1, :],
        lambda row, density: density,
        band_ref[...],
        [wide(shift_ref[n], columns) for n in range(4)],
        scratch,
        write,
    )


def inner_steps(tiles, drift, levels, table):
    scenarios = levels.shape[1]
    rows, columns = drift.shape[1:]
    per = tiles.shape[0] // scenarios
    size = scenario_block(scenarios)
    inner = max(rows - 4, 1) * columns
    sent = jax.ShapeDtypeStruct((scenarios + EXTRA, 2 * columns), bf16)
    shifts = jax.ShapeDtypeStruct((4, scenarios, LANES), f32)
    band = jax.ShapeDtypeStruct((2 * columns, columns), bf16)
    return pl.pallas_call(
        functools.partial(inner_kernel, rows, size),
        grid=(scenarios // size,),
        in_specs=[pl.BlockSpec((size * per, LANES), lambda i: (i, 0))] + [pl.BlockSpec(memory_space=pltpu.HBM)] * 3,
        out_specs=[pl.BlockSpec(sent.shape, lambda i: (0, 0))] * 2
        + [
            pl.BlockSpec((4, size, LANES), lambda i: (0, i, 0)),
            pl.BlockSpec(band.shape, lambda i: (0, 0)),
            pl.BlockSpec((size, rows * columns), lambda i: (i, 0)),
            pl.BlockSpec((size, inner), lambda i: (i, 0)),
        ],
        out_shape=[
            sent,
            sent,
            pltpu.HBM(shifts.shape, f32),
            band,
            pltpu.HBM((scenarios, rows * columns), bf16),
            jax.ShapeDtypeStruct((scenarios, inner), bf16),
        ],
        scratch_shapes=[
            pltpu.VMEM(drift.shape, f32),
            pltpu.VMEM(levels.shape, levels.dtype),
            pltpu.VMEM(table.shape, f32),
            pltpu.SemaphoreType.DMA((3,)),
            pltpu.VMEM(shifts.shape, f32),
        ]
        + step_scratch([(2, max(rows - 3, 2))], size, columns),
        compiler_params=params(),
        cost_estimate=pl.CostEstimate(flops=1, bytes_accessed=1, transcendentals=0),
        name="inner_density_steps",
    )(tiles, drift, levels, table)


def halo_drift(ref, columns):
    tail = ref[...].astype(f32)
    both = 0.5 * (tail[0:2] + tail[2:4])
    rows = [[both[c : c + 1, k * columns : (k + 1) * columns] for k in range(2)] for c in range(2)]
    return rows, tail[4:5, :columns]


def with_halo(drift_ref, below_tail, above_tail):
    rows, columns = drift_ref.shape[1:]
    below, below_valid = halo_drift(below_tail, columns)
    above, above_valid = halo_drift(above_tail, columns)

    def half_drift(c, row):
        if row < 0:
            return below[c][row + 2]
        if row >= rows:
            return above[c][row - rows]
        return 0.5 * drift_ref[c, row : row + 1, :]

    def edge(row, density):
        if row < 0:
            return density * below_valid
        if row >= rows:
            return density * above_valid
        return density

    return half_drift, edge


def density_kernel(segments, drift_ref, shift_ref, band_ref, rows_ref, below_ref, above_ref, below_tail, above_tail, dep_ref, *refs):
    scratch = refs[-3:]
    rows, columns = drift_ref.shape[1:]
    size = shift_ref.shape[1]
    half_drift, edge = with_halo(drift_ref, below_tail, above_tail)

    def read(row):
        if row < 0:
            return below_ref[:, pl.ds((row + 2) * columns, columns)]
        if row >= rows:
            return above_ref[:, pl.ds((row - rows) * columns, columns)]
        return rows_ref[:, pl.ds(row * columns, columns)]

    if segments is None:
        next_ref, token_ref = refs[-5:-3]
        token_ref[...] = jnp.zeros(token_ref.shape, f32)

        def write(row, density):
            write_row(next_ref, 0, size, row, rows, columns, density)

    else:
        low_ref, high_ref = refs[-5:-3]

        def write(row, density):
            if row < 2:
                low_ref[:, pl.ds(row * columns, columns)] = density.astype(bf16)
            else:
                high_ref[:, pl.ds((row - rows + 2) * columns, columns)] = density.astype(bf16)

    shifts = [wide(shift_ref[n], columns) for n in range(4)]
    two_steps(segments or [(0, rows - 1)], read, half_drift, edge, band_ref[...], shifts, scratch, write)


def density_specs(drift, shifts, band, own, below, size, first):
    columns = drift.shape[2]
    scenarios = shifts.shape[1]
    halo = pl.BlockSpec((size, 2 * columns), lambda i: (first + i, 0))
    tail = pl.BlockSpec((EXTRA, 2 * columns), lambda i: (scenarios // EXTRA, 0))
    return [
        pl.BlockSpec(drift.shape, lambda i: (0, 0, 0)),
        pl.BlockSpec((4, size, LANES), lambda i: (0, first + i, 0)),
        pl.BlockSpec(band.shape, lambda i: (0, 0)),
        pl.BlockSpec((size, own.shape[1]), lambda i: (first + i, 0)),
        halo,
        halo,
        tail,
        tail,
        pl.BlockSpec(memory_space=pl.ANY),
    ]


def edge_steps(drift, shifts, band, own, below, above, dep):
    scenarios = shifts.shape[1]
    rows, columns = drift.shape[1:]
    size = 2 * scenario_block(scenarios)
    size = size if scenarios % size == 0 else size // 2
    edge = jax.ShapeDtypeStruct((scenarios, 2 * columns), bf16)
    spec = pl.BlockSpec((size, 2 * columns), lambda i: (i, 0))
    segments = edge_segments(rows)
    return pl.pallas_call(
        functools.partial(density_kernel, segments),
        grid=(scenarios // size,),
        in_specs=density_specs(drift, shifts, band, own, below, size, 0),
        out_specs=[spec, spec],
        out_shape=[edge, edge],
        scratch_shapes=step_scratch(segments, size, columns),
        compiler_params=params(),
        cost_estimate=pl.CostEstimate(flops=1, bytes_accessed=1, transcendentals=0),
        name="edge_density_steps",
    )(drift, shifts, band, own, below, above, below, above, dep)


def density_steps(drift, shifts, band, own, below, above, dep, so_far, turn, turns):
    scenarios = shifts.shape[1]
    rows, columns = drift.shape[1:]
    per = rows * (columns // LANES)
    size = 3 * GROUP if scenarios % (turns * GROUP * 3) == 0 else GROUP
    steps = scenarios // size // turns
    first = turn * steps
    args = [drift, shifts, band, own, below, above, below, above, dep]
    in_specs = density_specs(drift, shifts, band, own, below, size, first)
    aliases = {}
    if so_far is not None:
        aliases = {len(args): 0}
        args.append(so_far)
        in_specs.append(pl.BlockSpec(memory_space=pltpu.HBM))
    return pl.pallas_call(
        functools.partial(density_kernel, None),
        grid=(steps,),
        in_specs=in_specs,
        out_specs=[
            pl.BlockSpec((size * per, LANES), lambda i: (first + i, 0)),
            pl.BlockSpec((SUBLANES, LANES), lambda i: (0, 0)),
        ],
        out_shape=[pltpu.HBM((scenarios * per, LANES), f32), jax.ShapeDtypeStruct((SUBLANES, LANES), f32)],
        input_output_aliases=aliases,
        scratch_shapes=step_scratch([(0, rows - 1)], size, columns),
        compiler_params=params(),
        cost_estimate=pl.CostEstimate(flops=1, bytes_accessed=1, transcendentals=0),
        name="density_steps",
    )(*args)


def smem():
    return pl.BlockSpec(memory_space=pltpu.SMEM)


def vmem():
    return pl.BlockSpec(memory_space=pltpu.VMEM)


def swap(values, count, flip):
    return lax.ppermute(values, "grid", [(i, i ^ flip) for i in range(count)])


def inner_product_kernel(count, inputs_ref, *refs):
    weight = jnp.concatenate([ref[...] for ref in refs[:count]], axis=0)
    refs[-1][pl.program_id(0)] = jnp.dot(inputs_ref[...], weight, preferred_element_type=f32)


def inner_product(inner, weight, width, deps):
    scenarios, cells = inner.shape
    total, hidden = weight.shape
    size = (total - cells) // 2
    count = cells // size

    def spec(k):
        return pl.BlockSpec((size, width), lambda n: (1 + k, n))

    return pl.pallas_call(
        functools.partial(inner_product_kernel, count),
        grid=(hidden // width,),
        in_specs=[vmem()] + [spec(k) for k in range(count)] + any_specs(deps),
        out_specs=vmem(),
        out_shape=jax.ShapeDtypeStruct((hidden // width, scenarios, width), f32),
        compiler_params=params(),
        cost_estimate=pl.CostEstimate(flops=1, bytes_accessed=1, transcendentals=0),
        name="inner_product",
    )(inner, *([weight] * count), *deps)


def edge_product_kernel(block, with_inner, place_ref, low_ref, high_ref, top_ref, bottom_ref, *refs):
    keep_ref, send_ref, total = refs[-3:]
    step = pl.program_id(0)
    left = jnp.concatenate([low_ref[...], high_ref[...]], axis=1)
    weight = jnp.concatenate([top_ref[...], bottom_ref[...]], axis=0)
    product = jnp.dot(left, weight, preferred_element_type=f32)
    total[...] = product + refs[0][step] if with_inner else product
    core = place_ref[0]
    for out, half in ((keep_ref, core), (send_ref, 1 - core)):
        for side in range(2):
            start = pl.multiple_of((2 * half + side) * block, block)
            out[side, step] = total[pl.ds(start, block), :].astype(out.dtype)


def edge_product(place, low, high, weight, inner, parts, width):
    scenarios, size = low.shape
    block = scenarios // 4
    last = weight.shape[0] // size - 1
    shape = (2, parts, block, width)
    in_specs = [
        smem(),
        vmem(),
        vmem(),
        pl.BlockSpec((size, width), lambda n: (0, n)),
        pl.BlockSpec((size, width), lambda n: (last, n)),
    ]
    args = [place, low, high, weight, weight]
    if inner is not None:
        in_specs.append(vmem())
        args.append(inner)
    return pl.pallas_call(
        functools.partial(edge_product_kernel, block, inner is not None),
        grid=(parts,),
        in_specs=in_specs,
        out_specs=[vmem(), vmem()],
        out_shape=[jax.ShapeDtypeStruct(shape, f32), jax.ShapeDtypeStruct(shape, bf16)],
        scratch_shapes=[pltpu.VMEM((scenarios, width), f32)],
        compiler_params=params(),
        cost_estimate=pl.CostEstimate(flops=1, bytes_accessed=1, transcendentals=0),
        name="edge_product",
    )(*args)


def add_side_kernel(place_ref, mine_ref, other_ref, *refs):
    keep_ref, send_ref = refs[-2:]
    side = place_ref[1]
    keep_ref[...] = mine_ref[side] + other_ref[side].astype(f32)
    send_ref[...] = (mine_ref[1 - side] + other_ref[1 - side].astype(f32)).astype(bf16)


def any_specs(deps):
    return [pl.BlockSpec(memory_space=pl.ANY)] * len(deps)


def add_side(place, mine, other, deps=()):
    shape = mine.shape[1:]
    return pl.pallas_call(
        add_side_kernel,
        in_specs=[smem()] + [vmem()] * 2 + any_specs(deps),
        out_shape=[jax.ShapeDtypeStruct(shape, f32), jax.ShapeDtypeStruct(shape, bf16)],
        compiler_params=params(),
        cost_estimate=pl.CostEstimate(flops=1, bytes_accessed=1, transcendentals=0),
        name="add_side",
    )(place, mine, other, *deps)


def add_parts_kernel(dep_count, place_ref, mine_ref, other_ref, *refs):
    own_ref, *send_refs = refs[dep_count:]
    part = place_ref[2]
    own_ref[...] = mine_ref[part] + other_ref[part].astype(f32)
    for k, out in enumerate(send_refs):
        at = part ^ (k + 1)
        out[...] = (mine_ref[at] + other_ref[at].astype(f32)).astype(bf16)


def add_parts(place, mine, other, deps=()):
    parts = mine.shape[0]
    return pl.pallas_call(
        functools.partial(add_parts_kernel, len(deps)),
        in_specs=[smem(), vmem(), vmem()] + any_specs(deps),
        out_shape=[jax.ShapeDtypeStruct(mine.shape[1:], f32)]
        + [jax.ShapeDtypeStruct(mine.shape[1:], bf16)] * (parts - 1),
        compiler_params=params(),
        cost_estimate=pl.CostEstimate(flops=1, bytes_accessed=1, transcendentals=0),
        name="add_parts",
    )(place, mine, other, *deps)


def activate_kernel(count, *refs):
    total = refs[0][...]
    for ref in refs[1 : 1 + count]:
        total = total + ref[...].astype(f32)
    refs[-1][...] = jnp.tanh(total).astype(bf16)


def activate(own, received, deps=()):
    return pl.pallas_call(
        functools.partial(activate_kernel, len(received)),
        in_specs=[vmem()] * (1 + len(received)) + any_specs(deps),
        out_shape=jax.ShapeDtypeStruct(own.shape, bf16),
        compiler_params=params(),
        cost_estimate=pl.CostEstimate(flops=1, bytes_accessed=1, transcendentals=0),
        name="first_activation",
    )(own, *received, *deps)


def pack_kernel(mid_ref, head_ref, out_ref, head_row, arrived):
    hidden = mid_ref.shape[0]
    copies = [
        pltpu.make_async_copy(mid_ref, out_ref.at[pl.ds(0, hidden), :], arrived.at[0]),
        pltpu.make_async_copy(head_ref, head_row, arrived.at[1]),
    ]
    for copy in copies:
        copy.start()
    copies[1].wait()
    out_ref[pl.ds(hidden, EXTRA), :] = tail_rows(head_row[...])
    copies[0].wait()


def pack(mid_weight, head):
    hidden, units = mid_weight.shape
    return pl.pallas_call(
        pack_kernel,
        in_specs=[pl.BlockSpec(memory_space=pltpu.HBM)] * 2,
        out_specs=vmem(),
        out_shape=jax.ShapeDtypeStruct((hidden + EXTRA, units), bf16),
        scratch_shapes=[pltpu.VMEM(head.shape, f32), pltpu.SemaphoreType.DMA((2,))],
        compiler_params=params(),
        cost_estimate=pl.CostEstimate(flops=1, bytes_accessed=1, transcendentals=0),
        name="mid_with_head",
    )(*[pltpu.with_memory_space_constraint(array, pltpu.HBM) for array in (mid_weight, head)])


def two_halves(exact):
    high = exact.astype(bf16)
    low = (exact - high.astype(f32)).astype(bf16)
    return high, low


def tail_rows(exact):
    high, low = two_halves(exact)
    zeros = jnp.zeros((EXTRA - 2, exact.shape[1]), bf16)
    return jnp.concatenate([high, low, zeros], axis=0)


def middle_kernel(chunks, parts, width, *refs):
    pieces = chunks * parts
    place_ref, cot_ref = refs[0], refs[1]
    first_refs = refs[2 : 2 + pieces]
    mid_refs = refs[2 + pieces : 6 + pieces]
    outs = refs[-(3 + parts) :]
    own_ref, value_ref, mid_keep_ref, mid_send_ref = outs[:4]
    send_refs = outs[4:]
    part = place_ref[2]
    block = cot_ref.shape[0]

    def mid_rows(start):
        return jnp.concatenate([ref[pl.ds(start, width), :] for ref in mid_refs], axis=1)

    def start_of(c, k):
        return pl.multiple_of((c * parts + (part ^ k)) * width, width)

    total = None
    for c in range(chunks):
        for k in range(parts):
            term = jnp.dot(first_refs[c * parts + k][...], mid_rows(start_of(c, k)), preferred_element_type=f32)
            total = term if total is None else total + term
    second_low = jnp.tanh(total).astype(bf16)
    second = second_low.astype(f32)
    heads = jnp.concatenate([ref[pl.ds(pieces * width, EXTRA), :] for ref in mid_refs], axis=1)
    head = heads[0:1].astype(f32) + heads[1:2].astype(f32)
    rows = lax.dot_general(heads, second_low, (((1,), (1,)), ((), ())), preferred_element_type=f32)
    value = rows[0:1] + rows[1:2]
    if width > block:
        value = jnp.concatenate([value, jnp.zeros((1, width - block), f32)], axis=1)
    value_ref[...] = value
    cot = cot_ref[...]
    head_part = jnp.sum(cot * second, axis=0, keepdims=True)
    back = (cot * head * (1.0 - second * second)).astype(bf16)
    units = mid_refs[0].shape[1]
    for k in range(parts):
        for c in range(chunks):
            piece = lax.dot_general(
                back, mid_rows(start_of(c, k)), (((1,), (1,)), ((), ())), preferred_element_type=f32
            )
            if k == 0:
                own_ref[pl.ds(c * block, block), :] = piece
            else:
                send_refs[k - 1][pl.ds(c * block, block), :] = piece.astype(bf16)
        if k > 0:
            send_refs[k - 1][pl.ds(chunks * block, EXTRA), :] = tail_rows(value)
    for c in range(chunks):
        for k in range(parts):
            product = lax.dot_general(
                first_refs[c * parts + k][...], back, (((0,), (0,)), ((), ())), preferred_element_type=f32
            ).astype(bf16)
            for p in range(4):
                out = (mid_keep_ref, mid_send_ref)[p % 2]
                out[p // 2, pl.ds(start_of(c, k), width), :] = product[:, p * units : (p + 1) * units]
    for p in range(4):
        out = (mid_keep_ref, mid_send_ref)[p % 2]
        out[p // 2, pl.ds(pieces * width, EXTRA), :] = tail_rows(head_part[:, p * units : (p + 1) * units])


def middle(place, cot, firsts, mids, chunks, parts, width, deps=()):
    block = cot.shape[0]
    partial = jax.ShapeDtypeStruct((2, *mids[0].shape), bf16)
    return pl.pallas_call(
        functools.partial(middle_kernel, chunks, parts, width),
        in_specs=[smem()] + [vmem()] * (1 + len(firsts) + 4) + any_specs(deps),
        out_shape=[
            jax.ShapeDtypeStruct((chunks * block, width), f32),
            jax.ShapeDtypeStruct((1, width), f32),
            partial,
            partial,
        ]
        + [jax.ShapeDtypeStruct((chunks * block + EXTRA, width), bf16)] * (parts - 1),
        compiler_params=params(),
        cost_estimate=pl.CostEstimate(flops=1, bytes_accessed=1, transcendentals=0),
        name="value_layers",
    )(place, cot, *firsts, *mids, *deps)


def add_tail(left, right, hidden):
    body = left[:hidden].astype(f32) + right[:hidden].astype(f32)
    tails = left[hidden:].astype(f32) + right[hidden:].astype(f32)
    return body.astype(bf16), tails[0:1] + tails[1:2]


def mid_add_kernel(keep_ref, other_ref, *refs):
    own_ref, send_ref = refs[-2:]
    hidden = own_ref.shape[0] - EXTRA
    for at, out in enumerate((own_ref, send_ref)):
        body, tail = add_tail(keep_ref[at], other_ref[at], hidden)
        out[pl.ds(0, hidden), :] = body
        out[pl.ds(hidden, EXTRA), :] = tail_rows(tail)


def mid_add(keep, other, deps=()):
    shape = jax.ShapeDtypeStruct(keep.shape[1:], bf16)
    return pl.pallas_call(
        mid_add_kernel,
        in_specs=[vmem()] * 2 + any_specs(deps),
        out_shape=[shape, shape],
        compiler_params=params(),
        cost_estimate=pl.CostEstimate(flops=1, bytes_accessed=1, transcendentals=0),
        name="mid_gradient_add",
    )(keep, other, *deps)


def mid_final_kernel(own_ref, other_ref, *refs):
    out_ref, head_ref = refs[-2:]
    body, tail = add_tail(own_ref[...], other_ref[...], out_ref.shape[0])
    out_ref[...] = body
    head_ref[...] = tail


def mid_final(own, other, deps=()):
    hidden = own.shape[0] - EXTRA
    return pl.pallas_call(
        mid_final_kernel,
        in_specs=[vmem()] * 2 + any_specs(deps),
        out_shape=[
            jax.ShapeDtypeStruct((hidden, own.shape[1]), bf16),
            jax.ShapeDtypeStruct((1, own.shape[1]), f32),
        ],
        compiler_params=params(),
        cost_estimate=pl.CostEstimate(flops=1, bytes_accessed=1, transcendentals=0),
        name="mid_gradient_final",
    )(own, other, *deps)


def back_first_kernel(chunks, count, *refs):
    own_ref, value_ref = refs[:2]
    received = refs[2 : 2 + count]
    first_refs = refs[2 + count : 2 + count + chunks]
    out_refs = refs[-1 - chunks : -1]
    tail_ref = refs[-1]
    block = first_refs[0].shape[0]
    value = value_ref[...]
    for ref in received:
        tail = ref[pl.ds(chunks * block, EXTRA), :].astype(f32)
        value = value + (tail[0:1] + tail[1:2])
    tail_ref[...] = tail_rows(value)
    for c in range(chunks):
        total = own_ref[pl.ds(c * block, block), :]
        for ref in received:
            total = total + ref[pl.ds(c * block, block), :].astype(f32)
        first = first_refs[c][...].astype(f32)
        out_refs[c][...] = (total * (1.0 - first * first)).astype(bf16)


def back_first(own, value, received, firsts, deps=()):
    chunks = len(firsts)
    shape = firsts[0].shape
    return pl.pallas_call(
        functools.partial(back_first_kernel, chunks, len(received)),
        in_specs=[vmem()] * (2 + len(received) + chunks) + any_specs(deps),
        out_shape=[jax.ShapeDtypeStruct(shape, bf16)] * chunks
        + [jax.ShapeDtypeStruct((EXTRA, shape[1]), bf16)],
        compiler_params=params(),
        cost_estimate=pl.CostEstimate(flops=1, bytes_accessed=1, transcendentals=0),
        name="back_first",
    )(own, value, *received, *firsts, *deps)


def stack_kernel(count, halves, *refs):
    outs = refs[-halves:]
    width = outs[0].shape[1]
    at = 0
    for ref in refs[:count]:
        for n, out in enumerate(outs):
            out[pl.ds(at, ref.shape[0]), :] = ref[:, pl.ds(n * width, width)]
        at += ref.shape[0]


def stack(pieces, halves, deps=()):
    rows = sum(piece.shape[0] for piece in pieces)
    shape = jax.ShapeDtypeStruct((rows, pieces[0].shape[1] // halves), bf16)
    return pl.pallas_call(
        functools.partial(stack_kernel, len(pieces), halves),
        in_specs=[vmem()] * len(pieces) + any_specs(deps),
        out_shape=[shape] * halves,
        compiler_params=params(),
        cost_estimate=pl.CostEstimate(flops=1, bytes_accessed=1, transcendentals=0),
        name="stack_parts",
    )(*pieces, *deps)


def turn_kernel(count, *refs):
    for ref, out in zip(refs[:count], refs[-count:]):
        out[...] = ref[...].T


def transposed(arrays, deps):
    return pl.pallas_call(
        functools.partial(turn_kernel, len(arrays)),
        in_specs=[vmem()] * len(arrays) + any_specs(deps),
        out_shape=[jax.ShapeDtypeStruct(array.shape[::-1], array.dtype) for array in arrays],
        compiler_params=params(),
        cost_estimate=pl.CostEstimate(flops=1, bytes_accessed=1, transcendentals=0),
        name="transposed_inputs",
    )(*arrays, *deps)


def first_grad_kernel(parts, block, count, with_value, *refs):
    place_ref = refs[0]
    lefts = refs[1 : 1 + count]
    stacks = refs[1 + count : 5 + count]
    outs = refs[-3:-1] if with_value else refs[-2:-1]
    whole = refs[-1]
    step = pl.program_id(0)
    mine = place_ref[3]
    for t, ref in enumerate(stacks):
        at = mine ^ (2 * (t % 2) + t // 2)
        piece = step ^ place_ref[2]
        whole[pl.ds(pl.multiple_of(at * block, block), block), :] = ref[
            pl.ds(pl.multiple_of(piece * block, block), block), :
        ]
        if with_value:
            tail = ref[pl.ds(parts * block, EXTRA), :].astype(f32)
            outs[1][pl.ds(at, 1), :] = tail[0:1] + tail[1:2]
    start = 0
    for ref in lefts:
        cells = ref.shape[0]
        outs[0][pl.ds(start, cells), :] = jnp.dot(ref[...], whole[...], preferred_element_type=f32).astype(bf16)
        start += cells


def first_grad(place, lefts, stacks, so_far, hidden, parts, block, half, halves, deps):
    scenarios = lefts[0].shape[1]
    cells = sum(left.shape[0] for left in lefts)
    width = stacks[0].shape[1]
    with_value = half == 0
    in_specs = [smem()] + [vmem()] * (len(lefts) + 4) + any_specs(deps)
    args = [place, *lefts, *stacks, *deps]
    aliases = {}
    if so_far is not None:
        aliases = {len(args): 0}
        in_specs.append(pl.BlockSpec(memory_space=pltpu.HBM))
        args.append(so_far)
    out_specs = [pl.BlockSpec((cells, width), lambda i: (0, i * halves + half))]
    out_shape = [pltpu.HBM((cells, hidden), bf16)]
    if with_value:
        out_specs.append(pl.BlockSpec((4, width), lambda i: (0, 0)))
        out_shape.append(jax.ShapeDtypeStruct((4, width), f32))
    return pl.pallas_call(
        functools.partial(first_grad_kernel, parts, block, len(lefts), with_value),
        grid=(parts,),
        in_specs=in_specs,
        out_specs=out_specs,
        out_shape=out_shape,
        input_output_aliases=aliases,
        scratch_shapes=[pltpu.VMEM((scenarios, width), bf16)],
        compiler_params=params(),
        cost_estimate=pl.CostEstimate(flops=1, bytes_accessed=1, transcendentals=0),
        name="first_gradient",
    )(*args)


def local(hist, drift, shocks, shock_table, first_weight, mid_weight, head_weight, cotangent):
    scenarios, rows, columns = hist.shape
    count = lax.axis_size("grid")
    hidden = first_weight.shape[1]
    units = mid_weight.shape[1]
    parts = count // 4
    width = hidden // parts
    block = scenarios // 4
    index = lax.axis_index("grid")
    core, side, part = index % 2, index // 2 % 2, index // 4
    mine = 2 * core + side
    tiles = pltpu.with_memory_space_constraint(to_tiles(hist), pltpu.HBM)

    place = jnp.stack([core, side, part, mine])
    cot = lax.dynamic_slice_in_dim(cotangent, mine * block, block)[:, None]
    halves = 1

    mids = [pack(mid_weight, head_weight[None, :])]
    mids += [swap(mids[0], count, 1), swap(mids[0], count, 2)]
    small = [pltpu.with_memory_space_constraint(array, pltpu.HBM) for array in (drift, shocks.T, shock_table.T)]
    first_rows, last_rows, shifts, band, own_rows, inner = inner_steps(tiles, *small)
    inner = inner if rows > 4 else None
    forward = [(i, i + 1) for i in range(count - 1)]
    backward = [(i + 1, i) for i in range(count - 1)]
    below = lax.ppermute(last_rows, "grid", forward)
    above = lax.ppermute(first_rows, "grid", backward)
    first_weight = pltpu.with_memory_space_constraint(first_weight, pltpu.HBM)
    product = None if inner is None else inner_product(inner, first_weight, width, mids[1:])
    low, high = edge_steps(drift, shifts, band, own_rows, below, above, own_rows if product is None else product)
    mids.append(swap(mids[2], count, 1))

    def density_turn(turn, dep, so_far):
        return density_steps(drift, shifts, band, own_rows, below, above, dep, so_far, turn, 2)

    keep, send = edge_product(place, low, high, first_weight, product, parts, width)
    keep, send = add_side(place, keep, swap(send, count, 1))
    other = swap(send, count, 2)
    density, token = density_turn(0, send, None)
    own, *sends = add_parts(place, keep, other, [token, mids[3]])
    received = [swap(piece, count, 4 * (k + 1)) for k, piece in enumerate(sends)]
    first = activate(own, received)
    firsts = [first] + [swap(first, count, 4 * k) for k in range(1, parts)]
    density, token = density_turn(1, first, density)
    own, value, mid_keep, mid_send, *sends = middle(place, cot, firsts, mids, 1, parts, width, [token])
    received = [swap(piece, count, 4 * (k + 1)) for k, piece in enumerate(sends)]
    back, tail = back_first(own, value, received, [first])
    mid_keep, mid_send = mid_add(mid_keep, swap(mid_send, count, 1), [back])
    lefts = transposed([low, high] if inner is None else [low, inner, high], [back])
    pieces = [back] + [swap(back, count, 4 * k) for k in range(1, parts)]
    grad_mid, grad_head = mid_final(mid_keep, swap(mid_send, count, 2))
    stacks = stack(pieces + [tail], halves, [lefts[0], grad_head])
    grad_first = None
    for half, own_stack in enumerate(stacks):
        gathered = [own_stack, swap(own_stack, count, 1), swap(own_stack, count, 2)]
        gathered.append(swap(gathered[2], count, 1))
        results = first_grad(
            place, lefts, gathered, grad_first, hidden, parts, block, half, halves, [grad_head]
        )
        grad_first = results[0]
        if half == 0:
            value = results[1][:, :block].reshape(scenarios)
    return from_tiles(density, hist.shape), value, grad_first, grad_mid, grad_head[0]


def solution(mesh):
    in_specs = (
        P("groups", "grid", None),
        P(None, "grid", None),
        P("groups", None),
        P("groups", None),
        P(("groups", "grid"), None),
        P("groups", "grid"),
        P(("groups", "grid")),
        P("groups"),
    )
    out_specs = (
        P("groups", "grid", None),
        P("groups"),
        P(("groups", "grid"), None),
        P("groups", "grid"),
        P(("groups", "grid")),
    )
    return jax.shard_map(local, mesh=mesh, in_specs=in_specs, out_specs=out_specs, check_vma=False)
```

```python
import functools
import jax
import jax.numpy as jnp
from jax import lax
from jax.experimental import pallas as pl
from jax.experimental.pallas import tpu as pltpu
from jax.sharding import PartitionSpec as P

diffusion_rate = 0.24
VMEM_BYTES = 24 * 1024 * 1024
EXTRA = 16
bf16 = jnp.bfloat16
f32 = jnp.float32


def params():
    return pltpu.CompilerParams(vmem_limit_bytes=VMEM_BYTES)


def scenario_block(scenarios):
    for size in (64, 32, 16):
        if scenarios % size == 0:
            return size
    return scenarios


LANES = 128
SUBLANES = 8
GROUP = 16


def to_tiles(hist):
    scenarios, rows, columns = hist.shape
    high = min(rows, SUBLANES)
    tiles = hist.reshape(scenarios, rows // high, high, columns // LANES, LANES)
    return tiles.transpose(0, 1, 3, 2, 4).reshape(scenarios * rows * (columns // LANES), LANES)


def from_tiles(tiles, shape):
    scenarios, rows, columns = shape
    high = min(rows, SUBLANES)
    parts = tiles.reshape(scenarios, rows // high, columns // LANES, high, LANES)
    return parts.transpose(0, 1, 3, 2, 4).reshape(shape)


def tile_offset(row, lane_tile, rows, lane_tiles):
    high = min(rows, SUBLANES)
    return (row // high * lane_tiles + lane_tile) * high + row % high


def read_row(ref, first_scenario, count, row, rows, columns):
    lane_tiles = columns // LANES
    per = rows * lane_tiles
    return jnp.concatenate(
        [
            ref[pl.ds(first_scenario * per + tile_offset(row, t, rows, lane_tiles), count, stride=per), :]
            for t in range(lane_tiles)
        ],
        axis=1,
    )


def write_row(ref, first_scenario, count, row, rows, columns, values):
    lane_tiles = columns // LANES
    per = rows * lane_tiles
    for t in range(lane_tiles):
        place = pl.ds(first_scenario * per + tile_offset(row, t, rows, lane_tiles), count, stride=per)
        ref[place, :] = values[:, t * LANES : (t + 1) * LANES]


def drift_tail(drift_ref, start):
    pieces = [
        jnp.concatenate([drift_ref[c, start : start + 1], drift_ref[c, start + 1 : start + 2]], axis=1)
        for c in range(2)
    ]
    high, low = two_halves(jnp.concatenate(pieces, axis=0))
    ones = jnp.ones((1, high.shape[1]), bf16)
    zeros = jnp.zeros((EXTRA - 5, high.shape[1]), bf16)
    return jnp.concatenate([high, low, ones, zeros], axis=0)


def band_matrix(columns):
    row = lax.broadcasted_iota(jnp.int32, (columns, columns), 0)
    column = lax.broadcasted_iota(jnp.int32, (columns, columns), 1)
    right = jnp.where(column == row + 1, 1.0, 0.0)
    left = jnp.where(column == row - 1, 1.0, 0.0)
    centre = jnp.where(column == row, 1.0 - 4.0 * diffusion_rate, diffusion_rate * (right + left))
    return centre.astype(bf16), (right - left).astype(bf16)


def half_shifts(levels_ref, table_ref, shift_ref):
    scenarios = levels_ref.shape[1]
    for t in range(levels_ref.shape[0]):
        level = jnp.broadcast_to(levels_ref[t : t + 1, :].astype(f32), (LANES, scenarios)).T
        for c in range(2):
            shift = jnp.zeros(level.shape, f32)
            for n in range(table_ref.shape[1]):
                shift = jnp.where(level == n, 0.5 * table_ref[c : c + 1, n : n + 1], shift)
            shift_ref[2 * t + c] = shift


def wide(values, columns):
    return jnp.concatenate([values] * (columns // LANES), axis=1)


def one_step(rows_of, places, half_drift, band, shift_x, shift_y, pairs, terms, write):
    size, columns = shift_x.shape
    whole = pl.ds(0, columns)

    def density(row):
        return pairs[pl.ds(rows_of[row] * size, size), whole].astype(f32)

    for row in places:
        flux = (half_drift(1, row) + shift_y) * density(row)
        pairs[pl.ds(rows_of[row] * size, size), pl.ds(columns, columns)] = flux.astype(bf16)
    start = rows_of[places[0]] * size
    count = (rows_of[places[-1]] + 1) * size - start
    terms[pl.ds(start, count), :] = jnp.dot(pairs[pl.ds(start, count), :], band, preferred_element_type=f32)
    for row in places:
        low = density(row - 1) * ((diffusion_rate + half_drift(0, row - 1)) + shift_x)
        high = density(row + 1) * ((diffusion_rate - half_drift(0, row + 1)) - shift_x)
        write(row, terms[pl.ds(rows_of[row] * size, size), :] + low + high)


def two_steps(segments, read, half_drift, edge, band, shifts, scratch, write):
    pairs, later, terms = scratch
    size, columns = shifts[0].shape
    before, between, after = [
        [row for first, last in segments for row in range(first - more, last + more + 1)] for more in (2, 1, 0)
    ]
    rows_of = {row: k for k, row in enumerate(before)}
    for row, k in rows_of.items():
        pairs[pl.ds(k * size, size), pl.ds(0, columns)] = read(row)

    def write_later(row, density):
        later[pl.ds(rows_of[row] * size, size), pl.ds(0, columns)] = edge(row, density).astype(bf16)

    one_step(rows_of, between, half_drift, band, shifts[0], shifts[1], pairs, terms, write_later)
    one_step(rows_of, after, half_drift, band, shifts[2], shifts[3], later, terms, write)


def step_scratch(segments, size, columns):
    rows = sum(last - first + 5 for first, last in segments)
    pairs = pltpu.VMEM((rows * size, 2 * columns), bf16)
    return [pairs, pairs, pltpu.VMEM((rows * size, columns), f32)]


def edge_segments(rows):
    return [(0, 1), (rows - 2, rows - 1)] if rows >= 8 else [(0, rows - 1)]


def inner_kernel(
    rows, size, hist_ref, drift_hbm, levels_hbm, table_hbm, cot_hbm,
    first_ref, last_ref, shift_ref, band_ref, cot_ref, rows_ref, inner_ref,
    drift_ref, levels_ref, table_ref, cot_row, arrived, all_shifts, *scratch,
):
    step = pl.program_id(0)
    columns = drift_ref.shape[2]

    @pl.when(step == 0)
    def _():
        sources = ((drift_hbm, drift_ref), (levels_hbm, levels_ref), (table_hbm, table_ref), (cot_hbm, cot_row))
        copies = [pltpu.make_async_copy(*pair, arrived.at[n]) for n, pair in enumerate(sources)]
        for copy in copies:
            copy.start()
        centre, flux = band_matrix(columns)
        band_ref[pl.ds(0, columns), :] = centre
        band_ref[pl.ds(columns, columns), :] = flux
        for copy in copies:
            copy.wait()
        half_shifts(levels_ref, table_ref, all_shifts)
        cot_ref[...] = jnp.broadcast_to(cot_row[...], (LANES, cot_row.shape[1])).T
        for out, start in ((first_ref, 0), (last_ref, rows - 2)):
            out[pl.ds(out.shape[0] - EXTRA, EXTRA), :] = drift_tail(drift_ref, start)

    where = pl.ds(pl.multiple_of(step * size, size), size)
    for n in range(4):
        shift_ref[n] = all_shifts[n, where, :]
    for row in range(rows):
        density = read_row(hist_ref, 0, size, row, rows, columns).astype(bf16)
        rows_ref[:, pl.ds(row * columns, columns)] = density
        if row < 2:
            first_ref[where, pl.ds(row * columns, columns)] = density
        if row >= rows - 2:
            last_ref[where, pl.ds((row - rows + 2) * columns, columns)] = density
    if rows <= 4:
        return

    def write(row, density):
        inner_ref[:, pl.ds((row - 2) * columns, columns)] = density.astype(bf16)

    two_steps(
        [(2, rows - 3)],
        lambda row: rows_ref[:, pl.ds(row * columns, columns)],
        lambda c, row: 0.5 * drift_ref[c, row : row + 1, :],
        lambda row, density: density,
        band_ref[...],
        [wide(shift_ref[n], columns) for n in range(4)],
        scratch,
        write,
    )


def inner_steps(tiles, drift, levels, table, cot):
    scenarios = levels.shape[1]
    rows, columns = drift.shape[1:]
    per = tiles.shape[0] // scenarios
    size = scenario_block(scenarios)
    inner = max(rows - 4, 1) * columns
    sent = jax.ShapeDtypeStruct((scenarios + EXTRA, 2 * columns), bf16)
    shifts = jax.ShapeDtypeStruct((4, scenarios, LANES), f32)
    band = jax.ShapeDtypeStruct((2 * columns, columns), bf16)
    return pl.pallas_call(
        functools.partial(inner_kernel, rows, size),
        grid=(scenarios // size,),
        in_specs=[pl.BlockSpec((size * per, LANES), lambda i: (i, 0))] + [pl.BlockSpec(memory_space=pltpu.HBM)] * 4,
        out_specs=[pl.BlockSpec(sent.shape, lambda i: (0, 0))] * 2
        + [
            pl.BlockSpec((4, size, LANES), lambda i: (0, i, 0)),
            pl.BlockSpec(band.shape, lambda i: (0, 0)),
            pl.BlockSpec((scenarios, LANES), lambda i: (0, 0)),
            pl.BlockSpec((size, rows * columns), lambda i: (i, 0)),
            pl.BlockSpec((size, inner), lambda i: (i, 0)),
        ],
        out_shape=[
            sent,
            sent,
            pltpu.HBM(shifts.shape, f32),
            band,
            jax.ShapeDtypeStruct((scenarios, LANES), f32),
            pltpu.HBM((scenarios, rows * columns), bf16),
            jax.ShapeDtypeStruct((scenarios, inner), bf16),
        ],
        scratch_shapes=[
            pltpu.VMEM(drift.shape, f32),
            pltpu.VMEM(levels.shape, levels.dtype),
            pltpu.VMEM(table.shape, f32),
            pltpu.VMEM(cot.shape, f32),
            pltpu.SemaphoreType.DMA((4,)),
            pltpu.VMEM(shifts.shape, f32),
        ]
        + step_scratch([(2, max(rows - 3, 2))], size, columns),
        compiler_params=params(),
        cost_estimate=pl.CostEstimate(flops=1, bytes_accessed=1, transcendentals=0),
        name="inner_density_steps",
    )(tiles, drift, levels, table, cot)


def halo_drift(ref, columns):
    tail = ref[...].astype(f32)
    both = 0.5 * (tail[0:2] + tail[2:4])
    rows = [[both[c : c + 1, k * columns : (k + 1) * columns] for k in range(2)] for c in range(2)]
    return rows, tail[4:5, :columns]


def with_halo(drift_ref, below_tail, above_tail):
    rows, columns = drift_ref.shape[1:]
    below, below_valid = halo_drift(below_tail, columns)
    above, above_valid = halo_drift(above_tail, columns)

    def half_drift(c, row):
        if row < 0:
            return below[c][row + 2]
        if row >= rows:
            return above[c][row - rows]
        return 0.5 * drift_ref[c, row : row + 1, :]

    def edge(row, density):
        if row < 0:
            return density * below_valid
        if row >= rows:
            return density * above_valid
        return density

    return half_drift, edge


def density_kernel(segments, drift_ref, shift_ref, band_ref, rows_ref, below_ref, above_ref, below_tail, above_tail, dep_ref, *refs):
    scratch = refs[-3:]
    rows, columns = drift_ref.shape[1:]
    size = shift_ref.shape[1]
    half_drift, edge = with_halo(drift_ref, below_tail, above_tail)

    def read(row):
        if row < 0:
            return below_ref[:, pl.ds((row + 2) * columns, columns)]
        if row >= rows:
            return above_ref[:, pl.ds((row - rows) * columns, columns)]
        return rows_ref[:, pl.ds(row * columns, columns)]

    if segments is None:
        next_ref, token_ref = refs[-5:-3]
        token_ref[...] = jnp.zeros(token_ref.shape, f32)

        def write(row, density):
            write_row(next_ref, 0, size, row, rows, columns, density)

    else:
        low_ref, high_ref = refs[-5:-3]

        def write(row, density):
            if row < 2:
                low_ref[:, pl.ds(row * columns, columns)] = density.astype(bf16)
            else:
                high_ref[:, pl.ds((row - rows + 2) * columns, columns)] = density.astype(bf16)

    shifts = [wide(shift_ref[n], columns) for n in range(4)]
    two_steps(segments or [(0, rows - 1)], read, half_drift, edge, band_ref[...], shifts, scratch, write)


def density_specs(drift, shifts, band, own, below, size, first):
    columns = drift.shape[2]
    scenarios = shifts.shape[1]
    halo = pl.BlockSpec((size, 2 * columns), lambda i: (first + i, 0))
    tail = pl.BlockSpec((EXTRA, 2 * columns), lambda i: (scenarios // EXTRA, 0))
    return [
        pl.BlockSpec(drift.shape, lambda i: (0, 0, 0)),
        pl.BlockSpec((4, size, LANES), lambda i: (0, first + i, 0)),
        pl.BlockSpec(band.shape, lambda i: (0, 0)),
        pl.BlockSpec((size, own.shape[1]), lambda i: (first + i, 0)),
        halo,
        halo,
        tail,
        tail,
        pl.BlockSpec(memory_space=pl.ANY),
    ]


def edge_steps(drift, shifts, band, own, below, above, dep):
    scenarios = shifts.shape[1]
    rows, columns = drift.shape[1:]
    size = 2 * scenario_block(scenarios)
    size = size if scenarios % size == 0 else size // 2
    edge = jax.ShapeDtypeStruct((scenarios, 2 * columns), bf16)
    spec = pl.BlockSpec((size, 2 * columns), lambda i: (i, 0))
    segments = edge_segments(rows)
    return pl.pallas_call(
        functools.partial(density_kernel, segments),
        grid=(scenarios // size,),
        in_specs=density_specs(drift, shifts, band, own, below, size, 0),
        out_specs=[spec, spec],
        out_shape=[edge, edge],
        scratch_shapes=step_scratch(segments, size, columns),
        compiler_params=params(),
        cost_estimate=pl.CostEstimate(flops=1, bytes_accessed=1, transcendentals=0),
        name="edge_density_steps",
    )(drift, shifts, band, own, below, above, below, above, dep)


def density_steps(drift, shifts, band, own, below, above, dep, so_far, turn, turns):
    scenarios = shifts.shape[1]
    rows, columns = drift.shape[1:]
    per = rows * (columns // LANES)
    size = 3 * GROUP if scenarios % (turns * GROUP * 3) == 0 else GROUP
    steps = scenarios // size // turns
    first = turn * steps
    args = [drift, shifts, band, own, below, above, below, above, dep]
    in_specs = density_specs(drift, shifts, band, own, below, size, first)
    aliases = {}
    if so_far is not None:
        aliases = {len(args): 0}
        args.append(so_far)
        in_specs.append(pl.BlockSpec(memory_space=pltpu.HBM))
    return pl.pallas_call(
        functools.partial(density_kernel, None),
        grid=(steps,),
        in_specs=in_specs,
        out_specs=[
            pl.BlockSpec((size * per, LANES), lambda i: (first + i, 0)),
            pl.BlockSpec((SUBLANES, LANES), lambda i: (0, 0)),
        ],
        out_shape=[pltpu.HBM((scenarios * per, LANES), f32), jax.ShapeDtypeStruct((SUBLANES, LANES), f32)],
        input_output_aliases=aliases,
        scratch_shapes=step_scratch([(0, rows - 1)], size, columns),
        compiler_params=params(),
        cost_estimate=pl.CostEstimate(flops=1, bytes_accessed=1, transcendentals=0),
        name="density_steps",
    )(*args)


def smem():
    return pl.BlockSpec(memory_space=pltpu.SMEM)


def vmem():
    return pl.BlockSpec(memory_space=pltpu.VMEM)


def swap(values, count, flip):
    return lax.ppermute(values, "grid", [(i, i ^ flip) for i in range(count)])


def inner_product_kernel(count, inputs_ref, *refs):
    weight = jnp.concatenate([ref[...] for ref in refs[:count]], axis=0)
    refs[-1][pl.program_id(0)] = jnp.dot(inputs_ref[...], weight, preferred_element_type=f32)


def inner_product(inner, weight, width, deps):
    scenarios, cells = inner.shape
    total, hidden = weight.shape
    size = (total - cells) // 2
    count = cells // size

    def spec(k):
        return pl.BlockSpec((size, width), lambda n: (1 + k, n))

    return pl.pallas_call(
        functools.partial(inner_product_kernel, count),
        grid=(hidden // width,),
        in_specs=[vmem()] + [spec(k) for k in range(count)] + any_specs(deps),
        out_specs=vmem(),
        out_shape=jax.ShapeDtypeStruct((hidden // width, scenarios, width), f32),
        compiler_params=params(),
        cost_estimate=pl.CostEstimate(flops=1, bytes_accessed=1, transcendentals=0),
        name="inner_product",
    )(inner, *([weight] * count), *deps)


def edge_product_kernel(block, with_inner, place_ref, low_ref, high_ref, top_ref, bottom_ref, *refs):
    keep_ref, send_ref, total = refs[-3:]
    step = pl.program_id(0)
    left = jnp.concatenate([low_ref[...], high_ref[...]], axis=1)
    weight = jnp.concatenate([top_ref[...], bottom_ref[...]], axis=0)
    product = jnp.dot(left, weight, preferred_element_type=f32)
    total[...] = product + refs[0][step] if with_inner else product
    core = place_ref[0]
    for out, half in ((keep_ref, core), (send_ref, 1 - core)):
        for side in range(2):
            start = pl.multiple_of((2 * half + side) * block, block)
            out[side, step] = total[pl.ds(start, block), :].astype(out.dtype)


def edge_product(place, low, high, weight, inner, parts, width):
    scenarios, size = low.shape
    block = scenarios // 4
    last = weight.shape[0] // size - 1
    shape = (2, parts, block, width)
    in_specs = [
        smem(),
        vmem(),
        vmem(),
        pl.BlockSpec((size, width), lambda n: (0, n)),
        pl.BlockSpec((size, width), lambda n: (last, n)),
    ]
    args = [place, low, high, weight, weight]
    if inner is not None:
        in_specs.append(vmem())
        args.append(inner)
    return pl.pallas_call(
        functools.partial(edge_product_kernel, block, inner is not None),
        grid=(parts,),
        in_specs=in_specs,
        out_specs=[vmem(), vmem()],
        out_shape=[jax.ShapeDtypeStruct(shape, f32), jax.ShapeDtypeStruct(shape, bf16)],
        scratch_shapes=[pltpu.VMEM((scenarios, width), f32)],
        compiler_params=params(),
        cost_estimate=pl.CostEstimate(flops=1, bytes_accessed=1, transcendentals=0),
        name="edge_product",
    )(*args)


def add_side_kernel(place_ref, mine_ref, other_ref, *refs):
    keep_ref, send_ref = refs[-2:]
    side = place_ref[1]
    keep_ref[...] = mine_ref[side] + other_ref[side].astype(f32)
    send_ref[...] = (mine_ref[1 - side] + other_ref[1 - side].astype(f32)).astype(bf16)


def any_specs(deps):
    return [pl.BlockSpec(memory_space=pl.ANY)] * len(deps)


def add_side(place, mine, other, deps=()):
    shape = mine.shape[1:]
    return pl.pallas_call(
        add_side_kernel,
        in_specs=[smem()] + [vmem()] * 2 + any_specs(deps),
        out_shape=[jax.ShapeDtypeStruct(shape, f32), jax.ShapeDtypeStruct(shape, bf16)],
        compiler_params=params(),
        cost_estimate=pl.CostEstimate(flops=1, bytes_accessed=1, transcendentals=0),
        name="add_side",
    )(place, mine, other, *deps)


def add_parts_kernel(dep_count, place_ref, mine_ref, other_ref, *refs):
    own_ref, *send_refs = refs[dep_count:]
    part = place_ref[2]
    own_ref[...] = mine_ref[part] + other_ref[part].astype(f32)
    for k, out in enumerate(send_refs):
        at = part ^ (k + 1)
        out[...] = (mine_ref[at] + other_ref[at].astype(f32)).astype(bf16)


def add_parts(place, mine, other, deps=()):
    parts = mine.shape[0]
    return pl.pallas_call(
        functools.partial(add_parts_kernel, len(deps)),
        in_specs=[smem(), vmem(), vmem()] + any_specs(deps),
        out_shape=[jax.ShapeDtypeStruct(mine.shape[1:], f32)]
        + [jax.ShapeDtypeStruct(mine.shape[1:], bf16)] * (parts - 1),
        compiler_params=params(),
        cost_estimate=pl.CostEstimate(flops=1, bytes_accessed=1, transcendentals=0),
        name="add_parts",
    )(place, mine, other, *deps)


def activate_kernel(count, *refs):
    total = refs[0][...]
    for ref in refs[1 : 1 + count]:
        total = total + ref[...].astype(f32)
    refs[-1][...] = jnp.tanh(total).astype(bf16)


def activate(own, received, deps=()):
    return pl.pallas_call(
        functools.partial(activate_kernel, len(received)),
        in_specs=[vmem()] * (1 + len(received)) + any_specs(deps),
        out_shape=jax.ShapeDtypeStruct(own.shape, bf16),
        compiler_params=params(),
        cost_estimate=pl.CostEstimate(flops=1, bytes_accessed=1, transcendentals=0),
        name="first_activation",
    )(own, *received, *deps)


def pack_kernel(place_ref, mid_ref, head_ref, first_ref, out_ref, place_out_ref, head_row, arrived):
    for n in range(4):
        place_out_ref[n] = place_ref[n]
    hidden = mid_ref.shape[0]
    copies = [
        pltpu.make_async_copy(mid_ref, out_ref.at[pl.ds(0, hidden), :], arrived.at[0]),
        pltpu.make_async_copy(head_ref, head_row, arrived.at[1]),
    ]
    for copy in copies:
        copy.start()
    copies[1].wait()
    out_ref[pl.ds(hidden, EXTRA), :] = tail_rows(head_row[...])
    copies[0].wait()


def pack(place, mid_weight, head, first):
    hidden, units = mid_weight.shape
    return pl.pallas_call(
        pack_kernel,
        in_specs=[smem()] + [pl.BlockSpec(memory_space=pltpu.HBM)] * 3,
        out_specs=[vmem(), smem()],
        out_shape=[jax.ShapeDtypeStruct((hidden + EXTRA, units), bf16), jax.ShapeDtypeStruct(place.shape, place.dtype)],
        scratch_shapes=[pltpu.VMEM(head.shape, f32), pltpu.SemaphoreType.DMA((2,))],
        compiler_params=params(),
        cost_estimate=pl.CostEstimate(flops=1, bytes_accessed=1, transcendentals=0),
        name="mid_with_head",
    )(place, *[pltpu.with_memory_space_constraint(array, pltpu.HBM) for array in (mid_weight, head)], first)


def two_halves(exact):
    high = exact.astype(bf16)
    low = (exact - high.astype(f32)).astype(bf16)
    return high, low


def tail_rows(exact):
    high, low = two_halves(exact)
    zeros = jnp.zeros((EXTRA - 2, exact.shape[1]), bf16)
    return jnp.concatenate([high, low, zeros], axis=0)


def middle_kernel(chunks, parts, width, *refs):
    pieces = chunks * parts
    place_ref, cot_ref = refs[0], refs[1]
    first_refs = refs[2 : 2 + pieces]
    mid_refs = refs[2 + pieces : 6 + pieces]
    outs = refs[-(3 + parts) :]
    own_ref, value_ref, mid_keep_ref, mid_send_ref = outs[:4]
    send_refs = outs[4:]
    part = place_ref[2]
    block = first_refs[0].shape[0]

    def mid_rows(start):
        return jnp.concatenate([ref[pl.ds(start, width), :] for ref in mid_refs], axis=1)

    def start_of(c, k):
        return pl.multiple_of((c * parts + (part ^ k)) * width, width)

    total = None
    for c in range(chunks):
        for k in range(parts):
            term = jnp.dot(first_refs[c * parts + k][...], mid_rows(start_of(c, k)), preferred_element_type=f32)
            total = term if total is None else total + term
    second_low = jnp.tanh(total).astype(bf16)
    second = second_low.astype(f32)
    heads = jnp.concatenate([ref[pl.ds(pieces * width, EXTRA), :] for ref in mid_refs], axis=1)
    head = heads[0:1].astype(f32) + heads[1:2].astype(f32)
    rows = lax.dot_general(heads, second_low, (((1,), (1,)), ((), ())), preferred_element_type=f32)
    value = rows[0:1] + rows[1:2]
    if width > block:
        value = jnp.concatenate([value, jnp.zeros((1, width - block), f32)], axis=1)
    value_ref[...] = value
    cot = cot_ref[pl.ds(pl.multiple_of(place_ref[3] * block, SUBLANES), block), :1]
    head_part = jnp.sum(cot * second, axis=0, keepdims=True)
    back = (cot * head * (1.0 - second * second)).astype(bf16)
    units = mid_refs[0].shape[1]
    for k in range(parts):
        for c in range(chunks):
            piece = lax.dot_general(
                back, mid_rows(start_of(c, k)), (((1,), (1,)), ((), ())), preferred_element_type=f32
            )
            if k == 0:
                own_ref[pl.ds(c * block, block), :] = piece
            else:
                send_refs[k - 1][pl.ds(c * block, block), :] = piece.astype(bf16)
        if k > 0:
            send_refs[k - 1][pl.ds(chunks * block, EXTRA), :] = tail_rows(value)
    for c in range(chunks):
        for k in range(parts):
            product = lax.dot_general(
                first_refs[c * parts + k][...], back, (((0,), (0,)), ((), ())), preferred_element_type=f32
            ).astype(bf16)
            for p in range(4):
                out = (mid_keep_ref, mid_send_ref)[p % 2]
                out[p // 2, pl.ds(start_of(c, k), width), :] = product[:, p * units : (p + 1) * units]
    for p in range(4):
        out = (mid_keep_ref, mid_send_ref)[p % 2]
        out[p // 2, pl.ds(pieces * width, EXTRA), :] = tail_rows(head_part[:, p * units : (p + 1) * units])


def middle(place, cot, firsts, mids, chunks, parts, width, deps=()):
    block = firsts[0].shape[0]
    partial = jax.ShapeDtypeStruct((2, *mids[0].shape), bf16)
    return pl.pallas_call(
        functools.partial(middle_kernel, chunks, parts, width),
        in_specs=[smem()] + [vmem()] * (1 + len(firsts) + 4) + any_specs(deps),
        out_shape=[
            jax.ShapeDtypeStruct((chunks * block, width), f32),
            jax.ShapeDtypeStruct((1, width), f32),
            partial,
            partial,
        ]
        + [jax.ShapeDtypeStruct((chunks * block + EXTRA, width), bf16)] * (parts - 1),
        compiler_params=params(),
        cost_estimate=pl.CostEstimate(flops=1, bytes_accessed=1, transcendentals=0),
        name="value_layers",
    )(place, cot, *firsts, *mids, *deps)


def add_tail(left, right, hidden):
    body = left[:hidden].astype(f32) + right[:hidden].astype(f32)
    tails = left[hidden:].astype(f32) + right[hidden:].astype(f32)
    return body.astype(bf16), tails[0:1] + tails[1:2]


def mid_add_kernel(keep_ref, other_ref, *refs):
    own_ref, send_ref = refs[-2:]
    hidden = own_ref.shape[0] - EXTRA
    for at, out in enumerate((own_ref, send_ref)):
        body, tail = add_tail(keep_ref[at], other_ref[at], hidden)
        out[pl.ds(0, hidden), :] = body
        out[pl.ds(hidden, EXTRA), :] = tail_rows(tail)


def mid_add(keep, other, deps=()):
    shape = jax.ShapeDtypeStruct(keep.shape[1:], bf16)
    return pl.pallas_call(
        mid_add_kernel,
        in_specs=[vmem()] * 2 + any_specs(deps),
        out_shape=[shape, shape],
        compiler_params=params(),
        cost_estimate=pl.CostEstimate(flops=1, bytes_accessed=1, transcendentals=0),
        name="mid_gradient_add",
    )(keep, other, *deps)


def mid_final_kernel(own_ref, other_ref, *refs):
    out_ref, head_ref, token_ref = refs[-3:]
    token_ref[...] = jnp.zeros(token_ref.shape, f32)
    body, tail = add_tail(own_ref[...], other_ref[...], out_ref.shape[0])
    out_ref[...] = body
    head_ref[...] = tail


def mid_final(own, other, deps=()):
    hidden = own.shape[0] - EXTRA
    return pl.pallas_call(
        mid_final_kernel,
        in_specs=[vmem()] * 2 + any_specs(deps),
        out_shape=[
            jax.ShapeDtypeStruct((hidden, own.shape[1]), bf16),
            jax.ShapeDtypeStruct((1, own.shape[1]), f32),
            jax.ShapeDtypeStruct((SUBLANES, LANES), f32),
        ],
        compiler_params=params(),
        cost_estimate=pl.CostEstimate(flops=1, bytes_accessed=1, transcendentals=0),
        name="mid_gradient_final",
    )(own, other, *deps)


def back_first_kernel(chunks, count, *refs):
    own_ref, value_ref = refs[:2]
    received = refs[2 : 2 + count]
    first_refs = refs[2 + count : 2 + count + chunks]
    out_refs = refs[-1 - chunks : -1]
    tail_ref = refs[-1]
    block = first_refs[0].shape[0]
    value = value_ref[...]
    for ref in received:
        tail = ref[pl.ds(chunks * block, EXTRA), :].astype(f32)
        value = value + (tail[0:1] + tail[1:2])
    tail_ref[...] = tail_rows(value)
    for c in range(chunks):
        total = own_ref[pl.ds(c * block, block), :]
        for ref in received:
            total = total + ref[pl.ds(c * block, block), :].astype(f32)
        first = first_refs[c][...].astype(f32)
        out_refs[c][...] = (total * (1.0 - first * first)).astype(bf16)


def back_first(own, value, received, firsts, deps=()):
    chunks = len(firsts)
    shape = firsts[0].shape
    return pl.pallas_call(
        functools.partial(back_first_kernel, chunks, len(received)),
        in_specs=[vmem()] * (2 + len(received) + chunks) + any_specs(deps),
        out_shape=[jax.ShapeDtypeStruct(shape, bf16)] * chunks
        + [jax.ShapeDtypeStruct((EXTRA, shape[1]), bf16)],
        compiler_params=params(),
        cost_estimate=pl.CostEstimate(flops=1, bytes_accessed=1, transcendentals=0),
        name="back_first",
    )(own, value, *received, *firsts, *deps)


def stack_kernel(count, halves, *refs):
    outs = refs[-halves:]
    width = outs[0].shape[1]
    at = 0
    for ref in refs[:count]:
        for n, out in enumerate(outs):
            out[pl.ds(at, ref.shape[0]), :] = ref[:, pl.ds(n * width, width)]
        at += ref.shape[0]


def stack(pieces, halves, deps=()):
    rows = sum(piece.shape[0] for piece in pieces)
    shape = jax.ShapeDtypeStruct((rows, pieces[0].shape[1] // halves), bf16)
    return pl.pallas_call(
        functools.partial(stack_kernel, len(pieces), halves),
        in_specs=[vmem()] * len(pieces) + any_specs(deps),
        out_shape=[shape] * halves,
        compiler_params=params(),
        cost_estimate=pl.CostEstimate(flops=1, bytes_accessed=1, transcendentals=0),
        name="stack_parts",
    )(*pieces, *deps)


def turn_kernel(count, *refs):
    for ref, out in zip(refs[:count], refs[-count:]):
        out[...] = ref[...].T


def transposed(arrays, deps):
    return pl.pallas_call(
        functools.partial(turn_kernel, len(arrays)),
        in_specs=[vmem()] * len(arrays) + any_specs(deps),
        out_shape=[jax.ShapeDtypeStruct(array.shape[::-1], array.dtype) for array in arrays],
        compiler_params=params(),
        cost_estimate=pl.CostEstimate(flops=1, bytes_accessed=1, transcendentals=0),
        name="transposed_inputs",
    )(*arrays, *deps)


def first_grad_kernel(parts, block, count, with_value, *refs):
    place_ref = refs[0]
    lefts = refs[1 : 1 + count]
    stacks = refs[1 + count : 5 + count]
    outs = refs[-3:-1] if with_value else refs[-2:-1]
    whole = refs[-1]
    step = pl.program_id(0)
    mine = place_ref[3]
    values = [jnp.zeros((1, block), f32)] * 4
    for t, ref in enumerate(stacks):
        at = mine ^ (2 * (t % 2) + t // 2)
        piece = step ^ place_ref[2]
        whole[pl.ds(pl.multiple_of(at * block, block), block), :] = ref[
            pl.ds(pl.multiple_of(piece * block, block), block), :
        ]
        if with_value:
            tail = ref[pl.ds(parts * block, EXTRA), :block].astype(f32)
            value = tail[0:1] + tail[1:2]
            for q in range(4):
                values[q] = jnp.where(at == q, value, values[q])
    if with_value:
        outs[1][...] = jnp.concatenate(values, axis=1)
    start = 0
    for ref in lefts:
        cells = ref.shape[0]
        outs[0][pl.ds(start, cells), :] = jnp.dot(ref[...], whole[...], preferred_element_type=f32).astype(bf16)
        start += cells


def first_grad(place, lefts, stacks, so_far, hidden, parts, block, half, halves, deps):
    scenarios = lefts[0].shape[1]
    cells = sum(left.shape[0] for left in lefts)
    width = stacks[0].shape[1]
    with_value = half == 0
    in_specs = [smem()] + [vmem()] * (len(lefts) + 4) + any_specs(deps)
    args = [place, *lefts, *stacks, *deps]
    aliases = {}
    if so_far is not None:
        aliases = {len(args): 0}
        in_specs.append(pl.BlockSpec(memory_space=pltpu.HBM))
        args.append(so_far)
    out_specs = [pl.BlockSpec((cells, width), lambda i: (0, i * halves + half))]
    out_shape = [pltpu.HBM((cells, hidden), bf16)]
    if with_value:
        out_specs.append(pl.BlockSpec((1, scenarios), lambda i: (0, 0)))
        out_shape.append(jax.ShapeDtypeStruct((1, scenarios), f32))
    return pl.pallas_call(
        functools.partial(first_grad_kernel, parts, block, len(lefts), with_value),
        grid=(parts,),
        in_specs=in_specs,
        out_specs=out_specs,
        out_shape=out_shape,
        input_output_aliases=aliases,
        scratch_shapes=[pltpu.VMEM((scenarios, width), bf16)],
        compiler_params=params(),
        cost_estimate=pl.CostEstimate(flops=1, bytes_accessed=1, transcendentals=0),
        name="first_gradient",
    )(*args)


def local(hist, drift, shocks, shock_table, first_weight, mid_weight, head_weight, cotangent):
    scenarios, rows, columns = hist.shape
    count = lax.axis_size("grid")
    hidden = first_weight.shape[1]
    units = mid_weight.shape[1]
    parts = count // 4
    width = hidden // parts
    block = scenarios // 4
    index = lax.axis_index("grid")
    core, side, part = index & 1, (index >> 1) & 1, index >> 2
    mine = 2 * core + side
    tiles = pltpu.with_memory_space_constraint(to_tiles(hist), pltpu.HBM)

    place = jnp.stack([core, side, part, mine])
    halves = 1

    small = [pltpu.with_memory_space_constraint(array, pltpu.HBM) for array in (drift, shocks.T, shock_table.T, cotangent[None, :])]
    packed, place = pack(place, mid_weight, head_weight[None, :], small[-1])
    mids = [packed]
    mids += [swap(mids[0], count, 1), swap(mids[0], count, 2)]
    first_rows, last_rows, shifts, band, cot, own_rows, inner = inner_steps(tiles, *small)
    inner = inner if rows > 4 else None
    forward = [(i, i + 1) for i in range(count - 1)]
    backward = [(i + 1, i) for i in range(count - 1)]
    below = lax.ppermute(last_rows, "grid", forward)
    above = lax.ppermute(first_rows, "grid", backward)
    first_weight = pltpu.with_memory_space_constraint(first_weight, pltpu.HBM)
    product = None if inner is None else inner_product(inner, first_weight, width, mids[1:])
    low, high = edge_steps(drift, shifts, band, own_rows, below, above, own_rows if product is None else product)
    mids.append(swap(mids[2], count, 1))

    def density_turn(turn, dep, so_far):
        return density_steps(drift, shifts, band, own_rows, below, above, dep, so_far, turn, 2)

    keep, send = edge_product(place, low, high, first_weight, product, parts, width)
    keep, send = add_side(place, keep, swap(send, count, 1))
    other = swap(send, count, 2)
    density, token = density_turn(0, send, None)
    own, *sends = add_parts(place, keep, other, [token, mids[3]])
    received = [swap(piece, count, 4 * (k + 1)) for k, piece in enumerate(sends)]
    first = activate(own, received)
    firsts = [first] + [swap(first, count, 4 * k) for k in range(1, parts)]
    density, token = density_turn(1, first, density)
    own, value, mid_keep, mid_send, *sends = middle(place, cot, firsts, mids, 1, parts, width, [token])
    received = [swap(piece, count, 4 * (k + 1)) for k, piece in enumerate(sends)]
    back, tail = back_first(own, value, received, [first])
    mid_keep, mid_send = mid_add(mid_keep, swap(mid_send, count, 1), [back])
    lefts = transposed([low, high] if inner is None else [low, inner, high], [back])
    pieces = [back] + [swap(back, count, 4 * k) for k in range(1, parts)]
    grad_mid, grad_head, token = mid_final(mid_keep, swap(mid_send, count, 2))
    stacks = stack(pieces + [tail], halves, [lefts[0], token])
    grad_first = None
    for half, own_stack in enumerate(stacks):
        gathered = [own_stack, swap(own_stack, count, 1), swap(own_stack, count, 2)]
        gathered.append(swap(gathered[2], count, 1))
        results = first_grad(
            place, lefts, gathered, grad_first, hidden, parts, block, half, halves, []
        )
        grad_first = results[0]
        if half == 0:
            value = results[1].reshape(scenarios)
    return from_tiles(density, hist.shape), value, grad_first, grad_mid, grad_head[0]


def solution(mesh):
    in_specs = (
        P("groups", "grid", None),
        P(None, "grid", None),
        P("groups", None),
        P("groups", None),
        P(("groups", "grid"), None),
        P("groups", "grid"),
        P(("groups", "grid")),
        P("groups"),
    )
    out_specs = (
        P("groups", "grid", None),
        P("groups"),
        P(("groups", "grid"), None),
        P("groups", "grid"),
        P(("groups", "grid")),
    )
    return jax.shard_map(local, mesh=mesh, in_specs=in_specs, out_specs=out_specs, check_vma=False)
```

```python
import functools
import jax
import jax.numpy as jnp
from jax import lax
from jax.experimental import pallas as pl
from jax.experimental.pallas import tpu as pltpu
from jax.sharding import PartitionSpec as P

diffusion_rate = 0.24
VMEM_BYTES = 24 * 1024 * 1024
EXTRA = 16
bf16 = jnp.bfloat16
f32 = jnp.float32


def params():
    return pltpu.CompilerParams(vmem_limit_bytes=VMEM_BYTES)


def scenario_block(scenarios):
    for size in (64, 32, 16):
        if scenarios % size == 0:
            return size
    return scenarios


LANES = 128
SUBLANES = 8
GROUP = 16


def to_tiles(hist):
    scenarios, rows, columns = hist.shape
    high = min(rows, SUBLANES)
    tiles = hist.reshape(scenarios, rows // high, high, columns // LANES, LANES)
    return tiles.transpose(0, 1, 3, 2, 4).reshape(scenarios * rows * (columns // LANES), LANES)


def from_tiles(tiles, shape):
    scenarios, rows, columns = shape
    high = min(rows, SUBLANES)
    parts = tiles.reshape(scenarios, rows // high, columns // LANES, high, LANES)
    return parts.transpose(0, 1, 3, 2, 4).reshape(shape)


def tile_offset(row, lane_tile, rows, lane_tiles):
    high = min(rows, SUBLANES)
    return (row // high * lane_tiles + lane_tile) * high + row % high


def read_row(ref, first_scenario, count, row, rows, columns):
    lane_tiles = columns // LANES
    per = rows * lane_tiles
    return jnp.concatenate(
        [
            ref[pl.ds(first_scenario * per + tile_offset(row, t, rows, lane_tiles), count, stride=per), :]
            for t in range(lane_tiles)
        ],
        axis=1,
    )


def write_row(ref, first_scenario, count, row, rows, columns, values):
    lane_tiles = columns // LANES
    per = rows * lane_tiles
    for t in range(lane_tiles):
        place = pl.ds(first_scenario * per + tile_offset(row, t, rows, lane_tiles), count, stride=per)
        ref[place, :] = values[:, t * LANES : (t + 1) * LANES]


def drift_tail(drift_ref, start):
    pieces = [
        jnp.concatenate([drift_ref[c, start : start + 1], drift_ref[c, start + 1 : start + 2]], axis=1)
        for c in range(2)
    ]
    high, low = two_halves(jnp.concatenate(pieces, axis=0))
    ones = jnp.ones((1, high.shape[1]), bf16)
    zeros = jnp.zeros((EXTRA - 5, high.shape[1]), bf16)
    return jnp.concatenate([high, low, ones, zeros], axis=0)


def band_matrix(columns):
    row = lax.broadcasted_iota(jnp.int32, (columns, columns), 0)
    column = lax.broadcasted_iota(jnp.int32, (columns, columns), 1)
    right = jnp.where(column == row + 1, 1.0, 0.0)
    left = jnp.where(column == row - 1, 1.0, 0.0)
    centre = jnp.where(column == row, 1.0 - 4.0 * diffusion_rate, diffusion_rate * (right + left))
    return centre.astype(bf16), (right - left).astype(bf16)


def half_shifts(levels_ref, table_ref, shift_ref):
    scenarios = levels_ref.shape[1]
    for t in range(levels_ref.shape[0]):
        level = jnp.broadcast_to(levels_ref[t : t + 1, :].astype(f32), (LANES, scenarios)).T
        for c in range(2):
            shift = jnp.zeros(level.shape, f32)
            for n in range(table_ref.shape[1]):
                shift = jnp.where(level == n, 0.5 * table_ref[c : c + 1, n : n + 1], shift)
            shift_ref[2 * t + c] = shift


def wide(values, columns):
    return jnp.concatenate([values] * (columns // LANES), axis=1)


def one_step(rows_of, places, half_drift, band, shift_x, shift_y, pairs, terms, write):
    size, columns = shift_x.shape
    whole = pl.ds(0, columns)

    def density(row):
        return pairs[pl.ds(rows_of[row] * size, size), whole].astype(f32)

    for row in places:
        flux = (half_drift(1, row) + shift_y) * density(row)
        pairs[pl.ds(rows_of[row] * size, size), pl.ds(columns, columns)] = flux.astype(bf16)
    start = rows_of[places[0]] * size
    count = (rows_of[places[-1]] + 1) * size - start
    terms[pl.ds(start, count), :] = jnp.dot(pairs[pl.ds(start, count), :], band, preferred_element_type=f32)
    for row in places:
        low = density(row - 1) * ((diffusion_rate + half_drift(0, row - 1)) + shift_x)
        high = density(row + 1) * ((diffusion_rate - half_drift(0, row + 1)) - shift_x)
        write(row, terms[pl.ds(rows_of[row] * size, size), :] + low + high)


def two_steps(segments, read, half_drift, edge, band, shifts, scratch, write):
    pairs, later, terms = scratch
    size, columns = shifts[0].shape
    before, between, after = [
        [row for first, last in segments for row in range(first - more, last + more + 1)] for more in (2, 1, 0)
    ]
    rows_of = {row: k for k, row in enumerate(before)}
    for row, k in rows_of.items():
        pairs[pl.ds(k * size, size), pl.ds(0, columns)] = read(row)

    def write_later(row, density):
        later[pl.ds(rows_of[row] * size, size), pl.ds(0, columns)] = edge(row, density).astype(bf16)

    one_step(rows_of, between, half_drift, band, shifts[0], shifts[1], pairs, terms, write_later)
    one_step(rows_of, after, half_drift, band, shifts[2], shifts[3], later, terms, write)


def step_scratch(segments, size, columns):
    rows = sum(last - first + 5 for first, last in segments)
    pairs = pltpu.VMEM((rows * size, 2 * columns), bf16)
    return [pairs, pairs, pltpu.VMEM((rows * size, columns), f32)]


def edge_segments(rows):
    return [(0, 1), (rows - 2, rows - 1)] if rows >= 8 else [(0, rows - 1)]


def inner_kernel(
    rows, size, hist_ref, drift_hbm, levels_hbm, table_hbm, cot_hbm,
    first_ref, last_ref, shift_ref, band_ref, cot_ref, rows_ref, inner_ref,
    drift_ref, levels_ref, table_ref, cot_row, arrived, all_shifts, *scratch,
):
    step = pl.program_id(0)
    columns = drift_ref.shape[2]

    @pl.when(step == 0)
    def _():
        sources = ((drift_hbm, drift_ref), (levels_hbm, levels_ref), (table_hbm, table_ref), (cot_hbm, cot_row))
        copies = [pltpu.make_async_copy(*pair, arrived.at[n]) for n, pair in enumerate(sources)]
        for copy in copies:
            copy.start()
        centre, flux = band_matrix(columns)
        band_ref[pl.ds(0, columns), :] = centre
        band_ref[pl.ds(columns, columns), :] = flux
        for copy in copies:
            copy.wait()
        half_shifts(levels_ref, table_ref, all_shifts)
        cot_ref[...] = jnp.broadcast_to(cot_row[...].reshape(1, -1), (LANES, cot_row.shape[0])).T
        for out, start in ((first_ref, 0), (last_ref, rows - 2)):
            out[pl.ds(out.shape[0] - EXTRA, EXTRA), :] = drift_tail(drift_ref, start)

    where = pl.ds(pl.multiple_of(step * size, size), size)
    for n in range(4):
        shift_ref[n] = all_shifts[n, where, :]
    for row in range(rows):
        density = read_row(hist_ref, 0, size, row, rows, columns).astype(bf16)
        rows_ref[:, pl.ds(row * columns, columns)] = density
        if row < 2:
            first_ref[where, pl.ds(row * columns, columns)] = density
        if row >= rows - 2:
            last_ref[where, pl.ds((row - rows + 2) * columns, columns)] = density
    if rows <= 4:
        return

    def write(row, density):
        inner_ref[:, pl.ds((row - 2) * columns, columns)] = density.astype(bf16)

    two_steps(
        [(2, rows - 3)],
        lambda row: rows_ref[:, pl.ds(row * columns, columns)],
        lambda c, row: 0.5 * drift_ref[c, row : row + 1, :],
        lambda row, density: density,
        band_ref[...],
        [wide(shift_ref[n], columns) for n in range(4)],
        scratch,
        write,
    )


def inner_steps(tiles, drift, levels, table, cot):
    scenarios = levels.shape[1]
    rows, columns = drift.shape[1:]
    per = tiles.shape[0] // scenarios
    size = scenario_block(scenarios)
    inner = max(rows - 4, 1) * columns
    sent = jax.ShapeDtypeStruct((scenarios + EXTRA, 2 * columns), bf16)
    shifts = jax.ShapeDtypeStruct((4, scenarios, LANES), f32)
    band = jax.ShapeDtypeStruct((2 * columns, columns), bf16)
    return pl.pallas_call(
        functools.partial(inner_kernel, rows, size),
        grid=(scenarios // size,),
        in_specs=[pl.BlockSpec((size * per, LANES), lambda i: (i, 0))] + [pl.BlockSpec(memory_space=pltpu.HBM)] * 4,
        out_specs=[pl.BlockSpec(sent.shape, lambda i: (0, 0))] * 2
        + [
            pl.BlockSpec((4, size, LANES), lambda i: (0, i, 0)),
            pl.BlockSpec(band.shape, lambda i: (0, 0)),
            pl.BlockSpec((scenarios, LANES), lambda i: (0, 0)),
            pl.BlockSpec((size, rows * columns), lambda i: (i, 0)),
            pl.BlockSpec((size, inner), lambda i: (i, 0)),
        ],
        out_shape=[
            sent,
            sent,
            pltpu.HBM(shifts.shape, f32),
            band,
            jax.ShapeDtypeStruct((scenarios, LANES), f32),
            pltpu.HBM((scenarios, rows * columns), bf16),
            jax.ShapeDtypeStruct((scenarios, inner), bf16),
        ],
        scratch_shapes=[
            pltpu.VMEM(drift.shape, f32),
            pltpu.VMEM(levels.shape, levels.dtype),
            pltpu.VMEM(table.shape, f32),
            pltpu.VMEM(cot.shape, f32),
            pltpu.SemaphoreType.DMA((4,)),
            pltpu.VMEM(shifts.shape, f32),
        ]
        + step_scratch([(2, max(rows - 3, 2))], size, columns),
        compiler_params=params(),
        cost_estimate=pl.CostEstimate(flops=1, bytes_accessed=1, transcendentals=0),
        name="inner_density_steps",
    )(tiles, drift, levels, table, cot)


def halo_drift(ref, columns):
    tail = ref[...].astype(f32)
    both = 0.5 * (tail[0:2] + tail[2:4])
    rows = [[both[c : c + 1, k * columns : (k + 1) * columns] for k in range(2)] for c in range(2)]
    return rows, tail[4:5, :columns]


def with_halo(drift_ref, below_tail, above_tail):
    rows, columns = drift_ref.shape[1:]
    below, below_valid = halo_drift(below_tail, columns)
    above, above_valid = halo_drift(above_tail, columns)

    def half_drift(c, row):
        if row < 0:
            return below[c][row + 2]
        if row >= rows:
            return above[c][row - rows]
        return 0.5 * drift_ref[c, row : row + 1, :]

    def edge(row, density):
        if row < 0:
            return density * below_valid
        if row >= rows:
            return density * above_valid
        return density

    return half_drift, edge


def density_kernel(segments, drift_ref, shift_ref, band_ref, rows_ref, below_ref, above_ref, below_tail, above_tail, dep_ref, *refs):
    scratch = refs[-3:]
    rows, columns = drift_ref.shape[1:]
    size = shift_ref.shape[1]
    half_drift, edge = with_halo(drift_ref, below_tail, above_tail)

    def read(row):
        if row < 0:
            return below_ref[:, pl.ds((row + 2) * columns, columns)]
        if row >= rows:
            return above_ref[:, pl.ds((row - rows) * columns, columns)]
        return rows_ref[:, pl.ds(row * columns, columns)]

    if segments is None:
        next_ref, token_ref = refs[-5:-3]
        token_ref[...] = jnp.zeros(token_ref.shape, f32)

        def write(row, density):
            write_row(next_ref, 0, size, row, rows, columns, density)

    else:
        low_ref, high_ref = refs[-5:-3]

        def write(row, density):
            if row < 2:
                low_ref[:, pl.ds(row * columns, columns)] = density.astype(bf16)
            else:
                high_ref[:, pl.ds((row - rows + 2) * columns, columns)] = density.astype(bf16)

    shifts = [wide(shift_ref[n], columns) for n in range(4)]
    two_steps(segments or [(0, rows - 1)], read, half_drift, edge, band_ref[...], shifts, scratch, write)


def density_specs(drift, shifts, band, own, below, size, first):
    columns = drift.shape[2]
    scenarios = shifts.shape[1]
    halo = pl.BlockSpec((size, 2 * columns), lambda i: (first + i, 0))
    tail = pl.BlockSpec((EXTRA, 2 * columns), lambda i: (scenarios // EXTRA, 0))
    return [
        pl.BlockSpec(drift.shape, lambda i: (0, 0, 0)),
        pl.BlockSpec((4, size, LANES), lambda i: (0, first + i, 0)),
        pl.BlockSpec(band.shape, lambda i: (0, 0)),
        pl.BlockSpec((size, own.shape[1]), lambda i: (first + i, 0)),
        halo,
        halo,
        tail,
        tail,
        pl.BlockSpec(memory_space=pl.ANY),
    ]


def edge_steps(drift, shifts, band, own, below, above, dep):
    scenarios = shifts.shape[1]
    rows, columns = drift.shape[1:]
    size = 2 * scenario_block(scenarios)
    size = size if scenarios % size == 0 else size // 2
    edge = jax.ShapeDtypeStruct((scenarios, 2 * columns), bf16)
    spec = pl.BlockSpec((size, 2 * columns), lambda i: (i, 0))
    segments = edge_segments(rows)
    return pl.pallas_call(
        functools.partial(density_kernel, segments),
        grid=(scenarios // size,),
        in_specs=density_specs(drift, shifts, band, own, below, size, 0),
        out_specs=[spec, spec],
        out_shape=[edge, edge],
        scratch_shapes=step_scratch(segments, size, columns),
        compiler_params=params(),
        cost_estimate=pl.CostEstimate(flops=1, bytes_accessed=1, transcendentals=0),
        name="edge_density_steps",
    )(drift, shifts, band, own, below, above, below, above, dep)


def density_steps(drift, shifts, band, own, below, above, dep, so_far, turn, turns):
    scenarios = shifts.shape[1]
    rows, columns = drift.shape[1:]
    per = rows * (columns // LANES)
    size = 3 * GROUP if scenarios % (turns * GROUP * 3) == 0 else GROUP
    steps = scenarios // size // turns
    first = turn * steps
    args = [drift, shifts, band, own, below, above, below, above, dep]
    in_specs = density_specs(drift, shifts, band, own, below, size, first)
    aliases = {}
    if so_far is not None:
        aliases = {len(args): 0}
        args.append(so_far)
        in_specs.append(pl.BlockSpec(memory_space=pltpu.HBM))
    return pl.pallas_call(
        functools.partial(density_kernel, None),
        grid=(steps,),
        in_specs=in_specs,
        out_specs=[
            pl.BlockSpec((size * per, LANES), lambda i: (first + i, 0)),
            pl.BlockSpec((SUBLANES, LANES), lambda i: (0, 0)),
        ],
        out_shape=[pltpu.HBM((scenarios * per, LANES), f32), jax.ShapeDtypeStruct((SUBLANES, LANES), f32)],
        input_output_aliases=aliases,
        scratch_shapes=step_scratch([(0, rows - 1)], size, columns),
        compiler_params=params(),
        cost_estimate=pl.CostEstimate(flops=1, bytes_accessed=1, transcendentals=0),
        name="density_steps",
    )(*args)


def smem():
    return pl.BlockSpec(memory_space=pltpu.SMEM)


def vmem():
    return pl.BlockSpec(memory_space=pltpu.VMEM)


def swap(values, count, flip):
    return lax.ppermute(values, "grid", [(i, i ^ flip) for i in range(count)])


def inner_product_kernel(count, inputs_ref, *refs):
    weight = jnp.concatenate([ref[...] for ref in refs[:count]], axis=0)
    refs[-1][pl.program_id(0)] = jnp.dot(inputs_ref[...], weight, preferred_element_type=f32)


def inner_product(inner, weight, width, deps):
    scenarios, cells = inner.shape
    total, hidden = weight.shape
    size = (total - cells) // 2
    count = cells // size

    def spec(k):
        return pl.BlockSpec((size, width), lambda n: (1 + k, n))

    return pl.pallas_call(
        functools.partial(inner_product_kernel, count),
        grid=(hidden // width,),
        in_specs=[vmem()] + [spec(k) for k in range(count)] + any_specs(deps),
        out_specs=vmem(),
        out_shape=jax.ShapeDtypeStruct((hidden // width, scenarios, width), f32),
        compiler_params=params(),
        cost_estimate=pl.CostEstimate(flops=1, bytes_accessed=1, transcendentals=0),
        name="inner_product",
    )(inner, *([weight] * count), *deps)


def edge_product_kernel(block, with_inner, place_ref, low_ref, high_ref, top_ref, bottom_ref, *refs):
    keep_ref, send_ref, total = refs[-3:]
    step = pl.program_id(0)
    left = jnp.concatenate([low_ref[...], high_ref[...]], axis=1)
    weight = jnp.concatenate([top_ref[...], bottom_ref[...]], axis=0)
    product = jnp.dot(left, weight, preferred_element_type=f32)
    total[...] = product + refs[0][step] if with_inner else product
    core = place_ref[0]
    for out, half in ((keep_ref, core), (send_ref, 1 - core)):
        for side in range(2):
            start = pl.multiple_of((2 * half + side) * block, block)
            out[side, step] = total[pl.ds(start, block), :].astype(out.dtype)


def edge_product(place, low, high, weight, inner, parts, width):
    scenarios, size = low.shape
    block = scenarios // 4
    last = weight.shape[0] // size - 1
    shape = (2, parts, block, width)
    in_specs = [
        smem(),
        vmem(),
        vmem(),
        pl.BlockSpec((size, width), lambda n: (0, n)),
        pl.BlockSpec((size, width), lambda n: (last, n)),
    ]
    args = [place, low, high, weight, weight]
    if inner is not None:
        in_specs.append(vmem())
        args.append(inner)
    return pl.pallas_call(
        functools.partial(edge_product_kernel, block, inner is not None),
        grid=(parts,),
        in_specs=in_specs,
        out_specs=[vmem(), vmem()],
        out_shape=[jax.ShapeDtypeStruct(shape, f32), jax.ShapeDtypeStruct(shape, bf16)],
        scratch_shapes=[pltpu.VMEM((scenarios, width), f32)],
        compiler_params=params(),
        cost_estimate=pl.CostEstimate(flops=1, bytes_accessed=1, transcendentals=0),
        name="edge_product",
    )(*args)


def any_specs(deps):
    return [pl.BlockSpec(memory_space=pl.ANY)] * len(deps)


def other_places(parts):
    return [(side, part) for side in range(2) for part in range(parts) if side or part]


def add_core_kernel(place_ref, mine_ref, other_ref, own_ref, *send_refs):
    side, part = place_ref[1], place_ref[2]
    own_ref[...] = mine_ref[side, part] + other_ref[side, part].astype(f32)
    for (by_side, by_part), out in zip(other_places(mine_ref.shape[1]), send_refs):
        at = side ^ by_side, part ^ by_part
        out[...] = (mine_ref[at] + other_ref[at].astype(f32)).astype(bf16)


def add_core(place, mine, other):
    parts, *piece = mine.shape[1:]
    return pl.pallas_call(
        add_core_kernel,
        in_specs=[smem(), vmem(), vmem()],
        out_shape=[jax.ShapeDtypeStruct(piece, f32)] + [jax.ShapeDtypeStruct(piece, bf16)] * (2 * parts - 1),
        compiler_params=params(),
        cost_estimate=pl.CostEstimate(flops=1, bytes_accessed=1, transcendentals=0),
        name="add_core",
    )(place, mine, other)


def activate_kernel(count, *refs):
    total = refs[0][...]
    for ref in refs[1 : 1 + count]:
        total = total + ref[...].astype(f32)
    refs[-1][...] = jnp.tanh(total).astype(bf16)


def activate(own, received, deps=()):
    return pl.pallas_call(
        functools.partial(activate_kernel, len(received)),
        in_specs=[vmem()] * (1 + len(received)) + any_specs(deps),
        out_shape=jax.ShapeDtypeStruct(own.shape, bf16),
        compiler_params=params(),
        cost_estimate=pl.CostEstimate(flops=1, bytes_accessed=1, transcendentals=0),
        name="first_activation",
    )(own, *received, *deps)


def pack_kernel(place_ref, mid_ref, head_ref, first_ref, out_ref, place_out_ref, head_row, arrived):
    for n in range(4):
        place_out_ref[n] = place_ref[n]
    hidden = mid_ref.shape[0]
    copies = [
        pltpu.make_async_copy(mid_ref, out_ref.at[pl.ds(0, hidden), :], arrived.at[0]),
        pltpu.make_async_copy(head_ref, head_row, arrived.at[1]),
    ]
    for copy in copies:
        copy.start()
    copies[1].wait()
    out_ref[pl.ds(hidden, EXTRA), :] = tail_rows(head_row[...])
    copies[0].wait()


def pack(place, mid_weight, head, first):
    hidden, units = mid_weight.shape
    return pl.pallas_call(
        pack_kernel,
        in_specs=[smem()] + [pl.BlockSpec(memory_space=pltpu.HBM)] * 3,
        out_specs=[vmem(), smem()],
        out_shape=[jax.ShapeDtypeStruct((hidden + EXTRA, units), bf16), jax.ShapeDtypeStruct(place.shape, place.dtype)],
        scratch_shapes=[pltpu.VMEM(head.shape, f32), pltpu.SemaphoreType.DMA((2,))],
        compiler_params=params(),
        cost_estimate=pl.CostEstimate(flops=1, bytes_accessed=1, transcendentals=0),
        name="mid_with_head",
    )(place, *[pltpu.with_memory_space_constraint(array, pltpu.HBM) for array in (mid_weight, head)], first)


def two_halves(exact):
    high = exact.astype(bf16)
    low = (exact - high.astype(f32)).astype(bf16)
    return high, low


def tail_rows(exact):
    high, low = two_halves(exact)
    zeros = jnp.zeros((EXTRA - 2, exact.shape[1]), bf16)
    return jnp.concatenate([high, low, zeros], axis=0)


def middle_kernel(chunks, parts, width, *refs):
    pieces = chunks * parts
    place_ref, cot_ref = refs[0], refs[1]
    first_refs = refs[2 : 2 + pieces]
    mid_refs = refs[2 + pieces : 6 + pieces]
    outs = refs[-(3 + parts) :]
    own_ref, value_ref, mid_keep_ref, mid_send_ref = outs[:4]
    send_refs = outs[4:]
    part = place_ref[2]
    block = first_refs[0].shape[0]

    def mid_rows(start):
        return jnp.concatenate([ref[pl.ds(start, width), :] for ref in mid_refs], axis=1)

    def start_of(c, k):
        return pl.multiple_of((c * parts + (part ^ k)) * width, width)

    total = None
    for c in range(chunks):
        for k in range(parts):
            term = jnp.dot(first_refs[c * parts + k][...], mid_rows(start_of(c, k)), preferred_element_type=f32)
            total = term if total is None else total + term
    second_low = jnp.tanh(total).astype(bf16)
    second = second_low.astype(f32)
    heads = jnp.concatenate([ref[pl.ds(pieces * width, EXTRA), :] for ref in mid_refs], axis=1)
    head = heads[0:1].astype(f32) + heads[1:2].astype(f32)
    rows = lax.dot_general(heads, second_low, (((1,), (1,)), ((), ())), preferred_element_type=f32)
    value = rows[0:1] + rows[1:2]
    if width > block:
        value = jnp.concatenate([value, jnp.zeros((1, width - block), f32)], axis=1)
    value_ref[...] = value
    cot = cot_ref[pl.ds(pl.multiple_of(place_ref[3] * block, SUBLANES), block), :1]
    head_part = jnp.sum(cot * second, axis=0, keepdims=True)
    back = (cot * head * (1.0 - second * second)).astype(bf16)
    units = mid_refs[0].shape[1]
    for k in range(parts):
        for c in range(chunks):
            piece = lax.dot_general(
                back, mid_rows(start_of(c, k)), (((1,), (1,)), ((), ())), preferred_element_type=f32
            )
            if k == 0:
                own_ref[pl.ds(c * block, block), :] = piece
            else:
                send_refs[k - 1][pl.ds(c * block, block), :] = piece.astype(bf16)
        if k > 0:
            send_refs[k - 1][pl.ds(chunks * block, EXTRA), :] = tail_rows(value)
    for c in range(chunks):
        for k in range(parts):
            product = lax.dot_general(
                first_refs[c * parts + k][...], back, (((0,), (0,)), ((), ())), preferred_element_type=f32
            ).astype(bf16)
            for p in range(4):
                out = (mid_keep_ref, mid_send_ref)[p % 2]
                out[p // 2, pl.ds(start_of(c, k), width), :] = product[:, p * units : (p + 1) * units]
    for p in range(4):
        out = (mid_keep_ref, mid_send_ref)[p % 2]
        out[p // 2, pl.ds(pieces * width, EXTRA), :] = tail_rows(head_part[:, p * units : (p + 1) * units])


def middle(place, cot, firsts, mids, chunks, parts, width, deps=()):
    block = firsts[0].shape[0]
    partial = jax.ShapeDtypeStruct((2, *mids[0].shape), bf16)
    return pl.pallas_call(
        functools.partial(middle_kernel, chunks, parts, width),
        in_specs=[smem()] + [vmem()] * (1 + len(firsts) + 4) + any_specs(deps),
        out_shape=[
            jax.ShapeDtypeStruct((chunks * block, width), f32),
            jax.ShapeDtypeStruct((1, width), f32),
            partial,
            partial,
        ]
        + [jax.ShapeDtypeStruct((chunks * block + EXTRA, width), bf16)] * (parts - 1),
        compiler_params=params(),
        cost_estimate=pl.CostEstimate(flops=1, bytes_accessed=1, transcendentals=0),
        name="value_layers",
    )(place, cot, *firsts, *mids, *deps)


def add_tail(left, right, hidden):
    body = left[:hidden].astype(f32) + right[:hidden].astype(f32)
    tails = left[hidden:].astype(f32) + right[hidden:].astype(f32)
    return body.astype(bf16), tails[0:1] + tails[1:2]


def mid_add_kernel(keep_ref, other_ref, *refs):
    own_ref, send_ref = refs[-2:]
    hidden = own_ref.shape[0] - EXTRA
    for at, out in enumerate((own_ref, send_ref)):
        body, tail = add_tail(keep_ref[at], other_ref[at], hidden)
        out[pl.ds(0, hidden), :] = body
        out[pl.ds(hidden, EXTRA), :] = tail_rows(tail)


def mid_add(keep, other, deps=()):
    shape = jax.ShapeDtypeStruct(keep.shape[1:], bf16)
    return pl.pallas_call(
        mid_add_kernel,
        in_specs=[vmem()] * 2 + any_specs(deps),
        out_shape=[shape, shape],
        compiler_params=params(),
        cost_estimate=pl.CostEstimate(flops=1, bytes_accessed=1, transcendentals=0),
        name="mid_gradient_add",
    )(keep, other, *deps)


def mid_final_kernel(own_ref, other_ref, *refs):
    out_ref, head_ref, token_ref = refs[-3:]
    token_ref[...] = jnp.zeros(token_ref.shape, f32)
    body, tail = add_tail(own_ref[...], other_ref[...], out_ref.shape[0])
    out_ref[...] = body
    head_ref[...] = tail


def mid_final(own, other, deps=()):
    hidden = own.shape[0] - EXTRA
    return pl.pallas_call(
        mid_final_kernel,
        in_specs=[vmem()] * 2 + any_specs(deps),
        out_shape=[
            jax.ShapeDtypeStruct((hidden, own.shape[1]), bf16),
            jax.ShapeDtypeStruct((1, own.shape[1]), f32),
            jax.ShapeDtypeStruct((SUBLANES, LANES), f32),
        ],
        compiler_params=params(),
        cost_estimate=pl.CostEstimate(flops=1, bytes_accessed=1, transcendentals=0),
        name="mid_gradient_final",
    )(own, other, *deps)


def back_first_kernel(count, own_ref, value_ref, *refs):
    received = refs[:count]
    first_ref, out_ref, with_tail_ref = refs[count:]
    block = first_ref.shape[0]
    value = value_ref[...]
    total = own_ref[...]
    for ref in received:
        tail = ref[pl.ds(block, EXTRA), :].astype(f32)
        value = value + (tail[0:1] + tail[1:2])
        total = total + ref[pl.ds(0, block), :].astype(f32)
    first = first_ref[...].astype(f32)
    back = (total * (1.0 - first * first)).astype(bf16)
    out_ref[...] = back
    with_tail_ref[pl.ds(0, block), :] = back
    with_tail_ref[pl.ds(block, EXTRA), :] = tail_rows(value)


def back_first(own, value, received, first):
    block, width = first.shape
    return pl.pallas_call(
        functools.partial(back_first_kernel, len(received)),
        in_specs=[vmem()] * (3 + len(received)),
        out_shape=[jax.ShapeDtypeStruct((rows, width), bf16) for rows in (block, block + EXTRA)],
        compiler_params=params(),
        cost_estimate=pl.CostEstimate(flops=1, bytes_accessed=1, transcendentals=0),
        name="back_first",
    )(own, value, *received, first)


def stack_kernel(count, *refs):
    out_ref = refs[-1]
    block = refs[0].shape[0] - EXTRA
    parts = count // 2
    at = 0
    for side in range(2):
        section = refs[side * parts : (side + 1) * parts]
        for ref in section:
            out_ref[pl.ds(at, block), :] = ref[pl.ds(0, block), :]
            at += block
        out_ref[pl.ds(at, EXTRA), :] = section[0][pl.ds(block, EXTRA), :]
        at += EXTRA


def stack(pieces, deps):
    rows = sum(piece.shape[0] for piece in pieces)
    return pl.pallas_call(
        functools.partial(stack_kernel, len(pieces)),
        in_specs=[vmem()] * len(pieces) + any_specs(deps),
        out_shape=jax.ShapeDtypeStruct((rows, pieces[0].shape[1]), bf16),
        compiler_params=params(),
        cost_estimate=pl.CostEstimate(flops=1, bytes_accessed=1, transcendentals=0),
        name="stack_parts",
    )(*pieces, *deps)


def turn_kernel(count, *refs):
    for ref, out in zip(refs[:count], refs[-count:]):
        out[...] = ref[...].T


def transposed(arrays, deps):
    return pl.pallas_call(
        functools.partial(turn_kernel, len(arrays)),
        in_specs=[vmem()] * len(arrays) + any_specs(deps),
        out_shape=[jax.ShapeDtypeStruct(array.shape[::-1], array.dtype) for array in arrays],
        compiler_params=params(),
        cost_estimate=pl.CostEstimate(flops=1, bytes_accessed=1, transcendentals=0),
        name="transposed_inputs",
    )(*arrays, *deps)


def first_grad_kernel(parts, block, count, *refs):
    place_ref = refs[0]
    lefts = refs[1 : 1 + count]
    stacks = refs[1 + count : 3 + count]
    out_ref, value_ref, whole = refs[-3:]
    piece = pl.program_id(0) ^ place_ref[2]
    mine = place_ref[3]
    values = [jnp.zeros((1, block), f32)] * 4
    for by_core in range(2):
        for by_side in range(2):
            ref = stacks[by_core]
            start = by_side * (parts * block + EXTRA)
            at = mine ^ (2 * by_core + by_side)
            whole[pl.ds(pl.multiple_of(at * block, block), block), :] = ref[
                pl.ds(pl.multiple_of(start + piece * block, EXTRA), block), :
            ]
            tail = ref[pl.ds(start + parts * block, EXTRA), :block].astype(f32)
            value = tail[0:1] + tail[1:2]
            for q in range(4):
                values[q] = jnp.where(at == q, value, values[q])
    value_ref[...] = jnp.concatenate(values, axis=1)
    start = 0
    for ref in lefts:
        cells = ref.shape[0]
        out_ref[pl.ds(start, cells), :] = jnp.dot(ref[...], whole[...], preferred_element_type=f32).astype(bf16)
        start += cells


def first_grad(place, lefts, stacks, parts, block, deps):
    scenarios = lefts[0].shape[1]
    cells = sum(left.shape[0] for left in lefts)
    width = stacks[0].shape[1]
    return pl.pallas_call(
        functools.partial(first_grad_kernel, parts, block, len(lefts)),
        grid=(parts,),
        in_specs=[smem()] + [vmem()] * (len(lefts) + 2) + any_specs(deps),
        out_specs=[pl.BlockSpec((cells, width), lambda i: (0, i)), pl.BlockSpec((1, scenarios), lambda i: (0, 0))],
        out_shape=[pltpu.HBM((cells, parts * width), bf16), jax.ShapeDtypeStruct((1, scenarios), f32)],
        scratch_shapes=[pltpu.VMEM((scenarios, width), bf16)],
        compiler_params=params(),
        cost_estimate=pl.CostEstimate(flops=1, bytes_accessed=1, transcendentals=0),
        name="first_gradient",
    )(place, *lefts, *stacks, *deps)


def local(hist, drift, shocks, shock_table, first_weight, mid_weight, head_weight, cotangent):
    scenarios, rows, columns = hist.shape
    count = lax.axis_size("grid")
    hidden = first_weight.shape[1]
    units = mid_weight.shape[1]
    parts = count // 4
    width = hidden // parts
    block = scenarios // 4
    index = lax.axis_index("grid")
    core, side, part = index & 1, (index >> 1) & 1, index >> 2
    mine = 2 * core + side
    tiles = pltpu.with_memory_space_constraint(to_tiles(hist), pltpu.HBM)

    place = jnp.stack([core, side, part, mine])

    small = [pltpu.with_memory_space_constraint(array, pltpu.HBM) for array in (drift, shocks.T, shock_table.T, cotangent)]
    packed, place = pack(place, mid_weight, head_weight[None, :], small[-1])
    mids = [packed]
    mids += [swap(mids[0], count, 1), swap(mids[0], count, 2)]
    first_rows, last_rows, shifts, band, cot, own_rows, inner = inner_steps(tiles, *small)
    inner = inner if rows > 4 else None
    forward = [(i, i + 1) for i in range(count - 1)]
    backward = [(i + 1, i) for i in range(count - 1)]
    below = lax.ppermute(last_rows, "grid", forward)
    above = lax.ppermute(first_rows, "grid", backward)
    first_weight = pltpu.with_memory_space_constraint(first_weight, pltpu.HBM)
    product = None if inner is None else inner_product(inner, first_weight, width, mids[1:])
    low, high = edge_steps(drift, shifts, band, own_rows, below, above, own_rows if product is None else product)
    mids.append(swap(mids[2], count, 1))

    def density_turn(turn, dep, so_far):
        return density_steps(drift, shifts, band, own_rows, below, above, dep, so_far, turn, 2)

    keep, send = edge_product(place, low, high, first_weight, product, parts, width)
    own, *sends = add_core(place, keep, swap(send, count, 1))
    flips = [2 * by_side + 4 * by_part for by_side, by_part in other_places(parts)]
    received = [swap(piece, count, flip) for piece, flip in zip(sends, flips)]
    density, token = density_turn(0, sends[-1], None)
    first = activate(own, received, [token])
    firsts = [first] + [swap(first, count, 4 * k) for k in range(1, parts)]
    density, token = density_turn(1, first, density)
    own, value, mid_keep, mid_send, *sends = middle(place, cot, firsts, mids, 1, parts, width, [token, mids[1], mids[3]])
    received = [swap(piece, count, 4 * (k + 1)) for k, piece in enumerate(sends)]
    back, with_tail = back_first(own, value, received, first)
    mid_keep, mid_send = mid_add(mid_keep, swap(mid_send, count, 1), [back])
    lefts = transposed([low, high] if inner is None else [low, inner, high], [back])
    grad_mid, grad_head, token = mid_final(mid_keep, swap(mid_send, count, 2))
    pieces = [with_tail] + [swap(with_tail if flip == 2 else back, count, flip) for flip in flips]
    own_stack = stack(pieces, [lefts[0]])
    grad_first, value = first_grad(place, lefts, [own_stack, swap(own_stack, count, 1)], parts, block, [token])
    value = value.reshape(scenarios)
    return from_tiles(density, hist.shape), value, grad_first, grad_mid, grad_head[0]


def solution(mesh):
    in_specs = (
        P("groups", "grid", None),
        P(None, "grid", None),
        P("groups", None),
        P("groups", None),
        P(("groups", "grid"), None),
        P("groups", "grid"),
        P(("groups", "grid")),
        P("groups"),
    )
    out_specs = (
        P("groups", "grid", None),
        P("groups"),
        P(("groups", "grid"), None),
        P("groups", "grid"),
        P(("groups", "grid")),
    )
    return jax.shard_map(local, mesh=mesh, in_specs=in_specs, out_specs=out_specs, check_vma=False)
```

```python
import functools
import jax
import jax.numpy as jnp
from jax import lax
from jax.experimental import pallas as pl
from jax.experimental.pallas import tpu as pltpu
from jax.sharding import PartitionSpec as P

diffusion_rate = 0.24
VMEM_BYTES = 24 * 1024 * 1024
EXTRA = 16
bf16 = jnp.bfloat16
f32 = jnp.float32


def params():
    return pltpu.CompilerParams(vmem_limit_bytes=VMEM_BYTES)


def scenario_block(scenarios):
    for size in (64, 32, 16):
        if scenarios % size == 0:
            return size
    return scenarios


LANES = 128
SUBLANES = 8
GROUP = 16


def to_tiles(hist):
    scenarios, rows, columns = hist.shape
    high = min(rows, SUBLANES)
    tiles = hist.reshape(scenarios, rows // high, high, columns // LANES, LANES)
    return tiles.transpose(0, 1, 3, 2, 4).reshape(scenarios * rows * (columns // LANES), LANES)


def from_tiles(tiles, shape):
    scenarios, rows, columns = shape
    high = min(rows, SUBLANES)
    parts = tiles.reshape(scenarios, rows // high, columns // LANES, high, LANES)
    return parts.transpose(0, 1, 3, 2, 4).reshape(shape)


def tile_offset(row, lane_tile, rows, lane_tiles):
    high = min(rows, SUBLANES)
    return (row // high * lane_tiles + lane_tile) * high + row % high


def read_row(ref, first_scenario, count, row, rows, columns):
    lane_tiles = columns // LANES
    per = rows * lane_tiles
    return jnp.concatenate(
        [
            ref[pl.ds(first_scenario * per + tile_offset(row, t, rows, lane_tiles), count, stride=per), :]
            for t in range(lane_tiles)
        ],
        axis=1,
    )


def write_row(ref, first_scenario, count, row, rows, columns, values):
    lane_tiles = columns // LANES
    per = rows * lane_tiles
    for t in range(lane_tiles):
        place = pl.ds(first_scenario * per + tile_offset(row, t, rows, lane_tiles), count, stride=per)
        ref[place, :] = values[:, t * LANES : (t + 1) * LANES]


def drift_tail(drift_ref, start):
    pieces = [
        jnp.concatenate([drift_ref[c, start : start + 1], drift_ref[c, start + 1 : start + 2]], axis=1)
        for c in range(2)
    ]
    high, low = two_halves(jnp.concatenate(pieces, axis=0))
    ones = jnp.ones((1, high.shape[1]), bf16)
    zeros = jnp.zeros((EXTRA - 5, high.shape[1]), bf16)
    return jnp.concatenate([high, low, ones, zeros], axis=0)


def band_matrix(columns):
    row = lax.broadcasted_iota(jnp.int32, (columns, columns), 0)
    column = lax.broadcasted_iota(jnp.int32, (columns, columns), 1)
    right = jnp.where(column == row + 1, 1.0, 0.0)
    left = jnp.where(column == row - 1, 1.0, 0.0)
    centre = jnp.where(column == row, 1.0 - 4.0 * diffusion_rate, diffusion_rate * (right + left))
    return centre.astype(bf16), (right - left).astype(bf16)


def half_shifts(levels_ref, table_ref, shift_ref):
    scenarios = levels_ref.shape[1]
    for t in range(levels_ref.shape[0]):
        level = jnp.broadcast_to(levels_ref[t : t + 1, :].astype(f32), (LANES, scenarios)).T
        for c in range(2):
            shift = jnp.zeros(level.shape, f32)
            for n in range(table_ref.shape[1]):
                shift = jnp.where(level == n, 0.5 * table_ref[c : c + 1, n : n + 1], shift)
            shift_ref[2 * t + c] = shift


def wide(values, columns):
    return jnp.concatenate([values] * (columns // LANES), axis=1)


def one_step(rows_of, places, half_drift, band, shift_x, shift_y, pairs, terms, write):
    size, columns = shift_x.shape
    whole = pl.ds(0, columns)

    def density(row):
        return pairs[pl.ds(rows_of[row] * size, size), whole].astype(f32)

    for row in places:
        flux = (half_drift(1, row) + shift_y) * density(row)
        pairs[pl.ds(rows_of[row] * size, size), pl.ds(columns, columns)] = flux.astype(bf16)
    yield
    start = rows_of[places[0]] * size
    count = (rows_of[places[-1]] + 1) * size - start
    terms[pl.ds(start, count), :] = jnp.dot(pairs[pl.ds(start, count), :], band, preferred_element_type=f32)
    yield
    for row in places:
        low = density(row - 1) * ((diffusion_rate + half_drift(0, row - 1)) + shift_x)
        high = density(row + 1) * ((diffusion_rate - half_drift(0, row + 1)) - shift_x)
        write(row, terms[pl.ds(rows_of[row] * size, size), :] + low + high)


def step_stages(segments, read, half_drift, edge, band, shifts, scratch, write):
    pairs, later, terms = scratch
    size, columns = shifts[0].shape
    before, between, after = [
        [row for first, last in segments for row in range(first - more, last + more + 1)] for more in (2, 1, 0)
    ]
    rows_of = {row: k for k, row in enumerate(before)}
    for row, k in rows_of.items():
        pairs[pl.ds(k * size, size), pl.ds(0, columns)] = read(row)

    def write_later(row, density):
        later[pl.ds(rows_of[row] * size, size), pl.ds(0, columns)] = edge(row, density).astype(bf16)

    yield from one_step(rows_of, between, half_drift, band, shifts[0], shifts[1], pairs, terms, write_later)
    yield from one_step(rows_of, after, half_drift, band, shifts[2], shifts[3], later, terms, write)


def interleave(runs):
    ahead, live = list(runs), []
    while ahead or live:
        if ahead:
            live.append(ahead.pop(0))
        for run in list(live):
            if next(run, live) is live:
                live.remove(run)


def two_steps(*args):
    interleave([step_stages(*args)])


def step_scratch(segments, size, columns):
    rows = sum(last - first + 5 for first, last in segments)
    pairs = pltpu.VMEM((rows * size, 2 * columns), bf16)
    return [pairs, pairs, pltpu.VMEM((rows * size, columns), f32)]


def edge_segments(rows):
    return [(0, 1), (rows - 2, rows - 1)] if rows >= 8 else [(0, rows - 1)]


def inner_kernel(
    rows, size, hist_ref, drift_hbm, levels_hbm, table_hbm, cot_hbm,
    first_ref, last_ref, shift_ref, band_ref, cot_ref, rows_ref, inner_ref,
    drift_ref, levels_ref, table_ref, cot_row, arrived, all_shifts, *scratch,
):
    step = pl.program_id(0)
    columns = drift_ref.shape[2]

    @pl.when(step == 0)
    def _():
        sources = ((drift_hbm, drift_ref), (levels_hbm, levels_ref), (table_hbm, table_ref), (cot_hbm, cot_row))
        copies = [pltpu.make_async_copy(*pair, arrived.at[n]) for n, pair in enumerate(sources)]
        for copy in copies:
            copy.start()
        centre, flux = band_matrix(columns)
        band_ref[pl.ds(0, columns), :] = centre
        band_ref[pl.ds(columns, columns), :] = flux
        for copy in copies:
            copy.wait()
        half_shifts(levels_ref, table_ref, all_shifts)
        cot_ref[...] = jnp.broadcast_to(cot_row[...].reshape(1, -1), (LANES, cot_row.shape[0])).T
        for out, start in ((first_ref, 0), (last_ref, rows - 2)):
            out[pl.ds(out.shape[0] - EXTRA, EXTRA), :] = drift_tail(drift_ref, start)

    where = pl.ds(pl.multiple_of(step * size, size), size)
    for n in range(4):
        shift_ref[n] = all_shifts[n, where, :]
    for row in range(rows):
        density = read_row(hist_ref, 0, size, row, rows, columns).astype(bf16)
        rows_ref[:, pl.ds(row * columns, columns)] = density
        if row < 2:
            first_ref[where, pl.ds(row * columns, columns)] = density
        if row >= rows - 2:
            last_ref[where, pl.ds((row - rows + 2) * columns, columns)] = density
    if rows <= 4:
        return
    band = band_ref[...]
    count = len(scratch) // 3
    part = size // count

    def run(n):
        here = pl.ds(n * part, part)

        def write(row, density):
            inner_ref[here, pl.ds((row - 2) * columns, columns)] = density.astype(bf16)

        return step_stages(
            [(2, rows - 3)],
            lambda row: rows_ref[here, pl.ds(row * columns, columns)],
            lambda c, row: 0.5 * drift_ref[c, row : row + 1, :],
            lambda row, density: density,
            band,
            [wide(shift_ref[k, here, :], columns) for k in range(4)],
            scratch[3 * n : 3 * n + 3],
            write,
        )

    interleave([run(n) for n in range(count)])


def inner_steps(tiles, drift, levels, table, cot):
    scenarios = levels.shape[1]
    rows, columns = drift.shape[1:]
    per = tiles.shape[0] // scenarios
    size = scenario_block(scenarios)
    inner = max(rows - 4, 1) * columns
    sent = jax.ShapeDtypeStruct((scenarios + EXTRA, 2 * columns), bf16)
    shifts = jax.ShapeDtypeStruct((4, scenarios, LANES), f32)
    band = jax.ShapeDtypeStruct((2 * columns, columns), bf16)
    return pl.pallas_call(
        functools.partial(inner_kernel, rows, size),
        grid=(scenarios // size,),
        in_specs=[pl.BlockSpec((size * per, LANES), lambda i: (i, 0))] + [pl.BlockSpec(memory_space=pltpu.HBM)] * 4,
        out_specs=[pl.BlockSpec(sent.shape, lambda i: (0, 0))] * 2
        + [
            pl.BlockSpec((4, size, LANES), lambda i: (0, i, 0)),
            pl.BlockSpec(band.shape, lambda i: (0, 0)),
            pl.BlockSpec((scenarios, LANES), lambda i: (0, 0)),
            pl.BlockSpec((size, rows * columns), lambda i: (i, 0)),
            pl.BlockSpec((size, inner), lambda i: (i, 0)),
        ],
        out_shape=[
            sent,
            sent,
            pltpu.HBM(shifts.shape, f32),
            band,
            jax.ShapeDtypeStruct((scenarios, LANES), f32),
            pltpu.HBM((scenarios, rows * columns), bf16),
            jax.ShapeDtypeStruct((scenarios, inner), bf16),
        ],
        scratch_shapes=[
            pltpu.VMEM(drift.shape, f32),
            pltpu.VMEM(levels.shape, levels.dtype),
            pltpu.VMEM(table.shape, f32),
            pltpu.VMEM(cot.shape, f32),
            pltpu.SemaphoreType.DMA((4,)),
            pltpu.VMEM(shifts.shape, f32),
        ]
        + step_scratch([(2, max(rows - 3, 2))], size // 2, columns) * 2,
        compiler_params=params(),
        cost_estimate=pl.CostEstimate(flops=1, bytes_accessed=1, transcendentals=0),
        name="inner_density_steps",
    )(tiles, drift, levels, table, cot)


def halo_drift(ref, columns):
    tail = ref[...].astype(f32)
    both = 0.5 * (tail[0:2] + tail[2:4])
    rows = [[both[c : c + 1, k * columns : (k + 1) * columns] for k in range(2)] for c in range(2)]
    return rows, tail[4:5, :columns]


def with_halo(drift_ref, below_tail, above_tail):
    rows, columns = drift_ref.shape[1:]
    below, below_valid = halo_drift(below_tail, columns)
    above, above_valid = halo_drift(above_tail, columns)

    def half_drift(c, row):
        if row < 0:
            return below[c][row + 2]
        if row >= rows:
            return above[c][row - rows]
        return 0.5 * drift_ref[c, row : row + 1, :]

    def edge(row, density):
        if row < 0:
            return density * below_valid
        if row >= rows:
            return density * above_valid
        return density

    return half_drift, edge


def density_read(rows_ref, below_ref, above_ref, rows, columns):
    def read(row):
        if row < 0:
            return below_ref[:, pl.ds((row + 2) * columns, columns)]
        if row >= rows:
            return above_ref[:, pl.ds((row - rows) * columns, columns)]
        return rows_ref[:, pl.ds(row * columns, columns)]

    return read


def density_kernel(drift_ref, shift_ref, band_ref, rows_ref, below_ref, above_ref, below_tail, above_tail, dep_ref, *refs):
    next_ref, token_ref, *scratch = refs[-5:]
    rows, columns = drift_ref.shape[1:]
    size = shift_ref.shape[1]
    half_drift, edge = with_halo(drift_ref, below_tail, above_tail)
    token_ref[...] = jnp.zeros(token_ref.shape, f32)

    def write(row, density):
        write_row(next_ref, 0, size, row, rows, columns, density)

    read = density_read(rows_ref, below_ref, above_ref, rows, columns)
    shifts = [wide(shift_ref[n], columns) for n in range(4)]
    two_steps([(0, rows - 1)], read, half_drift, edge, band_ref[...], shifts, scratch, write)


def density_specs(drift, shifts, band, own, below, size, place):
    columns = drift.shape[2]
    scenarios = shifts.shape[1]
    halo = pl.BlockSpec((size, 2 * columns), lambda i: (place(i), 0))
    tail = pl.BlockSpec((EXTRA, 2 * columns), lambda i: (scenarios // EXTRA, 0))
    return [
        pl.BlockSpec(drift.shape, lambda i: (0, 0, 0)),
        pl.BlockSpec((4, size, LANES), lambda i: (0, place(i), 0)),
        pl.BlockSpec(band.shape, lambda i: (0, 0)),
        pl.BlockSpec((size, own.shape[1]), lambda i: (place(i), 0)),
        halo,
        halo,
        tail,
        tail,
    ]


def edge_kernel(
    blocks, with_inner, drift_ref, shift_ref, band_ref, rows_ref, below_ref, above_ref, below_tail, above_tail,
    place_ref, top_ref, bottom_ref, *refs,
):
    low_ref, high_ref, keep_ref, send_ref, total, *scratch = refs[-8:]
    step = pl.program_id(0)
    rows, columns = drift_ref.shape[1:]
    size = shift_ref.shape[1]
    block = keep_ref.shape[2]

    @pl.when(step < blocks)
    def _():
        half_drift, edge = with_halo(drift_ref, below_tail, above_tail)
        where = pl.ds(pl.multiple_of(step * size, size), size)

        def write(row, density):
            out, at = (low_ref, row) if row < 2 else (high_ref, row - rows + 2)
            out[where, pl.ds(at * columns, columns)] = density.astype(bf16)

        read = density_read(rows_ref, below_ref, above_ref, rows, columns)
        shifts = [wide(shift_ref[n], columns) for n in range(4)]
        two_steps(edge_segments(rows), read, half_drift, edge, band_ref[...], shifts, scratch, write)

    @pl.when(step >= blocks)
    def _():
        part = step - blocks
        left = jnp.concatenate([low_ref[...], high_ref[...]], axis=1)
        weight = jnp.concatenate([top_ref[...], bottom_ref[...]], axis=0)
        product = jnp.dot(left, weight, preferred_element_type=f32)
        total[...] = product + refs[0][part] if with_inner else product
        core = place_ref[0]
        for out, half in ((keep_ref, core), (send_ref, 1 - core)):
            for side in range(2):
                start = pl.multiple_of((2 * half + side) * block, block)
                out[side, part] = total[pl.ds(start, block), :].astype(out.dtype)


def edge_product(place, drift, shifts, band, own, below, above, weight, inner, parts, width):
    scenarios = shifts.shape[1]
    rows, columns = drift.shape[1:]
    size = 2 * scenario_block(scenarios)
    size = size if scenarios % size == 0 else size // 2
    blocks = scenarios // size
    edge = jax.ShapeDtypeStruct((scenarios, 2 * columns), bf16)
    last = weight.shape[0] // (2 * columns) - 1
    shape = (2, parts, scenarios // 4, width)

    def column(i):
        return jnp.maximum(i - blocks, 0)

    in_specs = density_specs(drift, shifts, band, own, below, size, lambda i: jnp.minimum(i, blocks - 1))
    in_specs += [
        smem(),
        pl.BlockSpec((2 * columns, width), lambda i: (0, column(i))),
        pl.BlockSpec((2 * columns, width), lambda i: (last, column(i))),
    ]
    args = [drift, shifts, band, own, below, above, below, above, place, weight, weight]
    if inner is not None:
        in_specs.append(vmem())
        args.append(inner)
    return pl.pallas_call(
        functools.partial(edge_kernel, blocks, inner is not None),
        grid=(blocks + parts,),
        in_specs=in_specs,
        out_specs=[vmem()] * 4,
        out_shape=[edge, edge, jax.ShapeDtypeStruct(shape, f32), jax.ShapeDtypeStruct(shape, bf16)],
        scratch_shapes=[pltpu.VMEM((scenarios, width), f32)] + step_scratch(edge_segments(rows), size, columns),
        compiler_params=params(),
        cost_estimate=pl.CostEstimate(flops=1, bytes_accessed=1, transcendentals=0),
        name="edge_steps_and_product",
    )(*args)


def density_steps(drift, shifts, band, own, below, above, dep, so_far, turn, turns):
    scenarios = shifts.shape[1]
    rows, columns = drift.shape[1:]
    per = rows * (columns // LANES)
    size = 3 * GROUP if scenarios % (turns * GROUP * 3) == 0 else GROUP
    steps = scenarios // size // turns
    first = turn * steps
    args = [drift, shifts, band, own, below, above, below, above, dep]
    in_specs = density_specs(drift, shifts, band, own, below, size, lambda i: first + i) + any_specs([dep])
    aliases = {}
    if so_far is not None:
        aliases = {len(args): 0}
        args.append(so_far)
        in_specs.append(pl.BlockSpec(memory_space=pltpu.HBM))
    return pl.pallas_call(
        density_kernel,
        grid=(steps,),
        in_specs=in_specs,
        out_specs=[
            pl.BlockSpec((size * per, LANES), lambda i: (first + i, 0)),
            pl.BlockSpec((SUBLANES, LANES), lambda i: (0, 0)),
        ],
        out_shape=[pltpu.HBM((scenarios * per, LANES), f32), jax.ShapeDtypeStruct((SUBLANES, LANES), f32)],
        input_output_aliases=aliases,
        scratch_shapes=step_scratch([(0, rows - 1)], size, columns),
        compiler_params=params(),
        cost_estimate=pl.CostEstimate(flops=1, bytes_accessed=1, transcendentals=0),
        name="density_steps",
    )(*args)


def smem():
    return pl.BlockSpec(memory_space=pltpu.SMEM)


def vmem():
    return pl.BlockSpec(memory_space=pltpu.VMEM)


def swap(values, count, flip):
    return lax.ppermute(values, "grid", [(i, i ^ flip) for i in range(count)])


def inner_product_kernel(count, inputs_ref, *refs):
    weight = jnp.concatenate([ref[...] for ref in refs[:count]], axis=0)
    refs[-1][pl.program_id(0)] = jnp.dot(inputs_ref[...], weight, preferred_element_type=f32)


def inner_product(inner, weight, width, deps):
    scenarios, cells = inner.shape
    total, hidden = weight.shape
    size = (total - cells) // 2
    count = cells // size

    def spec(k):
        return pl.BlockSpec((size, width), lambda n: (1 + k, n))

    return pl.pallas_call(
        functools.partial(inner_product_kernel, count),
        grid=(hidden // width,),
        in_specs=[vmem()] + [spec(k) for k in range(count)] + any_specs(deps),
        out_specs=vmem(),
        out_shape=jax.ShapeDtypeStruct((hidden // width, scenarios, width), f32),
        compiler_params=params(),
        cost_estimate=pl.CostEstimate(flops=1, bytes_accessed=1, transcendentals=0),
        name="inner_product",
    )(inner, *([weight] * count), *deps)


def any_specs(deps):
    return [pl.BlockSpec(memory_space=pl.ANY)] * len(deps)


def other_places(parts):
    return [(side, part) for side in range(2) for part in range(parts) if side or part]


def add_core_kernel(place_ref, mine_ref, other_ref, own_ref, *send_refs):
    side, part = place_ref[1], place_ref[2]
    own_ref[...] = mine_ref[side, part] + other_ref[side, part].astype(f32)
    for (by_side, by_part), out in zip(other_places(mine_ref.shape[1]), send_refs):
        at = side ^ by_side, part ^ by_part
        out[...] = (mine_ref[at] + other_ref[at].astype(f32)).astype(bf16)


def add_core(place, mine, other):
    parts, *piece = mine.shape[1:]
    return pl.pallas_call(
        add_core_kernel,
        in_specs=[smem(), vmem(), vmem()],
        out_shape=[jax.ShapeDtypeStruct(piece, f32)] + [jax.ShapeDtypeStruct(piece, bf16)] * (2 * parts - 1),
        compiler_params=params(),
        cost_estimate=pl.CostEstimate(flops=1, bytes_accessed=1, transcendentals=0),
        name="add_core",
    )(place, mine, other)


def activate_kernel(count, *refs):
    total = refs[0][...]
    for ref in refs[1 : 1 + count]:
        total = total + ref[...].astype(f32)
    refs[-1][...] = jnp.tanh(total).astype(bf16)


def activate(own, received, deps=()):
    return pl.pallas_call(
        functools.partial(activate_kernel, len(received)),
        in_specs=[vmem()] * (1 + len(received)) + any_specs(deps),
        out_shape=jax.ShapeDtypeStruct(own.shape, bf16),
        compiler_params=params(),
        cost_estimate=pl.CostEstimate(flops=1, bytes_accessed=1, transcendentals=0),
        name="first_activation",
    )(own, *received, *deps)


def pack_kernel(place_ref, mid_ref, head_ref, first_ref, out_ref, place_out_ref, head_row, arrived):
    for n in range(4):
        place_out_ref[n] = place_ref[n]
    hidden = mid_ref.shape[0]
    copies = [
        pltpu.make_async_copy(mid_ref, out_ref.at[pl.ds(0, hidden), :], arrived.at[0]),
        pltpu.make_async_copy(head_ref, head_row, arrived.at[1]),
    ]
    for copy in copies:
        copy.start()
    copies[1].wait()
    out_ref[pl.ds(hidden, EXTRA), :] = tail_rows(head_row[...])
    copies[0].wait()


def pack(place, mid_weight, head, first):
    hidden, units = mid_weight.shape
    return pl.pallas_call(
        pack_kernel,
        in_specs=[smem()] + [pl.BlockSpec(memory_space=pltpu.HBM)] * 3,
        out_specs=[vmem(), smem()],
        out_shape=[jax.ShapeDtypeStruct((hidden + EXTRA, units), bf16), jax.ShapeDtypeStruct(place.shape, place.dtype)],
        scratch_shapes=[pltpu.VMEM(head.shape, f32), pltpu.SemaphoreType.DMA((2,))],
        compiler_params=params(),
        cost_estimate=pl.CostEstimate(flops=1, bytes_accessed=1, transcendentals=0),
        name="mid_with_head",
    )(place, *[pltpu.with_memory_space_constraint(array, pltpu.HBM) for array in (mid_weight, head)], first)


def two_halves(exact):
    high = exact.astype(bf16)
    low = (exact - high.astype(f32)).astype(bf16)
    return high, low


def tail_rows(exact):
    high, low = two_halves(exact)
    zeros = jnp.zeros((EXTRA - 2, exact.shape[1]), bf16)
    return jnp.concatenate([high, low, zeros], axis=0)


def middle_kernel(chunks, parts, width, *refs):
    pieces = chunks * parts
    place_ref, cot_ref = refs[0], refs[1]
    first_refs = refs[2 : 2 + pieces]
    mid_refs = refs[2 + pieces : 6 + pieces]
    outs = refs[-(3 + parts) :]
    own_ref, value_ref, mid_keep_ref, mid_send_ref = outs[:4]
    send_refs = outs[4:]
    part = place_ref[2]
    block = first_refs[0].shape[0]

    def mid_rows(start):
        return jnp.concatenate([ref[pl.ds(start, width), :] for ref in mid_refs], axis=1)

    def start_of(c, k):
        return pl.multiple_of((c * parts + (part ^ k)) * width, width)

    total = None
    for c in range(chunks):
        for k in range(parts):
            term = jnp.dot(first_refs[c * parts + k][...], mid_rows(start_of(c, k)), preferred_element_type=f32)
            total = term if total is None else total + term
    second_low = jnp.tanh(total).astype(bf16)
    second = second_low.astype(f32)
    heads = jnp.concatenate([ref[pl.ds(pieces * width, EXTRA), :] for ref in mid_refs], axis=1)
    head = heads[0:1].astype(f32) + heads[1:2].astype(f32)
    rows = lax.dot_general(heads, second_low, (((1,), (1,)), ((), ())), preferred_element_type=f32)
    value = rows[0:1] + rows[1:2]
    if width > block:
        value = jnp.concatenate([value, jnp.zeros((1, width - block), f32)], axis=1)
    value_ref[...] = value
    cot = cot_ref[pl.ds(pl.multiple_of(place_ref[3] * block, SUBLANES), block), :1]
    head_part = jnp.sum(cot * second, axis=0, keepdims=True)
    back = (cot * head * (1.0 - second * second)).astype(bf16)
    units = mid_refs[0].shape[1]
    for k in range(parts):
        for c in range(chunks):
            piece = lax.dot_general(
                back, mid_rows(start_of(c, k)), (((1,), (1,)), ((), ())), preferred_element_type=f32
            )
            if k == 0:
                own_ref[pl.ds(c * block, block), :] = piece
            else:
                send_refs[k - 1][pl.ds(c * block, block), :] = piece.astype(bf16)
        if k > 0:
            send_refs[k - 1][pl.ds(chunks * block, EXTRA), :] = tail_rows(value)
    for c in range(chunks):
        for k in range(parts):
            product = lax.dot_general(
                first_refs[c * parts + k][...], back, (((0,), (0,)), ((), ())), preferred_element_type=f32
            ).astype(bf16)
            for p in range(4):
                out = (mid_keep_ref, mid_send_ref)[p % 2]
                out[p // 2, pl.ds(start_of(c, k), width), :] = product[:, p * units : (p + 1) * units]
    for p in range(4):
        out = (mid_keep_ref, mid_send_ref)[p % 2]
        out[p // 2, pl.ds(pieces * width, EXTRA), :] = tail_rows(head_part[:, p * units : (p + 1) * units])


def middle(place, cot, firsts, mids, chunks, parts, width, deps=()):
    block = firsts[0].shape[0]
    partial = jax.ShapeDtypeStruct((2, *mids[0].shape), bf16)
    return pl.pallas_call(
        functools.partial(middle_kernel, chunks, parts, width),
        in_specs=[smem()] + [vmem()] * (1 + len(firsts) + 4) + any_specs(deps),
        out_shape=[
            jax.ShapeDtypeStruct((chunks * block, width), f32),
            jax.ShapeDtypeStruct((1, width), f32),
            partial,
            partial,
        ]
        + [jax.ShapeDtypeStruct((chunks * block + EXTRA, width), bf16)] * (parts - 1),
        compiler_params=params(),
        cost_estimate=pl.CostEstimate(flops=1, bytes_accessed=1, transcendentals=0),
        name="value_layers",
    )(place, cot, *firsts, *mids, *deps)


def add_tail(left, right, hidden):
    body = left[:hidden].astype(f32) + right[:hidden].astype(f32)
    tails = left[hidden:].astype(f32) + right[hidden:].astype(f32)
    return body.astype(bf16), tails[0:1] + tails[1:2]


def mid_add_kernel(keep_ref, other_ref, *refs):
    own_ref, send_ref = refs[-2:]
    hidden = own_ref.shape[0] - EXTRA
    for at, out in enumerate((own_ref, send_ref)):
        body, tail = add_tail(keep_ref[at], other_ref[at], hidden)
        out[pl.ds(0, hidden), :] = body
        out[pl.ds(hidden, EXTRA), :] = tail_rows(tail)


def mid_add(keep, other, deps=()):
    shape = jax.ShapeDtypeStruct(keep.shape[1:], bf16)
    return pl.pallas_call(
        mid_add_kernel,
        in_specs=[vmem()] * 2 + any_specs(deps),
        out_shape=[shape, shape],
        compiler_params=params(),
        cost_estimate=pl.CostEstimate(flops=1, bytes_accessed=1, transcendentals=0),
        name="mid_gradient_add",
    )(keep, other, *deps)


def mid_final_kernel(own_ref, other_ref, *refs):
    out_ref, head_ref, token_ref = refs[-3:]
    token_ref[...] = jnp.zeros(token_ref.shape, f32)
    body, tail = add_tail(own_ref[...], other_ref[...], out_ref.shape[0])
    out_ref[...] = body
    head_ref[...] = tail


def mid_final(own, other, deps=()):
    hidden = own.shape[0] - EXTRA
    return pl.pallas_call(
        mid_final_kernel,
        in_specs=[vmem()] * 2 + any_specs(deps),
        out_shape=[
            jax.ShapeDtypeStruct((hidden, own.shape[1]), bf16),
            jax.ShapeDtypeStruct((1, own.shape[1]), f32),
            jax.ShapeDtypeStruct((SUBLANES, LANES), f32),
        ],
        compiler_params=params(),
        cost_estimate=pl.CostEstimate(flops=1, bytes_accessed=1, transcendentals=0),
        name="mid_gradient_final",
    )(own, other, *deps)


def back_first_kernel(count, own_ref, value_ref, *refs):
    received = refs[:count]
    first_ref, out_ref, tail_ref = refs[count:]
    block = first_ref.shape[0]
    value = value_ref[...]
    total = own_ref[...]
    for ref in received:
        tail = ref[pl.ds(block, EXTRA), :].astype(f32)
        value = value + (tail[0:1] + tail[1:2])
        total = total + ref[pl.ds(0, block), :].astype(f32)
    first = first_ref[...].astype(f32)
    out_ref[...] = (total * (1.0 - first * first)).astype(bf16)
    tail_ref[...] = tail_rows(value)


def back_first(own, value, received, first):
    block, width = first.shape
    return pl.pallas_call(
        functools.partial(back_first_kernel, len(received)),
        in_specs=[vmem()] * (3 + len(received)),
        out_shape=[jax.ShapeDtypeStruct((rows, width), bf16) for rows in (block, EXTRA)],
        compiler_params=params(),
        cost_estimate=pl.CostEstimate(flops=1, bytes_accessed=1, transcendentals=0),
        name="back_first",
    )(own, value, *received, first)


def stack_kernel(count, *refs):
    at = 0
    for ref in refs[:count]:
        refs[-1][pl.ds(at, ref.shape[0]), :] = ref[...]
        at += ref.shape[0]


def stack(pieces, deps):
    rows = sum(piece.shape[0] for piece in pieces)
    return pl.pallas_call(
        functools.partial(stack_kernel, len(pieces)),
        in_specs=[vmem()] * len(pieces) + any_specs(deps),
        out_shape=jax.ShapeDtypeStruct((rows, pieces[0].shape[1]), bf16),
        compiler_params=params(),
        cost_estimate=pl.CostEstimate(flops=1, bytes_accessed=1, transcendentals=0),
        name="stack_parts",
    )(*pieces, *deps)


def turn_kernel(count, *refs):
    for ref, out in zip(refs[:count], refs[-count:]):
        out[...] = ref[...].T


def transposed(arrays, deps):
    return pl.pallas_call(
        functools.partial(turn_kernel, len(arrays)),
        in_specs=[vmem()] * len(arrays) + any_specs(deps),
        out_shape=[jax.ShapeDtypeStruct(array.shape[::-1], array.dtype) for array in arrays],
        compiler_params=params(),
        cost_estimate=pl.CostEstimate(flops=1, bytes_accessed=1, transcendentals=0),
        name="transposed_inputs",
    )(*arrays, *deps)


def first_grad_kernel(parts, block, tiles, count, *refs):
    place_ref = refs[0]
    lefts = refs[1 : 1 + count]
    stacks = refs[1 + count : 5 + count]
    out_ref, value_ref, whole = refs[-3:]
    width = out_ref.shape[1]
    step = pl.program_id(0)
    piece = step // tiles ^ place_ref[2]
    column = pl.ds(pl.multiple_of(step % tiles * width, width), width)
    mine = place_ref[3]
    values = [jnp.zeros((1, block), f32)] * 4
    for t, ref in enumerate(stacks):
        at = mine ^ (2 * (t % 2) + t // 2)
        whole[pl.ds(pl.multiple_of(at * block, block), block), :] = ref[
            pl.ds(pl.multiple_of(piece * block, block), block), column
        ]
        tail = ref[pl.ds(parts * block, EXTRA), :block].astype(f32)
        value = tail[0:1] + tail[1:2]
        for q in range(4):
            values[q] = jnp.where(at == q, value, values[q])
    value_ref[...] = jnp.concatenate(values, axis=1)
    start = 0
    for ref in lefts:
        cells = ref.shape[0]
        out_ref[pl.ds(start, cells), :] = jnp.dot(ref[...], whole[...], preferred_element_type=f32).astype(bf16)
        start += cells


def first_grad(place, lefts, stacks, parts, block, deps):
    scenarios = lefts[0].shape[1]
    cells = sum(left.shape[0] for left in lefts)
    width = stacks[0].shape[1]
    tile = min(width, 256)
    tiles = width // tile
    return pl.pallas_call(
        functools.partial(first_grad_kernel, parts, block, tiles, len(lefts)),
        grid=(parts * tiles,),
        in_specs=[smem()] + [vmem()] * (len(lefts) + 4) + any_specs(deps),
        out_specs=[pl.BlockSpec((cells, tile), lambda i: (0, i)), pl.BlockSpec((1, scenarios), lambda i: (0, 0))],
        out_shape=[pltpu.HBM((cells, parts * width), bf16), jax.ShapeDtypeStruct((1, scenarios), f32)],
        scratch_shapes=[pltpu.VMEM((scenarios, tile), bf16)],
        compiler_params=params(),
        cost_estimate=pl.CostEstimate(flops=1, bytes_accessed=1, transcendentals=0),
        name="first_gradient",
    )(place, *lefts, *stacks, *deps)


def local(hist, drift, shocks, shock_table, first_weight, mid_weight, head_weight, cotangent):
    scenarios, rows, columns = hist.shape
    count = lax.axis_size("grid")
    hidden = first_weight.shape[1]
    units = mid_weight.shape[1]
    parts = count // 4
    width = hidden // parts
    block = scenarios // 4
    index = lax.axis_index("grid")
    core, side, part = index & 1, (index >> 1) & 1, index >> 2
    mine = 2 * core + side
    tiles = pltpu.with_memory_space_constraint(to_tiles(hist), pltpu.HBM)

    place = jnp.stack([core, side, part, mine])

    small = [pltpu.with_memory_space_constraint(array, pltpu.HBM) for array in (drift, shocks.T, shock_table.T, cotangent)]
    packed, place = pack(place, mid_weight, head_weight[None, :], small[-1])
    mids = [packed]
    mids += [swap(mids[0], count, 1), swap(mids[0], count, 2)]
    first_rows, last_rows, shifts, band, cot, own_rows, inner = inner_steps(tiles, *small)
    inner = inner if rows > 4 else None
    forward = [(i, i + 1) for i in range(count - 1)]
    backward = [(i + 1, i) for i in range(count - 1)]
    below = lax.ppermute(last_rows, "grid", forward)
    above = lax.ppermute(first_rows, "grid", backward)
    first_weight = pltpu.with_memory_space_constraint(first_weight, pltpu.HBM)
    product = None if inner is None else inner_product(inner, first_weight, width, mids[1:])
    low, high, keep, send = edge_product(
        place, drift, shifts, band, own_rows, below, above, first_weight, product, parts, width
    )
    mids.append(swap(mids[2], count, 1))

    def density_turn(turn, dep, so_far):
        return density_steps(drift, shifts, band, own_rows, below, above, dep, so_far, turn, 2)

    own, *sends = add_core(place, keep, swap(send, count, 1))
    flips = [2 * by_side + 4 * by_part for by_side, by_part in other_places(parts)]
    received = [swap(piece, count, flip) for piece, flip in zip(sends, flips)]
    density, token = density_turn(0, sends[-1], None)
    first = activate(own, received, [token])
    firsts = [first] + [swap(first, count, 4 * k) for k in range(1, parts)]
    density, token = density_turn(1, first, density)
    own, value, mid_keep, mid_send, *sends = middle(place, cot, firsts, mids, 1, parts, width, [token, mids[1], mids[3]])
    received = [swap(piece, count, 4 * (k + 1)) for k, piece in enumerate(sends)]
    back, tail = back_first(own, value, received, first)
    lefts = transposed([low, high] if inner is None else [low, inner, high], [back])
    pieces = [back] + [swap(back, count, 4 * k) for k in range(1, parts)] + [tail]
    stacks = [stack(pieces, [lefts[0]])]
    stacks += [swap(stacks[0], count, 1), swap(stacks[0], count, 2)]
    mid_keep, mid_send = mid_add(mid_keep, swap(mid_send, count, 1), [stacks[2]])
    stacks.append(swap(stacks[2], count, 1))
    grad_first, value = first_grad(place, lefts, stacks, parts, block, [mid_send])
    grad_mid, grad_head, _ = mid_final(mid_keep, swap(mid_send, count, 2), [value])
    value = value.reshape(scenarios)
    return from_tiles(density, hist.shape), value, grad_first, grad_mid, grad_head[0]


def solution(mesh):
    in_specs = (
        P("groups", "grid", None),
        P(None, "grid", None),
        P("groups", None),
        P("groups", None),
        P(("groups", "grid"), None),
        P("groups", "grid"),
        P(("groups", "grid")),
        P("groups"),
    )
    out_specs = (
        P("groups", "grid", None),
        P("groups"),
        P(("groups", "grid"), None),
        P("groups", "grid"),
        P(("groups", "grid")),
    )
    return jax.shard_map(local, mesh=mesh, in_specs=in_specs, out_specs=out_specs, check_vma=False)
```

```python
import functools
import jax
import jax.numpy as jnp
from jax import lax
from jax.experimental import pallas as pl
from jax.experimental.pallas import tpu as pltpu
from jax.sharding import PartitionSpec as P

diffusion_rate = 0.24
VMEM_BYTES = 24 * 1024 * 1024
EXTRA = 16
bf16 = jnp.bfloat16
f32 = jnp.float32


def params():
    return pltpu.CompilerParams(vmem_limit_bytes=VMEM_BYTES)


def scenario_block(scenarios):
    for size in (64, 32, 16):
        if scenarios % size == 0:
            return size
    return scenarios


LANES = 128
SUBLANES = 8
GROUP = 16


def to_tiles(hist):
    scenarios, rows, columns = hist.shape
    high = min(rows, SUBLANES)
    tiles = hist.reshape(scenarios, rows // high, high, columns // LANES, LANES)
    return tiles.transpose(0, 1, 3, 2, 4).reshape(scenarios * rows * (columns // LANES), LANES)


def from_tiles(tiles, shape):
    scenarios, rows, columns = shape
    high = min(rows, SUBLANES)
    parts = tiles.reshape(scenarios, rows // high, columns // LANES, high, LANES)
    return parts.transpose(0, 1, 3, 2, 4).reshape(shape)


def tile_offset(row, lane_tile, rows, lane_tiles):
    high = min(rows, SUBLANES)
    return (row // high * lane_tiles + lane_tile) * high + row % high


def read_row(ref, first_scenario, count, row, rows, columns):
    lane_tiles = columns // LANES
    per = rows * lane_tiles
    return jnp.concatenate(
        [
            ref[pl.ds(first_scenario * per + tile_offset(row, t, rows, lane_tiles), count, stride=per), :]
            for t in range(lane_tiles)
        ],
        axis=1,
    )


def write_row(ref, first_scenario, count, row, rows, columns, values):
    lane_tiles = columns // LANES
    per = rows * lane_tiles
    for t in range(lane_tiles):
        place = pl.ds(first_scenario * per + tile_offset(row, t, rows, lane_tiles), count, stride=per)
        ref[place, :] = values[:, t * LANES : (t + 1) * LANES]


def drift_tail(drift_ref, start):
    pieces = [
        jnp.concatenate([drift_ref[c, start : start + 1], drift_ref[c, start + 1 : start + 2]], axis=1)
        for c in range(2)
    ]
    high, low = two_halves(jnp.concatenate(pieces, axis=0))
    ones = jnp.ones((1, high.shape[1]), bf16)
    zeros = jnp.zeros((EXTRA - 5, high.shape[1]), bf16)
    return jnp.concatenate([high, low, ones, zeros], axis=0)


def band_matrix(columns):
    row = lax.broadcasted_iota(jnp.int32, (columns, columns), 0)
    column = lax.broadcasted_iota(jnp.int32, (columns, columns), 1)
    right = jnp.where(column == row + 1, 1.0, 0.0)
    left = jnp.where(column == row - 1, 1.0, 0.0)
    centre = jnp.where(column == row, 1.0 - 4.0 * diffusion_rate, diffusion_rate * (right + left))
    return centre.astype(bf16), (right - left).astype(bf16)


def half_shifts(levels_ref, table_ref, shift_ref):
    scenarios = levels_ref.shape[1]
    for t in range(levels_ref.shape[0]):
        level = jnp.broadcast_to(levels_ref[t : t + 1, :].astype(f32), (LANES, scenarios)).T
        for c in range(2):
            shift = jnp.zeros(level.shape, f32)
            for n in range(table_ref.shape[1]):
                shift = jnp.where(level == n, 0.5 * table_ref[c : c + 1, n : n + 1], shift)
            shift_ref[2 * t + c] = shift


def wide(values, columns):
    return jnp.concatenate([values] * (columns // LANES), axis=1)


def one_step(rows_of, places, half_drift, band, shift_x, shift_y, pairs, terms, write):
    size, columns = shift_x.shape
    whole = pl.ds(0, columns)

    def density(row):
        return pairs[pl.ds(rows_of[row] * size, size), whole].astype(f32)

    for row in places:
        flux = (half_drift(1, row) + shift_y) * density(row)
        pairs[pl.ds(rows_of[row] * size, size), pl.ds(columns, columns)] = flux.astype(bf16)
    yield
    start = rows_of[places[0]] * size
    count = (rows_of[places[-1]] + 1) * size - start
    terms[pl.ds(start, count), :] = jnp.dot(pairs[pl.ds(start, count), :], band, preferred_element_type=f32)
    yield
    for row in places:
        low = density(row - 1) * ((diffusion_rate + half_drift(0, row - 1)) + shift_x)
        high = density(row + 1) * ((diffusion_rate - half_drift(0, row + 1)) - shift_x)
        write(row, terms[pl.ds(rows_of[row] * size, size), :] + low + high)


def step_stages(segments, read, half_drift, edge, band, shifts, scratch, write):
    pairs, later, terms = scratch
    size, columns = shifts[0].shape
    before, between, after = [
        [row for first, last in segments for row in range(first - more, last + more + 1)] for more in (2, 1, 0)
    ]
    rows_of = {row: k for k, row in enumerate(before)}
    for row, k in rows_of.items():
        pairs[pl.ds(k * size, size), pl.ds(0, columns)] = read(row)

    def write_later(row, density):
        later[pl.ds(rows_of[row] * size, size), pl.ds(0, columns)] = edge(row, density).astype(bf16)

    yield from one_step(rows_of, between, half_drift, band, shifts[0], shifts[1], pairs, terms, write_later)
    yield from one_step(rows_of, after, half_drift, band, shifts[2], shifts[3], later, terms, write)


def interleave(runs):
    ahead, live = list(runs), []
    while ahead or live:
        if ahead:
            live.append(ahead.pop(0))
        for run in list(live):
            if next(run, live) is live:
                live.remove(run)


def two_steps(*args):
    interleave([step_stages(*args)])


def step_scratch(segments, size, columns):
    rows = sum(last - first + 5 for first, last in segments)
    pairs = pltpu.VMEM((rows * size, 2 * columns), bf16)
    return [pairs, pairs, pltpu.VMEM((rows * size, columns), f32)]


def edge_segments(rows):
    return [(0, 1), (rows - 2, rows - 1)] if rows >= 8 else [(0, rows - 1)]


def inner_kernel(
    rows, size, hist_ref, drift_hbm, levels_hbm, table_hbm, cot_hbm,
    first_ref, last_ref, shift_ref, band_ref, cot_ref, rows_ref, inner_ref,
    drift_ref, levels_ref, table_ref, cot_row, arrived, all_shifts, *scratch,
):
    step = pl.program_id(0)
    columns = drift_ref.shape[2]

    @pl.when(step == 0)
    def _():
        sources = ((drift_hbm, drift_ref), (levels_hbm, levels_ref), (table_hbm, table_ref), (cot_hbm, cot_row))
        copies = [pltpu.make_async_copy(*pair, arrived.at[n]) for n, pair in enumerate(sources)]
        for copy in copies:
            copy.start()
        centre, flux = band_matrix(columns)
        band_ref[pl.ds(0, columns), :] = centre
        band_ref[pl.ds(columns, columns), :] = flux
        for copy in copies:
            copy.wait()
        half_shifts(levels_ref, table_ref, all_shifts)
        cot_ref[...] = jnp.broadcast_to(cot_row[...].reshape(1, -1), (LANES, cot_row.shape[0])).T
        for out, start in ((first_ref, 0), (last_ref, rows - 2)):
            out[pl.ds(out.shape[0] - EXTRA, EXTRA), :] = drift_tail(drift_ref, start)

    where = pl.ds(pl.multiple_of(step * size, size), size)
    for n in range(4):
        shift_ref[n] = all_shifts[n, where, :]
    for row in range(rows):
        density = read_row(hist_ref, 0, size, row, rows, columns).astype(bf16)
        rows_ref[:, pl.ds(row * columns, columns)] = density
        if row < 2:
            first_ref[where, pl.ds(row * columns, columns)] = density
        if row >= rows - 2:
            last_ref[where, pl.ds((row - rows + 2) * columns, columns)] = density
    if rows <= 4:
        return
    band = band_ref[...]
    count = len(scratch) // 3
    part = size // count

    def run(n):
        here = pl.ds(n * part, part)

        def write(row, density):
            inner_ref[here, pl.ds((row - 2) * columns, columns)] = density.astype(bf16)

        return step_stages(
            [(2, rows - 3)],
            lambda row: rows_ref[here, pl.ds(row * columns, columns)],
            lambda c, row: 0.5 * drift_ref[c, row : row + 1, :],
            lambda row, density: density,
            band,
            [wide(shift_ref[k, here, :], columns) for k in range(4)],
            scratch[3 * n : 3 * n + 3],
            write,
        )

    interleave([run(n) for n in range(count)])


def inner_steps(tiles, drift, levels, table, cot):
    scenarios = levels.shape[1]
    rows, columns = drift.shape[1:]
    per = tiles.shape[0] // scenarios
    size = scenario_block(scenarios)
    inner = max(rows - 4, 1) * columns
    sent = jax.ShapeDtypeStruct((scenarios + EXTRA, 2 * columns), bf16)
    shifts = jax.ShapeDtypeStruct((4, scenarios, LANES), f32)
    band = jax.ShapeDtypeStruct((2 * columns, columns), bf16)
    return pl.pallas_call(
        functools.partial(inner_kernel, rows, size),
        grid=(scenarios // size,),
        in_specs=[pl.BlockSpec((size * per, LANES), lambda i: (i, 0))] + [pl.BlockSpec(memory_space=pltpu.HBM)] * 4,
        out_specs=[pl.BlockSpec(sent.shape, lambda i: (0, 0))] * 2
        + [
            pl.BlockSpec((4, size, LANES), lambda i: (0, i, 0)),
            pl.BlockSpec(band.shape, lambda i: (0, 0)),
            pl.BlockSpec((scenarios, LANES), lambda i: (0, 0)),
            pl.BlockSpec((size, rows * columns), lambda i: (i, 0)),
            pl.BlockSpec((size, inner), lambda i: (i, 0)),
        ],
        out_shape=[
            sent,
            sent,
            pltpu.HBM(shifts.shape, f32),
            band,
            jax.ShapeDtypeStruct((scenarios, LANES), f32),
            pltpu.HBM((scenarios, rows * columns), bf16),
            jax.ShapeDtypeStruct((scenarios, inner), bf16),
        ],
        scratch_shapes=[
            pltpu.VMEM(drift.shape, f32),
            pltpu.VMEM(levels.shape, levels.dtype),
            pltpu.VMEM(table.shape, f32),
            pltpu.VMEM(cot.shape, f32),
            pltpu.SemaphoreType.DMA((4,)),
            pltpu.VMEM(shifts.shape, f32),
        ]
        + step_scratch([(2, max(rows - 3, 2))], size // 2, columns) * 2,
        compiler_params=params(),
        cost_estimate=pl.CostEstimate(flops=1, bytes_accessed=1, transcendentals=0),
        name="inner_density_steps",
    )(tiles, drift, levels, table, cot)


def halo_drift(ref, columns):
    tail = ref[...].astype(f32)
    both = 0.5 * (tail[0:2] + tail[2:4])
    rows = [[both[c : c + 1, k * columns : (k + 1) * columns] for k in range(2)] for c in range(2)]
    return rows, tail[4:5, :columns]


def with_halo(drift_ref, below_tail, above_tail):
    rows, columns = drift_ref.shape[1:]
    below, below_valid = halo_drift(below_tail, columns)
    above, above_valid = halo_drift(above_tail, columns)

    def half_drift(c, row):
        if row < 0:
            return below[c][row + 2]
        if row >= rows:
            return above[c][row - rows]
        return 0.5 * drift_ref[c, row : row + 1, :]

    def edge(row, density):
        if row < 0:
            return density * below_valid
        if row >= rows:
            return density * above_valid
        return density

    return half_drift, edge


def density_read(rows_ref, below_ref, above_ref, rows, columns):
    def read(row):
        if row < 0:
            return below_ref[:, pl.ds((row + 2) * columns, columns)]
        if row >= rows:
            return above_ref[:, pl.ds((row - rows) * columns, columns)]
        return rows_ref[:, pl.ds(row * columns, columns)]

    return read


def density_kernel(drift_ref, shift_ref, band_ref, rows_ref, below_ref, above_ref, below_tail, above_tail, dep_ref, *refs):
    next_ref, token_ref, *scratch = refs[-5:]
    rows, columns = drift_ref.shape[1:]
    size = shift_ref.shape[1]
    half_drift, edge = with_halo(drift_ref, below_tail, above_tail)
    token_ref[...] = jnp.zeros(token_ref.shape, f32)

    def write(row, density):
        write_row(next_ref, 0, size, row, rows, columns, density)

    read = density_read(rows_ref, below_ref, above_ref, rows, columns)
    shifts = [wide(shift_ref[n], columns) for n in range(4)]
    two_steps([(0, rows - 1)], read, half_drift, edge, band_ref[...], shifts, scratch, write)


def density_specs(drift, shifts, band, own, below, size, place):
    columns = drift.shape[2]
    scenarios = shifts.shape[1]
    halo = pl.BlockSpec((size, 2 * columns), lambda i: (place(i), 0))
    tail = pl.BlockSpec((EXTRA, 2 * columns), lambda i: (scenarios // EXTRA, 0))
    return [
        pl.BlockSpec(drift.shape, lambda i: (0, 0, 0)),
        pl.BlockSpec((4, size, LANES), lambda i: (0, place(i), 0)),
        pl.BlockSpec(band.shape, lambda i: (0, 0)),
        pl.BlockSpec((size, own.shape[1]), lambda i: (place(i), 0)),
        halo,
        halo,
        tail,
        tail,
    ]


def edge_kernel(drift_ref, shift_ref, band_ref, rows_ref, below_ref, above_ref, below_tail, above_tail, dep_ref, *refs):
    low_ref, high_ref, *scratch = refs
    rows, columns = drift_ref.shape[1:]
    half_drift, edge = with_halo(drift_ref, below_tail, above_tail)

    def write(row, density):
        out, at = (low_ref, row) if row < 2 else (high_ref, row - rows + 2)
        out[:, pl.ds(at * columns, columns)] = density.astype(bf16)

    read = density_read(rows_ref, below_ref, above_ref, rows, columns)
    shifts = [wide(shift_ref[n], columns) for n in range(4)]
    two_steps(edge_segments(rows), read, half_drift, edge, band_ref[...], shifts, scratch, write)


def edge_steps(drift, shifts, band, own, below, above, dep):
    scenarios = shifts.shape[1]
    rows, columns = drift.shape[1:]
    size = 2 * scenario_block(scenarios)
    size = size if scenarios % size == 0 else size // 2
    edge = jax.ShapeDtypeStruct((scenarios, 2 * columns), bf16)
    spec = pl.BlockSpec((size, 2 * columns), lambda i: (i, 0))
    return pl.pallas_call(
        edge_kernel,
        grid=(scenarios // size,),
        in_specs=density_specs(drift, shifts, band, own, below, size, lambda i: i) + any_specs([dep]),
        out_specs=[spec, spec],
        out_shape=[edge, edge],
        scratch_shapes=step_scratch(edge_segments(rows), size, columns),
        compiler_params=params(),
        cost_estimate=pl.CostEstimate(flops=1, bytes_accessed=1, transcendentals=0),
        name="edge_density_steps",
    )(drift, shifts, band, own, below, above, below, above, dep)


def density_steps(drift, shifts, band, own, below, above, dep, so_far, turn, turns):
    scenarios = shifts.shape[1]
    rows, columns = drift.shape[1:]
    per = rows * (columns // LANES)
    size = 3 * GROUP if scenarios % (turns * GROUP * 3) == 0 else GROUP
    steps = scenarios // size // turns
    first = turn * steps
    args = [drift, shifts, band, own, below, above, below, above, dep]
    in_specs = density_specs(drift, shifts, band, own, below, size, lambda i: first + i) + any_specs([dep])
    aliases = {}
    if so_far is not None:
        aliases = {len(args): 0}
        args.append(so_far)
        in_specs.append(pl.BlockSpec(memory_space=pltpu.HBM))
    return pl.pallas_call(
        density_kernel,
        grid=(steps,),
        in_specs=in_specs,
        out_specs=[
            pl.BlockSpec((size * per, LANES), lambda i: (first + i, 0)),
            pl.BlockSpec((SUBLANES, LANES), lambda i: (0, 0)),
        ],
        out_shape=[pltpu.HBM((scenarios * per, LANES), f32), jax.ShapeDtypeStruct((SUBLANES, LANES), f32)],
        input_output_aliases=aliases,
        scratch_shapes=step_scratch([(0, rows - 1)], size, columns),
        compiler_params=params(),
        cost_estimate=pl.CostEstimate(flops=1, bytes_accessed=1, transcendentals=0),
        name="density_steps",
    )(*args)


def smem():
    return pl.BlockSpec(memory_space=pltpu.SMEM)


def vmem():
    return pl.BlockSpec(memory_space=pltpu.VMEM)


def swap(values, count, flip):
    return lax.ppermute(values, "grid", [(i, i ^ flip) for i in range(count)])


def inner_product_kernel(count, inputs_ref, *refs):
    weight = jnp.concatenate([ref[...] for ref in refs[:count]], axis=0)
    refs[-1][pl.program_id(0)] = jnp.dot(inputs_ref[...], weight, preferred_element_type=f32)


def inner_product(inner, weight, width, deps):
    scenarios, cells = inner.shape
    total, hidden = weight.shape
    size = (total - cells) // 2
    count = cells // size

    def spec(k):
        return pl.BlockSpec((size, width), lambda n: (1 + k, n))

    return pl.pallas_call(
        functools.partial(inner_product_kernel, count),
        grid=(hidden // width,),
        in_specs=[vmem()] + [spec(k) for k in range(count)] + any_specs(deps),
        out_specs=vmem(),
        out_shape=jax.ShapeDtypeStruct((hidden // width, scenarios, width), f32),
        compiler_params=params(),
        cost_estimate=pl.CostEstimate(flops=1, bytes_accessed=1, transcendentals=0),
        name="inner_product",
    )(inner, *([weight] * count), *deps)


def edge_product_kernel(block, with_inner, place_ref, low_ref, high_ref, top_ref, bottom_ref, *refs):
    keep_ref, send_ref, total = refs[-3:]
    step = pl.program_id(0)
    left = jnp.concatenate([low_ref[...], high_ref[...]], axis=1)
    weight = jnp.concatenate([top_ref[...], bottom_ref[...]], axis=0)
    product = jnp.dot(left, weight, preferred_element_type=f32)
    total[...] = product + refs[0][step] if with_inner else product
    core = place_ref[0]
    for out, half in ((keep_ref, core), (send_ref, 1 - core)):
        for side in range(2):
            start = pl.multiple_of((2 * half + side) * block, block)
            out[side, step] = total[pl.ds(start, block), :].astype(out.dtype)


def edge_product(place, low, high, weight, inner, parts, width):
    scenarios, size = low.shape
    block = scenarios // 4
    last = weight.shape[0] // size - 1
    shape = (2, parts, block, width)
    in_specs = [
        smem(),
        vmem(),
        vmem(),
        pl.BlockSpec((size, width), lambda n: (0, n)),
        pl.BlockSpec((size, width), lambda n: (last, n)),
    ]
    args = [place, low, high, weight, weight]
    if inner is not None:
        in_specs.append(vmem())
        args.append(inner)
    return pl.pallas_call(
        functools.partial(edge_product_kernel, block, inner is not None),
        grid=(parts,),
        in_specs=in_specs,
        out_specs=[vmem(), vmem()],
        out_shape=[jax.ShapeDtypeStruct(shape, f32), jax.ShapeDtypeStruct(shape, bf16)],
        scratch_shapes=[pltpu.VMEM((scenarios, width), f32)],
        compiler_params=params(),
        cost_estimate=pl.CostEstimate(flops=1, bytes_accessed=1, transcendentals=0),
        name="edge_product",
    )(*args)


def any_specs(deps):
    return [pl.BlockSpec(memory_space=pl.ANY)] * len(deps)


def other_places(parts):
    return [(side, part) for side in range(2) for part in range(parts) if side or part]


def add_core_kernel(place_ref, mine_ref, other_ref, own_ref, *send_refs):
    side, part = place_ref[1], place_ref[2]
    own_ref[...] = mine_ref[side, part] + other_ref[side, part].astype(f32)
    for (by_side, by_part), out in zip(other_places(mine_ref.shape[1]), send_refs):
        at = side ^ by_side, part ^ by_part
        out[...] = (mine_ref[at] + other_ref[at].astype(f32)).astype(bf16)


def add_core(place, mine, other):
    parts, *piece = mine.shape[1:]
    return pl.pallas_call(
        add_core_kernel,
        in_specs=[smem(), vmem(), vmem()],
        out_shape=[jax.ShapeDtypeStruct(piece, f32)] + [jax.ShapeDtypeStruct(piece, bf16)] * (2 * parts - 1),
        compiler_params=params(),
        cost_estimate=pl.CostEstimate(flops=1, bytes_accessed=1, transcendentals=0),
        name="add_core",
    )(place, mine, other)


def activate_kernel(count, *refs):
    total = refs[0][...]
    for ref in refs[1 : 1 + count]:
        total = total + ref[...].astype(f32)
    refs[-1][...] = jnp.tanh(total).astype(bf16)


def activate(own, received, deps=()):
    return pl.pallas_call(
        functools.partial(activate_kernel, len(received)),
        in_specs=[vmem()] * (1 + len(received)) + any_specs(deps),
        out_shape=jax.ShapeDtypeStruct(own.shape, bf16),
        compiler_params=params(),
        cost_estimate=pl.CostEstimate(flops=1, bytes_accessed=1, transcendentals=0),
        name="first_activation",
    )(own, *received, *deps)


def pack_kernel(place_ref, mid_ref, head_ref, first_ref, out_ref, place_out_ref, head_row, arrived):
    for n in range(4):
        place_out_ref[n] = place_ref[n]
    hidden = mid_ref.shape[0]
    copies = [
        pltpu.make_async_copy(mid_ref, out_ref.at[pl.ds(0, hidden), :], arrived.at[0]),
        pltpu.make_async_copy(head_ref, head_row, arrived.at[1]),
    ]
    for copy in copies:
        copy.start()
    copies[1].wait()
    out_ref[pl.ds(hidden, EXTRA), :] = tail_rows(head_row[...])
    copies[0].wait()


def pack(place, mid_weight, head, first):
    hidden, units = mid_weight.shape
    return pl.pallas_call(
        pack_kernel,
        in_specs=[smem()] + [pl.BlockSpec(memory_space=pltpu.HBM)] * 3,
        out_specs=[vmem(), smem()],
        out_shape=[jax.ShapeDtypeStruct((hidden + EXTRA, units), bf16), jax.ShapeDtypeStruct(place.shape, place.dtype)],
        scratch_shapes=[pltpu.VMEM(head.shape, f32), pltpu.SemaphoreType.DMA((2,))],
        compiler_params=params(),
        cost_estimate=pl.CostEstimate(flops=1, bytes_accessed=1, transcendentals=0),
        name="mid_with_head",
    )(place, *[pltpu.with_memory_space_constraint(array, pltpu.HBM) for array in (mid_weight, head)], first)


def two_halves(exact):
    high = exact.astype(bf16)
    low = (exact - high.astype(f32)).astype(bf16)
    return high, low


def tail_rows(exact):
    high, low = two_halves(exact)
    zeros = jnp.zeros((EXTRA - 2, exact.shape[1]), bf16)
    return jnp.concatenate([high, low, zeros], axis=0)


def middle_kernel(chunks, parts, width, *refs):
    pieces = chunks * parts
    place_ref, cot_ref = refs[0], refs[1]
    first_refs = refs[2 : 2 + pieces]
    mid_refs = refs[2 + pieces : 6 + pieces]
    outs = refs[-(3 + parts) :]
    own_ref, value_ref, mid_keep_ref, mid_send_ref = outs[:4]
    send_refs = outs[4:]
    part = place_ref[2]
    block = first_refs[0].shape[0]

    def mid_rows(start):
        return jnp.concatenate([ref[pl.ds(start, width), :] for ref in mid_refs], axis=1)

    def start_of(c, k):
        return pl.multiple_of((c * parts + (part ^ k)) * width, width)

    total = None
    for c in range(chunks):
        for k in range(parts):
            term = jnp.dot(first_refs[c * parts + k][...], mid_rows(start_of(c, k)), preferred_element_type=f32)
            total = term if total is None else total + term
    second_low = jnp.tanh(total).astype(bf16)
    second = second_low.astype(f32)
    heads = jnp.concatenate([ref[pl.ds(pieces * width, EXTRA), :] for ref in mid_refs], axis=1)
    head = heads[0:1].astype(f32) + heads[1:2].astype(f32)
    rows = lax.dot_general(heads, second_low, (((1,), (1,)), ((), ())), preferred_element_type=f32)
    value = rows[0:1] + rows[1:2]
    if width > block:
        value = jnp.concatenate([value, jnp.zeros((1, width - block), f32)], axis=1)
    value_ref[...] = value
    cot = cot_ref[pl.ds(pl.multiple_of(place_ref[3] * block, SUBLANES), block), :1]
    head_part = jnp.sum(cot * second, axis=0, keepdims=True)
    back = (cot * head * (1.0 - second * second)).astype(bf16)
    units = mid_refs[0].shape[1]
    for k in range(parts):
        for c in range(chunks):
            piece = lax.dot_general(
                back, mid_rows(start_of(c, k)), (((1,), (1,)), ((), ())), preferred_element_type=f32
            )
            if k == 0:
                own_ref[pl.ds(c * block, block), :] = piece
            else:
                send_refs[k - 1][pl.ds(c * block, block), :] = piece.astype(bf16)
        if k > 0:
            send_refs[k - 1][pl.ds(chunks * block, EXTRA), :] = tail_rows(value)
    for c in range(chunks):
        for k in range(parts):
            product = lax.dot_general(
                first_refs[c * parts + k][...], back, (((0,), (0,)), ((), ())), preferred_element_type=f32
            ).astype(bf16)
            for p in range(4):
                out = (mid_keep_ref, mid_send_ref)[p % 2]
                out[p // 2, pl.ds(start_of(c, k), width), :] = product[:, p * units : (p + 1) * units]
    for p in range(4):
        out = (mid_keep_ref, mid_send_ref)[p % 2]
        out[p // 2, pl.ds(pieces * width, EXTRA), :] = tail_rows(head_part[:, p * units : (p + 1) * units])


def middle(place, cot, firsts, mids, chunks, parts, width, deps=()):
    block = firsts[0].shape[0]
    partial = jax.ShapeDtypeStruct((2, *mids[0].shape), bf16)
    return pl.pallas_call(
        functools.partial(middle_kernel, chunks, parts, width),
        in_specs=[smem()] + [vmem()] * (1 + len(firsts) + 4) + any_specs(deps),
        out_shape=[
            jax.ShapeDtypeStruct((chunks * block, width), f32),
            jax.ShapeDtypeStruct((1, width), f32),
            partial,
            partial,
        ]
        + [jax.ShapeDtypeStruct((chunks * block + EXTRA, width), bf16)] * (parts - 1),
        compiler_params=params(),
        cost_estimate=pl.CostEstimate(flops=1, bytes_accessed=1, transcendentals=0),
        name="value_layers",
    )(place, cot, *firsts, *mids, *deps)


def add_tail(left, right, hidden):
    body = left[:hidden].astype(f32) + right[:hidden].astype(f32)
    tails = left[hidden:].astype(f32) + right[hidden:].astype(f32)
    return body.astype(bf16), tails[0:1] + tails[1:2]


def mid_add_kernel(keep_ref, other_ref, *refs):
    own_ref, send_ref = refs[-2:]
    hidden = own_ref.shape[0] - EXTRA
    for at, out in enumerate((own_ref, send_ref)):
        body, tail = add_tail(keep_ref[at], other_ref[at], hidden)
        out[pl.ds(0, hidden), :] = body
        out[pl.ds(hidden, EXTRA), :] = tail_rows(tail)


def mid_add(keep, other, deps=()):
    shape = jax.ShapeDtypeStruct(keep.shape[1:], bf16)
    return pl.pallas_call(
        mid_add_kernel,
        in_specs=[vmem()] * 2 + any_specs(deps),
        out_shape=[shape, shape],
        compiler_params=params(),
        cost_estimate=pl.CostEstimate(flops=1, bytes_accessed=1, transcendentals=0),
        name="mid_gradient_add",
    )(keep, other, *deps)


def mid_final_kernel(own_ref, other_ref, *refs):
    out_ref, head_ref, token_ref = refs[-3:]
    token_ref[...] = jnp.zeros(token_ref.shape, f32)
    body, tail = add_tail(own_ref[...], other_ref[...], out_ref.shape[0])
    out_ref[...] = body
    head_ref[...] = tail


def mid_final(own, other, deps=()):
    hidden = own.shape[0] - EXTRA
    return pl.pallas_call(
        mid_final_kernel,
        in_specs=[vmem()] * 2 + any_specs(deps),
        out_shape=[
            jax.ShapeDtypeStruct((hidden, own.shape[1]), bf16),
            jax.ShapeDtypeStruct((1, own.shape[1]), f32),
            jax.ShapeDtypeStruct((SUBLANES, LANES), f32),
        ],
        compiler_params=params(),
        cost_estimate=pl.CostEstimate(flops=1, bytes_accessed=1, transcendentals=0),
        name="mid_gradient_final",
    )(own, other, *deps)


def back_first_kernel(count, own_ref, value_ref, *refs):
    received = refs[:count]
    first_ref, out_ref, tail_ref = refs[count], *refs[-2:]
    block = first_ref.shape[0]
    value = value_ref[...]
    total = own_ref[...]
    for ref in received:
        tail = ref[pl.ds(block, EXTRA), :].astype(f32)
        value = value + (tail[0:1] + tail[1:2])
        total = total + ref[pl.ds(0, block), :].astype(f32)
    first = first_ref[...].astype(f32)
    out_ref[...] = (total * (1.0 - first * first)).astype(bf16)
    tail_ref[...] = tail_rows(value)


def back_first(own, value, received, first, deps):
    block, width = first.shape
    return pl.pallas_call(
        functools.partial(back_first_kernel, len(received)),
        in_specs=[vmem()] * (3 + len(received)) + any_specs(deps),
        out_shape=[jax.ShapeDtypeStruct((rows, width), bf16) for rows in (block, EXTRA)],
        compiler_params=params(),
        cost_estimate=pl.CostEstimate(flops=1, bytes_accessed=1, transcendentals=0),
        name="back_first",
    )(own, value, *received, first, *deps)


def stack_kernel(count, *refs):
    at = 0
    for ref in refs[:count]:
        refs[-1][pl.ds(at, ref.shape[0]), :] = ref[...]
        at += ref.shape[0]


def stack(pieces, deps):
    rows = sum(piece.shape[0] for piece in pieces)
    return pl.pallas_call(
        functools.partial(stack_kernel, len(pieces)),
        in_specs=[vmem()] * len(pieces) + any_specs(deps),
        out_shape=jax.ShapeDtypeStruct((rows, pieces[0].shape[1]), bf16),
        compiler_params=params(),
        cost_estimate=pl.CostEstimate(flops=1, bytes_accessed=1, transcendentals=0),
        name="stack_parts",
    )(*pieces, *deps)


def turn_kernel(count, *refs):
    for ref, out in zip(refs[:count], refs[-count:]):
        out[...] = ref[...].T


def transposed(arrays, deps):
    return pl.pallas_call(
        functools.partial(turn_kernel, len(arrays)),
        in_specs=[vmem()] * len(arrays) + any_specs(deps),
        out_shape=[jax.ShapeDtypeStruct(array.shape[::-1], array.dtype) for array in arrays],
        compiler_params=params(),
        cost_estimate=pl.CostEstimate(flops=1, bytes_accessed=1, transcendentals=0),
        name="transposed_inputs",
    )(*arrays, *deps)


def first_grad_kernel(parts, block, tiles, count, *refs):
    place_ref = refs[0]
    lefts = refs[1 : 1 + count]
    stacks = refs[1 + count : 5 + count]
    out_ref, value_ref, whole = refs[-3:]
    width = out_ref.shape[1]
    step = pl.program_id(0)
    piece = step // tiles ^ place_ref[2]
    column = pl.ds(pl.multiple_of(step % tiles * width, width), width)
    mine = place_ref[3]
    values = [jnp.zeros((1, block), f32)] * 4
    for t, ref in enumerate(stacks):
        at = mine ^ (2 * (t % 2) + t // 2)
        whole[pl.ds(pl.multiple_of(at * block, block), block), :] = ref[
            pl.ds(pl.multiple_of(piece * block, block), block), column
        ]
        tail = ref[pl.ds(parts * block, EXTRA), :block].astype(f32)
        value = tail[0:1] + tail[1:2]
        for q in range(4):
            values[q] = jnp.where(at == q, value, values[q])
    value_ref[...] = jnp.concatenate(values, axis=1)
    start = 0
    for ref in lefts:
        cells = ref.shape[0]
        out_ref[pl.ds(start, cells), :] = jnp.dot(ref[...], whole[...], preferred_element_type=f32).astype(bf16)
        start += cells


def first_grad(place, lefts, stacks, parts, block, deps):
    scenarios = lefts[0].shape[1]
    cells = sum(left.shape[0] for left in lefts)
    width = stacks[0].shape[1]
    tile = min(width, 256)
    tiles = width // tile
    return pl.pallas_call(
        functools.partial(first_grad_kernel, parts, block, tiles, len(lefts)),
        grid=(parts * tiles,),
        in_specs=[smem()] + [vmem()] * (len(lefts) + 4) + any_specs(deps),
        out_specs=[pl.BlockSpec((cells, tile), lambda i: (0, i)), pl.BlockSpec((1, scenarios), lambda i: (0, 0))],
        out_shape=[pltpu.HBM((cells, parts * width), bf16), jax.ShapeDtypeStruct((1, scenarios), f32)],
        scratch_shapes=[pltpu.VMEM((scenarios, tile), bf16)],
        compiler_params=params(),
        cost_estimate=pl.CostEstimate(flops=1, bytes_accessed=1, transcendentals=0),
        name="first_gradient",
    )(place, *lefts, *stacks, *deps)


def local(hist, drift, shocks, shock_table, first_weight, mid_weight, head_weight, cotangent):
    scenarios, rows, columns = hist.shape
    count = lax.axis_size("grid")
    hidden = first_weight.shape[1]
    units = mid_weight.shape[1]
    parts = count // 4
    width = hidden // parts
    block = scenarios // 4
    index = lax.axis_index("grid")
    core, side, part = index & 1, (index >> 1) & 1, index >> 2
    mine = 2 * core + side
    tiles = pltpu.with_memory_space_constraint(to_tiles(hist), pltpu.HBM)

    place = jnp.stack([core, side, part, mine])

    small = [pltpu.with_memory_space_constraint(array, pltpu.HBM) for array in (drift, shocks.T, shock_table.T, cotangent)]
    packed, place = pack(place, mid_weight, head_weight[None, :], small[-1])
    mids = [packed]
    mids += [swap(mids[0], count, 1), swap(mids[0], count, 2)]
    first_rows, last_rows, shifts, band, cot, own_rows, inner = inner_steps(tiles, *small)
    inner = inner if rows > 4 else None
    forward = [(i, i + 1) for i in range(count - 1)]
    backward = [(i + 1, i) for i in range(count - 1)]
    below = lax.ppermute(last_rows, "grid", forward)
    above = lax.ppermute(first_rows, "grid", backward)
    first_weight = pltpu.with_memory_space_constraint(first_weight, pltpu.HBM)
    product = None if inner is None else inner_product(inner, first_weight, width, mids[1:])
    low, high = edge_steps(drift, shifts, band, own_rows, below, above, own_rows if product is None else product)
    keep, send = edge_product(place, low, high, first_weight, product, parts, width)
    mids.append(swap(mids[2], count, 1))

    def density_turn(turn, dep, so_far):
        return density_steps(drift, shifts, band, own_rows, below, above, dep, so_far, turn, 2)

    own, *sends = add_core(place, keep, swap(send, count, 1))
    flips = [2 * by_side + 4 * by_part for by_side, by_part in other_places(parts)]
    received = [swap(piece, count, flip) for piece, flip in zip(sends, flips)]
    first = activate(own, received)
    firsts = [first] + [swap(first, count, 4 * k) for k in range(1, parts)]
    density, token = density_turn(0, first, None)
    own, value, mid_keep, mid_send, *sends = middle(place, cot, firsts, mids, 1, parts, width, [token, mids[1], mids[3]])
    received = [swap(piece, count, 4 * (k + 1)) for k, piece in enumerate(sends)]
    density, token = density_turn(1, sends[-1], density)
    mid_keep, mid_send = mid_add(mid_keep, swap(mid_send, count, 1), [token])
    back, tail = back_first(own, value, received, first, [token, mid_send])
    mid_other = swap(mid_send, count, 2)
    lefts = transposed([low, high] if inner is None else [low, inner, high], [back])
    pieces = [back] + [swap(back, count, 4 * k) for k in range(1, parts)] + [tail]
    stacks = [stack(pieces, [lefts[0], mid_other])]
    stacks += [swap(stacks[0], count, 1), swap(stacks[0], count, 2)]
    grad_mid, grad_head, token = mid_final(mid_keep, mid_other, [stacks[0]])
    stacks.append(swap(stacks[2], count, 1))
    grad_first, value = first_grad(place, lefts, stacks, parts, block, [token])
    value = value.reshape(scenarios)
    return from_tiles(density, hist.shape), value, grad_first, grad_mid, grad_head[0]


def solution(mesh):
    in_specs = (
        P("groups", "grid", None),
        P(None, "grid", None),
        P("groups", None),
        P("groups", None),
        P(("groups", "grid"), None),
        P("groups", "grid"),
        P(("groups", "grid")),
        P("groups"),
    )
    out_specs = (
        P("groups", "grid", None),
        P("groups"),
        P(("groups", "grid"), None),
        P("groups", "grid"),
        P(("groups", "grid")),
    )
    return jax.shard_map(local, mesh=mesh, in_specs=in_specs, out_specs=out_specs, check_vma=False)
```

```python
import functools
import jax
import jax.numpy as jnp
from jax import lax
from jax.experimental import pallas as pl
from jax.experimental.pallas import tpu as pltpu
from jax.sharding import PartitionSpec as P

diffusion_rate = 0.24
VMEM_BYTES = 24 * 1024 * 1024
EXTRA = 16
bf16 = jnp.bfloat16
f32 = jnp.float32


def params():
    return pltpu.CompilerParams(vmem_limit_bytes=VMEM_BYTES)


def scenario_block(scenarios):
    for size in (64, 32, 16):
        if scenarios % size == 0:
            return size
    return scenarios


LANES = 128
SUBLANES = 8
GROUP = 16


def to_tiles(hist):
    scenarios, rows, columns = hist.shape
    high = min(rows, SUBLANES)
    tiles = hist.reshape(scenarios, rows // high, high, columns // LANES, LANES)
    return tiles.transpose(0, 1, 3, 2, 4).reshape(scenarios * rows * (columns // LANES), LANES)


def from_tiles(tiles, shape):
    scenarios, rows, columns = shape
    high = min(rows, SUBLANES)
    parts = tiles.reshape(scenarios, rows // high, columns // LANES, high, LANES)
    return parts.transpose(0, 1, 3, 2, 4).reshape(shape)


def tile_offset(row, lane_tile, rows, lane_tiles):
    high = min(rows, SUBLANES)
    return (row // high * lane_tiles + lane_tile) * high + row % high


def read_row(ref, first_scenario, count, row, rows, columns):
    lane_tiles = columns // LANES
    per = rows * lane_tiles
    return jnp.concatenate(
        [
            ref[pl.ds(first_scenario * per + tile_offset(row, t, rows, lane_tiles), count, stride=per), :]
            for t in range(lane_tiles)
        ],
        axis=1,
    )


def write_row(ref, first_scenario, count, row, rows, columns, values):
    lane_tiles = columns // LANES
    per = rows * lane_tiles
    for t in range(lane_tiles):
        place = pl.ds(first_scenario * per + tile_offset(row, t, rows, lane_tiles), count, stride=per)
        ref[place, :] = values[:, t * LANES : (t + 1) * LANES]


def drift_tail(drift_ref, start):
    pieces = [
        jnp.concatenate([drift_ref[c, start : start + 1], drift_ref[c, start + 1 : start + 2]], axis=1)
        for c in range(2)
    ]
    high, low = two_halves(jnp.concatenate(pieces, axis=0))
    ones = jnp.ones((1, high.shape[1]), bf16)
    zeros = jnp.zeros((EXTRA - 5, high.shape[1]), bf16)
    return jnp.concatenate([high, low, ones, zeros], axis=0)


def band_matrix(columns):
    row = lax.broadcasted_iota(jnp.int32, (columns, columns), 0)
    column = lax.broadcasted_iota(jnp.int32, (columns, columns), 1)
    right = jnp.where(column == row + 1, 1.0, 0.0)
    left = jnp.where(column == row - 1, 1.0, 0.0)
    centre = jnp.where(column == row, 1.0 - 4.0 * diffusion_rate, diffusion_rate * (right + left))
    return centre.astype(bf16), (right - left).astype(bf16)


def half_shifts(levels_ref, table_ref, shift_ref):
    scenarios = levels_ref.shape[1]
    for t in range(levels_ref.shape[0]):
        level = jnp.broadcast_to(levels_ref[t : t + 1, :].astype(f32), (LANES, scenarios)).T
        for c in range(2):
            shift = jnp.zeros(level.shape, f32)
            for n in range(table_ref.shape[1]):
                shift = jnp.where(level == n, 0.5 * table_ref[c : c + 1, n : n + 1], shift)
            shift_ref[2 * t + c] = shift


def wide(values, columns):
    return jnp.concatenate([values] * (columns // LANES), axis=1)


def one_step(rows_of, places, half_drift, band, shift_x, shift_y, pairs, terms, write):
    size, columns = shift_x.shape
    whole = pl.ds(0, columns)

    def density(row):
        return pairs[pl.ds(rows_of[row] * size, size), whole].astype(f32)

    for row in places:
        flux = (half_drift(1, row) + shift_y) * density(row)
        pairs[pl.ds(rows_of[row] * size, size), pl.ds(columns, columns)] = flux.astype(bf16)
    yield
    start = rows_of[places[0]] * size
    count = (rows_of[places[-1]] + 1) * size - start
    terms[pl.ds(start, count), :] = jnp.dot(pairs[pl.ds(start, count), :], band, preferred_element_type=f32)
    yield
    for row in places:
        low = density(row - 1) * ((diffusion_rate + half_drift(0, row - 1)) + shift_x)
        high = density(row + 1) * ((diffusion_rate - half_drift(0, row + 1)) - shift_x)
        write(row, terms[pl.ds(rows_of[row] * size, size), :] + low + high)


def step_stages(segments, read, half_drift, edge, band, shifts, scratch, write):
    pairs, later, terms = scratch
    size, columns = shifts[0].shape
    before, between, after = [
        [row for first, last in segments for row in range(first - more, last + more + 1)] for more in (2, 1, 0)
    ]
    rows_of = {row: k for k, row in enumerate(before)}
    for row, k in rows_of.items():
        pairs[pl.ds(k * size, size), pl.ds(0, columns)] = read(row)

    def write_later(row, density):
        later[pl.ds(rows_of[row] * size, size), pl.ds(0, columns)] = edge(row, density).astype(bf16)

    yield from one_step(rows_of, between, half_drift, band, shifts[0], shifts[1], pairs, terms, write_later)
    yield from one_step(rows_of, after, half_drift, band, shifts[2], shifts[3], later, terms, write)


def interleave(runs):
    ahead, live = list(runs), []
    while ahead or live:
        if ahead:
            live.append(ahead.pop(0))
        for run in list(live):
            if next(run, live) is live:
                live.remove(run)


def two_steps(*args):
    interleave([step_stages(*args)])


def step_scratch(segments, size, columns):
    rows = sum(last - first + 5 for first, last in segments)
    pairs = pltpu.VMEM((rows * size, 2 * columns), bf16)
    return [pairs, pairs, pltpu.VMEM((rows * size, columns), f32)]


def edge_segments(rows):
    return [(0, 1), (rows - 2, rows - 1)] if rows >= 8 else [(0, rows - 1)]


def inner_kernel(
    rows, size, hist_ref, drift_hbm, levels_hbm, table_hbm, cot_hbm,
    first_ref, last_ref, shift_ref, band_ref, cot_ref, rows_ref, inner_ref,
    drift_ref, levels_ref, table_ref, cot_row, arrived, all_shifts, *scratch,
):
    step = pl.program_id(0)
    columns = drift_ref.shape[2]

    @pl.when(step == 0)
    def _():
        sources = ((drift_hbm, drift_ref), (levels_hbm, levels_ref), (table_hbm, table_ref), (cot_hbm, cot_row))
        copies = [pltpu.make_async_copy(*pair, arrived.at[n]) for n, pair in enumerate(sources)]
        for copy in copies:
            copy.start()
        centre, flux = band_matrix(columns)
        band_ref[pl.ds(0, columns), :] = centre
        band_ref[pl.ds(columns, columns), :] = flux
        for copy in copies:
            copy.wait()
        half_shifts(levels_ref, table_ref, all_shifts)
        cot_ref[...] = jnp.broadcast_to(cot_row[...].reshape(1, -1), (LANES, cot_row.shape[0])).T
        for out, start in ((first_ref, 0), (last_ref, rows - 2)):
            out[pl.ds(out.shape[0] - EXTRA, EXTRA), :] = drift_tail(drift_ref, start)

    where = pl.ds(pl.multiple_of(step * size, size), size)
    for n in range(4):
        shift_ref[n] = all_shifts[n, where, :]
    for row in range(rows):
        density = read_row(hist_ref, 0, size, row, rows, columns).astype(bf16)
        rows_ref[:, pl.ds(row * columns, columns)] = density
        if row < 2:
            first_ref[where, pl.ds(row * columns, columns)] = density
        if row >= rows - 2:
            last_ref[where, pl.ds((row - rows + 2) * columns, columns)] = density
    if rows <= 4:
        return
    band = band_ref[...]
    count = len(scratch) // 3
    part = size // count

    def run(n):
        here = pl.ds(n * part, part)

        def write(row, density):
            inner_ref[here, pl.ds((row - 2) * columns, columns)] = density.astype(bf16)

        return step_stages(
            [(2, rows - 3)],
            lambda row: rows_ref[here, pl.ds(row * columns, columns)],
            lambda c, row: 0.5 * drift_ref[c, row : row + 1, :],
            lambda row, density: density,
            band,
            [wide(shift_ref[k, here, :], columns) for k in range(4)],
            scratch[3 * n : 3 * n + 3],
            write,
        )

    interleave([run(n) for n in range(count)])


def inner_steps(tiles, drift, levels, table, cot):
    scenarios = levels.shape[1]
    rows, columns = drift.shape[1:]
    per = tiles.shape[0] // scenarios
    size = scenario_block(scenarios)
    inner = max(rows - 4, 1) * columns
    sent = jax.ShapeDtypeStruct((scenarios + EXTRA, 2 * columns), bf16)
    shifts = jax.ShapeDtypeStruct((4, scenarios, LANES), f32)
    band = jax.ShapeDtypeStruct((2 * columns, columns), bf16)
    return pl.pallas_call(
        functools.partial(inner_kernel, rows, size),
        grid=(scenarios // size,),
        in_specs=[pl.BlockSpec((size * per, LANES), lambda i: (i, 0))] + [pl.BlockSpec(memory_space=pltpu.HBM)] * 4,
        out_specs=[pl.BlockSpec(sent.shape, lambda i: (0, 0))] * 2
        + [
            pl.BlockSpec((4, size, LANES), lambda i: (0, i, 0)),
            pl.BlockSpec(band.shape, lambda i: (0, 0)),
            pl.BlockSpec((scenarios, LANES), lambda i: (0, 0)),
            pl.BlockSpec((size, rows * columns), lambda i: (i, 0)),
            pl.BlockSpec((size, inner), lambda i: (i, 0)),
        ],
        out_shape=[
            sent,
            sent,
            pltpu.HBM(shifts.shape, f32),
            band,
            jax.ShapeDtypeStruct((scenarios, LANES), f32),
            pltpu.HBM((scenarios, rows * columns), bf16),
            jax.ShapeDtypeStruct((scenarios, inner), bf16),
        ],
        scratch_shapes=[
            pltpu.VMEM(drift.shape, f32),
            pltpu.VMEM(levels.shape, levels.dtype),
            pltpu.VMEM(table.shape, f32),
            pltpu.VMEM(cot.shape, f32),
            pltpu.SemaphoreType.DMA((4,)),
            pltpu.VMEM(shifts.shape, f32),
        ]
        + step_scratch([(2, max(rows - 3, 2))], size // 2, columns) * 2,
        compiler_params=params(),
        cost_estimate=pl.CostEstimate(flops=1, bytes_accessed=1, transcendentals=0),
        name="inner_density_steps",
    )(tiles, drift, levels, table, cot)


def halo_drift(ref, columns):
    tail = ref[...].astype(f32)
    both = 0.5 * (tail[0:2] + tail[2:4])
    rows = [[both[c : c + 1, k * columns : (k + 1) * columns] for k in range(2)] for c in range(2)]
    return rows, tail[4:5, :columns]


def with_halo(drift_ref, below_tail, above_tail):
    rows, columns = drift_ref.shape[1:]
    below, below_valid = halo_drift(below_tail, columns)
    above, above_valid = halo_drift(above_tail, columns)

    def half_drift(c, row):
        if row < 0:
            return below[c][row + 2]
        if row >= rows:
            return above[c][row - rows]
        return 0.5 * drift_ref[c, row : row + 1, :]

    def edge(row, density):
        if row < 0:
            return density * below_valid
        if row >= rows:
            return density * above_valid
        return density

    return half_drift, edge


def density_read(rows_ref, below_ref, above_ref, rows, columns):
    def read(row):
        if row < 0:
            return below_ref[:, pl.ds((row + 2) * columns, columns)]
        if row >= rows:
            return above_ref[:, pl.ds((row - rows) * columns, columns)]
        return rows_ref[:, pl.ds(row * columns, columns)]

    return read


def density_kernel(drift_ref, shift_ref, band_ref, rows_ref, below_ref, above_ref, below_tail, above_tail, dep_ref, *refs):
    next_ref, token_ref, *scratch = refs[-5:]
    rows, columns = drift_ref.shape[1:]
    size = shift_ref.shape[1]
    half_drift, edge = with_halo(drift_ref, below_tail, above_tail)
    token_ref[...] = jnp.zeros(token_ref.shape, f32)

    def write(row, density):
        write_row(next_ref, 0, size, row, rows, columns, density)

    read = density_read(rows_ref, below_ref, above_ref, rows, columns)
    shifts = [wide(shift_ref[n], columns) for n in range(4)]
    two_steps([(0, rows - 1)], read, half_drift, edge, band_ref[...], shifts, scratch, write)


def density_specs(drift, shifts, band, own, below, size, place):
    columns = drift.shape[2]
    scenarios = shifts.shape[1]
    halo = pl.BlockSpec((size, 2 * columns), lambda i: (place(i), 0))
    tail = pl.BlockSpec((EXTRA, 2 * columns), lambda i: (scenarios // EXTRA, 0))
    return [
        pl.BlockSpec(drift.shape, lambda i: (0, 0, 0)),
        pl.BlockSpec((4, size, LANES), lambda i: (0, place(i), 0)),
        pl.BlockSpec(band.shape, lambda i: (0, 0)),
        pl.BlockSpec((size, own.shape[1]), lambda i: (place(i), 0)),
        halo,
        halo,
        tail,
        tail,
    ]


def edge_kernel(drift_ref, shift_ref, band_ref, rows_ref, below_ref, above_ref, below_tail, above_tail, dep_ref, *refs):
    low_ref, high_ref, *scratch = refs
    rows, columns = drift_ref.shape[1:]
    half_drift, edge = with_halo(drift_ref, below_tail, above_tail)

    def write(row, density):
        out, at = (low_ref, row) if row < 2 else (high_ref, row - rows + 2)
        out[:, pl.ds(at * columns, columns)] = density.astype(bf16)

    read = density_read(rows_ref, below_ref, above_ref, rows, columns)
    shifts = [wide(shift_ref[n], columns) for n in range(4)]
    two_steps(edge_segments(rows), read, half_drift, edge, band_ref[...], shifts, scratch, write)


def edge_steps(drift, shifts, band, own, below, above, dep):
    scenarios = shifts.shape[1]
    rows, columns = drift.shape[1:]
    size = 2 * scenario_block(scenarios)
    size = size if scenarios % size == 0 else size // 2
    edge = jax.ShapeDtypeStruct((scenarios, 2 * columns), bf16)
    spec = pl.BlockSpec((size, 2 * columns), lambda i: (i, 0))
    return pl.pallas_call(
        edge_kernel,
        grid=(scenarios // size,),
        in_specs=density_specs(drift, shifts, band, own, below, size, lambda i: i) + any_specs([dep]),
        out_specs=[spec, spec],
        out_shape=[edge, edge],
        scratch_shapes=step_scratch(edge_segments(rows), size, columns),
        compiler_params=params(),
        cost_estimate=pl.CostEstimate(flops=1, bytes_accessed=1, transcendentals=0),
        name="edge_density_steps",
    )(drift, shifts, band, own, below, above, below, above, dep)


def density_steps(drift, shifts, band, own, below, above, dep, so_far, turn, turns):
    scenarios = shifts.shape[1]
    rows, columns = drift.shape[1:]
    per = rows * (columns // LANES)
    size = 3 * GROUP if scenarios % (turns * GROUP * 3) == 0 else GROUP
    steps = scenarios // size // turns
    first = turn * steps
    args = [drift, shifts, band, own, below, above, below, above, dep]
    in_specs = density_specs(drift, shifts, band, own, below, size, lambda i: first + i) + any_specs([dep])
    aliases = {}
    if so_far is not None:
        aliases = {len(args): 0}
        args.append(so_far)
        in_specs.append(pl.BlockSpec(memory_space=pltpu.HBM))
    return pl.pallas_call(
        density_kernel,
        grid=(steps,),
        in_specs=in_specs,
        out_specs=[
            pl.BlockSpec((size * per, LANES), lambda i: (first + i, 0)),
            pl.BlockSpec((SUBLANES, LANES), lambda i: (0, 0)),
        ],
        out_shape=[pltpu.HBM((scenarios * per, LANES), f32), jax.ShapeDtypeStruct((SUBLANES, LANES), f32)],
        input_output_aliases=aliases,
        scratch_shapes=step_scratch([(0, rows - 1)], size, columns),
        compiler_params=params(),
        cost_estimate=pl.CostEstimate(flops=1, bytes_accessed=1, transcendentals=0),
        name="density_steps",
    )(*args)


def smem():
    return pl.BlockSpec(memory_space=pltpu.SMEM)


def vmem():
    return pl.BlockSpec(memory_space=pltpu.VMEM)


def swap(values, count, flip):
    return lax.ppermute(values, "grid", [(i, i ^ flip) for i in range(count)])


def inner_product_kernel(count, inputs_ref, *refs):
    weight = jnp.concatenate([ref[...] for ref in refs[:count]], axis=0)
    refs[-1][pl.program_id(0)] = jnp.dot(inputs_ref[...], weight, preferred_element_type=f32)


def inner_product(inner, weight, width, deps):
    scenarios, cells = inner.shape
    total, hidden = weight.shape
    size = (total - cells) // 2
    count = cells // size

    def spec(k):
        return pl.BlockSpec((size, width), lambda n: (1 + k, n))

    return pl.pallas_call(
        functools.partial(inner_product_kernel, count),
        grid=(hidden // width,),
        in_specs=[vmem()] + [spec(k) for k in range(count)] + any_specs(deps),
        out_specs=vmem(),
        out_shape=jax.ShapeDtypeStruct((hidden // width, scenarios, width), f32),
        compiler_params=params(),
        cost_estimate=pl.CostEstimate(flops=1, bytes_accessed=1, transcendentals=0),
        name="inner_product",
    )(inner, *([weight] * count), *deps)


def edge_product_kernel(block, with_inner, place_ref, low_ref, high_ref, top_ref, bottom_ref, *refs):
    keep_ref, send_ref, total = refs[-3:]
    step = pl.program_id(0)
    left = jnp.concatenate([low_ref[...], high_ref[...]], axis=1)
    weight = jnp.concatenate([top_ref[...], bottom_ref[...]], axis=0)
    product = jnp.dot(left, weight, preferred_element_type=f32)
    total[...] = product + refs[0][step] if with_inner else product
    core = place_ref[0]
    for out, half in ((keep_ref, core), (send_ref, 1 - core)):
        for side in range(2):
            start = pl.multiple_of((2 * half + side) * block, block)
            out[side, step] = total[pl.ds(start, block), :].astype(out.dtype)


def edge_product(place, low, high, weight, inner, parts, width):
    scenarios, size = low.shape
    block = scenarios // 4
    last = weight.shape[0] // size - 1
    shape = (2, parts, block, width)
    in_specs = [
        smem(),
        vmem(),
        vmem(),
        pl.BlockSpec((size, width), lambda n: (0, n)),
        pl.BlockSpec((size, width), lambda n: (last, n)),
    ]
    args = [place, low, high, weight, weight]
    if inner is not None:
        in_specs.append(vmem())
        args.append(inner)
    return pl.pallas_call(
        functools.partial(edge_product_kernel, block, inner is not None),
        grid=(parts,),
        in_specs=in_specs,
        out_specs=[vmem(), vmem()],
        out_shape=[jax.ShapeDtypeStruct(shape, f32), jax.ShapeDtypeStruct(shape, bf16)],
        scratch_shapes=[pltpu.VMEM((scenarios, width), f32)],
        compiler_params=params(),
        cost_estimate=pl.CostEstimate(flops=1, bytes_accessed=1, transcendentals=0),
        name="edge_product",
    )(*args)


def any_specs(deps):
    return [pl.BlockSpec(memory_space=pl.ANY)] * len(deps)


def other_places(parts):
    return [(side, part) for side in range(2) for part in range(parts) if side or part]


def add_core_kernel(place_ref, mine_ref, other_ref, own_ref, *send_refs):
    side, part = place_ref[1], place_ref[2]
    own_ref[...] = mine_ref[side, part] + other_ref[side, part].astype(f32)
    for (by_side, by_part), out in zip(other_places(mine_ref.shape[1]), send_refs):
        at = side ^ by_side, part ^ by_part
        out[...] = (mine_ref[at] + other_ref[at].astype(f32)).astype(bf16)


def add_core(place, mine, other):
    parts, *piece = mine.shape[1:]
    return pl.pallas_call(
        add_core_kernel,
        in_specs=[smem(), vmem(), vmem()],
        out_shape=[jax.ShapeDtypeStruct(piece, f32)] + [jax.ShapeDtypeStruct(piece, bf16)] * (2 * parts - 1),
        compiler_params=params(),
        cost_estimate=pl.CostEstimate(flops=1, bytes_accessed=1, transcendentals=0),
        name="add_core",
    )(place, mine, other)


def activate_kernel(count, *refs):
    total = refs[0][...]
    for ref in refs[1 : 1 + count]:
        total = total + ref[...].astype(f32)
    refs[-1][...] = jnp.tanh(total).astype(bf16)


def activate(own, received, deps=()):
    return pl.pallas_call(
        functools.partial(activate_kernel, len(received)),
        in_specs=[vmem()] * (1 + len(received)) + any_specs(deps),
        out_shape=jax.ShapeDtypeStruct(own.shape, bf16),
        compiler_params=params(),
        cost_estimate=pl.CostEstimate(flops=1, bytes_accessed=1, transcendentals=0),
        name="first_activation",
    )(own, *received, *deps)


def pack_kernel(place_ref, mid_ref, head_ref, first_ref, out_ref, place_out_ref, head_row, arrived):
    for n in range(4):
        place_out_ref[n] = place_ref[n]
    hidden = mid_ref.shape[0]
    copies = [
        pltpu.make_async_copy(mid_ref, out_ref.at[pl.ds(0, hidden), :], arrived.at[0]),
        pltpu.make_async_copy(head_ref, head_row, arrived.at[1]),
    ]
    for copy in copies:
        copy.start()
    copies[1].wait()
    out_ref[pl.ds(hidden, EXTRA), :] = tail_rows(head_row[...])
    copies[0].wait()


def pack(place, mid_weight, head, first):
    hidden, units = mid_weight.shape
    return pl.pallas_call(
        pack_kernel,
        in_specs=[smem()] + [pl.BlockSpec(memory_space=pltpu.HBM)] * 3,
        out_specs=[vmem(), smem()],
        out_shape=[jax.ShapeDtypeStruct((hidden + EXTRA, units), bf16), jax.ShapeDtypeStruct(place.shape, place.dtype)],
        scratch_shapes=[pltpu.VMEM(head.shape, f32), pltpu.SemaphoreType.DMA((2,))],
        compiler_params=params(),
        cost_estimate=pl.CostEstimate(flops=1, bytes_accessed=1, transcendentals=0),
        name="mid_with_head",
    )(place, *[pltpu.with_memory_space_constraint(array, pltpu.HBM) for array in (mid_weight, head)], first)


def two_halves(exact):
    high = exact.astype(bf16)
    low = (exact - high.astype(f32)).astype(bf16)
    return high, low


def tail_rows(exact):
    high, low = two_halves(exact)
    zeros = jnp.zeros((EXTRA - 2, exact.shape[1]), bf16)
    return jnp.concatenate([high, low, zeros], axis=0)


def middle_kernel(chunks, parts, width, *refs):
    pieces = chunks * parts
    place_ref, cot_ref = refs[0], refs[1]
    first_refs = refs[2 : 2 + pieces]
    mid_refs = refs[2 + pieces : 6 + pieces]
    outs = refs[-(3 + parts) :]
    own_ref, value_ref, mid_keep_ref, mid_send_ref = outs[:4]
    send_refs = outs[4:]
    part = place_ref[2]
    block = first_refs[0].shape[0]

    def mid_rows(start):
        return jnp.concatenate([ref[pl.ds(start, width), :] for ref in mid_refs], axis=1)

    def start_of(c, k):
        return pl.multiple_of((c * parts + (part ^ k)) * width, width)

    total = None
    for c in range(chunks):
        for k in range(parts):
            term = jnp.dot(first_refs[c * parts + k][...], mid_rows(start_of(c, k)), preferred_element_type=f32)
            total = term if total is None else total + term
    second_low = jnp.tanh(total).astype(bf16)
    second = second_low.astype(f32)
    heads = jnp.concatenate([ref[pl.ds(pieces * width, EXTRA), :] for ref in mid_refs], axis=1)
    head = heads[0:1].astype(f32) + heads[1:2].astype(f32)
    rows = lax.dot_general(heads, second_low, (((1,), (1,)), ((), ())), preferred_element_type=f32)
    value = rows[0:1] + rows[1:2]
    if width > block:
        value = jnp.concatenate([value, jnp.zeros((1, width - block), f32)], axis=1)
    value_ref[...] = value
    cot = cot_ref[pl.ds(pl.multiple_of(place_ref[3] * block, SUBLANES), block), :1]
    head_part = jnp.sum(cot * second, axis=0, keepdims=True)
    back = (cot * head * (1.0 - second * second)).astype(bf16)
    units = mid_refs[0].shape[1]
    for k in range(parts):
        for c in range(chunks):
            piece = lax.dot_general(
                back, mid_rows(start_of(c, k)), (((1,), (1,)), ((), ())), preferred_element_type=f32
            )
            if k == 0:
                own_ref[pl.ds(c * block, block), :] = piece
            else:
                send_refs[k - 1][pl.ds(c * block, block), :] = piece.astype(bf16)
        if k > 0:
            send_refs[k - 1][pl.ds(chunks * block, EXTRA), :] = tail_rows(value)
    for c in range(chunks):
        for k in range(parts):
            product = lax.dot_general(
                first_refs[c * parts + k][...], back, (((0,), (0,)), ((), ())), preferred_element_type=f32
            ).astype(bf16)
            for p in range(4):
                out = (mid_keep_ref, mid_send_ref)[p % 2]
                out[p // 2, pl.ds(start_of(c, k), width), :] = product[:, p * units : (p + 1) * units]
    for p in range(4):
        out = (mid_keep_ref, mid_send_ref)[p % 2]
        out[p // 2, pl.ds(pieces * width, EXTRA), :] = tail_rows(head_part[:, p * units : (p + 1) * units])


def middle(place, cot, firsts, mids, chunks, parts, width, deps=()):
    block = firsts[0].shape[0]
    partial = jax.ShapeDtypeStruct((2, *mids[0].shape), bf16)
    return pl.pallas_call(
        functools.partial(middle_kernel, chunks, parts, width),
        in_specs=[smem()] + [vmem()] * (1 + len(firsts) + 4) + any_specs(deps),
        out_shape=[
            jax.ShapeDtypeStruct((chunks * block, width), f32),
            jax.ShapeDtypeStruct((1, width), f32),
            partial,
            partial,
        ]
        + [jax.ShapeDtypeStruct((chunks * block + EXTRA, width), bf16)] * (parts - 1),
        compiler_params=params(),
        cost_estimate=pl.CostEstimate(flops=1, bytes_accessed=1, transcendentals=0),
        name="value_layers",
    )(place, cot, *firsts, *mids, *deps)


def add_tail(left, right, hidden):
    body = left[:hidden].astype(f32) + right[:hidden].astype(f32)
    tails = left[hidden:].astype(f32) + right[hidden:].astype(f32)
    return body.astype(bf16), tails[0:1] + tails[1:2]


def mid_add_kernel(keep_ref, other_ref, *refs):
    own_ref, send_ref = refs[-2:]
    hidden = own_ref.shape[0] - EXTRA
    for at, out in enumerate((own_ref, send_ref)):
        body, tail = add_tail(keep_ref[at], other_ref[at], hidden)
        out[pl.ds(0, hidden), :] = body
        out[pl.ds(hidden, EXTRA), :] = tail_rows(tail)


def mid_add(keep, other, deps=()):
    shape = jax.ShapeDtypeStruct(keep.shape[1:], bf16)
    return pl.pallas_call(
        mid_add_kernel,
        in_specs=[vmem()] * 2 + any_specs(deps),
        out_shape=[shape, shape],
        compiler_params=params(),
        cost_estimate=pl.CostEstimate(flops=1, bytes_accessed=1, transcendentals=0),
        name="mid_gradient_add",
    )(keep, other, *deps)


def mid_final_kernel(own_ref, other_ref, *refs):
    out_ref, head_ref, token_ref = refs[-3:]
    token_ref[...] = jnp.zeros(token_ref.shape, f32)
    body, tail = add_tail(own_ref[...], other_ref[...], out_ref.shape[0])
    out_ref[...] = body
    head_ref[...] = tail


def mid_final(own, other, deps=()):
    hidden = own.shape[0] - EXTRA
    return pl.pallas_call(
        mid_final_kernel,
        in_specs=[vmem()] * 2 + any_specs(deps),
        out_shape=[
            jax.ShapeDtypeStruct((hidden, own.shape[1]), bf16),
            jax.ShapeDtypeStruct((1, own.shape[1]), f32),
            jax.ShapeDtypeStruct((SUBLANES, LANES), f32),
        ],
        compiler_params=params(),
        cost_estimate=pl.CostEstimate(flops=1, bytes_accessed=1, transcendentals=0),
        name="mid_gradient_final",
    )(own, other, *deps)


def back_first_kernel(count, own_ref, value_ref, *refs):
    received = refs[:count]
    first_ref, out_ref, tail_ref = refs[count], *refs[-2:]
    block = first_ref.shape[0]
    value = value_ref[...]
    total = own_ref[...]
    for ref in received:
        tail = ref[pl.ds(block, EXTRA), :].astype(f32)
        value = value + (tail[0:1] + tail[1:2])
        total = total + ref[pl.ds(0, block), :].astype(f32)
    first = first_ref[...].astype(f32)
    out_ref[...] = (total * (1.0 - first * first)).astype(bf16)
    tail_ref[...] = tail_rows(value)


def back_first(own, value, received, first, deps):
    block, width = first.shape
    return pl.pallas_call(
        functools.partial(back_first_kernel, len(received)),
        in_specs=[vmem()] * (3 + len(received)) + any_specs(deps),
        out_shape=[jax.ShapeDtypeStruct((rows, width), bf16) for rows in (block, EXTRA)],
        compiler_params=params(),
        cost_estimate=pl.CostEstimate(flops=1, bytes_accessed=1, transcendentals=0),
        name="back_first",
    )(own, value, *received, first, *deps)


def stack_kernel(count, *refs):
    at = 0
    for ref in refs[:count]:
        refs[-1][pl.ds(at, ref.shape[0]), :] = ref[...]
        at += ref.shape[0]


def stack(pieces, deps):
    rows = sum(piece.shape[0] for piece in pieces)
    return pl.pallas_call(
        functools.partial(stack_kernel, len(pieces)),
        in_specs=[vmem()] * len(pieces) + any_specs(deps),
        out_shape=jax.ShapeDtypeStruct((rows, pieces[0].shape[1]), bf16),
        compiler_params=params(),
        cost_estimate=pl.CostEstimate(flops=1, bytes_accessed=1, transcendentals=0),
        name="stack_parts",
    )(*pieces, *deps)


def turn_kernel(count, *refs):
    out_ref = refs[-1]
    at = 0
    for ref in refs[:count]:
        out_ref[pl.ds(at, ref.shape[1]), :] = ref[...].T
        at += ref.shape[1]


def transposed(arrays, deps):
    cells = sum(array.shape[1] for array in arrays)
    return pl.pallas_call(
        functools.partial(turn_kernel, len(arrays)),
        in_specs=[vmem()] * len(arrays) + any_specs(deps),
        out_shape=jax.ShapeDtypeStruct((cells, arrays[0].shape[0]), bf16),
        compiler_params=params(),
        cost_estimate=pl.CostEstimate(flops=1, bytes_accessed=1, transcendentals=0),
        name="transposed_inputs",
    )(*arrays, *deps)


def first_grad_kernel(parts, block, tiles, *refs):
    place_ref, left_ref = refs[:2]
    stacks = refs[2:6]
    out_ref, value_ref, whole = refs[-3:]
    width = out_ref.shape[1]
    step = pl.program_id(0)
    piece = step // tiles ^ place_ref[2]
    column = pl.ds(pl.multiple_of(step % tiles * width, width), width)
    mine = place_ref[3]
    values = [jnp.zeros((1, block), f32)] * 4
    for t, ref in enumerate(stacks):
        at = mine ^ (2 * (t % 2) + t // 2)
        whole[pl.ds(pl.multiple_of(at * block, block), block), :] = ref[
            pl.ds(pl.multiple_of(piece * block, block), block), column
        ]
        tail = ref[pl.ds(parts * block, EXTRA), :block].astype(f32)
        value = tail[0:1] + tail[1:2]
        for q in range(4):
            values[q] = jnp.where(at == q, value, values[q])
    value_ref[...] = jnp.concatenate(values, axis=1).reshape(4 * block)
    out_ref[...] = jnp.dot(left_ref[...], whole[...], preferred_element_type=f32).astype(bf16)


def first_grad(place, left, stacks, parts, block, deps):
    cells, scenarios = left.shape
    width = stacks[0].shape[1]
    tile = min(width, 256)
    tiles = width // tile
    return pl.pallas_call(
        functools.partial(first_grad_kernel, parts, block, tiles),
        grid=(parts * tiles,),
        in_specs=[smem()] + [vmem()] * 5 + any_specs(deps),
        out_specs=[pl.BlockSpec((cells, tile), lambda i: (0, i)), pl.BlockSpec((scenarios,), lambda i: (0,))],
        out_shape=[pltpu.HBM((cells, parts * width), bf16), jax.ShapeDtypeStruct((scenarios,), f32)],
        scratch_shapes=[pltpu.VMEM((scenarios, tile), bf16)],
        compiler_params=params(),
        cost_estimate=pl.CostEstimate(flops=1, bytes_accessed=1, transcendentals=0),
        name="first_gradient",
    )(place, left, *stacks, *deps)


def local(hist, drift, shocks, shock_table, first_weight, mid_weight, head_weight, cotangent):
    scenarios, rows, columns = hist.shape
    count = lax.axis_size("grid")
    hidden = first_weight.shape[1]
    units = mid_weight.shape[1]
    parts = count // 4
    width = hidden // parts
    block = scenarios // 4
    index = lax.axis_index("grid")
    core, side, part = index & 1, (index >> 1) & 1, index >> 2
    mine = 2 * core + side
    tiles = pltpu.with_memory_space_constraint(to_tiles(hist), pltpu.HBM)

    place = jnp.stack([core, side, part, mine])

    small = [pltpu.with_memory_space_constraint(array, pltpu.HBM) for array in (drift, shocks.T, shock_table.T, cotangent)]
    packed, place = pack(place, mid_weight, head_weight[None, :], small[-1])
    mids = [packed]
    mids += [swap(mids[0], count, 1), swap(mids[0], count, 2)]
    first_rows, last_rows, shifts, band, cot, own_rows, inner = inner_steps(tiles, *small)
    inner = inner if rows > 4 else None
    forward = [(i, i + 1) for i in range(count - 1)]
    backward = [(i + 1, i) for i in range(count - 1)]
    below = lax.ppermute(last_rows, "grid", forward)
    above = lax.ppermute(first_rows, "grid", backward)
    first_weight = pltpu.with_memory_space_constraint(first_weight, pltpu.HBM)
    product = None if inner is None else inner_product(inner, first_weight, width, mids[1:])
    low, high = edge_steps(drift, shifts, band, own_rows, below, above, own_rows if product is None else product)
    keep, send = edge_product(place, low, high, first_weight, product, parts, width)
    mids.append(swap(mids[2], count, 1))

    def density_turn(turn, dep, so_far):
        return density_steps(drift, shifts, band, own_rows, below, above, dep, so_far, turn, 2)

    own, *sends = add_core(place, keep, swap(send, count, 1))
    flips = [2 * by_side + 4 * by_part for by_side, by_part in other_places(parts)]
    received = [swap(piece, count, flip) for piece, flip in zip(sends, flips)]
    first = activate(own, received)
    firsts = [first] + [swap(first, count, 4 * k) for k in range(1, parts)]
    density, token = density_turn(0, first, None)
    own, value, mid_keep, mid_send, *sends = middle(place, cot, firsts, mids, 1, parts, width, [token, mids[1], mids[3]])
    received = [swap(piece, count, 4 * (k + 1)) for k, piece in enumerate(sends)]
    density, token = density_turn(1, sends[-1], density)
    back, tail = back_first(own, value, received, first, [token])
    mid_keep, mid_send = mid_add(mid_keep, swap(mid_send, count, 1), [back])
    mid_other = swap(mid_send, count, 2)
    left = transposed([low, high] if inner is None else [low, inner, high], [back])
    pieces = [back] + [swap(back, count, 4 * k) for k in range(1, parts)] + [tail]
    stacks = [stack(pieces, [left, mid_other])]
    stacks += [swap(stacks[0], count, 1), swap(stacks[0], count, 2)]
    grad_mid, grad_head, token = mid_final(mid_keep, mid_other, [stacks[0]])
    stacks.append(swap(stacks[2], count, 1))
    grad_first, value = first_grad(place, left, stacks, parts, block, [token])
    return from_tiles(density, hist.shape), value, grad_first, grad_mid, grad_head[0]


def solution(mesh):
    in_specs = (
        P("groups", "grid", None),
        P(None, "grid", None),
        P("groups", None),
        P("groups", None),
        P(("groups", "grid"), None),
        P("groups", "grid"),
        P(("groups", "grid")),
        P("groups"),
    )
    out_specs = (
        P("groups", "grid", None),
        P("groups"),
        P(("groups", "grid"), None),
        P("groups", "grid"),
        P(("groups", "grid")),
    )
    return jax.shard_map(local, mesh=mesh, in_specs=in_specs, out_specs=out_specs, check_vma=False)
```

```python
import functools
import jax
import jax.numpy as jnp
from jax import lax
from jax.experimental import pallas as pl
from jax.experimental.pallas import tpu as pltpu
from jax.sharding import PartitionSpec as P

diffusion_rate = 0.24
VMEM_BYTES = 24 * 1024 * 1024
EXTRA = 16
bf16 = jnp.bfloat16
f32 = jnp.float32


def params():
    return pltpu.CompilerParams(vmem_limit_bytes=VMEM_BYTES)


def scenario_block(scenarios):
    for size in (64, 32, 16):
        if scenarios % size == 0:
            return size
    return scenarios


LANES = 128
SUBLANES = 8
GROUP = 16


def to_tiles(hist):
    scenarios, rows, columns = hist.shape
    high = min(rows, SUBLANES)
    tiles = hist.reshape(scenarios, rows // high, high, columns // LANES, LANES)
    return tiles.transpose(0, 1, 3, 2, 4).reshape(scenarios * rows * (columns // LANES), LANES)


def from_tiles(tiles, shape):
    scenarios, rows, columns = shape
    high = min(rows, SUBLANES)
    parts = tiles.reshape(scenarios, rows // high, columns // LANES, high, LANES)
    return parts.transpose(0, 1, 3, 2, 4).reshape(shape)


def tile_offset(row, lane_tile, rows, lane_tiles):
    high = min(rows, SUBLANES)
    return (row // high * lane_tiles + lane_tile) * high + row % high


def read_row(ref, first_scenario, count, row, rows, columns):
    lane_tiles = columns // LANES
    per = rows * lane_tiles
    return jnp.concatenate(
        [
            ref[pl.ds(first_scenario * per + tile_offset(row, t, rows, lane_tiles), count, stride=per), :]
            for t in range(lane_tiles)
        ],
        axis=1,
    )


def write_row(ref, first_scenario, count, row, rows, columns, values):
    lane_tiles = columns // LANES
    per = rows * lane_tiles
    for t in range(lane_tiles):
        place = pl.ds(first_scenario * per + tile_offset(row, t, rows, lane_tiles), count, stride=per)
        ref[place, :] = values[:, t * LANES : (t + 1) * LANES]


def drift_tail(drift_ref, start):
    pieces = [
        jnp.concatenate([drift_ref[c, start : start + 1], drift_ref[c, start + 1 : start + 2]], axis=1)
        for c in range(2)
    ]
    high, low = two_halves(jnp.concatenate(pieces, axis=0))
    ones = jnp.ones((1, high.shape[1]), bf16)
    zeros = jnp.zeros((EXTRA - 5, high.shape[1]), bf16)
    return jnp.concatenate([high, low, ones, zeros], axis=0)


def band_matrix(columns):
    row = lax.broadcasted_iota(jnp.int32, (columns, columns), 0)
    column = lax.broadcasted_iota(jnp.int32, (columns, columns), 1)
    right = jnp.where(column == row + 1, 1.0, 0.0)
    left = jnp.where(column == row - 1, 1.0, 0.0)
    centre = jnp.where(column == row, 1.0 - 4.0 * diffusion_rate, diffusion_rate * (right + left))
    return centre.astype(bf16), (right - left).astype(bf16)


def half_shifts(levels_ref, table_ref, shift_ref):
    scenarios = levels_ref.shape[1]
    for t in range(levels_ref.shape[0]):
        level = jnp.broadcast_to(levels_ref[t : t + 1, :].astype(f32), (LANES, scenarios)).T
        for c in range(2):
            shift = jnp.zeros(level.shape, f32)
            for n in range(table_ref.shape[1]):
                shift = jnp.where(level == n, 0.5 * table_ref[c : c + 1, n : n + 1], shift)
            shift_ref[2 * t + c] = shift


def wide(values, columns):
    return jnp.concatenate([values] * (columns // LANES), axis=1)


def one_step(rows_of, places, half_drift, band, shift_x, shift_y, pairs, terms, write):
    size, columns = shift_x.shape
    whole = pl.ds(0, columns)

    def density(row):
        return pairs[pl.ds(rows_of[row] * size, size), whole].astype(f32)

    for row in places:
        flux = (half_drift(1, row) + shift_y) * density(row)
        pairs[pl.ds(rows_of[row] * size, size), pl.ds(columns, columns)] = flux.astype(bf16)
    yield
    start = rows_of[places[0]] * size
    count = (rows_of[places[-1]] + 1) * size - start
    terms[pl.ds(start, count), :] = jnp.dot(pairs[pl.ds(start, count), :], band, preferred_element_type=f32)
    yield
    for row in places:
        low = density(row - 1) * ((diffusion_rate + half_drift(0, row - 1)) + shift_x)
        high = density(row + 1) * ((diffusion_rate - half_drift(0, row + 1)) - shift_x)
        write(row, terms[pl.ds(rows_of[row] * size, size), :] + low + high)


def step_stages(segments, read, half_drift, edge, band, shifts, scratch, write):
    pairs, later, terms = scratch
    size, columns = shifts[0].shape
    before, between, after = [
        [row for first, last in segments for row in range(first - more, last + more + 1)] for more in (2, 1, 0)
    ]
    rows_of = {row: k for k, row in enumerate(before)}
    for row, k in rows_of.items():
        pairs[pl.ds(k * size, size), pl.ds(0, columns)] = read(row)

    def write_later(row, density):
        later[pl.ds(rows_of[row] * size, size), pl.ds(0, columns)] = edge(row, density).astype(bf16)

    yield from one_step(rows_of, between, half_drift, band, shifts[0], shifts[1], pairs, terms, write_later)
    yield from one_step(rows_of, after, half_drift, band, shifts[2], shifts[3], later, terms, write)


def interleave(runs):
    ahead, live = list(runs), []
    while ahead or live:
        if ahead:
            live.append(ahead.pop(0))
        for run in list(live):
            if next(run, live) is live:
                live.remove(run)


def two_steps(*args):
    interleave([step_stages(*args)])


def step_scratch(segments, size, columns):
    rows = sum(last - first + 5 for first, last in segments)
    pairs = pltpu.VMEM((rows * size, 2 * columns), bf16)
    return [pairs, pairs, pltpu.VMEM((rows * size, columns), f32)]


def edge_segments(rows):
    return [(0, 1), (rows - 2, rows - 1)] if rows >= 8 else [(0, rows - 1)]


def inner_kernel(
    rows, size, place_ref, hist_ref, drift_hbm, levels_hbm, table_hbm, cot_hbm,
    place_out_ref, first_ref, last_ref, shift_ref, band_ref, cot_ref, rows_ref, inner_ref,
    drift_ref, levels_ref, table_ref, cot_row, arrived, all_shifts, *scratch,
):
    step = pl.program_id(0)
    columns = drift_ref.shape[2]

    @pl.when(step == 0)
    def _():
        for n in range(4):
            place_out_ref[n] = place_ref[n]
        sources = ((drift_hbm, drift_ref), (levels_hbm, levels_ref), (table_hbm, table_ref), (cot_hbm, cot_row))
        copies = [pltpu.make_async_copy(*pair, arrived.at[n]) for n, pair in enumerate(sources)]
        for copy in copies:
            copy.start()
        centre, flux = band_matrix(columns)
        band_ref[pl.ds(0, columns), :] = centre
        band_ref[pl.ds(columns, columns), :] = flux
        for copy in copies:
            copy.wait()
        half_shifts(levels_ref, table_ref, all_shifts)
        cot_ref[...] = jnp.broadcast_to(cot_row[...].reshape(1, -1), (LANES, cot_row.shape[0])).T
        for out, start in ((first_ref, 0), (last_ref, rows - 2)):
            out[pl.ds(out.shape[0] - EXTRA, EXTRA), :] = drift_tail(drift_ref, start)

    where = pl.ds(pl.multiple_of(step * size, size), size)
    for n in range(4):
        shift_ref[n] = all_shifts[n, where, :]
    for row in range(rows):
        density = read_row(hist_ref, 0, size, row, rows, columns).astype(bf16)
        rows_ref[:, pl.ds(row * columns, columns)] = density
        if row < 2:
            first_ref[where, pl.ds(row * columns, columns)] = density
        if row >= rows - 2:
            last_ref[where, pl.ds((row - rows + 2) * columns, columns)] = density
    if rows <= 4:
        return
    band = band_ref[...]
    count = len(scratch) // 3
    part = size // count

    def run(n):
        here = pl.ds(n * part, part)

        def write(row, density):
            inner_ref[here, pl.ds((row - 2) * columns, columns)] = density.astype(bf16)

        return step_stages(
            [(2, rows - 3)],
            lambda row: rows_ref[here, pl.ds(row * columns, columns)],
            lambda c, row: 0.5 * drift_ref[c, row : row + 1, :],
            lambda row, density: density,
            band,
            [wide(shift_ref[k, here, :], columns) for k in range(4)],
            scratch[3 * n : 3 * n + 3],
            write,
        )

    interleave([run(n) for n in range(count)])


def inner_steps(place, tiles, drift, levels, table, cot):
    scenarios = levels.shape[1]
    rows, columns = drift.shape[1:]
    per = tiles.shape[0] // scenarios
    size = scenario_block(scenarios)
    inner = max(rows - 4, 1) * columns
    sent = jax.ShapeDtypeStruct((scenarios + EXTRA, 2 * columns), bf16)
    shifts = jax.ShapeDtypeStruct((4, scenarios, LANES), f32)
    band = jax.ShapeDtypeStruct((2 * columns, columns), bf16)
    return pl.pallas_call(
        functools.partial(inner_kernel, rows, size),
        grid=(scenarios // size,),
        in_specs=[smem(), pl.BlockSpec((size * per, LANES), lambda i: (i, 0))] + [pl.BlockSpec(memory_space=pltpu.HBM)] * 4,
        out_specs=[smem()]
        + [pl.BlockSpec(sent.shape, lambda i: (0, 0))] * 2
        + [
            pl.BlockSpec((4, size, LANES), lambda i: (0, i, 0)),
            pl.BlockSpec(band.shape, lambda i: (0, 0)),
            pl.BlockSpec((scenarios, LANES), lambda i: (0, 0)),
            pl.BlockSpec((size, rows * columns), lambda i: (i, 0)),
            pl.BlockSpec((size, inner), lambda i: (i, 0)),
        ],
        out_shape=[
            jax.ShapeDtypeStruct(place.shape, place.dtype),
            sent,
            sent,
            pltpu.HBM(shifts.shape, f32),
            band,
            jax.ShapeDtypeStruct((scenarios, LANES), f32),
            pltpu.HBM((scenarios, rows * columns), bf16),
            jax.ShapeDtypeStruct((scenarios, inner), bf16),
        ],
        scratch_shapes=[
            pltpu.VMEM(drift.shape, f32),
            pltpu.VMEM(levels.shape, levels.dtype),
            pltpu.VMEM(table.shape, f32),
            pltpu.VMEM(cot.shape, f32),
            pltpu.SemaphoreType.DMA((4,)),
            pltpu.VMEM(shifts.shape, f32),
        ]
        + step_scratch([(2, max(rows - 3, 2))], size // 2, columns) * 2,
        compiler_params=params(),
        cost_estimate=pl.CostEstimate(flops=1, bytes_accessed=1, transcendentals=0),
        name="inner_density_steps",
    )(place, tiles, drift, levels, table, cot)


def halo_drift(ref, columns):
    tail = ref[...].astype(f32)
    both = 0.5 * (tail[0:2] + tail[2:4])
    rows = [[both[c : c + 1, k * columns : (k + 1) * columns] for k in range(2)] for c in range(2)]
    return rows, tail[4:5, :columns]


def with_halo(drift_ref, below_tail, above_tail):
    rows, columns = drift_ref.shape[1:]
    below, below_valid = halo_drift(below_tail, columns)
    above, above_valid = halo_drift(above_tail, columns)

    def half_drift(c, row):
        if row < 0:
            return below[c][row + 2]
        if row >= rows:
            return above[c][row - rows]
        return 0.5 * drift_ref[c, row : row + 1, :]

    def edge(row, density):
        if row < 0:
            return density * below_valid
        if row >= rows:
            return density * above_valid
        return density

    return half_drift, edge


def density_read(rows_ref, below_ref, above_ref, rows, columns):
    def read(row):
        if row < 0:
            return below_ref[:, pl.ds((row + 2) * columns, columns)]
        if row >= rows:
            return above_ref[:, pl.ds((row - rows) * columns, columns)]
        return rows_ref[:, pl.ds(row * columns, columns)]

    return read


def density_kernel(drift_ref, shift_ref, band_ref, rows_ref, below_ref, above_ref, below_tail, above_tail, dep_ref, *refs):
    next_ref, token_ref, *scratch = refs[-5:]
    rows, columns = drift_ref.shape[1:]
    size = shift_ref.shape[1]
    half_drift, edge = with_halo(drift_ref, below_tail, above_tail)
    token_ref[...] = jnp.zeros(token_ref.shape, f32)

    def write(row, density):
        write_row(next_ref, 0, size, row, rows, columns, density)

    read = density_read(rows_ref, below_ref, above_ref, rows, columns)
    shifts = [wide(shift_ref[n], columns) for n in range(4)]
    two_steps([(0, rows - 1)], read, half_drift, edge, band_ref[...], shifts, scratch, write)


def density_specs(drift, shifts, band, own, below, size, place):
    columns = drift.shape[2]
    scenarios = shifts.shape[1]
    halo = pl.BlockSpec((size, 2 * columns), lambda i: (place(i), 0))
    tail = pl.BlockSpec((EXTRA, 2 * columns), lambda i: (scenarios // EXTRA, 0))
    return [
        pl.BlockSpec(drift.shape, lambda i: (0, 0, 0)),
        pl.BlockSpec((4, size, LANES), lambda i: (0, place(i), 0)),
        pl.BlockSpec(band.shape, lambda i: (0, 0)),
        pl.BlockSpec((size, own.shape[1]), lambda i: (place(i), 0)),
        halo,
        halo,
        tail,
        tail,
    ]


def edge_kernel(drift_ref, shift_ref, band_ref, rows_ref, below_ref, above_ref, below_tail, above_tail, dep_ref, *refs):
    low_ref, high_ref, *scratch = refs
    rows, columns = drift_ref.shape[1:]
    half_drift, edge = with_halo(drift_ref, below_tail, above_tail)

    def write(row, density):
        out, at = (low_ref, row) if row < 2 else (high_ref, row - rows + 2)
        out[:, pl.ds(at * columns, columns)] = density.astype(bf16)

    read = density_read(rows_ref, below_ref, above_ref, rows, columns)
    shifts = [wide(shift_ref[n], columns) for n in range(4)]
    two_steps(edge_segments(rows), read, half_drift, edge, band_ref[...], shifts, scratch, write)


def edge_steps(drift, shifts, band, own, below, above, dep):
    scenarios = shifts.shape[1]
    rows, columns = drift.shape[1:]
    size = 2 * scenario_block(scenarios)
    size = size if scenarios % size == 0 else size // 2
    edge = jax.ShapeDtypeStruct((scenarios, 2 * columns), bf16)
    spec = pl.BlockSpec((size, 2 * columns), lambda i: (i, 0))
    return pl.pallas_call(
        edge_kernel,
        grid=(scenarios // size,),
        in_specs=density_specs(drift, shifts, band, own, below, size, lambda i: i) + any_specs([dep]),
        out_specs=[spec, spec],
        out_shape=[edge, edge],
        scratch_shapes=step_scratch(edge_segments(rows), size, columns),
        compiler_params=params(),
        cost_estimate=pl.CostEstimate(flops=1, bytes_accessed=1, transcendentals=0),
        name="edge_density_steps",
    )(drift, shifts, band, own, below, above, below, above, dep)


def density_steps(drift, shifts, band, own, below, above, dep, so_far, turn, turns):
    scenarios = shifts.shape[1]
    rows, columns = drift.shape[1:]
    per = rows * (columns // LANES)
    size = 3 * GROUP if scenarios % (turns * GROUP * 3) == 0 else GROUP
    steps = scenarios // size // turns
    first = turn * steps
    args = [drift, shifts, band, own, below, above, below, above, dep]
    in_specs = density_specs(drift, shifts, band, own, below, size, lambda i: first + i) + any_specs([dep])
    aliases = {}
    if so_far is not None:
        aliases = {len(args): 0}
        args.append(so_far)
        in_specs.append(pl.BlockSpec(memory_space=pltpu.HBM))
    return pl.pallas_call(
        density_kernel,
        grid=(steps,),
        in_specs=in_specs,
        out_specs=[
            pl.BlockSpec((size * per, LANES), lambda i: (first + i, 0)),
            pl.BlockSpec((SUBLANES, LANES), lambda i: (0, 0)),
        ],
        out_shape=[pltpu.HBM((scenarios * per, LANES), f32), jax.ShapeDtypeStruct((SUBLANES, LANES), f32)],
        input_output_aliases=aliases,
        scratch_shapes=step_scratch([(0, rows - 1)], size, columns),
        compiler_params=params(),
        cost_estimate=pl.CostEstimate(flops=1, bytes_accessed=1, transcendentals=0),
        name="density_steps",
    )(*args)


def smem():
    return pl.BlockSpec(memory_space=pltpu.SMEM)


def vmem():
    return pl.BlockSpec(memory_space=pltpu.VMEM)


def swap(values, count, flip):
    return lax.ppermute(values, "grid", [(i, i ^ flip) for i in range(count)])


def inner_product_kernel(count, tiles, inputs_ref, *refs):
    weight = jnp.concatenate([ref[...] for ref in refs[:count]], axis=0)
    step = pl.program_id(0)
    tile = weight.shape[1]
    column = pl.ds(pl.multiple_of(step % tiles * tile, tile), tile)
    refs[-1][step // tiles, :, column] = jnp.dot(inputs_ref[...], weight, preferred_element_type=f32)


def inner_product(inner, weight, width, deps):
    scenarios, cells = inner.shape
    total, hidden = weight.shape
    size = (total - cells) // 2
    count = cells // size

    tile = min(width, 256)

    def spec(k):
        return pl.BlockSpec((size, tile), lambda n: (1 + k, n))

    return pl.pallas_call(
        functools.partial(inner_product_kernel, count, width // tile),
        grid=(hidden // tile,),
        in_specs=[vmem()] + [spec(k) for k in range(count)] + any_specs(deps),
        out_specs=vmem(),
        out_shape=jax.ShapeDtypeStruct((hidden // width, scenarios, width), f32),
        compiler_params=params(),
        cost_estimate=pl.CostEstimate(flops=1, bytes_accessed=1, transcendentals=0),
        name="inner_product",
    )(inner, *([weight] * count), *deps)


def edge_product_kernel(block, with_inner, place_ref, head_ref, low_ref, high_ref, top_ref, bottom_ref, *refs):
    keep_ref, send_ref, total = refs[-3:]
    step = pl.program_id(0)
    left = jnp.concatenate([low_ref[...], high_ref[...]], axis=1)
    weight = jnp.concatenate([top_ref[...], bottom_ref[...]], axis=0)
    product = jnp.dot(left, weight, preferred_element_type=f32)
    total[...] = product + refs[0][step] if with_inner else product
    core = place_ref[0]
    for out, half in ((keep_ref, core), (send_ref, 1 - core)):
        for side in range(2):
            start = pl.multiple_of((2 * half + side) * block, block)
            out[side, step, pl.ds(0, block), :] = total[pl.ds(start, block), :].astype(out.dtype)
    for side in range(2):
        send_ref[side, step, pl.ds(block, EXTRA), :] = tail_rows(padded(head_ref[...], send_ref.shape[-1]))


def padded(row, width):
    return jnp.concatenate([row, jnp.zeros((1, width - row.shape[1]), f32)], axis=1)


def edge_product(place, head, low, high, weight, inner, parts, width):
    scenarios, size = low.shape
    block = scenarios // 4
    last = weight.shape[0] // size - 1
    in_specs = [
        smem(),
        pl.BlockSpec(head.shape, lambda n: (0, 0)),
        vmem(),
        vmem(),
        pl.BlockSpec((size, width), lambda n: (0, n)),
        pl.BlockSpec((size, width), lambda n: (last, n)),
    ]
    args = [place, head, low, high, weight, weight]
    if inner is not None:
        in_specs.append(vmem())
        args.append(inner)
    return pl.pallas_call(
        functools.partial(edge_product_kernel, block, inner is not None),
        grid=(parts,),
        in_specs=in_specs,
        out_specs=[vmem(), vmem()],
        out_shape=[
            jax.ShapeDtypeStruct((2, parts, block, width), f32),
            jax.ShapeDtypeStruct((2, parts, block + EXTRA, width), bf16),
        ],
        scratch_shapes=[pltpu.VMEM((scenarios, width), f32)],
        compiler_params=params(),
        cost_estimate=pl.CostEstimate(flops=1, bytes_accessed=1, transcendentals=0),
        name="edge_product",
    )(*args)


def any_specs(deps):
    return [pl.BlockSpec(memory_space=pl.ANY)] * len(deps)


def other_places(parts):
    return [(side, part) for side in range(2) for part in range(parts) if side or part]


def add_core_kernel(place_ref, head_ref, mine_ref, other_ref, own_ref, heads_ref, *send_refs):
    side, part = place_ref[1], place_ref[2]
    block = mine_ref.shape[2]
    units = head_ref.shape[1]
    rows = pl.ds(0, block)
    tail = other_ref[0, 0, pl.ds(block, EXTRA), :].astype(f32)
    core_head = tail[0:1] + tail[1:2]
    own_head = padded(head_ref[...], core_head.shape[1])
    heads_ref[0:1, :] = own_head[:, :units]
    heads_ref[1:2, :] = core_head[:, :units]
    own_ref[...] = mine_ref[side, part] + other_ref[side, part, rows, :].astype(f32)
    for (by_side, by_part), out in zip(other_places(mine_ref.shape[1]), send_refs):
        at = side ^ by_side, part ^ by_part
        out[rows, :] = (mine_ref[at] + other_ref[(*at, rows, slice(None))].astype(f32)).astype(bf16)
        if by_part == 0:
            pieces = [piece for head in (own_head, core_head) for piece in two_halves(head)]
            pieces.append(jnp.zeros((EXTRA - 4, own_head.shape[1]), bf16))
            out[pl.ds(block, EXTRA), :] = jnp.concatenate(pieces, axis=0)


def add_core(place, head, mine, other):
    parts, block, width = mine.shape[1:]
    sends = [
        jax.ShapeDtypeStruct((block if by_part else block + EXTRA, width), bf16) for _, by_part in other_places(parts)
    ]
    return pl.pallas_call(
        add_core_kernel,
        in_specs=[smem(), vmem(), vmem(), vmem()],
        out_shape=[jax.ShapeDtypeStruct((block, width), f32), jax.ShapeDtypeStruct((2, head.shape[1]), f32)] + sends,
        compiler_params=params(),
        cost_estimate=pl.CostEstimate(flops=1, bytes_accessed=1, transcendentals=0),
        name="add_core",
    )(place, head, mine, other)


def activate_kernel(own_ref, heads_ref, *refs):
    received, (first_ref, head_row_ref) = refs[:-2], refs[-2:]
    block = own_ref.shape[0]
    units = heads_ref.shape[1]
    total = own_ref[...]
    heads = [heads_ref[0:1, :], heads_ref[1:2, :]]
    for ref in received:
        total = total + ref[pl.ds(0, block), :].astype(f32)
        if ref.shape[0] > block:
            tail = ref[pl.ds(block, EXTRA), :].astype(f32)
            heads += [(tail[0:1] + tail[1:2])[:, :units], (tail[2:3] + tail[3:4])[:, :units]]
    first_ref[...] = jnp.tanh(total).astype(bf16)
    head_row_ref[...] = jnp.concatenate(heads, axis=1)


def activate(own, heads, received):
    return pl.pallas_call(
        activate_kernel,
        in_specs=[vmem()] * (2 + len(received)),
        out_shape=[jax.ShapeDtypeStruct(own.shape, bf16), jax.ShapeDtypeStruct((1, 4 * heads.shape[1]), f32)],
        compiler_params=params(),
        cost_estimate=pl.CostEstimate(flops=1, bytes_accessed=1, transcendentals=0),
        name="first_activation",
    )(own, heads, *received)


def two_halves(exact):
    high = exact.astype(bf16)
    low = (exact - high.astype(f32)).astype(bf16)
    return high, low


def tail_rows(exact):
    high, low = two_halves(exact)
    zeros = jnp.zeros((EXTRA - 2, exact.shape[1]), bf16)
    return jnp.concatenate([high, low, zeros], axis=0)


def middle_kernel(chunks, parts, width, *refs):
    pieces = chunks * parts
    place_ref, cot_ref = refs[0], refs[1]
    first_refs = refs[2 : 2 + pieces]
    mid_refs = refs[2 + pieces : 6 + pieces]
    outs = refs[-(3 + parts) :]
    own_ref, value_ref, mid_keep_ref, mid_send_ref = outs[:4]
    send_refs = outs[4:]
    part = place_ref[2]
    block = first_refs[0].shape[0]

    def mid_rows(start):
        return jnp.concatenate([ref[pl.ds(start, width), :] for ref in mid_refs], axis=1)

    def start_of(c, k):
        return pl.multiple_of((c * parts + (part ^ k)) * width, width)

    total = None
    for c in range(chunks):
        for k in range(parts):
            term = jnp.dot(first_refs[c * parts + k][...], mid_rows(start_of(c, k)), preferred_element_type=f32)
            total = term if total is None else total + term
    second_low = jnp.tanh(total).astype(bf16)
    second = second_low.astype(f32)
    head = refs[6 + pieces][...]
    heads = tail_rows(head)
    rows = lax.dot_general(heads, second_low, (((1,), (1,)), ((), ())), preferred_element_type=f32)
    value = rows[0:1] + rows[1:2]
    if width > block:
        value = jnp.concatenate([value, jnp.zeros((1, width - block), f32)], axis=1)
    value_ref[...] = value
    cot = cot_ref[pl.ds(pl.multiple_of(place_ref[3] * block, SUBLANES), block), :1]
    head_part = jnp.sum(cot * second, axis=0, keepdims=True)
    back = (cot * head * (1.0 - second * second)).astype(bf16)
    units = mid_refs[0].shape[1]
    for k in range(parts):
        for c in range(chunks):
            piece = lax.dot_general(
                back, mid_rows(start_of(c, k)), (((1,), (1,)), ((), ())), preferred_element_type=f32
            )
            if k == 0:
                own_ref[pl.ds(c * block, block), :] = piece
            else:
                send_refs[k - 1][pl.ds(c * block, block), :] = piece.astype(bf16)
        if k > 0:
            send_refs[k - 1][pl.ds(chunks * block, EXTRA), :] = tail_rows(value)
    for c in range(chunks):
        for k in range(parts):
            product = lax.dot_general(
                first_refs[c * parts + k][...], back, (((0,), (0,)), ((), ())), preferred_element_type=f32
            ).astype(bf16)
            for p in range(4):
                out = (mid_keep_ref, mid_send_ref)[p % 2]
                out[p // 2, pl.ds(start_of(c, k), width), :] = product[:, p * units : (p + 1) * units]
    for p in range(4):
        out = (mid_keep_ref, mid_send_ref)[p % 2]
        out[p // 2, pl.ds(pieces * width, EXTRA), :] = tail_rows(head_part[:, p * units : (p + 1) * units])


def middle(place, cot, firsts, mids, head, chunks, parts, width, deps=()):
    block = firsts[0].shape[0]
    hidden, units = mids[0].shape
    partial = jax.ShapeDtypeStruct((2, hidden + EXTRA, units), bf16)
    return pl.pallas_call(
        functools.partial(middle_kernel, chunks, parts, width),
        in_specs=[smem()] + [vmem()] * (1 + len(firsts) + 5) + any_specs(deps),
        out_shape=[
            jax.ShapeDtypeStruct((chunks * block, width), f32),
            jax.ShapeDtypeStruct((1, width), f32),
            partial,
            partial,
        ]
        + [jax.ShapeDtypeStruct((chunks * block + EXTRA, width), bf16)] * (parts - 1),
        compiler_params=params(),
        cost_estimate=pl.CostEstimate(flops=1, bytes_accessed=1, transcendentals=0),
        name="value_layers",
    )(place, cot, *firsts, *mids, head, *deps)


def add_tail(left, right, hidden):
    body = left[:hidden].astype(f32) + right[:hidden].astype(f32)
    tails = left[hidden:].astype(f32) + right[hidden:].astype(f32)
    return body.astype(bf16), tails[0:1] + tails[1:2]


def mid_add_kernel(keep_ref, other_ref, *refs):
    own_ref, send_ref = refs[-2:]
    hidden = own_ref.shape[0] - EXTRA
    for at, out in enumerate((own_ref, send_ref)):
        body, tail = add_tail(keep_ref[at], other_ref[at], hidden)
        out[pl.ds(0, hidden), :] = body
        out[pl.ds(hidden, EXTRA), :] = tail_rows(tail)


def mid_add(keep, other, deps=()):
    shape = jax.ShapeDtypeStruct(keep.shape[1:], bf16)
    return pl.pallas_call(
        mid_add_kernel,
        in_specs=[vmem()] * 2 + any_specs(deps),
        out_shape=[shape, shape],
        compiler_params=params(),
        cost_estimate=pl.CostEstimate(flops=1, bytes_accessed=1, transcendentals=0),
        name="mid_gradient_add",
    )(keep, other, *deps)


def mid_final_kernel(own_ref, other_ref, *refs):
    out_ref, head_ref, token_ref = refs[-3:]
    token_ref[...] = jnp.zeros(token_ref.shape, f32)
    body, tail = add_tail(own_ref[...], other_ref[...], out_ref.shape[0])
    out_ref[...] = body
    head_ref[...] = tail


def mid_final(own, other, deps=()):
    hidden = own.shape[0] - EXTRA
    return pl.pallas_call(
        mid_final_kernel,
        in_specs=[vmem()] * 2 + any_specs(deps),
        out_shape=[
            jax.ShapeDtypeStruct((hidden, own.shape[1]), bf16),
            jax.ShapeDtypeStruct((1, own.shape[1]), f32),
            jax.ShapeDtypeStruct((SUBLANES, LANES), f32),
        ],
        compiler_params=params(),
        cost_estimate=pl.CostEstimate(flops=1, bytes_accessed=1, transcendentals=0),
        name="mid_gradient_final",
    )(own, other, *deps)


def back_first_kernel(count, own_ref, value_ref, *refs):
    received = refs[:count]
    first_ref, out_ref, tail_ref = refs[count], *refs[-2:]
    block = first_ref.shape[0]
    value = value_ref[...]
    total = own_ref[...]
    for ref in received:
        tail = ref[pl.ds(block, EXTRA), :].astype(f32)
        value = value + (tail[0:1] + tail[1:2])
        total = total + ref[pl.ds(0, block), :].astype(f32)
    first = first_ref[...].astype(f32)
    out_ref[...] = (total * (1.0 - first * first)).astype(bf16)
    tail_ref[...] = tail_rows(value)


def back_first(own, value, received, first, deps):
    block, width = first.shape
    return pl.pallas_call(
        functools.partial(back_first_kernel, len(received)),
        in_specs=[vmem()] * (3 + len(received)) + any_specs(deps),
        out_shape=[jax.ShapeDtypeStruct((rows, width), bf16) for rows in (block, EXTRA)],
        compiler_params=params(),
        cost_estimate=pl.CostEstimate(flops=1, bytes_accessed=1, transcendentals=0),
        name="back_first",
    )(own, value, *received, first, *deps)


def stack_kernel(count, *refs):
    at = 0
    for ref in refs[:count]:
        refs[-1][pl.ds(at, ref.shape[0]), :] = ref[...]
        at += ref.shape[0]


def stack(pieces, deps):
    rows = sum(piece.shape[0] for piece in pieces)
    return pl.pallas_call(
        functools.partial(stack_kernel, len(pieces)),
        in_specs=[vmem()] * len(pieces) + any_specs(deps),
        out_shape=jax.ShapeDtypeStruct((rows, pieces[0].shape[1]), bf16),
        compiler_params=params(),
        cost_estimate=pl.CostEstimate(flops=1, bytes_accessed=1, transcendentals=0),
        name="stack_parts",
    )(*pieces, *deps)


def turn_kernel(count, *refs):
    out_ref = refs[-1]
    at = 0
    for ref in refs[:count]:
        out_ref[pl.ds(at, ref.shape[1]), :] = ref[...].T
        at += ref.shape[1]


def transposed(arrays, deps):
    cells = sum(array.shape[1] for array in arrays)
    return pl.pallas_call(
        functools.partial(turn_kernel, len(arrays)),
        in_specs=[vmem()] * len(arrays) + any_specs(deps),
        out_shape=jax.ShapeDtypeStruct((cells, arrays[0].shape[0]), bf16),
        compiler_params=params(),
        cost_estimate=pl.CostEstimate(flops=1, bytes_accessed=1, transcendentals=0),
        name="transposed_inputs",
    )(*arrays, *deps)


def first_grad_kernel(parts, block, tiles, *refs):
    place_ref, left_ref = refs[:2]
    stacks = refs[2:6]
    out_ref, value_ref, whole = refs[-3:]
    width = out_ref.shape[1]
    step = pl.program_id(0)
    piece = step // tiles ^ place_ref[2]
    column = pl.ds(pl.multiple_of(step % tiles * width, width), width)
    mine = place_ref[3]
    values = [jnp.zeros((1, block), f32)] * 4
    for t, ref in enumerate(stacks):
        at = mine ^ (2 * (t % 2) + t // 2)
        whole[pl.ds(pl.multiple_of(at * block, block), block), :] = ref[
            pl.ds(pl.multiple_of(piece * block, block), block), column
        ]
        tail = ref[pl.ds(parts * block, EXTRA), :block].astype(f32)
        value = tail[0:1] + tail[1:2]
        for q in range(4):
            values[q] = jnp.where(at == q, value, values[q])
    value_ref[...] = jnp.concatenate(values, axis=1).reshape(4 * block)
    out_ref[...] = jnp.dot(left_ref[...], whole[...], preferred_element_type=f32).astype(bf16)


def first_grad(place, left, stacks, parts, block, deps):
    cells, scenarios = left.shape
    width = stacks[0].shape[1]
    tile = min(width, 256)
    tiles = width // tile
    return pl.pallas_call(
        functools.partial(first_grad_kernel, parts, block, tiles),
        grid=(parts * tiles,),
        in_specs=[smem()] + [vmem()] * 5 + any_specs(deps),
        out_specs=[pl.BlockSpec((cells, tile), lambda i: (0, i)), pl.BlockSpec((scenarios,), lambda i: (0,))],
        out_shape=[pltpu.HBM((cells, parts * width), bf16), jax.ShapeDtypeStruct((scenarios,), f32)],
        scratch_shapes=[pltpu.VMEM((scenarios, tile), bf16)],
        compiler_params=params(),
        cost_estimate=pl.CostEstimate(flops=1, bytes_accessed=1, transcendentals=0),
        name="first_gradient",
    )(place, left, *stacks, *deps)


def local(hist, drift, shocks, shock_table, first_weight, mid_weight, head_weight, cotangent):
    scenarios, rows, columns = hist.shape
    count = lax.axis_size("grid")
    hidden = first_weight.shape[1]
    units = mid_weight.shape[1]
    parts = count // 4
    width = hidden // parts
    block = scenarios // 4
    index = lax.axis_index("grid")
    core, side, part = index & 1, (index >> 1) & 1, index >> 2
    mine = 2 * core + side
    tiles = pltpu.with_memory_space_constraint(to_tiles(hist), pltpu.HBM)

    place = jnp.stack([core, side, part, mine])

    small = [pltpu.with_memory_space_constraint(array, pltpu.HBM) for array in (drift, shocks.T, shock_table.T, cotangent)]
    mids = [mid_weight]
    mids += [swap(mids[0], count, 1), swap(mids[0], count, 2)]
    place, first_rows, last_rows, shifts, band, cot, own_rows, inner = inner_steps(place, tiles, *small)
    inner = inner if rows > 4 else None
    forward = [(i, i + 1) for i in range(count - 1)]
    backward = [(i + 1, i) for i in range(count - 1)]
    below = lax.ppermute(last_rows, "grid", forward)
    above = lax.ppermute(first_rows, "grid", backward)
    first_weight = pltpu.with_memory_space_constraint(first_weight, pltpu.HBM)
    product = None if inner is None else inner_product(inner, first_weight, width, mids[1:])
    low, high = edge_steps(drift, shifts, band, own_rows, below, above, own_rows if product is None else product)
    head = head_weight[None, :]
    keep, send = edge_product(place, head, low, high, first_weight, product, parts, width)
    mids.append(swap(mids[2], count, 1))

    def density_turn(turn, dep, so_far):
        return density_steps(drift, shifts, band, own_rows, below, above, dep, so_far, turn, 2)

    own, heads, *sends = add_core(place, head, keep, swap(send, count, 1))
    flips = [2 * by_side + 4 * by_part for by_side, by_part in other_places(parts)]
    received = [swap(piece, count, flip) for piece, flip in zip(sends, flips)]
    first, head = activate(own, heads, received)
    firsts = [first] + [swap(first, count, 4 * k) for k in range(1, parts)]
    density, token = density_turn(0, first, None)
    own, value, mid_keep, mid_send, *sends = middle(place, cot, firsts, mids, head, 1, parts, width, [token, mids[1], mids[3]])
    received = [swap(piece, count, 4 * (k + 1)) for k, piece in enumerate(sends)]
    density, token = density_turn(1, sends[-1], density)
    back, tail = back_first(own, value, received, first, [token])
    mid_keep, mid_send = mid_add(mid_keep, swap(mid_send, count, 1), [back])
    mid_other = swap(mid_send, count, 2)
    left = transposed([low, high] if inner is None else [low, inner, high], [back])
    pieces = [back] + [swap(back, count, 4 * k) for k in range(1, parts)] + [tail]
    stacks = [stack(pieces, [left, mid_other])]
    stacks += [swap(stacks[0], count, 1), swap(stacks[0], count, 2)]
    grad_mid, grad_head, token = mid_final(mid_keep, mid_other, [stacks[0]])
    stacks.append(swap(stacks[2], count, 1))
    grad_first, value = first_grad(place, left, stacks, parts, block, [token])
    return from_tiles(density, hist.shape), value, grad_first, grad_mid, grad_head[0]


def solution(mesh):
    in_specs = (
        P("groups", "grid", None),
        P(None, "grid", None),
        P("groups", None),
        P("groups", None),
        P(("groups", "grid"), None),
        P("groups", "grid"),
        P(("groups", "grid")),
        P("groups"),
    )
    out_specs = (
        P("groups", "grid", None),
        P("groups"),
        P(("groups", "grid"), None),
        P("groups", "grid"),
        P(("groups", "grid")),
    )
    return jax.shard_map(local, mesh=mesh, in_specs=in_specs, out_specs=out_specs, check_vma=False)
```

```python
import functools
import jax
import jax.numpy as jnp
from jax import lax
from jax.experimental import pallas as pl
from jax.experimental.pallas import tpu as pltpu
from jax.sharding import PartitionSpec as P

diffusion_rate = 0.24
VMEM_BYTES = 24 * 1024 * 1024
EXTRA = 16
bf16 = jnp.bfloat16
f32 = jnp.float32


def params():
    return pltpu.CompilerParams(vmem_limit_bytes=VMEM_BYTES)


def scenario_block(scenarios):
    for size in (64, 32, 16):
        if scenarios % size == 0:
            return size
    return scenarios


LANES = 128
SUBLANES = 8
GROUP = 16


def to_tiles(hist):
    scenarios, rows, columns = hist.shape
    high = min(rows, SUBLANES)
    tiles = hist.reshape(scenarios, rows // high, high, columns // LANES, LANES)
    return tiles.transpose(0, 1, 3, 2, 4).reshape(scenarios * rows * (columns // LANES), LANES)


def from_tiles(tiles, shape):
    scenarios, rows, columns = shape
    high = min(rows, SUBLANES)
    parts = tiles.reshape(scenarios, rows // high, columns // LANES, high, LANES)
    return parts.transpose(0, 1, 3, 2, 4).reshape(shape)


def tile_offset(row, lane_tile, rows, lane_tiles):
    high = min(rows, SUBLANES)
    return (row // high * lane_tiles + lane_tile) * high + row % high


def read_row(ref, first_scenario, count, row, rows, columns):
    lane_tiles = columns // LANES
    per = rows * lane_tiles
    return jnp.concatenate(
        [
            ref[pl.ds(first_scenario * per + tile_offset(row, t, rows, lane_tiles), count, stride=per), :]
            for t in range(lane_tiles)
        ],
        axis=1,
    )


def write_row(ref, first_scenario, count, row, rows, columns, values):
    lane_tiles = columns // LANES
    per = rows * lane_tiles
    for t in range(lane_tiles):
        place = pl.ds(first_scenario * per + tile_offset(row, t, rows, lane_tiles), count, stride=per)
        ref[place, :] = values[:, t * LANES : (t + 1) * LANES]


def drift_tail(drift_ref, start):
    pieces = [
        jnp.concatenate([drift_ref[c, start : start + 1], drift_ref[c, start + 1 : start + 2]], axis=1)
        for c in range(2)
    ]
    high, low = two_halves(jnp.concatenate(pieces, axis=0))
    ones = jnp.ones((1, high.shape[1]), bf16)
    zeros = jnp.zeros((EXTRA - 5, high.shape[1]), bf16)
    return jnp.concatenate([high, low, ones, zeros], axis=0)


def band_matrix(columns):
    row = lax.broadcasted_iota(jnp.int32, (columns, columns), 0)
    column = lax.broadcasted_iota(jnp.int32, (columns, columns), 1)
    right = jnp.where(column == row + 1, 1.0, 0.0)
    left = jnp.where(column == row - 1, 1.0, 0.0)
    centre = jnp.where(column == row, 1.0 - 4.0 * diffusion_rate, diffusion_rate * (right + left))
    return centre.astype(bf16), (right - left).astype(bf16)


def half_shifts(levels_ref, table_ref, shift_ref):
    scenarios = levels_ref.shape[1]
    for t in range(levels_ref.shape[0]):
        level = jnp.broadcast_to(levels_ref[t : t + 1, :].astype(f32), (LANES, scenarios)).T
        for c in range(2):
            shift = jnp.zeros(level.shape, f32)
            for n in range(table_ref.shape[1]):
                shift = jnp.where(level == n, 0.5 * table_ref[c : c + 1, n : n + 1], shift)
            shift_ref[2 * t + c] = shift


def wide(values, columns):
    return jnp.concatenate([values] * (columns // LANES), axis=1)


def one_step(rows_of, places, half_drift, band, shift_x, shift_y, pairs, terms, write):
    size, columns = shift_x.shape
    whole = pl.ds(0, columns)

    def density(row):
        return pairs[pl.ds(rows_of[row] * size, size), whole].astype(f32)

    for row in places:
        flux = (half_drift(1, row) + shift_y) * density(row)
        pairs[pl.ds(rows_of[row] * size, size), pl.ds(columns, columns)] = flux.astype(bf16)
    yield
    start = rows_of[places[0]] * size
    count = (rows_of[places[-1]] + 1) * size - start
    terms[pl.ds(start, count), :] = jnp.dot(pairs[pl.ds(start, count), :], band, preferred_element_type=f32)
    yield
    for row in places:
        low = density(row - 1) * ((diffusion_rate + half_drift(0, row - 1)) + shift_x)
        high = density(row + 1) * ((diffusion_rate - half_drift(0, row + 1)) - shift_x)
        write(row, terms[pl.ds(rows_of[row] * size, size), :] + low + high)


def step_stages(segments, read, half_drift, edge, band, shifts, scratch, write):
    pairs, later, terms = scratch
    size, columns = shifts[0].shape
    before, between, after = [
        [row for first, last in segments for row in range(first - more, last + more + 1)] for more in (2, 1, 0)
    ]
    rows_of = {row: k for k, row in enumerate(before)}
    for row, k in rows_of.items():
        pairs[pl.ds(k * size, size), pl.ds(0, columns)] = read(row)

    def write_later(row, density):
        later[pl.ds(rows_of[row] * size, size), pl.ds(0, columns)] = edge(row, density).astype(bf16)

    yield from one_step(rows_of, between, half_drift, band, shifts[0], shifts[1], pairs, terms, write_later)
    yield from one_step(rows_of, after, half_drift, band, shifts[2], shifts[3], later, terms, write)


def interleave(runs):
    ahead, live = list(runs), []
    while ahead or live:
        if ahead:
            live.append(ahead.pop(0))
        for run in list(live):
            if next(run, live) is live:
                live.remove(run)


def two_steps(*args):
    interleave([step_stages(*args)])


def step_scratch(segments, size, columns):
    rows = sum(last - first + 5 for first, last in segments)
    pairs = pltpu.VMEM((rows * size, 2 * columns), bf16)
    return [pairs, pairs, pltpu.VMEM((rows * size, columns), f32)]


def edge_segments(rows):
    return [(0, 1), (rows - 2, rows - 1)] if rows >= 8 else [(0, rows - 1)]


def inner_kernel(
    rows, size, place_ref, hist_ref, drift_hbm, levels_hbm, table_hbm, cot_hbm,
    place_out_ref, first_ref, last_ref, shift_ref, band_ref, cot_ref, rows_ref, inner_ref,
    drift_ref, levels_ref, table_ref, cot_row, arrived, all_shifts, *scratch,
):
    step = pl.program_id(0)
    columns = drift_ref.shape[2]

    @pl.when(step == 0)
    def _():
        for n in range(4):
            place_out_ref[n] = place_ref[n]
        sources = ((drift_hbm, drift_ref), (levels_hbm, levels_ref), (table_hbm, table_ref), (cot_hbm, cot_row))
        copies = [pltpu.make_async_copy(*pair, arrived.at[n]) for n, pair in enumerate(sources)]
        for copy in copies:
            copy.start()
        centre, flux = band_matrix(columns)
        band_ref[pl.ds(0, columns), :] = centre
        band_ref[pl.ds(columns, columns), :] = flux
        for copy in copies:
            copy.wait()
        half_shifts(levels_ref, table_ref, all_shifts)
        cot_ref[...] = jnp.broadcast_to(cot_row[...].reshape(1, -1), (LANES, cot_row.shape[0])).T
        for out, start in ((first_ref, 0), (last_ref, rows - 2)):
            out[pl.ds(out.shape[0] - EXTRA, EXTRA), :] = drift_tail(drift_ref, start)

    where = pl.ds(pl.multiple_of(step * size, size), size)
    for n in range(4):
        shift_ref[n] = all_shifts[n, where, :]
    for row in range(rows):
        density = read_row(hist_ref, 0, size, row, rows, columns).astype(bf16)
        rows_ref[:, pl.ds(row * columns, columns)] = density
        if row < 2:
            first_ref[where, pl.ds(row * columns, columns)] = density
        if row >= rows - 2:
            last_ref[where, pl.ds((row - rows + 2) * columns, columns)] = density
    if rows <= 4:
        return
    band = band_ref[...]
    count = len(scratch) // 3
    part = size // count

    def run(n):
        here = pl.ds(n * part, part)

        def write(row, density):
            inner_ref[here, pl.ds((row - 2) * columns, columns)] = density.astype(bf16)

        return step_stages(
            [(2, rows - 3)],
            lambda row: rows_ref[here, pl.ds(row * columns, columns)],
            lambda c, row: 0.5 * drift_ref[c, row : row + 1, :],
            lambda row, density: density,
            band,
            [wide(shift_ref[k, here, :], columns) for k in range(4)],
            scratch[3 * n : 3 * n + 3],
            write,
        )

    interleave([run(n) for n in range(count)])


def inner_steps(place, tiles, drift, levels, table, cot):
    scenarios = levels.shape[1]
    rows, columns = drift.shape[1:]
    per = tiles.shape[0] // scenarios
    size = scenario_block(scenarios)
    inner = max(rows - 4, 1) * columns
    sent = jax.ShapeDtypeStruct((scenarios + EXTRA, 2 * columns), bf16)
    shifts = jax.ShapeDtypeStruct((4, scenarios, LANES), f32)
    band = jax.ShapeDtypeStruct((2 * columns, columns), bf16)
    return pl.pallas_call(
        functools.partial(inner_kernel, rows, size),
        grid=(scenarios // size,),
        in_specs=[smem(), pl.BlockSpec((size * per, LANES), lambda i: (i, 0))] + [pl.BlockSpec(memory_space=pltpu.HBM)] * 4,
        out_specs=[smem()]
        + [pl.BlockSpec(sent.shape, lambda i: (0, 0))] * 2
        + [
            pl.BlockSpec((4, size, LANES), lambda i: (0, i, 0)),
            pl.BlockSpec(band.shape, lambda i: (0, 0)),
            pl.BlockSpec((scenarios, LANES), lambda i: (0, 0)),
            pl.BlockSpec((size, rows * columns), lambda i: (i, 0)),
            pl.BlockSpec((size, inner), lambda i: (i, 0)),
        ],
        out_shape=[
            jax.ShapeDtypeStruct(place.shape, place.dtype),
            sent,
            sent,
            pltpu.HBM(shifts.shape, f32),
            band,
            jax.ShapeDtypeStruct((scenarios, LANES), f32),
            pltpu.HBM((scenarios, rows * columns), bf16),
            jax.ShapeDtypeStruct((scenarios, inner), bf16),
        ],
        scratch_shapes=[
            pltpu.VMEM(drift.shape, f32),
            pltpu.VMEM(levels.shape, levels.dtype),
            pltpu.VMEM(table.shape, f32),
            pltpu.VMEM(cot.shape, f32),
            pltpu.SemaphoreType.DMA((4,)),
            pltpu.VMEM(shifts.shape, f32),
        ]
        + step_scratch([(2, max(rows - 3, 2))], size // 2, columns) * 2,
        compiler_params=params(),
        cost_estimate=pl.CostEstimate(flops=1, bytes_accessed=1, transcendentals=0),
        name="inner_density_steps",
    )(place, tiles, drift, levels, table, cot)


def halo_drift(ref, columns):
    tail = ref[...].astype(f32)
    both = 0.5 * (tail[0:2] + tail[2:4])
    rows = [[both[c : c + 1, k * columns : (k + 1) * columns] for k in range(2)] for c in range(2)]
    return rows, tail[4:5, :columns]


def with_halo(drift_ref, below_tail, above_tail):
    rows, columns = drift_ref.shape[1:]
    below, below_valid = halo_drift(below_tail, columns)
    above, above_valid = halo_drift(above_tail, columns)

    def half_drift(c, row):
        if row < 0:
            return below[c][row + 2]
        if row >= rows:
            return above[c][row - rows]
        return 0.5 * drift_ref[c, row : row + 1, :]

    def edge(row, density):
        if row < 0:
            return density * below_valid
        if row >= rows:
            return density * above_valid
        return density

    return half_drift, edge


def density_read(rows_ref, below_ref, above_ref, rows, columns):
    def read(row):
        if row < 0:
            return below_ref[:, pl.ds((row + 2) * columns, columns)]
        if row >= rows:
            return above_ref[:, pl.ds((row - rows) * columns, columns)]
        return rows_ref[:, pl.ds(row * columns, columns)]

    return read


def density_kernel(drift_ref, shift_ref, band_ref, rows_ref, below_ref, above_ref, below_tail, above_tail, dep_ref, *refs):
    next_ref, token_ref, *scratch = refs[-5:]
    rows, columns = drift_ref.shape[1:]
    size = shift_ref.shape[1]
    half_drift, edge = with_halo(drift_ref, below_tail, above_tail)
    token_ref[...] = jnp.zeros(token_ref.shape, f32)

    def write(row, density):
        write_row(next_ref, 0, size, row, rows, columns, density)

    read = density_read(rows_ref, below_ref, above_ref, rows, columns)
    shifts = [wide(shift_ref[n], columns) for n in range(4)]
    two_steps([(0, rows - 1)], read, half_drift, edge, band_ref[...], shifts, scratch, write)


def density_specs(drift, shifts, band, own, below, size, place):
    columns = drift.shape[2]
    scenarios = shifts.shape[1]
    halo = pl.BlockSpec((size, 2 * columns), lambda i: (place(i), 0))
    tail = pl.BlockSpec((EXTRA, 2 * columns), lambda i: (scenarios // EXTRA, 0))
    return [
        pl.BlockSpec(drift.shape, lambda i: (0, 0, 0)),
        pl.BlockSpec((4, size, LANES), lambda i: (0, place(i), 0)),
        pl.BlockSpec(band.shape, lambda i: (0, 0)),
        pl.BlockSpec((size, own.shape[1]), lambda i: (place(i), 0)),
        halo,
        halo,
        tail,
        tail,
    ]


def edge_kernel(drift_ref, shift_ref, band_ref, rows_ref, below_ref, above_ref, below_tail, above_tail, dep_ref, *refs):
    low_ref, high_ref, *scratch = refs
    rows, columns = drift_ref.shape[1:]
    half_drift, edge = with_halo(drift_ref, below_tail, above_tail)

    def write(row, density):
        out, at = (low_ref, row) if row < 2 else (high_ref, row - rows + 2)
        out[:, pl.ds(at * columns, columns)] = density.astype(bf16)

    read = density_read(rows_ref, below_ref, above_ref, rows, columns)
    shifts = [wide(shift_ref[n], columns) for n in range(4)]
    two_steps(edge_segments(rows), read, half_drift, edge, band_ref[...], shifts, scratch, write)


def edge_steps(drift, shifts, band, own, below, above, dep):
    scenarios = shifts.shape[1]
    rows, columns = drift.shape[1:]
    size = 2 * scenario_block(scenarios)
    size = size if scenarios % size == 0 else size // 2
    edge = jax.ShapeDtypeStruct((scenarios, 2 * columns), bf16)
    spec = pl.BlockSpec((size, 2 * columns), lambda i: (i, 0))
    return pl.pallas_call(
        edge_kernel,
        grid=(scenarios // size,),
        in_specs=density_specs(drift, shifts, band, own, below, size, lambda i: i) + any_specs([dep]),
        out_specs=[spec, spec],
        out_shape=[edge, edge],
        scratch_shapes=step_scratch(edge_segments(rows), size, columns),
        compiler_params=params(),
        cost_estimate=pl.CostEstimate(flops=1, bytes_accessed=1, transcendentals=0),
        name="edge_density_steps",
    )(drift, shifts, band, own, below, above, below, above, dep)


def density_steps(drift, shifts, band, own, below, above, dep, so_far, turn, turns):
    scenarios = shifts.shape[1]
    rows, columns = drift.shape[1:]
    per = rows * (columns // LANES)
    size = 3 * GROUP if scenarios % (turns * GROUP * 3) == 0 else GROUP
    steps = scenarios // size // turns
    first = turn * steps
    args = [drift, shifts, band, own, below, above, below, above, dep]
    in_specs = density_specs(drift, shifts, band, own, below, size, lambda i: first + i) + any_specs([dep])
    aliases = {}
    if so_far is not None:
        aliases = {len(args): 0}
        args.append(so_far)
        in_specs.append(pl.BlockSpec(memory_space=pltpu.HBM))
    return pl.pallas_call(
        density_kernel,
        grid=(steps,),
        in_specs=in_specs,
        out_specs=[
            pl.BlockSpec((size * per, LANES), lambda i: (first + i, 0)),
            pl.BlockSpec((SUBLANES, LANES), lambda i: (0, 0)),
        ],
        out_shape=[pltpu.HBM((scenarios * per, LANES), f32), jax.ShapeDtypeStruct((SUBLANES, LANES), f32)],
        input_output_aliases=aliases,
        scratch_shapes=step_scratch([(0, rows - 1)], size, columns),
        compiler_params=params(),
        cost_estimate=pl.CostEstimate(flops=1, bytes_accessed=1, transcendentals=0),
        name="density_steps",
    )(*args)


def smem():
    return pl.BlockSpec(memory_space=pltpu.SMEM)


def vmem():
    return pl.BlockSpec(memory_space=pltpu.VMEM)


def swap(values, count, flip):
    return lax.ppermute(values, "grid", [(i, i ^ flip) for i in range(count)])


def inner_product_kernel(count, tiles, inputs_ref, *refs):
    weight = jnp.concatenate([ref[...] for ref in refs[:count]], axis=0)
    step = pl.program_id(0)
    tile = weight.shape[1]
    column = pl.ds(pl.multiple_of(step % tiles * tile, tile), tile)
    refs[-1][step // tiles, :, column] = jnp.dot(inputs_ref[...], weight, preferred_element_type=f32)


def inner_product(inner, weight, width, deps):
    scenarios, cells = inner.shape
    total, hidden = weight.shape
    size = (total - cells) // 2
    count = cells // size

    tile = width

    def spec(k):
        return pl.BlockSpec((size, tile), lambda n: (1 + k, n))

    return pl.pallas_call(
        functools.partial(inner_product_kernel, count, width // tile),
        grid=(hidden // tile,),
        in_specs=[vmem()] + [spec(k) for k in range(count)] + any_specs(deps),
        out_specs=vmem(),
        out_shape=jax.ShapeDtypeStruct((hidden // width, scenarios, width), f32),
        compiler_params=params(),
        cost_estimate=pl.CostEstimate(flops=1, bytes_accessed=1, transcendentals=0),
        name="inner_product",
    )(inner, *([weight] * count), *deps)


def edge_product_kernel(block, with_inner, place_ref, head_ref, low_ref, high_ref, top_ref, bottom_ref, *refs):
    keep_ref, send_ref, total = refs[-3:]
    step = pl.program_id(0)
    left = jnp.concatenate([low_ref[...], high_ref[...]], axis=1)
    weight = jnp.concatenate([top_ref[...], bottom_ref[...]], axis=0)
    product = jnp.dot(left, weight, preferred_element_type=f32)
    total[...] = product + refs[0][step] if with_inner else product
    core = place_ref[0]
    for out, half in ((keep_ref, core), (send_ref, 1 - core)):
        for side in range(2):
            start = pl.multiple_of((2 * half + side) * block, block)
            out[side, step, pl.ds(0, block), :] = total[pl.ds(start, block), :].astype(out.dtype)
    for side in range(2):
        send_ref[side, step, pl.ds(block, EXTRA), :] = tail_rows(padded(head_ref[...], send_ref.shape[-1]))


def padded(row, width):
    return jnp.concatenate([row, jnp.zeros((1, width - row.shape[1]), f32)], axis=1)


def edge_product(place, head, low, high, weight, inner, parts, width):
    scenarios, size = low.shape
    block = scenarios // 4
    last = weight.shape[0] // size - 1
    in_specs = [
        smem(),
        pl.BlockSpec(head.shape, lambda n: (0, 0)),
        vmem(),
        vmem(),
        pl.BlockSpec((size, width), lambda n: (0, n)),
        pl.BlockSpec((size, width), lambda n: (last, n)),
    ]
    args = [place, head, low, high, weight, weight]
    if inner is not None:
        in_specs.append(vmem())
        args.append(inner)
    return pl.pallas_call(
        functools.partial(edge_product_kernel, block, inner is not None),
        grid=(parts,),
        in_specs=in_specs,
        out_specs=[vmem(), vmem()],
        out_shape=[
            jax.ShapeDtypeStruct((2, parts, block, width), f32),
            jax.ShapeDtypeStruct((2, parts, block + EXTRA, width), bf16),
        ],
        scratch_shapes=[pltpu.VMEM((scenarios, width), f32)],
        compiler_params=params(),
        cost_estimate=pl.CostEstimate(flops=1, bytes_accessed=1, transcendentals=0),
        name="edge_product",
    )(*args)


def any_specs(deps):
    return [pl.BlockSpec(memory_space=pl.ANY)] * len(deps)


def other_places(parts):
    return [(side, part) for part in reversed(range(parts)) for side in range(2) if side or part]


def add_core_kernel(dep_count, place_ref, head_ref, mine_ref, other_ref, *refs):
    own_ref, heads_ref, *send_refs = refs[dep_count:]
    side, part = place_ref[1], place_ref[2]
    block = mine_ref.shape[2]
    units = head_ref.shape[1]
    rows = pl.ds(0, block)
    tail = other_ref[0, 0, pl.ds(block, EXTRA), :].astype(f32)
    core_head = tail[0:1] + tail[1:2]
    own_head = padded(head_ref[...], core_head.shape[1])
    heads_ref[0:1, :] = own_head[:, :units]
    heads_ref[1:2, :] = core_head[:, :units]
    own_ref[...] = mine_ref[side, part] + other_ref[side, part, rows, :].astype(f32)
    for (by_side, by_part), out in zip(other_places(mine_ref.shape[1]), send_refs):
        at = side ^ by_side, part ^ by_part
        out[rows, :] = (mine_ref[at] + other_ref[(*at, rows, slice(None))].astype(f32)).astype(bf16)
        if by_part == 0:
            pieces = [piece for head in (own_head, core_head) for piece in two_halves(head)]
            pieces.append(jnp.zeros((EXTRA - 4, own_head.shape[1]), bf16))
            out[pl.ds(block, EXTRA), :] = jnp.concatenate(pieces, axis=0)


def add_core(place, head, mine, other, deps):
    parts, block, width = mine.shape[1:]
    sends = [
        jax.ShapeDtypeStruct((block if by_part else block + EXTRA, width), bf16) for _, by_part in other_places(parts)
    ]
    return pl.pallas_call(
        functools.partial(add_core_kernel, len(deps)),
        in_specs=[smem(), vmem(), vmem(), vmem()] + any_specs(deps),
        out_shape=[jax.ShapeDtypeStruct((block, width), f32), jax.ShapeDtypeStruct((2, head.shape[1]), f32)] + sends,
        compiler_params=params(),
        cost_estimate=pl.CostEstimate(flops=1, bytes_accessed=1, transcendentals=0),
        name="add_core",
    )(place, head, mine, other, *deps)


def activate_kernel(own_ref, heads_ref, *refs):
    received, (first_ref, head_row_ref) = refs[:-2], refs[-2:]
    block = own_ref.shape[0]
    units = heads_ref.shape[1]
    total = own_ref[...]
    heads = [heads_ref[0:1, :], heads_ref[1:2, :]]
    for ref in received:
        total = total + ref[pl.ds(0, block), :].astype(f32)
        if ref.shape[0] > block:
            tail = ref[pl.ds(block, EXTRA), :].astype(f32)
            heads += [(tail[0:1] + tail[1:2])[:, :units], (tail[2:3] + tail[3:4])[:, :units]]
    first_ref[...] = jnp.tanh(total).astype(bf16)
    head_row_ref[...] = jnp.concatenate(heads, axis=1)


def activate(own, heads, received):
    return pl.pallas_call(
        activate_kernel,
        in_specs=[vmem()] * (2 + len(received)),
        out_shape=[jax.ShapeDtypeStruct(own.shape, bf16), jax.ShapeDtypeStruct((1, 4 * heads.shape[1]), f32)],
        compiler_params=params(),
        cost_estimate=pl.CostEstimate(flops=1, bytes_accessed=1, transcendentals=0),
        name="first_activation",
    )(own, heads, *received)


def two_halves(exact):
    high = exact.astype(bf16)
    low = (exact - high.astype(f32)).astype(bf16)
    return high, low


def tail_rows(exact):
    high, low = two_halves(exact)
    zeros = jnp.zeros((EXTRA - 2, exact.shape[1]), bf16)
    return jnp.concatenate([high, low, zeros], axis=0)


def middle_kernel(chunks, parts, width, *refs):
    pieces = chunks * parts
    place_ref, cot_ref = refs[0], refs[1]
    first_refs = refs[2 : 2 + pieces]
    mid_refs = refs[2 + pieces : 6 + pieces]
    outs = refs[-(3 + parts) :]
    own_ref, value_ref, mid_keep_ref, mid_send_ref = outs[:4]
    send_refs = outs[4:]
    part = place_ref[2]
    block = first_refs[0].shape[0]

    def mid_rows(start):
        return jnp.concatenate([ref[pl.ds(start, width), :] for ref in mid_refs], axis=1)

    def start_of(c, k):
        return pl.multiple_of((c * parts + (part ^ k)) * width, width)

    total = None
    for c in range(chunks):
        for k in range(parts):
            term = jnp.dot(first_refs[c * parts + k][...], mid_rows(start_of(c, k)), preferred_element_type=f32)
            total = term if total is None else total + term
    second_low = jnp.tanh(total).astype(bf16)
    second = second_low.astype(f32)
    head = refs[6 + pieces][...]
    heads = tail_rows(head)
    rows = lax.dot_general(heads, second_low, (((1,), (1,)), ((), ())), preferred_element_type=f32)
    value = rows[0:1] + rows[1:2]
    if width > block:
        value = jnp.concatenate([value, jnp.zeros((1, width - block), f32)], axis=1)
    value_ref[...] = value
    cot = cot_ref[pl.ds(pl.multiple_of(place_ref[3] * block, SUBLANES), block), :1]
    head_part = jnp.sum(cot * second, axis=0, keepdims=True)
    back = (cot * head * (1.0 - second * second)).astype(bf16)
    units = mid_refs[0].shape[1]
    for k in range(parts):
        for c in range(chunks):
            piece = lax.dot_general(
                back, mid_rows(start_of(c, k)), (((1,), (1,)), ((), ())), preferred_element_type=f32
            )
            if k == 0:
                own_ref[pl.ds(c * block, block), :] = piece
            else:
                send_refs[k - 1][pl.ds(c * block, block), :] = piece.astype(bf16)
        if k > 0:
            send_refs[k - 1][pl.ds(chunks * block, EXTRA), :] = tail_rows(value)
    for c in range(chunks):
        for k in range(parts):
            product = lax.dot_general(
                first_refs[c * parts + k][...], back, (((0,), (0,)), ((), ())), preferred_element_type=f32
            ).astype(bf16)
            for p in range(4):
                out = (mid_keep_ref, mid_send_ref)[p % 2]
                out[p // 2, pl.ds(start_of(c, k), width), :] = product[:, p * units : (p + 1) * units]
    for p in range(4):
        out = (mid_keep_ref, mid_send_ref)[p % 2]
        out[p // 2, pl.ds(pieces * width, EXTRA), :] = tail_rows(head_part[:, p * units : (p + 1) * units])


def middle(place, cot, firsts, mids, head, chunks, parts, width, deps=()):
    block = firsts[0].shape[0]
    hidden, units = mids[0].shape
    partial = jax.ShapeDtypeStruct((2, hidden + EXTRA, units), bf16)
    return pl.pallas_call(
        functools.partial(middle_kernel, chunks, parts, width),
        in_specs=[smem()] + [vmem()] * (1 + len(firsts) + 5) + any_specs(deps),
        out_shape=[
            jax.ShapeDtypeStruct((chunks * block, width), f32),
            jax.ShapeDtypeStruct((1, width), f32),
            partial,
            partial,
        ]
        + [jax.ShapeDtypeStruct((chunks * block + EXTRA, width), bf16)] * (parts - 1),
        compiler_params=params(),
        cost_estimate=pl.CostEstimate(flops=1, bytes_accessed=1, transcendentals=0),
        name="value_layers",
    )(place, cot, *firsts, *mids, head, *deps)


def add_tail(left, right, hidden):
    body = left[:hidden].astype(f32) + right[:hidden].astype(f32)
    tails = left[hidden:].astype(f32) + right[hidden:].astype(f32)
    return body.astype(bf16), tails[0:1] + tails[1:2]


def mid_add_kernel(keep_ref, other_ref, *refs):
    own_ref, send_ref = refs[-2:]
    hidden = own_ref.shape[0] - EXTRA
    for at, out in enumerate((own_ref, send_ref)):
        body, tail = add_tail(keep_ref[at], other_ref[at], hidden)
        out[pl.ds(0, hidden), :] = body
        out[pl.ds(hidden, EXTRA), :] = tail_rows(tail)


def mid_add(keep, other, deps=()):
    shape = jax.ShapeDtypeStruct(keep.shape[1:], bf16)
    return pl.pallas_call(
        mid_add_kernel,
        in_specs=[vmem()] * 2 + any_specs(deps),
        out_shape=[shape, shape],
        compiler_params=params(),
        cost_estimate=pl.CostEstimate(flops=1, bytes_accessed=1, transcendentals=0),
        name="mid_gradient_add",
    )(keep, other, *deps)


def mid_final_kernel(own_ref, other_ref, *refs):
    out_ref, head_ref, token_ref = refs[-3:]
    token_ref[...] = jnp.zeros(token_ref.shape, f32)
    body, tail = add_tail(own_ref[...], other_ref[...], out_ref.shape[0])
    out_ref[...] = body
    head_ref[...] = tail


def mid_final(own, other, deps=()):
    hidden = own.shape[0] - EXTRA
    return pl.pallas_call(
        mid_final_kernel,
        in_specs=[vmem()] * 2 + any_specs(deps),
        out_shape=[
            jax.ShapeDtypeStruct((hidden, own.shape[1]), bf16),
            jax.ShapeDtypeStruct((1, own.shape[1]), f32),
            jax.ShapeDtypeStruct((SUBLANES, LANES), f32),
        ],
        compiler_params=params(),
        cost_estimate=pl.CostEstimate(flops=1, bytes_accessed=1, transcendentals=0),
        name="mid_gradient_final",
    )(own, other, *deps)


def back_first_kernel(count, own_ref, value_ref, *refs):
    received = refs[:count]
    first_ref, out_ref, tail_ref = refs[count], *refs[-2:]
    block = first_ref.shape[0]
    value = value_ref[...]
    total = own_ref[...]
    for ref in received:
        tail = ref[pl.ds(block, EXTRA), :].astype(f32)
        value = value + (tail[0:1] + tail[1:2])
        total = total + ref[pl.ds(0, block), :].astype(f32)
    first = first_ref[...].astype(f32)
    out_ref[...] = (total * (1.0 - first * first)).astype(bf16)
    tail_ref[...] = tail_rows(value)


def back_first(own, value, received, first, deps):
    block, width = first.shape
    return pl.pallas_call(
        functools.partial(back_first_kernel, len(received)),
        in_specs=[vmem()] * (3 + len(received)) + any_specs(deps),
        out_shape=[jax.ShapeDtypeStruct((rows, width), bf16) for rows in (block, EXTRA)],
        compiler_params=params(),
        cost_estimate=pl.CostEstimate(flops=1, bytes_accessed=1, transcendentals=0),
        name="back_first",
    )(own, value, *received, first, *deps)


def stack_kernel(count, *refs):
    at = 0
    for ref in refs[:count]:
        refs[-1][pl.ds(at, ref.shape[0]), :] = ref[...]
        at += ref.shape[0]


def stack(pieces, deps):
    rows = sum(piece.shape[0] for piece in pieces)
    return pl.pallas_call(
        functools.partial(stack_kernel, len(pieces)),
        in_specs=[vmem()] * len(pieces) + any_specs(deps),
        out_shape=jax.ShapeDtypeStruct((rows, pieces[0].shape[1]), bf16),
        compiler_params=params(),
        cost_estimate=pl.CostEstimate(flops=1, bytes_accessed=1, transcendentals=0),
        name="stack_parts",
    )(*pieces, *deps)


def turn_kernel(count, *refs):
    out_ref = refs[-1]
    at = 0
    for ref in refs[:count]:
        out_ref[pl.ds(at, ref.shape[1]), :] = ref[...].T
        at += ref.shape[1]


def transposed(arrays, deps):
    cells = sum(array.shape[1] for array in arrays)
    return pl.pallas_call(
        functools.partial(turn_kernel, len(arrays)),
        in_specs=[vmem()] * len(arrays) + any_specs(deps),
        out_shape=jax.ShapeDtypeStruct((cells, arrays[0].shape[0]), bf16),
        compiler_params=params(),
        cost_estimate=pl.CostEstimate(flops=1, bytes_accessed=1, transcendentals=0),
        name="transposed_inputs",
    )(*arrays, *deps)


def first_grad_kernel(parts, block, tiles, *refs):
    place_ref, left_ref = refs[:2]
    stacks = refs[2:6]
    out_ref, value_ref, whole = refs[-3:]
    width = out_ref.shape[1]
    step = pl.program_id(0)
    piece = step // tiles ^ place_ref[2]
    column = pl.ds(pl.multiple_of(step % tiles * width, width), width)
    mine = place_ref[3]
    values = [jnp.zeros((1, block), f32)] * 4
    for t, ref in enumerate(stacks):
        at = mine ^ (2 * (t % 2) + t // 2)
        whole[pl.ds(pl.multiple_of(at * block, block), block), :] = ref[
            pl.ds(pl.multiple_of(piece * block, block), block), column
        ]
        tail = ref[pl.ds(parts * block, EXTRA), :block].astype(f32)
        value = tail[0:1] + tail[1:2]
        for q in range(4):
            values[q] = jnp.where(at == q, value, values[q])
    value_ref[...] = jnp.concatenate(values, axis=1).reshape(4 * block)
    out_ref[...] = jnp.dot(left_ref[...], whole[...], preferred_element_type=f32).astype(bf16)


def first_grad(place, left, stacks, parts, block, deps):
    cells, scenarios = left.shape
    width = stacks[0].shape[1]
    tile = min(width, 256)
    tiles = width // tile
    return pl.pallas_call(
        functools.partial(first_grad_kernel, parts, block, tiles),
        grid=(parts * tiles,),
        in_specs=[smem()] + [vmem()] * 5 + any_specs(deps),
        out_specs=[pl.BlockSpec((cells, tile), lambda i: (0, i)), pl.BlockSpec((scenarios,), lambda i: (0,))],
        out_shape=[pltpu.HBM((cells, parts * width), bf16), jax.ShapeDtypeStruct((scenarios,), f32)],
        scratch_shapes=[pltpu.VMEM((scenarios, tile), bf16)],
        compiler_params=params(),
        cost_estimate=pl.CostEstimate(flops=1, bytes_accessed=1, transcendentals=0),
        name="first_gradient",
    )(place, left, *stacks, *deps)


def local(hist, drift, shocks, shock_table, first_weight, mid_weight, head_weight, cotangent):
    scenarios, rows, columns = hist.shape
    count = lax.axis_size("grid")
    hidden = first_weight.shape[1]
    units = mid_weight.shape[1]
    parts = count // 4
    width = hidden // parts
    block = scenarios // 4
    index = lax.axis_index("grid")
    core, side, part = index & 1, (index >> 1) & 1, index >> 2
    mine = 2 * core + side
    tiles = pltpu.with_memory_space_constraint(to_tiles(hist), pltpu.HBM)

    place = jnp.stack([core, side, part, mine])

    small = [pltpu.with_memory_space_constraint(array, pltpu.HBM) for array in (drift, shocks.T, shock_table.T, cotangent)]
    mids = [mid_weight]
    mids += [swap(mids[0], count, 1), swap(mids[0], count, 2)]
    place, first_rows, last_rows, shifts, band, cot, own_rows, inner = inner_steps(place, tiles, *small)
    inner = inner if rows > 4 else None
    forward = [(i, i + 1) for i in range(count - 1)]
    backward = [(i + 1, i) for i in range(count - 1)]
    below = lax.ppermute(last_rows, "grid", forward)
    above = lax.ppermute(first_rows, "grid", backward)
    first_weight = pltpu.with_memory_space_constraint(first_weight, pltpu.HBM)
    product = None if inner is None else inner_product(inner, first_weight, width, mids[1:])
    low, high = edge_steps(drift, shifts, band, own_rows, below, above, own_rows if product is None else product)
    head = head_weight[None, :]
    keep, send = edge_product(place, head, low, high, first_weight, product, parts, width)
    mids.append(swap(mids[2], count, 1))

    def density_turn(turn, dep, so_far):
        return density_steps(drift, shifts, band, own_rows, below, above, dep, so_far, turn, 2)

    own, heads, *sends = add_core(place, head, keep, swap(send, count, 1), [mids[3]])
    flips = [2 * by_side + 4 * by_part for by_side, by_part in other_places(parts)]
    received = [swap(piece, count, flip) for piece, flip in zip(sends, flips)]
    first, head = activate(own, heads, received)
    firsts = [first] + [swap(first, count, 4 * k) for k in range(1, parts)]
    density, token = density_turn(0, first, None)
    own, value, mid_keep, mid_send, *sends = middle(place, cot, firsts, mids, head, 1, parts, width, [token, mids[1], mids[3]])
    received = [swap(piece, count, 4 * (k + 1)) for k, piece in enumerate(sends)]
    density, token = density_turn(1, sends[-1], density)
    back, tail = back_first(own, value, received, first, [token])
    mid_keep, mid_send = mid_add(mid_keep, swap(mid_send, count, 1), [back])
    mid_other = swap(mid_send, count, 2)
    left = transposed([low, high] if inner is None else [low, inner, high], [back])
    pieces = [back] + [swap(back, count, 4 * k) for k in range(1, parts)] + [tail]
    stacks = [stack(pieces, [left, mid_other])]
    stacks += [swap(stacks[0], count, 1), swap(stacks[0], count, 2)]
    grad_mid, grad_head, token = mid_final(mid_keep, mid_other, [stacks[0]])
    stacks.append(swap(stacks[2], count, 1))
    grad_first, value = first_grad(place, left, stacks, parts, block, [token])
    return from_tiles(density, hist.shape), value, grad_first, grad_mid, grad_head[0]


def solution(mesh):
    in_specs = (
        P("groups", "grid", None),
        P(None, "grid", None),
        P("groups", None),
        P("groups", None),
        P(("groups", "grid"), None),
        P("groups", "grid"),
        P(("groups", "grid")),
        P("groups"),
    )
    out_specs = (
        P("groups", "grid", None),
        P("groups"),
        P(("groups", "grid"), None),
        P("groups", "grid"),
        P(("groups", "grid")),
    )
    return jax.shard_map(local, mesh=mesh, in_specs=in_specs, out_specs=out_specs, check_vma=False)
```

```python
import functools
import jax
import jax.numpy as jnp
from jax import lax
from jax.experimental import pallas as pl
from jax.experimental.pallas import tpu as pltpu
from jax.sharding import PartitionSpec as P

diffusion_rate = 0.24
VMEM_BYTES = 24 * 1024 * 1024
EXTRA = 16
bf16 = jnp.bfloat16
f32 = jnp.float32


def params():
    return pltpu.CompilerParams(vmem_limit_bytes=VMEM_BYTES)


def scenario_block(scenarios):
    for size in (64, 32, 16):
        if scenarios % size == 0:
            return size
    return scenarios


LANES = 128
SUBLANES = 8
GROUP = 16


def to_tiles(hist):
    scenarios, rows, columns = hist.shape
    high = min(rows, SUBLANES)
    tiles = hist.reshape(scenarios, rows // high, high, columns // LANES, LANES)
    return tiles.transpose(0, 1, 3, 2, 4).reshape(scenarios * rows * (columns // LANES), LANES)


def from_tiles(tiles, shape):
    scenarios, rows, columns = shape
    high = min(rows, SUBLANES)
    parts = tiles.reshape(scenarios, rows // high, columns // LANES, high, LANES)
    return parts.transpose(0, 1, 3, 2, 4).reshape(shape)


def tile_offset(row, lane_tile, rows, lane_tiles):
    high = min(rows, SUBLANES)
    return (row // high * lane_tiles + lane_tile) * high + row % high


def read_row(ref, first_scenario, count, row, rows, columns):
    lane_tiles = columns // LANES
    per = rows * lane_tiles
    return jnp.concatenate(
        [
            ref[pl.ds(first_scenario * per + tile_offset(row, t, rows, lane_tiles), count, stride=per), :]
            for t in range(lane_tiles)
        ],
        axis=1,
    )


def write_row(ref, first_scenario, count, row, rows, columns, values):
    lane_tiles = columns // LANES
    per = rows * lane_tiles
    for t in range(lane_tiles):
        place = pl.ds(first_scenario * per + tile_offset(row, t, rows, lane_tiles), count, stride=per)
        ref[place, :] = values[:, t * LANES : (t + 1) * LANES]


def drift_tail(drift_ref, start):
    pieces = [
        jnp.concatenate([drift_ref[c, start : start + 1], drift_ref[c, start + 1 : start + 2]], axis=1)
        for c in range(2)
    ]
    high, low = two_halves(jnp.concatenate(pieces, axis=0))
    ones = jnp.ones((1, high.shape[1]), bf16)
    zeros = jnp.zeros((EXTRA - 5, high.shape[1]), bf16)
    return jnp.concatenate([high, low, ones, zeros], axis=0)


def band_matrix(columns):
    row = lax.broadcasted_iota(jnp.int32, (columns, columns), 0)
    column = lax.broadcasted_iota(jnp.int32, (columns, columns), 1)
    right = jnp.where(column == row + 1, 1.0, 0.0)
    left = jnp.where(column == row - 1, 1.0, 0.0)
    centre = jnp.where(column == row, 1.0 - 4.0 * diffusion_rate, diffusion_rate * (right + left))
    return centre.astype(bf16), (right - left).astype(bf16)


def half_shifts(levels_ref, table_ref, shift_ref):
    scenarios = levels_ref.shape[1]
    for t in range(levels_ref.shape[0]):
        level = jnp.broadcast_to(levels_ref[t : t + 1, :].astype(f32), (LANES, scenarios)).T
        for c in range(2):
            shift = jnp.zeros(level.shape, f32)
            for n in range(table_ref.shape[1]):
                shift = jnp.where(level == n, 0.5 * table_ref[c : c + 1, n : n + 1], shift)
            shift_ref[2 * t + c] = shift


def wide(values, columns):
    return jnp.concatenate([values] * (columns // LANES), axis=1)


def one_step(rows_of, places, half_drift, band, shift_x, shift_y, pairs, terms, write):
    size, columns = shift_x.shape
    whole = pl.ds(0, columns)

    def density(row):
        return pairs[pl.ds(rows_of[row] * size, size), whole].astype(f32)

    for row in places:
        flux = (half_drift(1, row) + shift_y) * density(row)
        pairs[pl.ds(rows_of[row] * size, size), pl.ds(columns, columns)] = flux.astype(bf16)
    yield
    start = rows_of[places[0]] * size
    count = (rows_of[places[-1]] + 1) * size - start
    terms[pl.ds(start, count), :] = jnp.dot(pairs[pl.ds(start, count), :], band, preferred_element_type=f32)
    yield
    for row in places:
        low = density(row - 1) * ((diffusion_rate + half_drift(0, row - 1)) + shift_x)
        high = density(row + 1) * ((diffusion_rate - half_drift(0, row + 1)) - shift_x)
        write(row, terms[pl.ds(rows_of[row] * size, size), :] + low + high)


def step_stages(segments, read, half_drift, edge, band, shifts, scratch, write):
    pairs, later, terms = scratch
    size, columns = shifts[0].shape
    before, between, after = [
        [row for first, last in segments for row in range(first - more, last + more + 1)] for more in (2, 1, 0)
    ]
    rows_of = {row: k for k, row in enumerate(before)}
    for row, k in rows_of.items():
        pairs[pl.ds(k * size, size), pl.ds(0, columns)] = read(row)

    def write_later(row, density):
        later[pl.ds(rows_of[row] * size, size), pl.ds(0, columns)] = edge(row, density).astype(bf16)

    yield from one_step(rows_of, between, half_drift, band, shifts[0], shifts[1], pairs, terms, write_later)
    yield from one_step(rows_of, after, half_drift, band, shifts[2], shifts[3], later, terms, write)


def interleave(runs):
    ahead, live = list(runs), []
    while ahead or live:
        if ahead:
            live.append(ahead.pop(0))
        for run in list(live):
            if next(run, live) is live:
                live.remove(run)


def two_steps(*args):
    interleave([step_stages(*args)])


def step_scratch(segments, size, columns):
    rows = sum(last - first + 5 for first, last in segments)
    pairs = pltpu.VMEM((rows * size, 2 * columns), bf16)
    return [pairs, pairs, pltpu.VMEM((rows * size, columns), f32)]


def edge_segments(rows):
    return [(0, 1), (rows - 2, rows - 1)] if rows >= 8 else [(0, rows - 1)]


def inner_kernel(
    rows, size, place_ref, hist_ref, drift_hbm, levels_hbm, table_hbm, cot_hbm,
    place_out_ref, first_ref, last_ref, shift_ref, band_ref, cot_ref, rows_ref, inner_ref,
    drift_ref, levels_ref, table_ref, cot_row, arrived, all_shifts, *scratch,
):
    step = pl.program_id(0)
    columns = drift_ref.shape[2]

    @pl.when(step == 0)
    def _():
        for n in range(4):
            place_out_ref[n] = place_ref[n]
        sources = ((drift_hbm, drift_ref), (levels_hbm, levels_ref), (table_hbm, table_ref), (cot_hbm, cot_row))
        copies = [pltpu.make_async_copy(*pair, arrived.at[n]) for n, pair in enumerate(sources)]
        for copy in copies:
            copy.start()
        centre, flux = band_matrix(columns)
        band_ref[pl.ds(0, columns), :] = centre
        band_ref[pl.ds(columns, columns), :] = flux
        for copy in copies:
            copy.wait()
        half_shifts(levels_ref, table_ref, all_shifts)
        cot_ref[...] = jnp.broadcast_to(cot_row[...].reshape(1, -1), (LANES, cot_row.shape[0])).T
        for out, start in ((first_ref, 0), (last_ref, rows - 2)):
            out[pl.ds(out.shape[0] - EXTRA, EXTRA), :] = drift_tail(drift_ref, start)

    where = pl.ds(pl.multiple_of(step * size, size), size)
    for n in range(4):
        shift_ref[n] = all_shifts[n, where, :]
    for row in range(rows):
        density = read_row(hist_ref, 0, size, row, rows, columns).astype(bf16)
        rows_ref[:, pl.ds(row * columns, columns)] = density
        if row < 2:
            first_ref[where, pl.ds(row * columns, columns)] = density
        if row >= rows - 2:
            last_ref[where, pl.ds((row - rows + 2) * columns, columns)] = density
    if rows <= 4:
        return
    band = band_ref[...]
    count = len(scratch) // 3
    part = size // count

    def run(n):
        here = pl.ds(n * part, part)

        def write(row, density):
            inner_ref[here, pl.ds((row - 2) * columns, columns)] = density.astype(bf16)

        return step_stages(
            [(2, rows - 3)],
            lambda row: rows_ref[here, pl.ds(row * columns, columns)],
            lambda c, row: 0.5 * drift_ref[c, row : row + 1, :],
            lambda row, density: density,
            band,
            [wide(shift_ref[k, here, :], columns) for k in range(4)],
            scratch[3 * n : 3 * n + 3],
            write,
        )

    interleave([run(n) for n in range(count)])


def inner_steps(place, tiles, drift, levels, table, cot):
    scenarios = levels.shape[1]
    rows, columns = drift.shape[1:]
    per = tiles.shape[0] // scenarios
    size = scenario_block(scenarios)
    inner = max(rows - 4, 1) * columns
    sent = jax.ShapeDtypeStruct((scenarios + EXTRA, 2 * columns), bf16)
    shifts = jax.ShapeDtypeStruct((4, scenarios, LANES), f32)
    band = jax.ShapeDtypeStruct((2 * columns, columns), bf16)
    return pl.pallas_call(
        functools.partial(inner_kernel, rows, size),
        grid=(scenarios // size,),
        in_specs=[smem(), pl.BlockSpec((size * per, LANES), lambda i: (i, 0))] + [pl.BlockSpec(memory_space=pltpu.HBM)] * 4,
        out_specs=[smem()]
        + [pl.BlockSpec(sent.shape, lambda i: (0, 0))] * 2
        + [
            pl.BlockSpec((4, size, LANES), lambda i: (0, i, 0)),
            pl.BlockSpec(band.shape, lambda i: (0, 0)),
            pl.BlockSpec((scenarios, LANES), lambda i: (0, 0)),
            pl.BlockSpec((size, rows * columns), lambda i: (i, 0)),
            pl.BlockSpec((size, inner), lambda i: (i, 0)),
        ],
        out_shape=[
            jax.ShapeDtypeStruct(place.shape, place.dtype),
            sent,
            sent,
            pltpu.HBM(shifts.shape, f32),
            band,
            jax.ShapeDtypeStruct((scenarios, LANES), f32),
            pltpu.HBM((scenarios, rows * columns), bf16),
            jax.ShapeDtypeStruct((scenarios, inner), bf16),
        ],
        scratch_shapes=[
            pltpu.VMEM(drift.shape, f32),
            pltpu.VMEM(levels.shape, levels.dtype),
            pltpu.VMEM(table.shape, f32),
            pltpu.VMEM(cot.shape, f32),
            pltpu.SemaphoreType.DMA((4,)),
            pltpu.VMEM(shifts.shape, f32),
        ]
        + step_scratch([(2, max(rows - 3, 2))], size // 2, columns) * 2,
        compiler_params=params(),
        cost_estimate=pl.CostEstimate(flops=1, bytes_accessed=1, transcendentals=0),
        name="inner_density_steps",
    )(place, tiles, drift, levels, table, cot)


def halo_drift(ref, columns):
    tail = ref[...].astype(f32)
    both = 0.5 * (tail[0:2] + tail[2:4])
    rows = [[both[c : c + 1, k * columns : (k + 1) * columns] for k in range(2)] for c in range(2)]
    return rows, tail[4:5, :columns]


def with_halo(drift_ref, below_tail, above_tail):
    rows, columns = drift_ref.shape[1:]
    below, below_valid = halo_drift(below_tail, columns)
    above, above_valid = halo_drift(above_tail, columns)

    def half_drift(c, row):
        if row < 0:
            return below[c][row + 2]
        if row >= rows:
            return above[c][row - rows]
        return 0.5 * drift_ref[c, row : row + 1, :]

    def edge(row, density):
        if row < 0:
            return density * below_valid
        if row >= rows:
            return density * above_valid
        return density

    return half_drift, edge


def density_read(rows_ref, below_ref, above_ref, rows, columns):
    def read(row):
        if row < 0:
            return below_ref[:, pl.ds((row + 2) * columns, columns)]
        if row >= rows:
            return above_ref[:, pl.ds((row - rows) * columns, columns)]
        return rows_ref[:, pl.ds(row * columns, columns)]

    return read


def density_kernel(drift_ref, shift_ref, band_ref, rows_ref, below_ref, above_ref, below_tail, above_tail, dep_ref, *refs):
    next_ref, token_ref, *scratch = refs[-5:]
    rows, columns = drift_ref.shape[1:]
    size = shift_ref.shape[1]
    half_drift, edge = with_halo(drift_ref, below_tail, above_tail)
    token_ref[...] = jnp.zeros(token_ref.shape, f32)

    def write(row, density):
        write_row(next_ref, 0, size, row, rows, columns, density)

    read = density_read(rows_ref, below_ref, above_ref, rows, columns)
    shifts = [wide(shift_ref[n], columns) for n in range(4)]
    two_steps([(0, rows - 1)], read, half_drift, edge, band_ref[...], shifts, scratch, write)


def density_specs(drift, shifts, band, own, below, size, place):
    columns = drift.shape[2]
    scenarios = shifts.shape[1]
    halo = pl.BlockSpec((size, 2 * columns), lambda i: (place(i), 0))
    tail = pl.BlockSpec((EXTRA, 2 * columns), lambda i: (scenarios // EXTRA, 0))
    return [
        pl.BlockSpec(drift.shape, lambda i: (0, 0, 0)),
        pl.BlockSpec((4, size, LANES), lambda i: (0, place(i), 0)),
        pl.BlockSpec(band.shape, lambda i: (0, 0)),
        pl.BlockSpec((size, own.shape[1]), lambda i: (place(i), 0)),
        halo,
        halo,
        tail,
        tail,
    ]


def edge_kernel(drift_ref, shift_ref, band_ref, rows_ref, below_ref, above_ref, below_tail, above_tail, dep_ref, *refs):
    low_ref, high_ref, *scratch = refs
    rows, columns = drift_ref.shape[1:]
    half_drift, edge = with_halo(drift_ref, below_tail, above_tail)

    def write(row, density):
        out, at = (low_ref, row) if row < 2 else (high_ref, row - rows + 2)
        out[:, pl.ds(at * columns, columns)] = density.astype(bf16)

    read = density_read(rows_ref, below_ref, above_ref, rows, columns)
    shifts = [wide(shift_ref[n], columns) for n in range(4)]
    two_steps(edge_segments(rows), read, half_drift, edge, band_ref[...], shifts, scratch, write)


def edge_steps(drift, shifts, band, own, below, above, dep):
    scenarios = shifts.shape[1]
    rows, columns = drift.shape[1:]
    size = 2 * scenario_block(scenarios)
    size = size if scenarios % size == 0 else size // 2
    edge = jax.ShapeDtypeStruct((scenarios, 2 * columns), bf16)
    spec = pl.BlockSpec((size, 2 * columns), lambda i: (i, 0))
    return pl.pallas_call(
        edge_kernel,
        grid=(scenarios // size,),
        in_specs=density_specs(drift, shifts, band, own, below, size, lambda i: i) + any_specs([dep]),
        out_specs=[spec, spec],
        out_shape=[edge, edge],
        scratch_shapes=step_scratch(edge_segments(rows), size, columns),
        compiler_params=params(),
        cost_estimate=pl.CostEstimate(flops=1, bytes_accessed=1, transcendentals=0),
        name="edge_density_steps",
    )(drift, shifts, band, own, below, above, below, above, dep)


def density_steps(drift, shifts, band, own, below, above, dep, so_far, turn, turns):
    scenarios = shifts.shape[1]
    rows, columns = drift.shape[1:]
    per = rows * (columns // LANES)
    size = 3 * GROUP if scenarios % (turns * GROUP * 3) == 0 else GROUP
    steps = scenarios // size // turns
    first = turn * steps
    args = [drift, shifts, band, own, below, above, below, above, dep]
    in_specs = density_specs(drift, shifts, band, own, below, size, lambda i: first + i) + any_specs([dep])
    aliases = {}
    if so_far is not None:
        aliases = {len(args): 0}
        args.append(so_far)
        in_specs.append(pl.BlockSpec(memory_space=pltpu.HBM))
    return pl.pallas_call(
        density_kernel,
        grid=(steps,),
        in_specs=in_specs,
        out_specs=[
            pl.BlockSpec((size * per, LANES), lambda i: (first + i, 0)),
            pl.BlockSpec((SUBLANES, LANES), lambda i: (0, 0)),
        ],
        out_shape=[pltpu.HBM((scenarios * per, LANES), f32), jax.ShapeDtypeStruct((SUBLANES, LANES), f32)],
        input_output_aliases=aliases,
        scratch_shapes=step_scratch([(0, rows - 1)], size, columns),
        compiler_params=params(),
        cost_estimate=pl.CostEstimate(flops=1, bytes_accessed=1, transcendentals=0),
        name="density_steps",
    )(*args)


def smem():
    return pl.BlockSpec(memory_space=pltpu.SMEM)


def vmem():
    return pl.BlockSpec(memory_space=pltpu.VMEM)


def swap(values, count, flip):
    return lax.ppermute(values, "grid", [(i, i ^ flip) for i in range(count)])


def inner_product_kernel(count, tiles, inputs_ref, *refs):
    weight = jnp.concatenate([ref[...] for ref in refs[:count]], axis=0)
    step = pl.program_id(0)
    tile = weight.shape[1]
    column = pl.ds(pl.multiple_of(step % tiles * tile, tile), tile)
    refs[-1][step // tiles, :, column] = jnp.dot(inputs_ref[...], weight, preferred_element_type=f32)


def inner_product(inner, weight, width, deps):
    scenarios, cells = inner.shape
    total, hidden = weight.shape
    size = (total - cells) // 2
    count = cells // size

    tile = width

    def spec(k):
        return pl.BlockSpec((size, tile), lambda n: (1 + k, n))

    return pl.pallas_call(
        functools.partial(inner_product_kernel, count, width // tile),
        grid=(hidden // tile,),
        in_specs=[vmem()] + [spec(k) for k in range(count)] + any_specs(deps),
        out_specs=vmem(),
        out_shape=jax.ShapeDtypeStruct((hidden // width, scenarios, width), f32),
        compiler_params=params(),
        cost_estimate=pl.CostEstimate(flops=1, bytes_accessed=1, transcendentals=0),
        name="inner_product",
    )(inner, *([weight] * count), *deps)


def edge_product_kernel(block, with_inner, place_ref, head_ref, low_ref, high_ref, top_ref, bottom_ref, *refs):
    keep_ref, send_ref, total = refs[-3:]
    step = pl.program_id(0)
    left = jnp.concatenate([low_ref[...], high_ref[...]], axis=1)
    weight = jnp.concatenate([top_ref[...], bottom_ref[...]], axis=0)
    product = jnp.dot(left, weight, preferred_element_type=f32)
    total[...] = product + refs[0][step] if with_inner else product
    core = place_ref[0]
    for out, half in ((keep_ref, core), (send_ref, 1 - core)):
        for side in range(2):
            start = pl.multiple_of((2 * half + side) * block, block)
            out[side, step, pl.ds(0, block), :] = total[pl.ds(start, block), :].astype(out.dtype)
    for side in range(2):
        send_ref[side, step, pl.ds(block, EXTRA), :] = tail_rows(padded(head_ref[...], send_ref.shape[-1]))


def padded(row, width):
    return jnp.concatenate([row, jnp.zeros((1, width - row.shape[1]), f32)], axis=1)


def edge_product(place, head, low, high, weight, inner, parts, width):
    scenarios, size = low.shape
    block = scenarios // 4
    last = weight.shape[0] // size - 1
    in_specs = [
        smem(),
        pl.BlockSpec(head.shape, lambda n: (0, 0)),
        vmem(),
        vmem(),
        pl.BlockSpec((size, width), lambda n: (0, n)),
        pl.BlockSpec((size, width), lambda n: (last, n)),
    ]
    args = [place, head, low, high, weight, weight]
    if inner is not None:
        in_specs.append(vmem())
        args.append(inner)
    return pl.pallas_call(
        functools.partial(edge_product_kernel, block, inner is not None),
        grid=(parts,),
        in_specs=in_specs,
        out_specs=[vmem(), vmem()],
        out_shape=[
            jax.ShapeDtypeStruct((2, parts, block, width), f32),
            jax.ShapeDtypeStruct((2, parts, block + EXTRA, width), bf16),
        ],
        scratch_shapes=[pltpu.VMEM((scenarios, width), f32)],
        compiler_params=params(),
        cost_estimate=pl.CostEstimate(flops=1, bytes_accessed=1, transcendentals=0),
        name="edge_product",
    )(*args)


def any_specs(deps):
    return [pl.BlockSpec(memory_space=pl.ANY)] * len(deps)


def other_places(parts):
    return [(side, part) for side in range(2) for part in range(parts) if side or part]


def add_core_kernel(place_ref, head_ref, mine_ref, other_ref, own_ref, heads_ref, *send_refs):
    side, part = place_ref[1], place_ref[2]
    block = mine_ref.shape[2]
    units = head_ref.shape[1]
    rows = pl.ds(0, block)
    tail = other_ref[0, 0, pl.ds(block, EXTRA), :].astype(f32)
    core_head = tail[0:1] + tail[1:2]
    own_head = padded(head_ref[...], core_head.shape[1])
    heads_ref[0:1, :] = own_head[:, :units]
    heads_ref[1:2, :] = core_head[:, :units]
    own_ref[...] = mine_ref[side, part] + other_ref[side, part, rows, :].astype(f32)
    for (by_side, by_part), out in zip(other_places(mine_ref.shape[1]), send_refs):
        at = side ^ by_side, part ^ by_part
        out[rows, :] = (mine_ref[at] + other_ref[(*at, rows, slice(None))].astype(f32)).astype(bf16)
        if by_part == 0:
            pieces = [piece for head in (own_head, core_head) for piece in two_halves(head)]
            pieces.append(jnp.zeros((EXTRA - 4, own_head.shape[1]), bf16))
            out[pl.ds(block, EXTRA), :] = jnp.concatenate(pieces, axis=0)


def add_core(place, head, mine, other):
    parts, block, width = mine.shape[1:]
    sends = [
        jax.ShapeDtypeStruct((block if by_part else block + EXTRA, width), bf16) for _, by_part in other_places(parts)
    ]
    return pl.pallas_call(
        add_core_kernel,
        in_specs=[smem(), vmem(), vmem(), vmem()],
        out_shape=[jax.ShapeDtypeStruct((block, width), f32), jax.ShapeDtypeStruct((2, head.shape[1]), f32)] + sends,
        compiler_params=params(),
        cost_estimate=pl.CostEstimate(flops=1, bytes_accessed=1, transcendentals=0),
        name="add_core",
    )(place, head, mine, other)


def activate_kernel(own_ref, heads_ref, *refs):
    received, (first_ref, head_row_ref) = refs[:-2], refs[-2:]
    block = own_ref.shape[0]
    units = heads_ref.shape[1]
    total = own_ref[...]
    heads = [heads_ref[0:1, :], heads_ref[1:2, :]]
    for ref in received:
        total = total + ref[pl.ds(0, block), :].astype(f32)
        if ref.shape[0] > block:
            tail = ref[pl.ds(block, EXTRA), :].astype(f32)
            heads += [(tail[0:1] + tail[1:2])[:, :units], (tail[2:3] + tail[3:4])[:, :units]]
    first_ref[...] = jnp.tanh(total).astype(bf16)
    head_row_ref[...] = jnp.concatenate(heads, axis=1)


def activate(own, heads, received):
    return pl.pallas_call(
        activate_kernel,
        in_specs=[vmem()] * (2 + len(received)),
        out_shape=[jax.ShapeDtypeStruct(own.shape, bf16), jax.ShapeDtypeStruct((1, 4 * heads.shape[1]), f32)],
        compiler_params=params(),
        cost_estimate=pl.CostEstimate(flops=1, bytes_accessed=1, transcendentals=0),
        name="first_activation",
    )(own, heads, *received)


def two_halves(exact):
    high = exact.astype(bf16)
    low = (exact - high.astype(f32)).astype(bf16)
    return high, low


def tail_rows(exact):
    high, low = two_halves(exact)
    zeros = jnp.zeros((EXTRA - 2, exact.shape[1]), bf16)
    return jnp.concatenate([high, low, zeros], axis=0)


def middle_kernel(chunks, parts, width, *refs):
    pieces = chunks * parts
    place_ref, cot_ref = refs[0], refs[1]
    first_refs = refs[2 : 2 + pieces]
    mid_refs = refs[2 + pieces : 6 + pieces]
    outs = refs[-(3 + parts) :]
    own_ref, value_ref, mid_keep_ref, mid_send_ref = outs[:4]
    send_refs = outs[4:]
    part = place_ref[2]
    block = first_refs[0].shape[0]

    def mid_rows(start):
        return jnp.concatenate([ref[pl.ds(start, width), :] for ref in mid_refs], axis=1)

    def start_of(c, k):
        return pl.multiple_of((c * parts + (part ^ k)) * width, width)

    total = None
    for c in range(chunks):
        for k in range(parts):
            term = jnp.dot(first_refs[c * parts + k][...], mid_rows(start_of(c, k)), preferred_element_type=f32)
            total = term if total is None else total + term
    second_low = jnp.tanh(total).astype(bf16)
    second = second_low.astype(f32)
    head = refs[6 + pieces][...]
    heads = tail_rows(head)
    rows = lax.dot_general(heads, second_low, (((1,), (1,)), ((), ())), preferred_element_type=f32)
    value = rows[0:1] + rows[1:2]
    if width > block:
        value = jnp.concatenate([value, jnp.zeros((1, width - block), f32)], axis=1)
    value_ref[...] = value
    cot = cot_ref[pl.ds(pl.multiple_of(place_ref[3] * block, SUBLANES), block), :1]
    head_part = jnp.sum(cot * second, axis=0, keepdims=True)
    back = (cot * head * (1.0 - second * second)).astype(bf16)
    units = mid_refs[0].shape[1]
    for k in range(parts):
        for c in range(chunks):
            piece = lax.dot_general(
                back, mid_rows(start_of(c, k)), (((1,), (1,)), ((), ())), preferred_element_type=f32
            )
            if k == 0:
                own_ref[pl.ds(c * block, block), :] = piece
            else:
                send_refs[k - 1][pl.ds(c * block, block), :] = piece.astype(bf16)
        if k > 0:
            send_refs[k - 1][pl.ds(chunks * block, EXTRA), :] = tail_rows(value)
    for c in range(chunks):
        for k in range(parts):
            product = lax.dot_general(
                first_refs[c * parts + k][...], back, (((0,), (0,)), ((), ())), preferred_element_type=f32
            ).astype(bf16)
            for p in range(4):
                out = (mid_keep_ref, mid_send_ref)[p % 2]
                out[p // 2, pl.ds(start_of(c, k), width), :] = product[:, p * units : (p + 1) * units]
    for p in range(4):
        out = (mid_keep_ref, mid_send_ref)[p % 2]
        out[p // 2, pl.ds(pieces * width, EXTRA), :] = tail_rows(head_part[:, p * units : (p + 1) * units])


def middle(place, cot, firsts, mids, head, chunks, parts, width, deps=()):
    block = firsts[0].shape[0]
    hidden, units = mids[0].shape
    partial = jax.ShapeDtypeStruct((2, hidden + EXTRA, units), bf16)
    return pl.pallas_call(
        functools.partial(middle_kernel, chunks, parts, width),
        in_specs=[smem()] + [vmem()] * (1 + len(firsts) + 5) + any_specs(deps),
        out_shape=[
            jax.ShapeDtypeStruct((chunks * block, width), f32),
            jax.ShapeDtypeStruct((1, width), f32),
            partial,
            partial,
        ]
        + [jax.ShapeDtypeStruct((chunks * block + EXTRA, width), bf16)] * (parts - 1),
        compiler_params=params(),
        cost_estimate=pl.CostEstimate(flops=1, bytes_accessed=1, transcendentals=0),
        name="value_layers",
    )(place, cot, *firsts, *mids, head, *deps)


def add_tail(left, right, hidden):
    body = left[:hidden].astype(f32) + right[:hidden].astype(f32)
    tails = left[hidden:].astype(f32) + right[hidden:].astype(f32)
    return body.astype(bf16), tails[0:1] + tails[1:2]


def mid_add_kernel(keep_ref, other_ref, *refs):
    own_ref, send_ref = refs[-2:]
    hidden = own_ref.shape[0] - EXTRA
    for at, out in enumerate((own_ref, send_ref)):
        body, tail = add_tail(keep_ref[at], other_ref[at], hidden)
        out[pl.ds(0, hidden), :] = body
        out[pl.ds(hidden, EXTRA), :] = tail_rows(tail)


def mid_add(keep, other, deps=()):
    shape = jax.ShapeDtypeStruct(keep.shape[1:], bf16)
    return pl.pallas_call(
        mid_add_kernel,
        in_specs=[vmem()] * 2 + any_specs(deps),
        out_shape=[shape, shape],
        compiler_params=params(),
        cost_estimate=pl.CostEstimate(flops=1, bytes_accessed=1, transcendentals=0),
        name="mid_gradient_add",
    )(keep, other, *deps)


def mid_final_kernel(own_ref, other_ref, *refs):
    out_ref, head_ref, token_ref = refs[-3:]
    token_ref[...] = jnp.zeros(token_ref.shape, f32)
    body, tail = add_tail(own_ref[...], other_ref[...], out_ref.shape[0])
    out_ref[...] = body
    head_ref[...] = tail


def mid_final(own, other, deps=()):
    hidden = own.shape[0] - EXTRA
    return pl.pallas_call(
        mid_final_kernel,
        in_specs=[vmem()] * 2 + any_specs(deps),
        out_shape=[
            jax.ShapeDtypeStruct((hidden, own.shape[1]), bf16),
            jax.ShapeDtypeStruct((1, own.shape[1]), f32),
            jax.ShapeDtypeStruct((SUBLANES, LANES), f32),
        ],
        compiler_params=params(),
        cost_estimate=pl.CostEstimate(flops=1, bytes_accessed=1, transcendentals=0),
        name="mid_gradient_final",
    )(own, other, *deps)


def back_first_kernel(count, own_ref, value_ref, *refs):
    received = refs[:count]
    first_ref, out_ref, tail_ref = refs[count], *refs[-2:]
    block = first_ref.shape[0]
    value = value_ref[...]
    total = own_ref[...]
    for ref in received:
        tail = ref[pl.ds(block, EXTRA), :].astype(f32)
        value = value + (tail[0:1] + tail[1:2])
        total = total + ref[pl.ds(0, block), :].astype(f32)
    first = first_ref[...].astype(f32)
    out_ref[...] = (total * (1.0 - first * first)).astype(bf16)
    tail_ref[...] = tail_rows(value)


def back_first(own, value, received, first, deps):
    block, width = first.shape
    return pl.pallas_call(
        functools.partial(back_first_kernel, len(received)),
        in_specs=[vmem()] * (3 + len(received)) + any_specs(deps),
        out_shape=[jax.ShapeDtypeStruct((rows, width), bf16) for rows in (block, EXTRA)],
        compiler_params=params(),
        cost_estimate=pl.CostEstimate(flops=1, bytes_accessed=1, transcendentals=0),
        name="back_first",
    )(own, value, *received, first, *deps)


def stack_kernel(count, *refs):
    at = 0
    for ref in refs[:count]:
        refs[-1][pl.ds(at, ref.shape[0]), :] = ref[...]
        at += ref.shape[0]


def stack(pieces, deps):
    rows = sum(piece.shape[0] for piece in pieces)
    return pl.pallas_call(
        functools.partial(stack_kernel, len(pieces)),
        in_specs=[vmem()] * len(pieces) + any_specs(deps),
        out_shape=jax.ShapeDtypeStruct((rows, pieces[0].shape[1]), bf16),
        compiler_params=params(),
        cost_estimate=pl.CostEstimate(flops=1, bytes_accessed=1, transcendentals=0),
        name="stack_parts",
    )(*pieces, *deps)


def turn_kernel(count, *refs):
    out_ref = refs[-1]
    at = 0
    for ref in refs[:count]:
        out_ref[pl.ds(at, ref.shape[1]), :] = ref[...].T
        at += ref.shape[1]


def transposed(arrays, deps):
    cells = sum(array.shape[1] for array in arrays)
    return pl.pallas_call(
        functools.partial(turn_kernel, len(arrays)),
        in_specs=[vmem()] * len(arrays) + any_specs(deps),
        out_shape=jax.ShapeDtypeStruct((cells, arrays[0].shape[0]), bf16),
        compiler_params=params(),
        cost_estimate=pl.CostEstimate(flops=1, bytes_accessed=1, transcendentals=0),
        name="transposed_inputs",
    )(*arrays, *deps)


def first_grad_kernel(parts, block, tiles, *refs):
    place_ref, left_ref = refs[:2]
    stacks = refs[2:6]
    out_ref, value_ref, whole = refs[-3:]
    width = out_ref.shape[1]
    step = pl.program_id(0)
    piece = step // tiles ^ place_ref[2]
    column = pl.ds(pl.multiple_of(step % tiles * width, width), width)
    mine = place_ref[3]
    values = [jnp.zeros((1, block), f32)] * 4
    for t, ref in enumerate(stacks):
        at = mine ^ (2 * (t % 2) + t // 2)
        whole[pl.ds(pl.multiple_of(at * block, block), block), :] = ref[
            pl.ds(pl.multiple_of(piece * block, block), block), column
        ]
        tail = ref[pl.ds(parts * block, EXTRA), :block].astype(f32)
        value = tail[0:1] + tail[1:2]
        for q in range(4):
            values[q] = jnp.where(at == q, value, values[q])
    value_ref[...] = jnp.concatenate(values, axis=1).reshape(4 * block)
    out_ref[...] = jnp.dot(left_ref[...], whole[...], preferred_element_type=f32).astype(bf16)


def first_grad(place, left, stacks, parts, block, deps):
    cells, scenarios = left.shape
    width = stacks[0].shape[1]
    tile = min(width, 256)
    tiles = width // tile
    return pl.pallas_call(
        functools.partial(first_grad_kernel, parts, block, tiles),
        grid=(parts * tiles,),
        in_specs=[smem()] + [vmem()] * 5 + any_specs(deps),
        out_specs=[pl.BlockSpec((cells, tile), lambda i: (0, i)), pl.BlockSpec((scenarios,), lambda i: (0,))],
        out_shape=[pltpu.HBM((cells, parts * width), bf16), jax.ShapeDtypeStruct((scenarios,), f32)],
        scratch_shapes=[pltpu.VMEM((scenarios, tile), bf16)],
        compiler_params=params(),
        cost_estimate=pl.CostEstimate(flops=1, bytes_accessed=1, transcendentals=0),
        name="first_gradient",
    )(place, left, *stacks, *deps)


def local(hist, drift, shocks, shock_table, first_weight, mid_weight, head_weight, cotangent):
    scenarios, rows, columns = hist.shape
    count = lax.axis_size("grid")
    hidden = first_weight.shape[1]
    units = mid_weight.shape[1]
    parts = count // 4
    width = hidden // parts
    block = scenarios // 4
    index = lax.axis_index("grid")
    core, side, part = index & 1, (index >> 1) & 1, index >> 2
    mine = 2 * core + side
    tiles = pltpu.with_memory_space_constraint(to_tiles(hist), pltpu.HBM)

    place = jnp.stack([core, side, part, mine])

    small = [pltpu.with_memory_space_constraint(array, pltpu.HBM) for array in (drift, shocks.T, shock_table.T, cotangent)]
    mids = [mid_weight]
    mids += [swap(mids[0], count, 1), swap(mids[0], count, 2)]
    place, first_rows, last_rows, shifts, band, cot, own_rows, inner = inner_steps(place, tiles, *small)
    inner = inner if rows > 4 else None
    forward = [(i, i + 1) for i in range(count - 1)]
    backward = [(i + 1, i) for i in range(count - 1)]
    below = lax.ppermute(last_rows, "grid", forward)
    above = lax.ppermute(first_rows, "grid", backward)
    first_weight = pltpu.with_memory_space_constraint(first_weight, pltpu.HBM)
    product = None if inner is None else inner_product(inner, first_weight, width, mids[1:])
    low, high = edge_steps(drift, shifts, band, own_rows, below, above, own_rows if product is None else product)
    head = head_weight[None, :]
    keep, send = edge_product(place, head, low, high, first_weight, product, parts, width)
    mids.append(swap(mids[2], count, 1))

    def density_turn(turn, dep, so_far):
        return density_steps(drift, shifts, band, own_rows, below, above, dep, so_far, turn, 2)

    own, heads, *sends = add_core(place, head, keep, swap(send, count, 1))
    flips = [2 * by_side + 4 * by_part for by_side, by_part in other_places(parts)]
    received = [swap(piece, count, flip) for piece, flip in zip(sends, flips)]
    first, head = activate(own, heads, received)
    firsts = [first] + [swap(first, count, 4 * k) for k in range(1, parts)]
    density, token = density_turn(0, first, None)
    own, value, mid_keep, mid_send, *sends = middle(place, cot, firsts, mids, head, 1, parts, width, [token, mids[1], mids[3]])
    received = [swap(piece, count, 4 * (k + 1)) for k, piece in enumerate(sends)]
    density, token = density_turn(1, sends[-1], density)
    back, tail = back_first(own, value, received, first, [token])
    mid_keep, mid_send = mid_add(mid_keep, swap(mid_send, count, 1), [back])
    mid_other = swap(mid_send, count, 2)
    left = transposed([low, high] if inner is None else [low, inner, high], [back])
    pieces = [back] + [swap(back, count, 4 * k) for k in range(1, parts)] + [tail]
    stacks = [stack(pieces, [left, mid_other])]
    stacks += [swap(stacks[0], count, 1), swap(stacks[0], count, 2)]
    grad_mid, grad_head, token = mid_final(mid_keep, mid_other, [stacks[0]])
    stacks.append(swap(stacks[2], count, 1))
    grad_first, value = first_grad(place, left, stacks, parts, block, [token])
    return from_tiles(density, hist.shape), value, grad_first, grad_mid, grad_head[0]


def solution(mesh):
    in_specs = (
        P("groups", "grid", None),
        P(None, "grid", None),
        P("groups", None),
        P("groups", None),
        P(("groups", "grid"), None),
        P("groups", "grid"),
        P(("groups", "grid")),
        P("groups"),
    )
    out_specs = (
        P("groups", "grid", None),
        P("groups"),
        P(("groups", "grid"), None),
        P("groups", "grid"),
        P(("groups", "grid")),
    )
    return jax.shard_map(local, mesh=mesh, in_specs=in_specs, out_specs=out_specs, check_vma=False)
```
